256 devices in a mesh: ctx: 64 (over y, z, x_lo), tp: 4 (over x_hi, core).
Axes of the slice: x: 4 (x_hi: 2, x_lo: 2; x = x_hi * 2 + x_lo), y: 4, z: 8, core: 2. Of those that a mesh axis runs over, the one named last changes fastest.
Arguments:
- tokens: bfloat16 [8192, 2048], P('ctx'), may hold values from -2.5 to 2.5
- project_weight: bfloat16 [2048, 3, 1024], P(None, None, 'tp'), may hold values from -12 to 12
- output_weight: bfloat16 [1024, 2048], P('tp'), may hold values from -0.5 to 0.5
- distance_slope: float32 [8], P('tp'), may hold values from 5e-06 to 0.05
- cache_keys: bfloat16 [16384, 1024], P('ctx', 'tp'), may hold values from -6 to 6
- cache_values: bfloat16 [16384, 1024], P('ctx', 'tp'), may hold values from -6 to 6
- cache_count: int32 [64], P('ctx'), may hold values from 1 to 256, 10240 in all
- short_project: bfloat16 [2048, 3, 1024], P(None, None, 'tp'), may hold values from -12 to 12
- short_output: bfloat16 [1024, 2048], P('tp'), may hold values from -0.5 to 0.5
- short_slope: float32 [8], P('tp'), may hold values from 5e-06 to 0.37
Outputs:
- mixed: bfloat16 [8192, 2048], P('ctx', 'tp')
The draws below stay inside these ranges and needn't reach their ends.
Inputs may be any that keep to these rules, and one draw needn't show every extreme that they name: `cache_count`: slots at and past a device's count hold values that no output reads. The counts sum to 10240 and one device is full.
All inputs are finite; a program needn't handle non-finite values.
Results may differ from the reference program's by a relative error of at most 0.039.
Values may be sent and summed in bfloat16 or wider, within the bound.
No kernel may reach another device: no remote copies, remote signals or barrier semaphores. Data moves between devices by JAX's collectives and lax.ppermute only.
A program may use at most 128 MiB of HBM per device.

```python
import math
import jax
import jax.numpy as jnp
import numpy as np
from jax import lax

D = 2048
HEADS = 8
HS = 128
GROUP = 4
CACHE_DEV = 256
OWNERS = 64
TOKENS = 8192
POOLED = 2048
CACHE = 16384
INNER = 1024


def projection_draw(key, sharpness):
    first = jax.random.fold_in(key, 0)
    base = jax.random.truncated_normal(first, -4.0, 4.0, (D, 3, INNER)) * D ** (-0.5)
    query = sharpness * base[:, 0, :]
    return jnp.stack([query, base[:, 1, :], base[:, 2, :]], axis=1).astype(jnp.bfloat16)


def slope_draw(key, lowest, highest):
    return jnp.exp(jax.random.uniform(key, (HEADS,), minval=lowest, maxval=highest)).astype(jnp.float32)


def draw_tokens(key, part):
    key = jax.random.fold_in(key, 11)
    first = jax.random.fold_in(key, 0)
    return (0.25 * jax.random.truncated_normal(first, -6.0, 6.0, (TOKENS, D))).astype(jnp.bfloat16)


def draw_project_weight(key, part):
    key = jax.random.fold_in(key, 23)
    return projection_draw(key, 3.0)


def draw_short_project(key, part):
    key = jax.random.fold_in(key, 37)
    return projection_draw(key, 3.0)


def draw_distance_slope(key, part):
    key = jax.random.fold_in(key, 41)
    return slope_draw(key, -11.5, -3.0)


def draw_short_slope(key, part):
    key = jax.random.fold_in(key, 53)
    return slope_draw(key, -11.5, -1.0)


def level_of(key, dims, shards, low, top_value):
    def one(position, blocks):
        steps = jax.random.uniform(jax.random.fold_in(jax.random.fold_in(key, 6), position), (blocks,), jnp.float32, low / len(shards), top_value / len(shards))
        return jnp.repeat(jnp.exp(steps), dims[position] // blocks).reshape((-1,) + (1,) * (len(dims) - position - 1))

    factor_of = one(*shards[0])
    for cut in shards[1:]:
        factor_of = factor_of * one(*cut)
    return factor_of


def length_profile(amount, total, most, skew):
    weights = [(1 << 20) // math.isqrt(rank ** skew) + 1 for rank in range(2, amount + 1)]
    surplus, counts = total - most - (amount - 1), [1] * (amount - 1)
    while surplus > 0:
        movable = [i for i in range(amount - 1) if counts[i] < most]
        mass, remaining = sum([weights[i] for i in movable]), surplus
        for i in movable:
            extra = min(most - counts[i], max(1, remaining * weights[i] // mass), surplus)
            counts[i] = counts[i] + extra
            surplus = surplus - extra
    return np.array([most] + counts)


def ragged(stream_key, number_of, total, reach, skew):
    if number_of == 2:
        one = jax.random.randint(stream_key, (), max(1, total - reach), min(reach, total - 1) + 1)
        return jnp.stack([one, total - one])
    sizes = jnp.asarray(length_profile(number_of, total, reach, skew), jnp.int32)
    twos = (number_of - 1) // 2
    source_of, receiver = sizes[1:1 + 2 * twos:2], sizes[2:2 + 2 * twos:2]
    room = jnp.minimum(source_of - 1, reach - receiver)
    moved = jax.random.randint(jax.random.fold_in(stream_key, 1), (twos,), 0, 1 << 20) % (room + 1)
    sizes = sizes.at[1:1 + 2 * twos:2].set(source_of - moved).at[2:2 + 2 * twos:2].set(receiver + moved)
    return sizes[jax.random.permutation(jax.random.fold_in(stream_key, 2), number_of)]


def normal_values(stream_key, shape, scale, reach, cuts=(), kind=jnp.bfloat16):
    array = jax.random.normal(stream_key, shape, jnp.float32) * scale
    if len(cuts) > 0:
        array = level_of(stream_key, shape, cuts, -0.22, 0.18) * array
    return jnp.clip(array, min=-reach, max=reach).astype(kind)


def setup_inputs(seed: int = 0) -> dict:
    keys = jax.random.split(jax.random.key(seed), 11)
    return {
        "tokens": draw_tokens(jax.random.fold_in(keys[10], 71), 0),
        "project_weight": draw_project_weight(jax.random.fold_in(keys[10], 71), 0),
        "output_weight": normal_values(keys[2], (INNER, D), HS ** -0.5, 0.5, ((0, 4),)),
        "distance_slope": draw_distance_slope(jax.random.fold_in(keys[10], 71), 0),
        "cache_keys": normal_values(keys[4], (CACHE, INNER), 1.0, 6.0, ((0, 64), (1, 4))),
        "cache_values": normal_values(keys[5], (CACHE, INNER), 1.0, 6.0, ((0, 64), (1, 4))),
        "cache_count": ragged(keys[6], OWNERS, CACHE_DEV * OWNERS * 5 // 8, CACHE_DEV, 2).astype(jnp.int32),
        "short_project": draw_short_project(jax.random.fold_in(keys[10], 71), 0),
        "short_output": normal_values(keys[8], (INNER, D), HS ** -0.5, 0.5, ((0, 4),)),
        "short_slope": draw_short_slope(jax.random.fold_in(keys[10], 71), 0),
    }


NEG = -1e+30

def rms_rows(row_block):
    values = row_block.astype(jnp.float32)
    scaled = values * lax.rsqrt(lax.optimization_barrier(jnp.mean(values * values, axis=-1, keepdims=True)) + 1e-06)
    return scaled.astype(jnp.bfloat16)

def project(normed, weight):
    row_count = normed.shape[0]
    mixed = jnp.dot(normed, weight.reshape(D, 3 * INNER), preferred_element_type=jnp.float32)
    mixed = mixed.reshape(row_count, 3, INNER).astype(jnp.bfloat16)
    return (mixed[:, 0], mixed[:, 1], mixed[:, 2])

def attend_all(queries, key_rows, value_rows, query_pos, key_pos, key_live, slopes):
    row_count = queries.shape[0]
    row_block = math.gcd(row_count, 512)
    block_count = row_count // row_block

    def one_head(head_index):
        query_head = lax.dynamic_slice_in_dim(queries, head_index * HS, HS, 1)
        key_head = lax.dynamic_slice_in_dim(key_rows, head_index * HS, HS, 1)
        value_head = lax.dynamic_slice_in_dim(value_rows, head_index * HS, HS, 1)
        slope = slopes[head_index]

        def one_block(block_index):
            query_part = lax.dynamic_slice_in_dim(query_head, block_index * row_block, row_block, 0)
            pos_part = lax.dynamic_slice_in_dim(query_pos, block_index * row_block, row_block, 0)
            scores = jnp.dot(query_part, key_head.T, preferred_element_type=jnp.float32) * HS ** (-0.5)
            scores = scores - slope * (pos_part[:, None] - key_pos[None, :])
            usable = key_live[None, :] & (key_pos[None, :] <= pos_part[:, None])
            scores = jnp.where(usable, scores, NEG)
            row_top = lax.optimization_barrier(jnp.max(scores, axis=1, keepdims=True))
            weights = jnp.where(usable, jnp.exp(scores - row_top), 0.0).astype(jnp.bfloat16)
            numer = jnp.dot(weights, value_head, preferred_element_type=jnp.float32)
            return numer / lax.optimization_barrier(jnp.sum(weights.astype(jnp.float32), axis=1, keepdims=True))
        result = lax.map(one_block, jnp.arange(block_count, dtype=jnp.int32))
        return result.reshape(row_count, HS)
    per_head = lax.map(one_head, jnp.arange(HEADS, dtype=jnp.int32))
    return jnp.transpose(per_head, (1, 0, 2)).reshape(row_count, INNER).astype(jnp.bfloat16)

def reference(tokens, project_weight, output_weight, distance_slope, cache_keys, cache_values, cache_count, short_project, short_output, short_slope):
    normed = rms_rows(tokens)
    queries, key_rows, value_rows = project(normed, project_weight)
    live_prefix = (jnp.cumsum(cache_count) - cache_count).astype(jnp.int32)
    cached_total = jnp.sum(cache_count).astype(jnp.int32)
    slot_all = jnp.arange(CACHE, dtype=jnp.int32)
    owner_index = slot_all // CACHE_DEV
    slot_index = slot_all - owner_index * CACHE_DEV
    cache_live = slot_index < cache_count[owner_index]
    cache_pos = (live_prefix[owner_index] + slot_index).astype(jnp.float32)
    query_pos = (cached_total + jnp.arange(TOKENS, dtype=jnp.int32)).astype(jnp.float32)
    all_keys = jnp.concatenate([cache_keys, key_rows], axis=0)
    all_values = jnp.concatenate([cache_values, value_rows], axis=0)
    all_pos = jnp.concatenate([cache_pos, query_pos], axis=0)
    all_live = jnp.concatenate([cache_live, jnp.ones((TOKENS,), dtype=bool)], axis=0)
    attended = attend_all(queries, all_keys, all_values, query_pos, all_pos, all_live, distance_slope)
    layer_out = (tokens.astype(jnp.float32) + jnp.dot(attended, output_weight, preferred_element_type=jnp.float32)).astype(jnp.bfloat16)
    shifted = jnp.concatenate([jnp.zeros((GROUP - 1, D), jnp.bfloat16), layer_out[:TOKENS - GROUP + 1]], axis=0)
    pooled = lax.optimization_barrier(jnp.mean(shifted.reshape(POOLED, GROUP, D).astype(jnp.float32), axis=1)).astype(jnp.bfloat16)
    short_query, short_key, short_value = project(rms_rows(pooled), short_project)
    group_pos = jnp.arange(POOLED, dtype=jnp.int32).astype(jnp.float32)
    short_attended = attend_all(short_query, short_key, short_value, group_pos, group_pos, jnp.ones((POOLED,), dtype=bool), short_slope)
    short_branch = jnp.dot(short_attended, short_output, preferred_element_type=jnp.float32)
    lifted = jnp.repeat(short_branch, GROUP, axis=0)
    return (layer_out.astype(jnp.float32) + lifted).astype(jnp.bfloat16)
```

```python
import functools
import math

import jax
import jax.numpy as jnp
from jax import lax
from jax.experimental import pallas as pl
from jax.experimental.pallas import tpu as pltpu
from jax.sharding import Mesh, PartitionSpec as P

HS = 128
GROUP = 4
NEG = -1e30
LOG2E = math.log2(math.e)
SCALE2 = HS ** -0.5 * LOG2E

VMEM = pltpu.VMEM
SMEM = pltpu.SMEM
F32 = jnp.float32
BF16 = jnp.bfloat16


def cost(flops, moved, trans=0):
    return pl.CostEstimate(flops=flops, bytes_accessed=moved, transcendentals=trans)


def params():
    return pltpu.CompilerParams(vmem_limit_bytes=48 * 1024 * 1024)


def rms_scaled(values):
    inv = lax.rsqrt(jnp.mean(values * values, axis=-1, keepdims=True) + 1e-06)
    return (values * inv).astype(BF16)


def dot_t(a, b):
    return lax.dot_general(a, b, (((1,), (1,)), ((), ())), preferred_element_type=F32)


def three_parts(x):
    hi = x.astype(BF16).astype(F32)
    mid = (x - hi).astype(BF16).astype(F32)
    lo = (x - hi - mid).astype(BF16).astype(F32)
    return hi, mid, lo


def project_kernel(copies, tok_ref, w_ref, bq_ref, bkv_ref, normed):
    step = pl.program_id(0)

    @pl.when(step == 0)
    def _():
        normed[...] = rms_scaled(tok_ref[...].astype(F32))

    out = jnp.dot(normed[...], w_ref[0], preferred_element_type=F32)

    @pl.when(step == 0)
    def _():
        scaled = (out * SCALE2).astype(BF16)
        for c in range(copies):
            bq_ref[c] = scaled

    @pl.when(step == 1)
    def _():
        rounded = out.astype(BF16)
        for c in range(copies):
            bkv_ref[c, 0] = rounded

    @pl.when(step == 2)
    def _():
        rounded = out.astype(BF16)
        for c in range(copies):
            bkv_ref[c, 1] = rounded


def project(rows, weight3, qcopies, kvcopies):
    n, d = rows.shape
    width = weight3.shape[2]
    assert qcopies == kvcopies
    return pl.pallas_call(
        functools.partial(project_kernel, qcopies),
        grid=(3,),
        in_specs=[
            pl.BlockSpec((n, d), lambda i: (0, 0)),
            pl.BlockSpec((1, d, width), lambda i: (i, 0, 0)),
        ],
        out_specs=[
            pl.BlockSpec((qcopies, n, width), lambda i: (0, 0, 0)),
            pl.BlockSpec((kvcopies, 2, n, width), lambda i: (0, 0, 0, 0)),
        ],
        out_shape=[
            jax.ShapeDtypeStruct((qcopies, n, width), BF16),
            jax.ShapeDtypeStruct((kvcopies, 2, n, width), BF16),
        ],
        scratch_shapes=[VMEM((n, d), BF16)],
        compiler_params=params(),
        cost_estimate=cost(6 * n * d * width, 2 * (n * d + 3 * d * width)),
        name="project",
    )(rows, weight3)


def attend_kernel(
    heads, idx_ref, counts_ref, slope_ref, q_ref, kc_ref, vc_ref, kv_ref, out_ref, prefix, bias
):
    tile = pl.program_id(0)
    y, z, xl = idx_ref[0], idx_ref[1], idx_ref[2]
    nq, rows, _ = q_ref.shape
    peers, slots, _ = kc_ref.shape
    span = kv_ref.shape[2]
    owners = counts_ref.shape[0]
    nc = peers * slots
    ns = peers * span

    @pl.when(tile == 0)
    def _():
        def one(i, total):
            prefix[i] = total
            return total + counts_ref[i]

        total = lax.fori_loop(0, owners, one, jnp.int32(0))
        for j in range(peers):
            ctx = (j // 2) * 16 + z * 2 + (j % 2)
            slot = lax.broadcasted_iota(jnp.int32, (1, slots), 1)
            live = slot < counts_ref[ctx]
            pos = (slot + (prefix[ctx] - total)).astype(F32)
            spot = (lax.broadcasted_iota(jnp.int32, (1, span), 1) + ctx * span).astype(F32)
            for h in range(heads):
                slope = slope_ref[h] * LOG2E
                bias[h : h + 1, j * slots : (j + 1) * slots] = jnp.where(live, slope * pos, NEG)
                bias[h : h + 1, nc + j * span : nc + (j + 1) * span] = slope * spot

    total_rows = nq * rows
    row = lax.broadcasted_iota(jnp.int32, (total_rows, 1), 0)
    row_pos = (y * 16 + xl) * rows + (tile * nq + row // rows) * (2 * rows) + row % rows
    key = lax.broadcasted_iota(jnp.int32, (1, ns), 1)
    block = key // span
    key_pos = ((block // 2) * 16 + z * 2 + block % 2) * span + key % span
    usable = key_pos <= row_pos
    lane = lax.broadcasted_iota(jnp.int32, (total_rows, HS), 1)
    packed = jnp.zeros((total_rows, HS), F32)
    for h in range(heads):
        cols = slice(h * HS, (h + 1) * HS)
        q = q_ref[:, :, cols].reshape(total_rows, HS)
        s1 = dot_t(q, kc_ref[:, :, cols].reshape(nc, HS)) + bias[h : h + 1, :nc]
        s2 = dot_t(q, kv_ref[:, 0, :, cols].reshape(ns, HS)) + bias[h : h + 1, nc:]
        s2 = jnp.where(usable, s2, NEG)
        top = jnp.maximum(
            jnp.max(s1, axis=1, keepdims=True), jnp.max(s2, axis=1, keepdims=True)
        )
        p1 = jnp.exp2(s1 - top).astype(BF16)
        p2 = jnp.exp2(s2 - top).astype(BF16)
        v1 = vc_ref[:, :, cols].reshape(nc, HS)
        v2 = kv_ref[:, 1, :, cols].reshape(ns, HS)
        a1 = jnp.concatenate([v1, jnp.ones_like(v1)], axis=1)
        a2 = jnp.concatenate([v2, jnp.ones_like(v2)], axis=1)
        both = jnp.dot(p1, a1, preferred_element_type=F32) + jnp.dot(
            p2, a2, preferred_element_type=F32
        )
        weight_total = both[:, HS:]
        part = (both[:, :HS] / weight_total).astype(BF16)
        out_ref[:, :rows, cols] = part.reshape(nq, rows, HS)
        level = top + jnp.log2(weight_total)
        for k, piece in enumerate(three_parts(level)):
            packed = jnp.where(lane == 3 * h + k, piece, packed)
    for b in range(nq):
        turned = jnp.transpose(packed[b * rows : (b + 1) * rows])[:16]
        out_ref[b, rows:, :] = jnp.concatenate(
            [turned, jnp.zeros_like(turned)], axis=1
        ).astype(BF16)


def attend(idx, counts, slopes, q, kc, vc, kv):
    blocks, rows, width = q.shape
    heads = width // HS
    peers, slots, _ = kc.shape
    span = kv.shape[2]
    keys = peers * (slots + span)
    nq = 2
    fixed = lambda shape: pl.BlockSpec(shape, lambda i, *_: (0,) * len(shape))
    return pl.pallas_call(
        functools.partial(attend_kernel, heads),
        grid_spec=pltpu.PrefetchScalarGridSpec(
            num_scalar_prefetch=3,
            grid=(blocks // nq,),
            in_specs=[
                pl.BlockSpec((nq, rows, width), lambda i, *_: (i, 0, 0)),
                fixed(kc.shape),
                fixed(vc.shape),
                fixed(kv.shape),
            ],
            out_specs=pl.BlockSpec((nq, rows + 16, width), lambda i, *_: (i, 0, 0)),
            scratch_shapes=[SMEM((counts.shape[0],), jnp.int32), VMEM((8, keys), F32)],
        ),
        out_shape=jax.ShapeDtypeStruct((blocks, rows + 16, width), BF16),
        compiler_params=params(),
        cost_estimate=cost(
            4 * blocks * rows * keys * width, 4 * keys * width, blocks * rows * keys * heads
        ),
        name="attend",
    )(idx, counts, slopes, q, kc, vc, kv)


def merge_kernel(heads, copies, parts_ref, out_ref):
    sources, padded, width = parts_ref.shape
    rows = padded - 16
    levels = jnp.concatenate(
        [parts_ref[s, rows:, :HS].astype(F32) for s in range(sources)], axis=0
    )
    turned = jnp.transpose(levels)
    for h in range(heads):
        cols = slice(h * HS, (h + 1) * HS)
        level = []
        for s in range(sources):
            at = s * 16 + 3 * h
            level.append(
                (turned[:, at : at + 1] + turned[:, at + 1 : at + 2]) + turned[:, at + 2 : at + 3]
            )
        top = functools.reduce(jnp.maximum, level)
        total = jnp.zeros((rows, 1), F32)
        acc = jnp.zeros((rows, HS), F32)
        for s in range(sources):
            weight = jnp.exp2(level[s] - top)
            total = total + weight
            acc = acc + weight * parts_ref[s, :rows, cols].astype(F32)
        done = (acc / total).astype(BF16)
        for c in range(copies):
            out_ref[c, :, cols] = done


def merge(parts, copies):
    sources, padded, width = parts.shape
    rows = padded - 16
    return pl.pallas_call(
        functools.partial(merge_kernel, width // HS, copies),
        out_shape=jax.ShapeDtypeStruct((copies, rows, width), BF16),
        compiler_params=params(),
        cost_estimate=cost(4 * sources * rows * width, 2 * sources * padded * width),
        name="merge",
    )(parts)


def layer_kernel(tok_ref, att_ref, w_ref, out_ref):
    parts, rows, width = att_ref.shape
    acc = tok_ref[...].astype(F32)
    for t in range(parts):
        acc = acc + jnp.dot(
            att_ref[t], w_ref[t * width : (t + 1) * width], preferred_element_type=F32
        )
    out_ref[...] = acc.astype(BF16)


def layer_output(tokens, att, weight):
    rows, d = tokens.shape
    step = 512
    inner = weight.shape[0]
    return pl.pallas_call(
        layer_kernel,
        grid=(d // step,),
        in_specs=[
            pl.BlockSpec((rows, step), lambda i: (0, i)),
            pl.BlockSpec(att.shape, lambda i: (0, 0, 0)),
            pl.BlockSpec((inner, step), lambda i: (0, i)),
        ],
        out_specs=pl.BlockSpec((rows, step), lambda i: (0, i)),
        out_shape=jax.ShapeDtypeStruct((rows, d), BF16),
        compiler_params=params(),
        cost_estimate=cost(2 * rows * d * inner, 2 * inner * d),
        name="layer_output",
    )(tokens, att, weight)


def short_project_kernel(copies, lay_ref, rim_ref, w_ref, bq_ref, bkv_ref, normed):
    step = pl.program_id(0)
    rows = lay_ref.shape[0]
    groups = rows // GROUP
    rim_rows = rim_ref.shape[0]

    @pl.when(step == 0)
    def _():
        g = lax.broadcasted_iota(jnp.int32, (groups, rows), 0) * GROUP
        t = lax.broadcasted_iota(jnp.int32, (groups, rows), 1)
        own = jnp.where((t <= g) & (t > g - GROUP), 1.0 / GROUP, 0.0).astype(BF16)
        g = lax.broadcasted_iota(jnp.int32, (groups, rim_rows), 0) * GROUP
        t = lax.broadcasted_iota(jnp.int32, (groups, rim_rows), 1) - rim_rows
        before = jnp.where(t > g - GROUP, 1.0 / GROUP, 0.0).astype(BF16)
        pooled = jnp.dot(own, lay_ref[...], preferred_element_type=F32) + jnp.dot(
            before, rim_ref[...], preferred_element_type=F32
        )
        normed[...] = rms_scaled(pooled.astype(BF16).astype(F32))

    out = jnp.dot(normed[...], w_ref[0], preferred_element_type=F32)

    @pl.when(step == 0)
    def _():
        scaled = (out * SCALE2).astype(BF16)
        for c in range(copies):
            bq_ref[c] = scaled

    @pl.when(step == 1)
    def _():
        rounded = out.astype(BF16)
        for c in range(copies):
            bkv_ref[c, 0] = rounded

    @pl.when(step == 2)
    def _():
        rounded = out.astype(BF16)
        for c in range(copies):
            bkv_ref[c, 1] = rounded


def short_project(layer, rim, weight3, copies):
    n, d = layer.shape
    groups = n // GROUP
    width = weight3.shape[2]
    return pl.pallas_call(
        functools.partial(short_project_kernel, copies),
        grid=(3,),
        in_specs=[
            pl.BlockSpec((n, d), lambda i: (0, 0)),
            pl.BlockSpec(rim.shape, lambda i: (0, 0)),
            pl.BlockSpec((1, d, width), lambda i: (i, 0, 0)),
        ],
        out_specs=[
            pl.BlockSpec((copies, groups, width), lambda i: (0, 0, 0)),
            pl.BlockSpec((copies, 2, groups, width), lambda i: (0, 0, 0, 0)),
        ],
        out_shape=[
            jax.ShapeDtypeStruct((copies, groups, width), BF16),
            jax.ShapeDtypeStruct((copies, 2, groups, width), BF16),
        ],
        scratch_shapes=[VMEM((groups, d), BF16)],
        compiler_params=params(),
        cost_estimate=cost(6 * groups * d * width, 2 * (n * d + 3 * d * width)),
        name="short_project",
    )(layer, rim, weight3)


def short_attend_kernel(heads, idx_ref, slope_ref, q_ref, kv_ref, out_ref):
    y, z, xl = idx_ref[0], idx_ref[1], idx_ref[2]
    blocks, groups, width = q_ref.shape
    peers = kv_ref.shape[0]
    nr, nk = blocks * groups, peers * groups
    row = lax.broadcasted_iota(jnp.int32, (nr, 1), 0)
    row_pos = (y * 16 + xl + (row // groups) * 2) * groups + row % groups
    key = lax.broadcasted_iota(jnp.int32, (1, nk), 1)
    block = key // groups
    key_pos = ((block // 2) * 16 + z * 2 + block % 2) * groups + key % groups
    usable = key_pos <= row_pos
    spot = key_pos.astype(F32)
    lane = lax.broadcasted_iota(jnp.int32, (nr, HS), 1)
    packed = jnp.zeros((nr, HS), F32)
    for h in range(heads):
        cols = slice(h * HS, (h + 1) * HS)
        q = q_ref[:, :, cols].reshape(nr, HS)
        s = dot_t(q, kv_ref[:, 0, :, cols].reshape(nk, HS)) + (slope_ref[h] * LOG2E) * spot
        s = jnp.where(usable, s, NEG)
        top = jnp.max(s, axis=1, keepdims=True)
        p = jnp.exp2(s - top).astype(BF16)
        v = kv_ref[:, 1, :, cols].reshape(nk, HS)
        both = jnp.dot(
            p, jnp.concatenate([v, jnp.ones_like(v)], axis=1), preferred_element_type=F32
        )
        weight_total = both[:, HS:]
        part = (both[:, :HS] / weight_total).astype(BF16)
        out_ref[:, :, cols] = part.reshape(blocks, groups, HS)
        level = top + jnp.log2(weight_total)
        for k, piece in enumerate(three_parts(level)):
            packed = jnp.where(lane == 3 * h + k, piece, packed)
    out_ref[:, :, width:] = packed.astype(BF16).reshape(blocks, groups, HS)


def short_attend(idx, slopes, q, kv):
    blocks, groups, width = q.shape
    smem = pl.BlockSpec(memory_space=SMEM)
    vmem = pl.BlockSpec(memory_space=VMEM)
    keys = kv.shape[0] * groups
    return pl.pallas_call(
        functools.partial(short_attend_kernel, width // HS),
        in_specs=[smem, smem, vmem, vmem],
        out_specs=vmem,
        out_shape=jax.ShapeDtypeStruct((blocks, groups, width + HS), BF16),
        compiler_params=params(),
        cost_estimate=cost(4 * blocks * groups * keys * width, 4 * keys * width),
        name="short_attend",
    )(idx, slopes, q, kv)


def short_merge_kernel(heads, copies, parts_ref, out_ref):
    sources, rows, padded = parts_ref.shape
    width = padded - HS
    for h in range(heads):
        cols = slice(h * HS, (h + 1) * HS)
        level = []
        for s in range(sources):
            lev = parts_ref[s, :, width:].astype(F32)
            level.append(
                (lev[:, 3 * h : 3 * h + 1] + lev[:, 3 * h + 1 : 3 * h + 2])
                + lev[:, 3 * h + 2 : 3 * h + 3]
            )
        top = functools.reduce(jnp.maximum, level)
        total = jnp.zeros((rows, 1), F32)
        acc = jnp.zeros((rows, HS), F32)
        for s in range(sources):
            weight = jnp.exp2(level[s] - top)
            total = total + weight
            acc = acc + weight * parts_ref[s, :, cols].astype(F32)
        done = (acc / total).astype(BF16)
        for c in range(copies):
            out_ref[c, :, cols] = done


def short_merge(parts, copies):
    sources, rows, padded = parts.shape
    width = padded - HS
    return pl.pallas_call(
        functools.partial(short_merge_kernel, width // HS, copies),
        out_shape=jax.ShapeDtypeStruct((copies, rows, width), BF16),
        compiler_params=params(),
        cost_estimate=cost(4 * sources * rows * width, 2 * sources * rows * padded),
        name="short_merge",
    )(parts)


def final_kernel(tp_ref, lay_ref, att_ref, w_ref, out_ref):
    parts, groups, width = att_ref.shape
    rows = lay_ref.shape[0]
    t = lax.broadcasted_iota(jnp.int32, (rows, groups), 0) // GROUP
    g = lax.broadcasted_iota(jnp.int32, (rows, groups), 1)
    spread = jnp.where(t == g, 1.0, 0.0).astype(BF16)
    acc = lay_ref[...].astype(F32)
    branch = jnp.zeros(acc.shape, F32)
    for p in range(parts):
        lifted = jnp.dot(spread, att_ref[p], preferred_element_type=F32).astype(BF16)
        branch = branch + jnp.dot(
            lifted, w_ref[p * width : (p + 1) * width], preferred_element_type=F32
        )
    out_ref[...] = (acc + branch).astype(BF16)


def final_sum(tp_index, layer, att, weight):
    rows, d = layer.shape
    parts = att.shape[0]
    cols = d // parts
    inner = weight.shape[0]
    return pl.pallas_call(
        final_kernel,
        grid_spec=pltpu.PrefetchScalarGridSpec(
            num_scalar_prefetch=1,
            grid=(1,),
            in_specs=[
                pl.BlockSpec((rows, cols), lambda i, tp: (0, tp[0])),
                pl.BlockSpec(att.shape, lambda i, tp: (0, 0, 0)),
                pl.BlockSpec((inner, cols), lambda i, tp: (0, tp[0])),
            ],
            out_specs=pl.BlockSpec((rows, cols), lambda i, tp: (0, 0)),
        ),
        out_shape=jax.ShapeDtypeStruct((rows, cols), BF16),
        compiler_params=params(),
        cost_estimate=cost(2 * rows * cols * inner, 2 * inner * cols),
        name="final_sum",
    )(tp_index, layer, att, weight)


def exchange(blocks, axis):
    return lax.all_to_all(blocks, axis, 0, 0)


def spread_to(block, axis, copies):
    return exchange(jnp.broadcast_to(block[None], (copies,) + block.shape), axis)


def on_device(
    tokens,
    project_weight,
    output_weight,
    distance_slope,
    cache_keys,
    cache_values,
    cache_count,
    short_project_weight,
    short_output,
    short_slope,
):
    ctx_axes = ("y", "z", "xl")
    key_axes = ("y", "xl")
    nk = lax.axis_size("y") * lax.axis_size("xl")
    nq = lax.axis_size("z")
    tp = lax.axis_size("tp")
    idx = jnp.stack([lax.axis_index("y"), lax.axis_index("z"), lax.axis_index("xl")]).astype(
        jnp.int32
    )
    tp_index = lax.axis_index("tp").astype(jnp.int32).reshape(1)

    counts = lax.all_gather(cache_count, ctx_axes, axis=0, tiled=True)
    out_weight = lax.all_gather(output_weight, "tp", axis=0, tiled=True)
    short_out_weight = lax.all_gather(short_output, "tp", axis=0, tiled=True)
    kc = spread_to(cache_keys, key_axes, nk)
    vc = spread_to(cache_values, key_axes, nk)

    bq, bkv = project(tokens, jnp.transpose(project_weight, (1, 0, 2)), nq, nk)
    q = exchange(bq, "z")
    kv = exchange(bkv, key_axes)
    parts = attend(idx, counts, distance_slope, q, kc, vc, kv)
    att = exchange(merge(exchange(parts, "z"), tp), "tp")
    layer = layer_output(tokens, att, out_weight)

    n = lax.axis_size(ctx_axes)
    rim = lax.ppermute(layer[-16:], ctx_axes, [(i, i + 1) for i in range(n - 1)])
    sbq, sbkv = short_project(layer, rim, jnp.transpose(short_project_weight, (1, 0, 2)), nq)
    sq = exchange(sbq, "z")
    skv = exchange(sbkv, key_axes)
    sparts = short_attend(idx, short_slope, sq, skv)
    satt = exchange(short_merge(exchange(sparts, "z"), tp), "tp")
    return final_sum(tp_index, layer, satt, short_out_weight)


def solution(mesh):
    split = Mesh(mesh.devices.reshape(4, 8, 2, 4), ("y", "z", "xl", "tp"))
    ctx = ("y", "z", "xl")
    return jax.shard_map(
        on_device,
        mesh=split,
        in_specs=(
            P(ctx, None),
            P(None, None, "tp"),
            P("tp", None),
            P("tp"),
            P(ctx, "tp"),
            P(ctx, "tp"),
            P(ctx),
            P(None, None, "tp"),
            P("tp", None),
            P("tp"),
        ),
        out_specs=P(ctx, "tp"),
        check_vma=False,
    )
```

```python
import functools
import math

import jax
import jax.numpy as jnp
from jax import lax
from jax.experimental import pallas as pl
from jax.experimental.pallas import tpu as pltpu
from jax.sharding import Mesh, PartitionSpec as P

HS = 128
GROUP = 4
NEG = -1e30
LOG2E = math.log2(math.e)
SCALE2 = HS ** -0.5 * LOG2E

VMEM = pltpu.VMEM
SMEM = pltpu.SMEM
F32 = jnp.float32
BF16 = jnp.bfloat16


def cost(flops, moved, trans=0):
    return pl.CostEstimate(flops=flops, bytes_accessed=moved, transcendentals=trans)


def params(mib):
    return pltpu.CompilerParams(vmem_limit_bytes=mib * 1024 * 1024)


def rms_scaled(values):
    inv = lax.rsqrt(jnp.mean(values * values, axis=-1, keepdims=True) + 1e-06)
    return (values * inv).astype(BF16)


def dot_t(a, b):
    return lax.dot_general(a, b, (((1,), (1,)), ((), ())), preferred_element_type=F32)


def three_parts(x):
    hi = x.astype(BF16).astype(F32)
    mid = (x - hi).astype(BF16).astype(F32)
    lo = (x - hi - mid).astype(BF16).astype(F32)
    return hi, mid, lo


def project_kernel(tok_ref, w_ref, q_ref, kv_ref, normed):
    step = pl.program_id(0)

    @pl.when(step == 0)
    def _():
        normed[...] = rms_scaled(tok_ref[...].astype(F32))

    out = jnp.dot(normed[...], w_ref[0], preferred_element_type=F32)
    store_projection(step, out, q_ref, kv_ref)


def store_projection(step, out, q_ref, kv_ref):
    @pl.when(step == 0)
    def _():
        q_ref[...] = (out * SCALE2).astype(BF16)

    @pl.when(step == 1)
    def _():
        kv_ref[0] = out.astype(BF16)

    @pl.when(step == 2)
    def _():
        kv_ref[1] = out.astype(BF16)


def project(rows, weight3):
    n, d = rows.shape
    width = weight3.shape[2]
    return pl.pallas_call(
        project_kernel,
        grid=(3,),
        in_specs=[
            pl.BlockSpec((n, d), lambda i: (0, 0)),
            pl.BlockSpec((1, d, width), lambda i: (i, 0, 0)),
        ],
        out_specs=[
            pl.BlockSpec((n, width), lambda i: (0, 0)),
            pl.BlockSpec((2, n, width), lambda i: (0, 0, 0)),
        ],
        out_shape=[
            jax.ShapeDtypeStruct((n, width), BF16),
            jax.ShapeDtypeStruct((2, n, width), BF16),
        ],
        scratch_shapes=[VMEM((n, d), BF16)],
        compiler_params=params(12),
        cost_estimate=cost(6 * n * d * width, 2 * (n * d + 3 * d * width)),
        name="project",
    )(rows, weight3)


def attend_kernel(blocks, cached, idx_ref, counts_ref, slope_ref, *refs):
    operands = 1 + max(b[0] for b in blocks)
    q_ref, refs = refs[0], refs[1:]
    key_refs, refs = refs[:operands], refs[operands:]
    if cached:
        acc_ref, stat_ref, prefix, bias = refs
    else:
        prior_acc, prior_stat, out_ref, bias = refs
    tile = pl.program_id(0)
    y, z, xl = idx_ref[0], idx_ref[1], idx_ref[2]
    _, nq, rows, width = q_ref.shape
    heads = width // HS
    size = key_refs[0].shape[1]
    owners = counts_ref.shape[0]

    def owner(back, other):
        side = 1 - xl if other else xl
        return ((y + 4 - back) % 4) * 16 + z * 2 + side

    @pl.when(tile == 0)
    def _():
        if cached:

            def one(i, total):
                prefix[i] = total
                return total + counts_ref[i]

            total = lax.fori_loop(0, owners, one, jnp.int32(0))
        place = lax.broadcasted_iota(jnp.int32, (1, size), 1)
        for j, (_, _, back, other) in enumerate(blocks):
            ctx = owner(back, other)
            if cached:
                pos = (place + (prefix[ctx] - total)).astype(F32)
            else:
                pos = (place + ctx * size).astype(F32)
            for h in range(heads):
                row = pos * (slope_ref[h] * LOG2E)
                if cached:
                    row = jnp.where(place < counts_ref[ctx], row, NEG)
                bias[h : h + 1, j * size : (j + 1) * size] = row

    total_rows = nq * rows
    zs = (z + 8 - 2 * tile) % 8
    row = lax.broadcasted_iota(jnp.int32, (total_rows, 1), 0)
    base = (y * 16 + xl) * rows
    row_pos = jnp.where(
        row < rows, base + zs * 2 * rows + row, base + (zs ^ 1) * 2 * rows + row - rows
    )
    place = lax.broadcasted_iota(jnp.int32, (1, size), 1)
    q_tile = q_ref[0].reshape(total_rows, width)
    odd = z % 2 == 1
    lane = lax.broadcasted_iota(jnp.int32, (total_rows, HS), 1)
    packed = jnp.zeros((total_rows, HS), F32)
    for h in range(heads):
        cols = slice(h * HS, (h + 1) * HS)
        q = q_tile[:, cols]
        scores = []
        for j, (ref, at, back, other) in enumerate(blocks):
            s = dot_t(q, key_refs[ref][at, :, cols])
            s = s + bias[h : h + 1, j * size : (j + 1) * size]
            if not cached:
                s = jnp.where(place + owner(back, other) * size <= row_pos, s, NEG)
            scores.append(s)
        top = jnp.max(functools.reduce(jnp.maximum, scores), axis=1, keepdims=True)
        if not cached:
            prior = prior_stat[:, h : h + 1]
            top = jnp.maximum(top, prior)
        both = jnp.zeros((total_rows, 2 * HS), F32)
        for s, (ref, at, _, _) in zip(scores, blocks):
            v = key_refs[ref][at + 1, :, cols]
            both = both + jnp.dot(
                jnp.exp2(s - top).astype(BF16),
                jnp.concatenate([v, jnp.ones_like(v)], axis=1),
                preferred_element_type=F32,
            )
        acc, weight_total = both[:, :HS], both[:, HS:]
        if cached:
            acc_ref[:, cols] = acc
            packed = jnp.where(lane == h, top, packed)
            packed = jnp.where(lane == heads + h, weight_total, packed)
            continue
        fade = jnp.exp2(prior - top)
        acc = acc + fade * prior_acc[:, cols]
        weight_total = weight_total + fade * prior_stat[:, heads + h : heads + h + 1]
        part = (acc / weight_total).astype(BF16)
        out_ref[0, :rows, cols] = jnp.where(odd, part[rows:], part[:rows])
        out_ref[1, :rows, cols] = jnp.where(odd, part[:rows], part[rows:])
        level = top + jnp.log2(weight_total)
        for k, piece in enumerate(three_parts(level)):
            packed = jnp.where(lane == 3 * h + k, piece, packed)
    if cached:
        stat_ref[...] = packed
        return
    first, second = packed[:rows], packed[rows:]
    for b, own in enumerate((jnp.where(odd, second, first), jnp.where(odd, first, second))):
        turned = jnp.transpose(own)[:16]
        out_ref[b, rows:, :] = jnp.concatenate([turned, jnp.zeros_like(turned)], axis=1).astype(
            BF16
        )


def attend(idx, counts, slopes, queries, blocks, keys, prior=None):
    _, nq, rows, width = queries.shape
    cached = prior is None
    size = keys[0].shape[1]
    nk = len(blocks) * size
    total = nq * rows
    whole = lambda a: pl.BlockSpec(a.shape, lambda i, *_: (0,) * a.ndim)
    scratch = []
    acc = jax.ShapeDtypeStruct((4 * total, width), F32)
    stat = jax.ShapeDtypeStruct((4 * total, HS), F32)
    state_specs = [
        pl.BlockSpec((total, width), lambda i, *_: (i, 0)),
        pl.BlockSpec((total, HS), lambda i, *_: (i, 0)),
    ]
    in_specs = [pl.BlockSpec((1, nq, rows, width), lambda i, *_: (i, 0, 0, 0))]
    in_specs += [whole(a) for a in keys]
    if cached:
        scratch.append(SMEM((counts.shape[0],), jnp.int32))
        out_specs, out_shape, prior = state_specs, [acc, stat], ()
    else:
        in_specs += state_specs
        out_specs = pl.BlockSpec(
            (nq, rows + 16, width), lambda i, idx, *_: ((idx[1] // 2 + 4 - i) % 4, 0, 0)
        )
        out_shape = jax.ShapeDtypeStruct((4 * nq, rows + 16, width), BF16)
    scratch.append(VMEM((8, nk), F32))
    return pl.pallas_call(
        functools.partial(attend_kernel, tuple(blocks), cached),
        grid_spec=pltpu.PrefetchScalarGridSpec(
            num_scalar_prefetch=3,
            grid=(4,),
            in_specs=in_specs,
            out_specs=out_specs,
            scratch_shapes=scratch,
        ),
        out_shape=out_shape,
        compiler_params=params(40),
        cost_estimate=cost(
            16 * total * nk * width, 4 * nk * width, 8 * total * nk * (width // HS)
        ),
        name="attend_cache" if cached else "attend_span",
    )(idx, counts, slopes, queries, *keys, *prior)


def merge_kernel(heads, parts_ref, out_ref):
    sources, padded, width = parts_ref.shape
    rows = padded - 16
    levels = jnp.concatenate(
        [parts_ref[s, rows:, :HS].astype(F32) for s in range(sources)], axis=0
    )
    turned = jnp.transpose(levels)
    for h in range(heads):
        cols = slice(h * HS, (h + 1) * HS)
        level = []
        for s in range(sources):
            at = s * 16 + 3 * h
            level.append(
                (turned[:, at : at + 1] + turned[:, at + 1 : at + 2]) + turned[:, at + 2 : at + 3]
            )
        top = functools.reduce(jnp.maximum, level)
        total = jnp.zeros((rows, 1), F32)
        acc = jnp.zeros((rows, HS), F32)
        for s in range(sources):
            weight = jnp.exp2(level[s] - top)
            total = total + weight
            acc = acc + weight * parts_ref[s, :rows, cols].astype(F32)
        out_ref[:, cols] = (acc / total).astype(BF16)


def merge(parts):
    sources, padded, width = parts.shape
    rows = padded - 16
    return pl.pallas_call(
        functools.partial(merge_kernel, width // HS),
        out_shape=jax.ShapeDtypeStruct((rows, width), BF16),
        compiler_params=params(16),
        cost_estimate=cost(4 * sources * rows * width, 2 * sources * padded * width),
        name="merge",
    )(parts)


def layer_kernel(tok_ref, *refs):
    parts = len(refs) // 2
    acc = tok_ref[...].astype(F32)
    for att, weight in zip(refs[:parts], refs[parts:-1]):
        acc = acc + jnp.dot(att[...], weight[...], preferred_element_type=F32)
    refs[-1][...] = acc.astype(BF16)


def layer_output(tokens, atts, weights):
    rows, d = tokens.shape
    step = 512
    inner, width = weights[0].shape[0], atts[0].shape[1]
    return pl.pallas_call(
        layer_kernel,
        grid=(d // step,),
        in_specs=[pl.BlockSpec((rows, step), lambda i: (0, i))]
        + [pl.BlockSpec((rows, width), lambda i: (0, 0))] * len(atts)
        + [pl.BlockSpec((inner, step), lambda i: (0, i))] * len(weights),
        out_specs=pl.BlockSpec((rows, step), lambda i: (0, i)),
        out_shape=jax.ShapeDtypeStruct((rows, d), BF16),
        compiler_params=params(16),
        cost_estimate=cost(8 * rows * d * inner, 8 * inner * d),
        name="layer_output",
    )(tokens, *atts, *weights)


def short_project_kernel(lay_ref, rim_ref, w_ref, q_ref, kv_ref, normed):
    step = pl.program_id(0)
    rows = lay_ref.shape[0]
    groups = rows // GROUP
    rim_rows = rim_ref.shape[0]

    @pl.when(step == 0)
    def _():
        g = lax.broadcasted_iota(jnp.int32, (groups, rows), 0) * GROUP
        t = lax.broadcasted_iota(jnp.int32, (groups, rows), 1)
        own = jnp.where((t <= g) & (t > g - GROUP), 1.0 / GROUP, 0.0).astype(BF16)
        g = lax.broadcasted_iota(jnp.int32, (groups, rim_rows), 0) * GROUP
        t = lax.broadcasted_iota(jnp.int32, (groups, rim_rows), 1) - rim_rows
        before = jnp.where(t > g - GROUP, 1.0 / GROUP, 0.0).astype(BF16)
        pooled = jnp.dot(own, lay_ref[...], preferred_element_type=F32) + jnp.dot(
            before, rim_ref[...], preferred_element_type=F32
        )
        normed[...] = rms_scaled(pooled.astype(BF16).astype(F32))

    out = jnp.dot(normed[...], w_ref[0], preferred_element_type=F32)

    store_projection(step, out, q_ref, kv_ref)


def short_project(layer, rim, weight3):
    n, d = layer.shape
    groups = n // GROUP
    width = weight3.shape[2]
    return pl.pallas_call(
        short_project_kernel,
        grid=(3,),
        in_specs=[
            pl.BlockSpec((n, d), lambda i: (0, 0)),
            pl.BlockSpec(rim.shape, lambda i: (0, 0)),
            pl.BlockSpec((1, d, width), lambda i: (i, 0, 0)),
        ],
        out_specs=[
            pl.BlockSpec((groups, width), lambda i: (0, 0)),
            pl.BlockSpec((2, groups, width), lambda i: (0, 0, 0)),
        ],
        out_shape=[
            jax.ShapeDtypeStruct((groups, width), BF16),
            jax.ShapeDtypeStruct((2, groups, width), BF16),
        ],
        scratch_shapes=[VMEM((groups, d), BF16)],
        compiler_params=params(16),
        cost_estimate=cost(6 * groups * d * width, 2 * (n * d + 3 * d * width)),
        name="short_project",
    )(layer, rim, weight3)


def short_attend_kernel(idx_ref, slope_ref, *refs):
    queries, key_refs, out_ref = refs[:4], refs[4:8], refs[8]
    y, z, xl = idx_ref[0], idx_ref[1], idx_ref[2]
    groups, width = queries[0].shape[1:]
    heads = width // HS
    nr = nk = 8 * groups
    row = lax.broadcasted_iota(jnp.int32, (nr, 1), 0)
    zs = row // groups
    row_pos = (y * 16 + zs * 2 + xl) * groups + row % groups
    back = (z // 2 + 4 - zs // 2) % 4
    came = (2 * back + (zs ^ z) % 2) * groups + row % groups
    order = jnp.where(lax.broadcasted_iota(jnp.int32, (nr, nr), 1) == came, 1.0, 0.0).astype(BF16)
    key = lax.broadcasted_iota(jnp.int32, (1, nk), 1)
    ys = (y + 4 - key // (2 * groups)) % 4
    side = jnp.where((key // groups) % 2 == 1, 1 - xl, xl)
    key_pos = (ys * 16 + z * 2 + side) * groups + key % groups
    usable = key_pos <= row_pos
    spot = key_pos.astype(F32)
    lane = lax.broadcasted_iota(jnp.int32, (nr, HS), 1)
    packed = jnp.zeros((nr, HS), F32)
    outs = []
    for h in range(heads):
        cols = slice(h * HS, (h + 1) * HS)
        q = jnp.concatenate([r[:, :, cols].reshape(2 * groups, HS) for r in queries], axis=0)
        q = jnp.dot(order, q, preferred_element_type=F32).astype(BF16)
        k = jnp.concatenate([r[:, 0, :, cols].reshape(2 * groups, HS) for r in key_refs], axis=0)
        v = jnp.concatenate([r[:, 1, :, cols].reshape(2 * groups, HS) for r in key_refs], axis=0)
        s = dot_t(q, k) + (slope_ref[h] * LOG2E) * spot
        s = jnp.where(usable, s, NEG)
        top = jnp.max(s, axis=1, keepdims=True)
        p = jnp.exp2(s - top).astype(BF16)
        both = jnp.dot(
            p, jnp.concatenate([v, jnp.ones_like(v)], axis=1), preferred_element_type=F32
        )
        weight_total = both[:, HS:]
        outs.append((both[:, :HS] / weight_total).astype(BF16))
        level = top + jnp.log2(weight_total)
        for k, piece in enumerate(three_parts(level)):
            packed = jnp.where(lane == 3 * h + k, piece, packed)
    out = jnp.concatenate(outs + [packed.astype(BF16)], axis=1)
    out_ref[...] = out.reshape(out_ref.shape)


def short_attend(idx, slopes, queries, keys):
    _, groups, width = queries[0].shape
    smem = pl.BlockSpec(memory_space=SMEM)
    vmem = pl.BlockSpec(memory_space=VMEM)
    n = 8 * groups
    return pl.pallas_call(
        short_attend_kernel,
        in_specs=[smem, smem] + [vmem] * 8,
        out_specs=vmem,
        out_shape=jax.ShapeDtypeStruct((8, groups, width + HS), BF16),
        compiler_params=params(16),
        cost_estimate=cost(4 * n * n * width, 8 * n * width),
        name="short_attend",
    )(idx, slopes, *queries, *keys)


def short_merge_kernel(heads, parts_ref, out_ref):
    sources, rows, padded = parts_ref.shape
    width = padded - HS
    for h in range(heads):
        cols = slice(h * HS, (h + 1) * HS)
        level = []
        for s in range(sources):
            lev = parts_ref[s, :, width:].astype(F32)
            level.append(
                (lev[:, 3 * h : 3 * h + 1] + lev[:, 3 * h + 1 : 3 * h + 2])
                + lev[:, 3 * h + 2 : 3 * h + 3]
            )
        top = functools.reduce(jnp.maximum, level)
        total = jnp.zeros((rows, 1), F32)
        acc = jnp.zeros((rows, HS), F32)
        for s in range(sources):
            weight = jnp.exp2(level[s] - top)
            total = total + weight
            acc = acc + weight * parts_ref[s, :, cols].astype(F32)
        out_ref[:, cols] = (acc / total).astype(BF16)


def short_merge(parts):
    sources, rows, padded = parts.shape
    width = padded - HS
    return pl.pallas_call(
        functools.partial(short_merge_kernel, width // HS),
        out_shape=jax.ShapeDtypeStruct((rows, width), BF16),
        compiler_params=params(16),
        cost_estimate=cost(4 * sources * rows * width, 2 * sources * rows * padded),
        name="short_merge",
    )(parts)


def final_kernel(tp_ref, lay_ref, *refs):
    parts = len(refs) // 2
    groups = refs[0].shape[0]
    rows = lay_ref.shape[0]
    t = lax.broadcasted_iota(jnp.int32, (rows, groups), 0) // GROUP
    g = lax.broadcasted_iota(jnp.int32, (rows, groups), 1)
    spread = jnp.where(t == g, 1.0, 0.0).astype(BF16)
    branch = jnp.zeros(lay_ref.shape, F32)
    for att, weight in zip(refs[:parts], refs[parts:-1]):
        lifted = jnp.dot(spread, att[...], preferred_element_type=F32).astype(BF16)
        branch = branch + jnp.dot(lifted, weight[...], preferred_element_type=F32)
    refs[-1][...] = (lay_ref[...].astype(F32) + branch).astype(BF16)


def final_sum(tp_index, layer, atts, weights):
    rows = layer.shape[0]
    inner, cols = weights[0].shape
    whole = lambda a: pl.BlockSpec(a.shape, lambda i, tp: (0, 0))
    return pl.pallas_call(
        final_kernel,
        grid_spec=pltpu.PrefetchScalarGridSpec(
            num_scalar_prefetch=1,
            grid=(1,),
            in_specs=[pl.BlockSpec((rows, cols), lambda i, tp: (0, tp[0]))]
            + [whole(a) for a in (*atts, *weights)],
            out_specs=pl.BlockSpec((rows, cols), lambda i, tp: (0, 0)),
        ),
        out_shape=jax.ShapeDtypeStruct((rows, cols), BF16),
        compiler_params=params(16),
        cost_estimate=cost(8 * rows * cols * inner, 8 * inner * cols),
        name="final_sum",
    )(tp_index, layer, *atts, *weights)


def exchange(blocks, axis):
    return lax.all_to_all(blocks, axis, 0, 0)


def swap(x, axis, flip=1):
    return lax.ppermute(x, axis, [(i, i ^ flip) for i in range(lax.axis_size(axis))])


def moved(x, axis, by):
    n = lax.axis_size(axis)
    return lax.ppermute(x, axis, [(i, (i + by) % n) for i in range(n)])


def round_tp(x):
    return [x] + [swap(x, "tp", flip) for flip in (1, 2, 3)]


def round_z(x):
    pair = jnp.stack([x, swap(x, "z")])
    return [pair] + [moved(pair, "z", by) for by in (2, 4, 6)]


def round_y(pair):
    half = pair.shape[0] // 2
    left, right = moved(pair, "y", 1), moved(pair, "y", -1)
    return [pair, left, right, moved(left[:half], "y", 1), moved(right[half:], "y", -1)]


KEY_BLOCKS = (
    (0, 0, 0, False),
    (0, 2, 0, True),
    (1, 0, 1, False),
    (1, 2, 1, True),
    (2, 0, 3, False),
    (2, 2, 3, True),
    (3, 0, 2, False),
    (4, 0, 2, True),
)


def after(x, *others):
    return lax.optimization_barrier((x, *others))[0]


def on_device(
    tokens,
    project_weight,
    output_weight,
    distance_slope,
    cache_keys,
    cache_values,
    cache_count,
    short_project_weight,
    short_output,
    short_slope,
):
    ctx_axes = ("y", "z", "xl")
    idx = jnp.stack([lax.axis_index("y"), lax.axis_index("z"), lax.axis_index("xl")]).astype(
        jnp.int32
    )
    tp = lax.axis_index("tp").astype(jnp.int32)

    own = [cache_keys, cache_values]
    counts = lax.all_gather(cache_count, ctx_axes, axis=0, tiled=True)
    cache = after(jnp.stack(own + [swap(a, "xl") for a in own]), counts)
    q, kv = project(tokens, jnp.transpose(project_weight, (1, 0, 2)))
    queries = jnp.stack(round_z(q))
    other_kv = swap(kv, "xl")
    cache_ring = round_y(cache)
    span_ring = round_y(after(jnp.concatenate([kv, other_kv], axis=0), cache_ring[1]))

    held = after(output_weight, other_kv)
    crossed = swap(held, "tp", 2)
    out_weights = [held, swap(held, "tp", 1), crossed, swap(crossed, "tp", 1)]
    width = short_output.shape[1] // 4
    late = after(short_output, crossed)
    short_weights = []
    for flip in range(4):
        piece = lax.dynamic_slice_in_dim(late, (tp ^ flip) * width, width, 1)
        short_weights.append(swap(piece, "tp", flip) if flip else piece)

    state = attend(idx, counts, distance_slope, queries, KEY_BLOCKS, cache_ring)
    parts = attend(idx, counts, distance_slope, queries, KEY_BLOCKS, span_ring, state)
    parts, *short_weights = lax.optimization_barrier((exchange(parts, "z"), *short_weights))
    atts = round_tp(merge(parts))
    layer = layer_output(tokens, atts, out_weights)

    n = lax.axis_size(ctx_axes)
    rim = lax.ppermute(layer[-16:], ctx_axes, [(i, i + 1) for i in range(n - 1)])
    sq, skv = short_project(layer, rim, jnp.transpose(short_project_weight, (1, 0, 2)))
    short_queries = round_z(sq)
    pair = jnp.stack([skv, swap(skv, "xl")])
    short_keys = [pair] + [moved(pair, "y", by) for by in (1, 2, 3)]
    sparts = short_attend(idx, short_slope, short_queries, short_keys)
    satts = round_tp(short_merge(exchange(sparts, "z")))
    return final_sum(tp.reshape(1), layer, satts, short_weights)


def solution(mesh):
    split = Mesh(mesh.devices.reshape(4, 8, 2, 4), ("y", "z", "xl", "tp"))
    ctx = ("y", "z", "xl")
    return jax.shard_map(
        on_device,
        mesh=split,
        in_specs=(
            P(ctx, None),
            P(None, None, "tp"),
            P("tp", None),
            P("tp"),
            P(ctx, "tp"),
            P(ctx, "tp"),
            P(ctx),
            P(None, None, "tp"),
            P("tp", None),
            P("tp"),
        ),
        out_specs=P(ctx, "tp"),
        check_vma=False,
    )
```

```python
import functools
import math

import jax
import jax.numpy as jnp
from jax import lax
from jax.experimental import pallas as pl
from jax.experimental.pallas import tpu as pltpu
from jax.sharding import Mesh, PartitionSpec as P

HS = 128
GROUP = 4
NEG = -1e30
LOG2E = math.log2(math.e)
SCALE2 = HS ** -0.5 * LOG2E

VMEM = pltpu.VMEM
SMEM = pltpu.SMEM
F32 = jnp.float32
BF16 = jnp.bfloat16


def cost(flops, moved, trans=0):
    return pl.CostEstimate(flops=flops, bytes_accessed=moved, transcendentals=trans)


def params(mib):
    return pltpu.CompilerParams(vmem_limit_bytes=mib * 1024 * 1024)


def rms_scaled(values):
    inv = lax.rsqrt(jnp.mean(values * values, axis=-1, keepdims=True) + 1e-06)
    return (values * inv).astype(BF16)


def dot_t(a, b):
    return lax.dot_general(a, b, (((1,), (1,)), ((), ())), preferred_element_type=F32)


def three_parts(x):
    hi = x.astype(BF16).astype(F32)
    mid = (x - hi).astype(BF16).astype(F32)
    lo = (x - hi - mid).astype(BF16).astype(F32)
    return hi, mid, lo


def project_kernel(tok_ref, w_ref, *refs):
    counts, (q_ref, pack_ref, normed) = refs[:-3], refs[-3:]
    step = pl.program_id(0)
    rows = tok_ref.shape[0]

    @pl.when(step == 0)
    def _():
        normed[...] = rms_scaled(tok_ref[...].astype(F32))

    out = jnp.dot(normed[...], w_ref[0], preferred_element_type=F32)

    @pl.when(step == 0)
    def _():
        q_ref[...] = (out * SCALE2).astype(BF16)

    @pl.when(step == 1)
    def _():
        pack_ref[:rows] = out.astype(BF16)

    @pl.when(step == 2)
    def _():
        pack_ref[rows : 2 * rows] = out.astype(BF16)
        tail = [c[:1] for c in counts]
        tail.append(jnp.zeros((16 - len(counts), out.shape[1]), BF16))
        pack_ref[2 * rows :] = jnp.concatenate(tail, axis=0)


def project(rows, weight3, counts):
    n, d = rows.shape
    width = weight3.shape[2]
    return pl.pallas_call(
        project_kernel,
        grid=(3,),
        in_specs=[
            pl.BlockSpec((n, d), lambda i: (0, 0)),
            pl.BlockSpec((1, d, width), lambda i: (i, 0, 0)),
        ]
        + [pl.BlockSpec(c.shape, lambda i: (0, 0)) for c in counts],
        out_specs=[
            pl.BlockSpec((n, width), lambda i: (0, 0)),
            pl.BlockSpec((2 * n + 16, width), lambda i: (0, 0)),
        ],
        out_shape=[
            jax.ShapeDtypeStruct((n, width), BF16),
            jax.ShapeDtypeStruct((2 * n + 16, width), BF16),
        ],
        scratch_shapes=[VMEM((n, d), BF16)],
        compiler_params=params(12),
        cost_estimate=cost(6 * n * d * width, 2 * (n * d + 3 * d * width)),
        name="project",
    )(rows, weight3, *counts)


RING = ((0, 0), (0, 1), (1, 0), (1, 1), (3, 0), (3, 1), (2, 0), (2, 1))


def owner(idx_ref, back, other):
    y, z, xl = idx_ref[0], idx_ref[1], idx_ref[2]
    side = 1 - xl if other else xl
    return (y + 4 - back) % 4, z, side


def attend_heads(qs, prior, score, value):
    heads = len(qs)
    pending = [score(0, qs[0], j) for j in range(len(RING))]
    results = []
    for h in range(heads):
        top = jnp.max(functools.reduce(jnp.maximum, pending), axis=1, keepdims=True)
        if prior is not None:
            top = jnp.maximum(top, prior[h])
        following = []
        both = None
        for j in range(len(RING)):
            term = jnp.dot(
                jnp.exp2(pending[j] - top).astype(BF16), value(h, j), preferred_element_type=F32
            )
            both = term if both is None else both + term
            if h + 1 < heads:
                following.append(score(h + 1, qs[h + 1], j))
        pending = following
        results.append((top, both[:, HS:], both[:, :HS]))
    return results


def with_ones(v):
    return jnp.concatenate([v, jnp.ones_like(v)], axis=1)


def span_kernel(idx_ref, slope_ref, *refs):
    queries, packs = refs[:8], refs[8:16]
    acc_ref, stat_ref, cache_bias, q_tile, bias = refs[16:]
    tile = pl.program_id(0)
    rows, width = queries[0].shape
    heads = width // HS
    size = (packs[0].shape[0] - 16) // 2
    slots = cache_bias.shape[1] // len(RING)
    y, z, xl = idx_ref[0], idx_ref[1], idx_ref[2]

    for t in range(4):

        @pl.when(tile == t)
        def _(t=t):
            q_tile[:rows] = queries[2 * t][...]
            q_tile[rows:] = queries[2 * t + 1][...]

    @pl.when(tile == 0)
    def _():
        steps = lax.broadcasted_iota(jnp.int32, (8, width), 0)
        before = (z + 8 - steps) % 8 < z
        totals, parts, owns = [], [], []
        for pack in packs:
            counts = pack[2 * size : 2 * size + 16].astype(F32)[:8]
            totals.append(jnp.sum(counts, axis=0, keepdims=True))
            parts.append(jnp.sum(jnp.where(before, counts, 0.0), axis=0, keepdims=True))
            owns.append(counts[:1])
        ys = [owner(idx_ref, back, other)[0] for back, other in RING]
        everything = functools.reduce(jnp.add, totals)
        slot = lax.broadcasted_iota(jnp.int32, (1, slots), 1).astype(F32)
        place = lax.broadcasted_iota(jnp.int32, (1, size), 1)
        for j, (back, other) in enumerate(RING):
            yj, zj, side = owner(idx_ref, back, other)
            start = -everything
            for i in range(len(RING)):
                start = start + jnp.where(ys[i] < yj, totals[i], 0.0)
            mate = j ^ 1
            start = start + parts[j] + parts[mate] + jnp.where(side == 1, owns[mate], 0.0)
            spot = (place + (yj * 16 + zj * 2 + side) * size).astype(F32)
            for h in range(heads):
                slope = slope_ref[h] * LOG2E
                cache_bias[h : h + 1, j * slots : (j + 1) * slots] = jnp.where(
                    slot < owns[j], slope * (slot + start), NEG
                )
                bias[h : h + 1, j * size : (j + 1) * size] = jnp.where(
                    yj <= y, slope * spot, NEG
                )

    row = lax.broadcasted_iota(jnp.int32, (2 * rows, 1), 0)
    first = (z + 8 - 2 * tile) % 8
    second = (z + 7 - 2 * tile) % 8
    row_ctx = y * 16 + xl + 2 * jnp.where(row < rows, first, second)
    row_pos = row_ctx * rows + jnp.where(row < rows, row, row - rows)
    place = lax.broadcasted_iota(jnp.int32, (1, size), 1)

    def score(h, q, j):
        cols = slice(h * HS, (h + 1) * HS)
        s = dot_t(q, packs[j][:size, cols]) + bias[h : h + 1, j * size : (j + 1) * size]
        back, other = RING[j]
        if back == 0:
            yj, zj, side = owner(idx_ref, back, other)
            s = jnp.where(place + (yj * 16 + zj * 2 + side) * size <= row_pos, s, NEG)
        return s

    def value(h, j):
        return with_ones(packs[j][size : 2 * size, h * HS : (h + 1) * HS])

    lane = lax.broadcasted_iota(jnp.int32, (2 * rows, HS), 1)
    packed = jnp.zeros((2 * rows, HS), F32)
    qs = [q_tile[:, h * HS : (h + 1) * HS] for h in range(heads)]
    for h, (top, total, acc) in enumerate(attend_heads(qs, None, score, value)):
        acc_ref[:, h * HS : (h + 1) * HS] = acc
        packed = jnp.where(lane == h, top, packed)
        packed = jnp.where(lane == heads + h, total, packed)
    stat_ref[...] = packed


def span_attend(idx, slopes, queries, packs, slots):
    rows, width = queries[0].shape
    size = (packs[0].shape[0] - 16) // 2
    nk = len(RING) * size
    whole = lambda a: pl.BlockSpec(a.shape, lambda i, *_: (0,) * a.ndim)
    return pl.pallas_call(
        span_kernel,
        grid_spec=pltpu.PrefetchScalarGridSpec(
            num_scalar_prefetch=2,
            grid=(4,),
            in_specs=[whole(a) for a in (*queries, *packs)],
            out_specs=[
                pl.BlockSpec((2 * rows, width), lambda i, *_: (i, 0)),
                pl.BlockSpec((2 * rows, HS), lambda i, *_: (i, 0)),
                pl.BlockSpec((8, len(RING) * slots), lambda i, *_: (0, 0)),
            ],
            scratch_shapes=[VMEM((2 * rows, width), BF16), VMEM((8, nk), F32)],
        ),
        out_shape=[
            jax.ShapeDtypeStruct((8 * rows, width), F32),
            jax.ShapeDtypeStruct((8 * rows, HS), F32),
            jax.ShapeDtypeStruct((8, len(RING) * slots), F32),
        ],
        compiler_params=params(32),
        cost_estimate=cost(32 * rows * nk * width, 4 * nk * width, 16 * rows * nk),
        name="span_attend",
    )(idx, slopes, *queries, *packs)


def cache_kernel(q0_ref, q1_ref, acc_ref, stat_ref, bias, *refs):
    packs, outs = refs[:8], refs[8:]
    rows, width = q0_ref.shape
    heads = width // HS
    slots = packs[0].shape[1]

    def score(h, q, j):
        cols = slice(h * HS, (h + 1) * HS)
        return dot_t(q, packs[j][0, :, cols]) + bias[h : h + 1, j * slots : (j + 1) * slots]

    def value(h, j):
        return with_ones(packs[j][1, :, h * HS : (h + 1) * HS])

    lane = lax.broadcasted_iota(jnp.int32, (2 * rows, HS), 1)
    packed = jnp.zeros((2 * rows, HS), F32)
    qs = [
        jnp.concatenate([r[:, h * HS : (h + 1) * HS] for r in (q0_ref, q1_ref)], axis=0)
        for h in range(heads)
    ]
    prior = [stat_ref[:, h : h + 1] for h in range(heads)]
    for h, (top, total, acc) in enumerate(attend_heads(qs, prior, score, value)):
        cols = slice(h * HS, (h + 1) * HS)
        fade = jnp.exp2(prior[h] - top)
        acc = acc + fade * acc_ref[:, cols]
        total = total + fade * stat_ref[:, heads + h : heads + h + 1]
        part = (acc / total).astype(BF16)
        outs[0][:rows, cols] = part[:rows]
        outs[1][:rows, cols] = part[rows:]
        for k, piece in enumerate(three_parts(top + jnp.log2(total))):
            packed = jnp.where(lane == 3 * h + k, piece, packed)
    for b, out in enumerate(outs):
        turned = jnp.transpose(packed[b * rows : (b + 1) * rows])[:16]
        out[rows:, :] = jnp.concatenate([turned, jnp.zeros_like(turned)], axis=1).astype(BF16)


def cache_attend(tile, q0, q1, state, packs):
    acc, stat, bias = state
    rows, width = q0.shape
    nk = bias.shape[1]
    whole = lambda a: pl.BlockSpec(a.shape, lambda i: (0,) * a.ndim)
    out = jax.ShapeDtypeStruct((rows + 16, width), BF16)
    return pl.pallas_call(
        cache_kernel,
        grid=(1,),
        in_specs=[
            whole(q0),
            whole(q1),
            pl.BlockSpec((2 * rows, width), lambda i: (tile, 0)),
            pl.BlockSpec((2 * rows, HS), lambda i: (tile, 0)),
            whole(bias),
        ]
        + [whole(a) for a in packs],
        out_specs=[whole(out)] * 2,
        out_shape=[out, out],
        compiler_params=params(32),
        cost_estimate=cost(8 * rows * nk * width, 4 * nk * width, 4 * rows * nk),
        name="cache_attend",
    )(q0, q1, acc, stat, bias, *packs)


def merge_kernel(*refs):
    parts, out_ref = refs[:-1], refs[-1]
    rows, width = out_ref.shape
    levels = jnp.concatenate([part[rows:, :HS].astype(F32) for part in parts], axis=0)
    turned = jnp.transpose(levels)
    for h in range(width // HS):
        cols = slice(h * HS, (h + 1) * HS)
        level = []
        for s in range(len(parts)):
            at = s * 16 + 3 * h
            level.append(
                (turned[:, at : at + 1] + turned[:, at + 1 : at + 2]) + turned[:, at + 2 : at + 3]
            )
        top = functools.reduce(jnp.maximum, level)
        total = jnp.zeros((rows, 1), F32)
        acc = jnp.zeros((rows, HS), F32)
        for s, part in enumerate(parts):
            weight = jnp.exp2(level[s] - top)
            total = total + weight
            acc = acc + weight * part[:rows, cols].astype(F32)
        out_ref[:, cols] = (acc / total).astype(BF16)


def merge(parts):
    padded, width = parts[0].shape
    rows = padded - 16
    return pl.pallas_call(
        merge_kernel,
        out_shape=jax.ShapeDtypeStruct((rows, width), BF16),
        compiler_params=params(16),
        cost_estimate=cost(32 * rows * width, 16 * padded * width),
        name="merge",
    )(*parts)


def layer_kernel(tok_ref, *refs):
    parts = len(refs) // 2
    acc = tok_ref[...].astype(F32)
    for att, weight in zip(refs[:parts], refs[parts:-1]):
        acc = acc + jnp.dot(att[...], weight[...], preferred_element_type=F32)
    refs[-1][...] = acc.astype(BF16)


def layer_output(tokens, atts, weights):
    rows, d = tokens.shape
    step = 512
    inner, width = weights[0].shape[0], atts[0].shape[1]
    return pl.pallas_call(
        layer_kernel,
        grid=(d // step,),
        in_specs=[pl.BlockSpec((rows, step), lambda i: (0, i))]
        + [pl.BlockSpec((rows, width), lambda i: (0, 0))] * len(atts)
        + [pl.BlockSpec((inner, step), lambda i: (0, i))] * len(weights),
        out_specs=pl.BlockSpec((rows, step), lambda i: (0, i)),
        out_shape=jax.ShapeDtypeStruct((rows, d), BF16),
        compiler_params=params(16),
        cost_estimate=cost(8 * rows * d * inner, 8 * inner * d),
        name="layer_output",
    )(tokens, *atts, *weights)


def short_project_kernel(lay_ref, rim_ref, w_ref, q_ref, kv_ref, normed):
    step = pl.program_id(0)
    rows = lay_ref.shape[0]
    groups = rows // GROUP
    rim_rows = rim_ref.shape[0]

    @pl.when(step == 0)
    def _():
        g = lax.broadcasted_iota(jnp.int32, (groups, rows), 0) * GROUP
        t = lax.broadcasted_iota(jnp.int32, (groups, rows), 1)
        own = jnp.where((t <= g) & (t > g - GROUP), 1.0 / GROUP, 0.0).astype(BF16)
        g = lax.broadcasted_iota(jnp.int32, (groups, rim_rows), 0) * GROUP
        t = lax.broadcasted_iota(jnp.int32, (groups, rim_rows), 1) - rim_rows
        before = jnp.where(t > g - GROUP, 1.0 / GROUP, 0.0).astype(BF16)
        pooled = jnp.dot(own, lay_ref[...], preferred_element_type=F32) + jnp.dot(
            before, rim_ref[...], preferred_element_type=F32
        )
        normed[...] = rms_scaled(pooled.astype(BF16).astype(F32))

    out = jnp.dot(normed[...], w_ref[0], preferred_element_type=F32)

    @pl.when(step == 0)
    def _():
        scaled = (out * SCALE2).astype(BF16)
        for c in range(q_ref.shape[0]):
            q_ref[c] = scaled

    @pl.when(step == 1)
    def _():
        kv_ref[0] = out.astype(BF16)

    @pl.when(step == 2)
    def _():
        kv_ref[1] = out.astype(BF16)


def short_project(layer, rim, weight3, copies):
    n, d = layer.shape
    groups = n // GROUP
    width = weight3.shape[2]
    return pl.pallas_call(
        short_project_kernel,
        grid=(3,),
        in_specs=[
            pl.BlockSpec((n, d), lambda i: (0, 0)),
            pl.BlockSpec(rim.shape, lambda i: (0, 0)),
            pl.BlockSpec((1, d, width), lambda i: (i, 0, 0)),
        ],
        out_specs=[
            pl.BlockSpec((copies, groups, width), lambda i: (0, 0, 0)),
            pl.BlockSpec((2, groups, width), lambda i: (0, 0, 0)),
        ],
        out_shape=[
            jax.ShapeDtypeStruct((copies, groups, width), BF16),
            jax.ShapeDtypeStruct((2, groups, width), BF16),
        ],
        scratch_shapes=[VMEM((groups, d), BF16)],
        compiler_params=params(16),
        cost_estimate=cost(6 * groups * d * width, 2 * (n * d + 3 * d * width)),
        name="short_project",
    )(layer, rim, weight3)


def short_attend_kernel(idx_ref, slope_ref, *refs):
    q_ref, key_refs, out_ref = refs[0], refs[1:5], refs[5]
    y, z, xl = idx_ref[0], idx_ref[1], idx_ref[2]
    groups, width = q_ref.shape[1:]
    heads = width // HS
    nr = nk = 8 * groups
    row = lax.broadcasted_iota(jnp.int32, (nr, 1), 0)
    zs = row // groups
    row_pos = (y * 16 + zs * 2 + xl) * groups + row % groups
    key = lax.broadcasted_iota(jnp.int32, (1, nk), 1)
    ys = (y + 4 - key // (2 * groups)) % 4
    side = jnp.where((key // groups) % 2 == 1, 1 - xl, xl)
    key_pos = (ys * 16 + z * 2 + side) * groups + key % groups
    usable = key_pos <= row_pos
    spot = key_pos.astype(F32)
    lane = lax.broadcasted_iota(jnp.int32, (nr, HS), 1)
    packed = jnp.zeros((nr, HS), F32)
    outs = []
    for h in range(heads):
        cols = slice(h * HS, (h + 1) * HS)
        q = q_ref[:, :, cols].reshape(nr, HS)
        k = jnp.concatenate([r[:, 0, :, cols].reshape(2 * groups, HS) for r in key_refs], axis=0)
        v = jnp.concatenate([r[:, 1, :, cols].reshape(2 * groups, HS) for r in key_refs], axis=0)
        s = dot_t(q, k) + (slope_ref[h] * LOG2E) * spot
        s = jnp.where(usable, s, NEG)
        top = jnp.max(s, axis=1, keepdims=True)
        p = jnp.exp2(s - top).astype(BF16)
        both = jnp.dot(
            p, jnp.concatenate([v, jnp.ones_like(v)], axis=1), preferred_element_type=F32
        )
        weight_total = both[:, HS:]
        outs.append((both[:, :HS] / weight_total).astype(BF16))
        level = top + jnp.log2(weight_total)
        for k, piece in enumerate(three_parts(level)):
            packed = jnp.where(lane == 3 * h + k, piece, packed)
    out = jnp.concatenate(outs + [packed.astype(BF16)], axis=1)
    out_ref[...] = out.reshape(out_ref.shape)


def short_attend(idx, slopes, queries, keys):
    _, groups, width = queries.shape
    smem = pl.BlockSpec(memory_space=SMEM)
    vmem = pl.BlockSpec(memory_space=VMEM)
    n = 8 * groups
    return pl.pallas_call(
        short_attend_kernel,
        in_specs=[smem, smem] + [vmem] * 5,
        out_specs=vmem,
        out_shape=jax.ShapeDtypeStruct((8, groups, width + HS), BF16),
        compiler_params=params(16),
        cost_estimate=cost(4 * n * n * width, 8 * n * width),
        name="short_attend",
    )(idx, slopes, queries, *keys)


def short_merge_kernel(heads, tp_ref, parts_ref, w_ref, *refs):
    outs, merged = refs[:-1], refs[-1]
    step = pl.program_id(0)
    sources, rows, padded = parts_ref.shape
    width = padded - HS

    @pl.when(step == 0)
    def _():
        for h in range(heads):
            cols = slice(h * HS, (h + 1) * HS)
            level = []
            for s in range(sources):
                lev = parts_ref[s, :, width:].astype(F32)
                level.append(
                    (lev[:, 3 * h : 3 * h + 1] + lev[:, 3 * h + 1 : 3 * h + 2])
                    + lev[:, 3 * h + 2 : 3 * h + 3]
                )
            top = functools.reduce(jnp.maximum, level)
            total = jnp.zeros((rows, 1), F32)
            acc = jnp.zeros((rows, HS), F32)
            for s in range(sources):
                weight = jnp.exp2(level[s] - top)
                total = total + weight
                acc = acc + weight * parts_ref[s, :, cols].astype(F32)
            merged[:, cols] = (acc / total).astype(BF16)

    out = jnp.dot(merged[...], w_ref[...], preferred_element_type=F32).astype(BF16)
    for flip, ref in enumerate(outs):

        @pl.when(step == flip)
        def _(ref=ref):
            ref[...] = out


def short_merge(tp_index, parts, weight):
    sources, rows, padded = parts.shape
    width = padded - HS
    cols = weight.shape[1] // 4
    out = jax.ShapeDtypeStruct((rows, cols), BF16)
    return pl.pallas_call(
        functools.partial(short_merge_kernel, width // HS),
        grid_spec=pltpu.PrefetchScalarGridSpec(
            num_scalar_prefetch=1,
            grid=(4,),
            in_specs=[
                pl.BlockSpec(parts.shape, lambda i, tp: (0, 0, 0)),
                pl.BlockSpec((width, cols), lambda i, tp: (0, tp[0] ^ i)),
            ],
            out_specs=[pl.BlockSpec((rows, cols), lambda i, tp: (0, 0))] * 4,
            scratch_shapes=[VMEM((rows, width), BF16)],
        ),
        out_shape=[out] * 4,
        compiler_params=params(16),
        cost_estimate=cost(8 * rows * width * cols, 8 * width * cols),
        name="short_merge",
    )(tp_index, parts, weight)


def final_kernel(tp_ref, lay_ref, *refs):
    terms, out_ref = refs[:-1], refs[-1]
    rows, groups = lay_ref.shape[0], terms[0].shape[0]
    t = lax.broadcasted_iota(jnp.int32, (rows, groups), 0) // GROUP
    g = lax.broadcasted_iota(jnp.int32, (rows, groups), 1)
    spread = jnp.where(t == g, 1.0, 0.0).astype(BF16)
    branch = jnp.zeros(lay_ref.shape, F32)
    for term in terms:
        branch = branch + jnp.dot(spread, term[...], preferred_element_type=F32)
    out_ref[...] = (lay_ref[...].astype(F32) + branch).astype(BF16)


def final_sum(tp_index, layer, terms):
    rows = layer.shape[0]
    groups, cols = terms[0].shape
    return pl.pallas_call(
        final_kernel,
        grid_spec=pltpu.PrefetchScalarGridSpec(
            num_scalar_prefetch=1,
            grid=(1,),
            in_specs=[pl.BlockSpec((rows, cols), lambda i, tp: (0, tp[0]))]
            + [pl.BlockSpec((groups, cols), lambda i, tp: (0, 0))] * len(terms),
            out_specs=pl.BlockSpec((rows, cols), lambda i, tp: (0, 0)),
        ),
        out_shape=jax.ShapeDtypeStruct((rows, cols), BF16),
        compiler_params=params(16),
        cost_estimate=cost(8 * rows * cols * groups, 4 * rows * cols),
        name="final_sum",
    )(tp_index, layer, *terms)


def exchange(blocks, axis):
    return lax.all_to_all(blocks, axis, 0, 0)


def swap(x, axis, flip=1):
    return lax.ppermute(x, axis, [(i, i ^ flip) for i in range(lax.axis_size(axis))])


def moved(x, axis, by):
    n = lax.axis_size(axis)
    return lax.ppermute(x, axis, [(i, (i + by) % n) for i in range(n)])


def round_tp(x):
    return [x] + [swap(x, "tp", flip) for flip in (1, 2, 3)]


def both_ways(x):
    return moved(x, "y", 1), moved(x, "y", -1)


def round_y(own, other, beside):
    left, right = beside
    left_other, right_other = both_ways(other)
    far, far_other = moved(left, "y", 1), moved(right_other, "y", -1)
    return [own, other, left, left_other, right, right_other, far, far_other]


def after(x, *others):
    return lax.optimization_barrier((x, *others))[0]


def on_device(
    tokens,
    project_weight,
    output_weight,
    distance_slope,
    cache_keys,
    cache_values,
    cache_count,
    short_project_weight,
    short_output,
    short_slope,
):
    ctx_axes = ("y", "z", "xl")
    nz = lax.axis_size("z")
    idx = jnp.stack([lax.axis_index("y"), lax.axis_index("z"), lax.axis_index("xl")]).astype(
        jnp.int32
    )
    tp = lax.axis_index("tp").astype(jnp.int32).reshape(1)

    cache = jnp.stack([cache_keys, cache_values])
    other_cache = swap(cache, "xl")
    beside = both_ways(cache)
    count = jnp.broadcast_to(cache_count.astype(BF16)[None], (16, cache_keys.shape[1]))
    count = after(count, cache)
    counts = [count] + [moved(count, "z", by) for by in range(1, nz)]
    rows = after(tokens, other_cache)
    q, pack = project(rows, jnp.transpose(project_weight, (1, 0, 2)), counts)
    q, pack, *beside = lax.optimization_barrier((q, pack, *beside))
    other_pack = swap(pack, "xl")
    queries = [q] + [moved(q, "z", by) for by in range(1, nz)]
    cache_ring = round_y(cache, other_cache, beside)
    span_ring = round_y(pack, other_pack, both_ways(pack))

    held = after(output_weight, other_pack)
    crossed = swap(held, "tp", 2)
    out_weights = [held, swap(held, "tp", 1), crossed, swap(crossed, "tp", 1)]

    state = span_attend(idx, distance_slope, queries, span_ring, cache_keys.shape[0])
    parts = []
    for tile in (2, 1, 3, 0):
        pair = cache_attend(tile, queries[2 * tile], queries[2 * tile + 1], state, cache_ring)
        for by, part in zip((2 * tile, 2 * tile + 1), pair):
            parts.append(moved(part, "z", -by) if by else part)
    atts = round_tp(merge(parts))
    layer = layer_output(tokens, atts, out_weights)

    n = lax.axis_size(ctx_axes)
    rim = lax.ppermute(layer[-16:], ctx_axes, [(i, i + 1) for i in range(n - 1)])
    sq, skv = short_project(layer, rim, jnp.transpose(short_project_weight, (1, 0, 2)), nz)
    short_queries = exchange(sq, "z")
    pair = jnp.stack([skv, swap(skv, "xl")])
    short_keys = [pair] + [moved(pair, "y", by) for by in (1, 2, 3)]
    sparts = short_attend(idx, short_slope, short_queries, short_keys)
    terms = short_merge(tp, exchange(sparts, "z"), short_output)
    terms = [swap(t, "tp", flip) if flip else t for flip, t in enumerate(terms)]
    return final_sum(tp, layer, terms)


def solution(mesh):
    split = Mesh(mesh.devices.reshape(4, 8, 2, 4), ("y", "z", "xl", "tp"))
    ctx = ("y", "z", "xl")
    return jax.shard_map(
        on_device,
        mesh=split,
        in_specs=(
            P(ctx, None),
            P(None, None, "tp"),
            P("tp", None),
            P("tp"),
            P(ctx, "tp"),
            P(ctx, "tp"),
            P(ctx),
            P(None, None, "tp"),
            P("tp", None),
            P("tp"),
        ),
        out_specs=P(ctx, "tp"),
        check_vma=False,
    )
```

```python
import functools
import math

import jax
import jax.numpy as jnp
from jax import lax
from jax.experimental import pallas as pl
from jax.experimental.pallas import tpu as pltpu
from jax.sharding import Mesh, PartitionSpec as P

HS = 128
GROUP = 4
NEG = -1e30
LOG2E = math.log2(math.e)
SCALE2 = HS ** -0.5 * LOG2E

VMEM = pltpu.VMEM
SMEM = pltpu.SMEM
F32 = jnp.float32
BF16 = jnp.bfloat16


def cost(flops, moved, trans=0):
    return pl.CostEstimate(flops=flops, bytes_accessed=moved, transcendentals=trans)


def params(mib):
    return pltpu.CompilerParams(vmem_limit_bytes=mib * 1024 * 1024)


def rms_scaled(values):
    inv = lax.rsqrt(jnp.mean(values * values, axis=-1, keepdims=True) + 1e-06)
    return (values * inv).astype(BF16)


def dot_t(a, b):
    return lax.dot_general(a, b, (((1,), (1,)), ((), ())), preferred_element_type=F32)


def three_parts(x):
    hi = x.astype(BF16).astype(F32)
    mid = (x - hi).astype(BF16).astype(F32)
    lo = (x - hi - mid).astype(BF16).astype(F32)
    return hi, mid, lo


def project_kernel(count_ref, tok_ref, w_ref, ck_ref, cv_ref, q_ref, pack_ref, normed):
    step = pl.program_id(0)
    rows = tok_ref.shape[0]
    slots = ck_ref.shape[0]

    @pl.when(step == 0)
    def _():
        normed[...] = rms_scaled(tok_ref[...].astype(F32))
        pack_ref[:slots] = ck_ref[...]
        pack_ref[slots : 2 * slots] = cv_ref[...]
        count = jnp.full((16, pack_ref.shape[1]), count_ref[0], jnp.int32)
        pack_ref[2 * (slots + rows) :] = count.astype(F32).astype(BF16)

    out = jnp.dot(normed[...], w_ref[0], preferred_element_type=F32)

    @pl.when(step == 0)
    def _():
        q_ref[...] = (out * SCALE2).astype(BF16)

    @pl.when(step == 1)
    def _():
        pack_ref[2 * slots : 2 * slots + rows] = out.astype(BF16)

    @pl.when(step == 2)
    def _():
        pack_ref[2 * slots + rows : 2 * (slots + rows)] = out.astype(BF16)


def project(count, rows, weight3, cache_keys, cache_values):
    n, d = rows.shape
    width = weight3.shape[2]
    total = 2 * (n + cache_keys.shape[0]) + 16
    whole = lambda shape: pl.BlockSpec(shape, lambda i: (0, 0))
    return pl.pallas_call(
        project_kernel,
        grid=(3,),
        in_specs=[
            pl.BlockSpec(memory_space=SMEM),
            whole((n, d)),
            pl.BlockSpec((1, d, width), lambda i: (i, 0, 0)),
            whole(cache_keys.shape),
            whole(cache_values.shape),
        ],
        out_specs=[whole((n, width)), whole((total, width))],
        out_shape=[
            jax.ShapeDtypeStruct((n, width), BF16),
            jax.ShapeDtypeStruct((total, width), BF16),
        ],
        scratch_shapes=[VMEM((n, d), BF16)],
        compiler_params=params(12),
        cost_estimate=cost(6 * n * d * width, 2 * (n * d + 3 * d * width)),
        name="project",
    )(count, rows, weight3, cache_keys, cache_values)


def mark_kernel(q_ref, own_ref, other_ref, out_ref):
    rows = q_ref.shape[0]
    out_ref[:rows] = q_ref[...]
    step = lax.broadcasted_iota(jnp.int32, own_ref.shape, 0)
    own, other = own_ref[...].astype(F32), other_ref[...].astype(F32)
    out_ref[rows:] = jnp.where(step < 8, own, other).astype(BF16)


def mark(q, own, other):
    n, width = q.shape
    last = own.shape[0] // 16 - 1
    return pl.pallas_call(
        mark_kernel,
        grid=(1,),
        in_specs=[pl.BlockSpec((n, width), lambda i: (0, 0))]
        + [pl.BlockSpec((16, width), lambda i: (last, 0))] * 2,
        out_specs=pl.BlockSpec((n + 16, width), lambda i: (0, 0)),
        out_shape=jax.ShapeDtypeStruct((n + 16, width), BF16),
        compiler_params=params(8),
        cost_estimate=cost(0, 4 * n * width),
        name="mark",
    )(q, own, other)


def join_kernel(a_ref, b_ref, out_ref):
    rows = a_ref.shape[0]
    out_ref[:rows] = a_ref[...]
    out_ref[rows:] = b_ref[...]


def join(a, b):
    n, width = a.shape
    return pl.pallas_call(
        join_kernel,
        out_shape=jax.ShapeDtypeStruct((2 * n, width), BF16),
        compiler_params=params(8),
        cost_estimate=cost(0, 8 * n * width),
        name="join",
    )(a, b)


def plane_kernel(*refs):
    rows = []
    for pair in refs[:-1]:
        half = pair.shape[0] // 2
        for at in (half - 16, 2 * half - 16):
            marks = pair[at : at + 16].astype(F32)
            rows += [marks[:1], marks[8:9]]
    refs[-1][...] = jnp.concatenate(rows, axis=0).astype(BF16)


def plane_counts(queries):
    return pl.pallas_call(
        plane_kernel,
        out_shape=jax.ShapeDtypeStruct((16, queries[0].shape[1]), BF16),
        compiler_params=params(8),
        cost_estimate=cost(0, 8 * queries[0].size),
        name="plane_counts",
    )(*queries)


RING = ((0, 0), (0, 1), (1, 0), (1, 1), (3, 0), (3, 1), (2, 0), (2, 1))


def place_of_device():
    return lax.axis_index("y"), lax.axis_index("z"), lax.axis_index("xl")


def columns_of(pieces):
    return [s[:, at : at + HS] for s in pieces for at in range(0, s.shape[1], HS)]


def attend_heads(qs, pieces, score, value):
    heads = len(qs)
    pending = [score(0, qs[0], j) for j in range(pieces)]
    results = []
    for h in range(heads):
        top = jnp.max(functools.reduce(jnp.maximum, columns_of(pending)), axis=1, keepdims=True)
        following = []
        both = None
        for j in range(pieces):
            term = jnp.dot(
                jnp.exp2(pending[j] - top).astype(BF16), value(h, j), preferred_element_type=F32
            )
            both = term if both is None else both + term
            if h + 1 < heads:
                following.append(score(h + 1, qs[h + 1], j))
        pending = following
        results.append((top, both[:, HS:], both[:, :HS]))
    return results


def with_ones(v):
    return jnp.concatenate([v, jnp.ones_like(v)], axis=1)


def attend_kernel(slots, slope_ref, *refs):
    queries, planes, packs = refs[:4], refs[4:8], refs[8:16]
    out_ref, q_tile, bias = refs[16:]
    tile = pl.program_id(0)
    y, z, xl = place_of_device()
    rows = q_tile.shape[0] // 2
    width = q_tile.shape[1]
    heads = width // HS
    owners = len(RING)
    cached = owners * slots

    def side_of(other):
        return 1 - xl if other else xl

    for t in range(4):

        @pl.when(tile == t)
        def _(t=t):
            q_tile[:rows] = queries[t][:rows]
            q_tile[rows:] = queries[t][rows + 16 : 2 * rows + 16]

    @pl.when(tile == 0)
    def _():
        steps = lax.broadcasted_iota(jnp.int32, (16, width), 0)
        zs = (z + 8 - 2 * (steps // 4)) % 8
        zs = jnp.where((steps // 2) % 2 == 1, zs ^ 1, zs)
        totals, parts, owns = [], [], []
        for plane in planes:
            counts = plane[...].astype(F32)
            totals.append(jnp.sum(counts, axis=0, keepdims=True))
            parts.append(jnp.sum(jnp.where(zs < z, counts, 0.0), axis=0, keepdims=True))
            owns.append((counts[0:1], counts[1:2]))
        ys = [(y + 4 - back) % 4 for back in range(4)]
        everything = functools.reduce(jnp.add, totals)
        slot = lax.broadcasted_iota(jnp.int32, (1, slots), 1).astype(F32)
        place = lax.broadcasted_iota(jnp.int32, (1, rows), 1)
        for j, (back, other) in enumerate(RING):
            side = side_of(other)
            start = parts[back] - everything
            for i in range(4):
                start = start + jnp.where(ys[i] < ys[back], totals[i], 0.0)
            start = start + jnp.where(side == 1, owns[back][1 - other], 0.0)
            spot = (place + (ys[back] * 16 + z * 2 + side) * rows).astype(F32)
            for h in range(heads):
                slope = slope_ref[h] * LOG2E
                bias[h : h + 1, j * slots : (j + 1) * slots] = jnp.where(
                    slot < owns[back][other], slope * (slot + start), NEG
                )
                at = cached + j * rows
                bias[h : h + 1, at : at + rows] = jnp.where(ys[back] <= y, slope * spot, NEG)

    row = lax.broadcasted_iota(jnp.int32, (2 * rows, 1), 0)
    first = (z + 8 - 2 * tile) % 8
    row_ctx = y * 16 + xl + 2 * jnp.where(row < rows, first, first ^ 1)
    row_pos = row_ctx * rows + jnp.where(row < rows, row, row - rows)
    place = lax.broadcasted_iota(jnp.int32, (1, rows), 1)

    def score(h, q, j):
        cols = slice(h * HS, (h + 1) * HS)
        if j < owners:
            s = dot_t(q, packs[j][:slots, cols])
            return s + bias[h : h + 1, j * slots : (j + 1) * slots]
        back, other = RING[j - owners]
        at = cached + (j - owners) * rows
        s = dot_t(q, packs[j - owners][2 * slots : 2 * slots + rows, cols])
        s = s + bias[h : h + 1, at : at + rows]
        if back == 0:
            first_key = (y * 16 + z * 2 + side_of(other)) * rows
            s = jnp.where(place + first_key <= row_pos, s, NEG)
        return s

    def value(h, j):
        cols = slice(h * HS, (h + 1) * HS)
        if j < owners:
            return with_ones(packs[j][slots : 2 * slots, cols])
        return with_ones(packs[j - owners][2 * slots + rows : 2 * (slots + rows), cols])

    lane = lax.broadcasted_iota(jnp.int32, (2 * rows, HS), 1)
    packed = jnp.zeros((2 * rows, HS), F32)
    qs = [q_tile[:, h * HS : (h + 1) * HS] for h in range(heads)]
    done = []
    for h, (top, total, acc) in enumerate(attend_heads(qs, 2 * owners, score, value)):
        done.append((acc / total).astype(BF16))
        for k, piece in enumerate(three_parts(top + jnp.log2(total))):
            packed = jnp.where(lane == 3 * h + k, piece, packed)
    both = jnp.concatenate(done, axis=1)
    odd = z % 2 == 1
    blocks = []
    for own, level in (
        (jnp.where(odd, both[rows:], both[:rows]), jnp.where(odd, packed[rows:], packed[:rows])),
        (jnp.where(odd, both[:rows], both[rows:]), jnp.where(odd, packed[:rows], packed[rows:])),
    ):
        turned = jnp.transpose(level)[:16]
        tail = jnp.concatenate([turned, jnp.zeros_like(turned)], axis=1).astype(BF16)
        blocks.append((own, tail))
    for p in range(4):

        @pl.when((z // 2 + 4 - tile) % 4 == p)
        def _(p=p):
            for b, (own, tail) in enumerate(blocks):
                out_ref[2 * p + b, :rows] = own
                out_ref[2 * p + b, rows:] = tail


def attend(slopes, queries, planes, packs, slots):
    padded, width = queries[0].shape
    rows = padded // 2 - 16
    nk = len(RING) * (slots + rows)
    whole = lambda a: pl.BlockSpec(a.shape, lambda i: (0,) * a.ndim)
    out = jax.ShapeDtypeStruct((8, rows + 16, width), BF16)
    return pl.pallas_call(
        functools.partial(attend_kernel, slots),
        grid=(4,),
        in_specs=[pl.BlockSpec(memory_space=SMEM)]
        + [whole(a) for a in (*queries, *planes, *packs)],
        out_specs=whole(out),
        out_shape=out,
        scratch_shapes=[VMEM((2 * rows, width), BF16), VMEM((8, nk), F32)],
        compiler_params=params(40),
        cost_estimate=cost(32 * rows * nk * width, 4 * nk * width, 16 * rows * nk),
        name="attend",
    )(slopes, *queries, *planes, *packs)


def merge_kernel(heads, parts_ref, out_ref):
    sources, padded, width = parts_ref.shape
    rows = padded - 16
    levels = jnp.concatenate(
        [parts_ref[s, rows:, :HS].astype(F32) for s in range(sources)], axis=0
    )
    turned = jnp.transpose(levels)
    for h in range(heads):
        cols = slice(h * HS, (h + 1) * HS)
        level = []
        for s in range(sources):
            at = s * 16 + 3 * h
            level.append(
                (turned[:, at : at + 1] + turned[:, at + 1 : at + 2]) + turned[:, at + 2 : at + 3]
            )
        top = functools.reduce(jnp.maximum, level)
        total = jnp.zeros((rows, 1), F32)
        acc = jnp.zeros((rows, HS), F32)
        for s in range(sources):
            weight = jnp.exp2(level[s] - top)
            total = total + weight
            acc = acc + weight * parts_ref[s, :rows, cols].astype(F32)
        out_ref[:, cols] = (acc / total).astype(BF16)


def merge(parts):
    sources, padded, width = parts.shape
    rows = padded - 16
    return pl.pallas_call(
        functools.partial(merge_kernel, width // HS),
        out_shape=jax.ShapeDtypeStruct((rows, width), BF16),
        compiler_params=params(16),
        cost_estimate=cost(4 * sources * rows * width, 2 * sources * padded * width),
        name="merge",
    )(parts)


def product_kernel(tok_ref, a_ref, b_ref, wa_ref, wb_ref, sum_ref, term_ref, rim_ref):
    term = jnp.dot(a_ref[...], wa_ref[...], preferred_element_type=F32) + jnp.dot(
        b_ref[...], wb_ref[...], preferred_element_type=F32
    )
    total = tok_ref[...].astype(F32) + term
    sum_ref[...] = total
    term_ref[...] = term.astype(BF16)
    rim_ref[:16] = total[-16:].astype(BF16)
    rim_ref[16:] = term[-16:].astype(BF16)


def layer_product(tokens, atts, weights):
    rows, d = tokens.shape
    step = 512
    inner, width = weights[0].shape[0], atts[0].shape[1]
    cols = lambda n: pl.BlockSpec((n, step), lambda i: (0, i))
    return pl.pallas_call(
        product_kernel,
        grid=(d // step,),
        in_specs=[cols(rows)]
        + [pl.BlockSpec((rows, width), lambda i: (0, 0))] * 2
        + [cols(inner)] * 2,
        out_specs=[cols(rows), cols(rows), cols(32)],
        out_shape=[
            jax.ShapeDtypeStruct((rows, d), F32),
            jax.ShapeDtypeStruct((rows, d), BF16),
            jax.ShapeDtypeStruct((32, d), BF16),
        ],
        compiler_params=params(16),
        cost_estimate=cost(4 * rows * d * inner, 4 * inner * d),
        name="layer_product",
    )(tokens, *atts, *weights)


def short_project_kernel(
    sum_ref, term_ref, rim_a, rim_b, w_ref, cols_ref, q_ref, kv_ref, normed
):
    step = pl.program_id(0)
    rows, d = sum_ref.shape
    groups = rows // GROUP
    rim_rows = 16
    width = q_ref.shape[1]

    @pl.when(step == 0)
    def _():
        layer = (sum_ref[...] + term_ref[...].astype(F32)).astype(BF16)
        part = d // 4
        tp = lax.axis_index("tp")
        mine = layer[:, :part]
        for t in range(1, 4):
            mine = jnp.where(tp == t, layer[:, t * part : (t + 1) * part], mine)
        cols_ref[...] = mine
        rim = (rim_a[:rim_rows].astype(F32) + rim_b[rim_rows:].astype(F32)).astype(BF16)
        g = lax.broadcasted_iota(jnp.int32, (groups, rows), 0) * GROUP
        t = lax.broadcasted_iota(jnp.int32, (groups, rows), 1)
        own = jnp.where((t <= g) & (t > g - GROUP), 1.0 / GROUP, 0.0).astype(BF16)
        g = lax.broadcasted_iota(jnp.int32, (groups, rim_rows), 0) * GROUP
        t = lax.broadcasted_iota(jnp.int32, (groups, rim_rows), 1) - rim_rows
        before = jnp.where(t > g - GROUP, 1.0 / GROUP, 0.0).astype(BF16)
        pooled = jnp.dot(own, layer, preferred_element_type=F32) + jnp.dot(
            before, rim, preferred_element_type=F32
        )
        normed[...] = rms_scaled(pooled.astype(BF16).astype(F32))

    out = jnp.dot(normed[...], w_ref[0], preferred_element_type=F32)

    @pl.when(step == 0)
    def _():
        q_ref[...] = (out * SCALE2).astype(BF16)

    @pl.when(step == 1)
    def _():
        kv_ref[:, :width] = out.astype(BF16)

    @pl.when(step == 2)
    def _():
        kv_ref[:, width:] = out.astype(BF16)


def short_project(total, term, rims, weight3):
    n, d = total.shape
    groups = n // GROUP
    width = weight3.shape[2]
    whole = lambda shape: pl.BlockSpec(shape, lambda i: (0, 0))
    shapes = [(n, d // 4), (groups, width), (groups, 2 * width)]
    return pl.pallas_call(
        short_project_kernel,
        grid=(3,),
        in_specs=[whole((n, d)), whole((n, d)), whole((32, d)), whole((32, d))]
        + [pl.BlockSpec((1, d, width), lambda i: (i, 0, 0))],
        out_specs=[whole(s) for s in shapes],
        out_shape=[jax.ShapeDtypeStruct(s, BF16) for s in shapes],
        scratch_shapes=[VMEM((groups, d), BF16)],
        compiler_params=params(16),
        cost_estimate=cost(6 * groups * d * width, 2 * (n * d + 3 * d * width)),
        name="short_project",
    )(total, term, *rims, weight3)


def join_two_kernel(a, b, c, d, left, right):
    for x, y, out in ((a, b, left), (c, d, right)):
        out[: x.shape[0]] = x[...]
        out[x.shape[0] :] = y[...]


def join_two(a, b, c, d):
    shapes = [(2 * x.shape[0], x.shape[1]) for x in (a, c)]
    return pl.pallas_call(
        join_two_kernel,
        out_shape=[jax.ShapeDtypeStruct(s, BF16) for s in shapes],
        compiler_params=params(8),
        cost_estimate=cost(0, 8 * (a.size + c.size)),
        name="join_two",
    )(a, b, c, d)


def short_attend_kernel(slope_ref, q0, q1, kv0, kv1, out_ref):
    y, z, xl = place_of_device()
    _, groups, _ = out_ref.shape
    width = q0.shape[1]
    heads = width // HS
    nr = nk = 8 * groups
    row = lax.broadcasted_iota(jnp.int32, (nr, 1), 0)
    zs = row // groups
    row_pos = (y * 16 + zs * 2 + xl) * groups + row % groups
    came = (zs ^ z) * groups + row % groups
    order = jnp.where(lax.broadcasted_iota(jnp.int32, (nr, nr), 1) == came, 1.0, 0.0).astype(BF16)
    key = lax.broadcasted_iota(jnp.int32, (1, nk), 1)
    block = key // groups
    key_pos = ((y ^ (block // 2)) * 16 + z * 2 + (xl ^ (block % 2))) * groups + key % groups
    usable = key_pos <= row_pos
    spot = key_pos.astype(F32)
    lane = lax.broadcasted_iota(jnp.int32, (nr, HS), 1)
    packed = jnp.zeros((nr, HS), F32)
    queries = jnp.concatenate([q0[...], q1[...]], axis=0)
    queries = jnp.dot(order, queries, preferred_element_type=F32).astype(BF16)
    outs = []
    for h in range(heads):
        cols = slice(h * HS, (h + 1) * HS)
        k = jnp.concatenate([kv0[:, cols], kv1[:, cols]], axis=0)
        cols_v = slice(width + h * HS, width + (h + 1) * HS)
        v = jnp.concatenate([kv0[:, cols_v], kv1[:, cols_v]], axis=0)
        s = dot_t(queries[:, cols], k) + (slope_ref[h] * LOG2E) * spot
        s = jnp.where(usable, s, NEG)
        top = jnp.max(s, axis=1, keepdims=True)
        p = jnp.exp2(s - top).astype(BF16)
        both = jnp.dot(p, with_ones(v), preferred_element_type=F32)
        weight_total = both[:, HS:]
        outs.append((both[:, :HS] / weight_total).astype(BF16))
        level = top + jnp.log2(weight_total)
        for k, piece in enumerate(three_parts(level)):
            packed = jnp.where(lane == 3 * h + k, piece, packed)
    out = jnp.concatenate(outs + [packed.astype(BF16)], axis=1)
    out_ref[...] = out.reshape(out_ref.shape)


def short_attend(slopes, q0, q1, kv0, kv1):
    n, width = q0.shape
    groups = n // 4
    smem = pl.BlockSpec(memory_space=SMEM)
    vmem = pl.BlockSpec(memory_space=VMEM)
    return pl.pallas_call(
        short_attend_kernel,
        in_specs=[smem] + [vmem] * 4,
        out_specs=vmem,
        out_shape=jax.ShapeDtypeStruct((8, groups, width + HS), BF16),
        compiler_params=params(16),
        cost_estimate=cost(16 * n * n * width, 8 * n * width),
        name="short_attend",
    )(slopes, q0, q1, kv0, kv1)


def short_merge_kernel(heads, parts_ref, w_ref, *outs):
    sources, rows, padded = parts_ref.shape
    width = padded - HS
    merged = []
    for h in range(heads):
        cols = slice(h * HS, (h + 1) * HS)
        level = []
        for s in range(sources):
            lev = parts_ref[s, :, width:].astype(F32)
            level.append(
                (lev[:, 3 * h : 3 * h + 1] + lev[:, 3 * h + 1 : 3 * h + 2])
                + lev[:, 3 * h + 2 : 3 * h + 3]
            )
        top = functools.reduce(jnp.maximum, level)
        total = jnp.zeros((rows, 1), F32)
        acc = jnp.zeros((rows, HS), F32)
        for s in range(sources):
            weight = jnp.exp2(level[s] - top)
            total = total + weight
            acc = acc + weight * parts_ref[s, :, cols].astype(F32)
        merged.append((acc / total).astype(BF16))
    att = jnp.concatenate(merged, axis=1)
    cols = outs[0].shape[1]
    terms = [
        jnp.dot(
            att, w_ref[:, t * cols : (t + 1) * cols], preferred_element_type=F32
        ).astype(BF16)
        for t in range(4)
    ]
    tp = lax.axis_index("tp")
    for flip, out in enumerate(outs):
        chosen = terms[flip]
        for t in range(1, 4):
            chosen = jnp.where(tp == t, terms[t ^ flip], chosen)
        out[...] = chosen


def short_merge(parts, weight):
    sources, rows, padded = parts.shape
    width = padded - HS
    cols = weight.shape[1] // 4
    out = jax.ShapeDtypeStruct((rows, cols), BF16)
    return pl.pallas_call(
        functools.partial(short_merge_kernel, width // HS),
        out_shape=[out] * 4,
        compiler_params=params(16),
        cost_estimate=cost(8 * rows * width * cols, 8 * width * cols),
        name="short_merge",
    )(parts, weight)


def final_kernel(lay_ref, *refs):
    terms, out_ref = refs[:-1], refs[-1]
    rows, groups = lay_ref.shape[0], terms[0].shape[0]
    t = lax.broadcasted_iota(jnp.int32, (rows, groups), 0) // GROUP
    g = lax.broadcasted_iota(jnp.int32, (rows, groups), 1)
    spread = jnp.where(t == g, 1.0, 0.0).astype(BF16)
    branch = jnp.zeros(lay_ref.shape, F32)
    for term in terms:
        branch = branch + jnp.dot(spread, term[...], preferred_element_type=F32)
    out_ref[...] = (lay_ref[...].astype(F32) + branch).astype(BF16)


def final_sum(layer, terms):
    rows, cols = layer.shape
    groups = terms[0].shape[0]
    return pl.pallas_call(
        final_kernel,
        out_shape=jax.ShapeDtypeStruct((rows, cols), BF16),
        compiler_params=params(16),
        cost_estimate=cost(8 * rows * cols * groups, 4 * rows * cols),
        name="final_sum",
    )(layer, *terms)


def exchange(blocks, axis):
    return lax.all_to_all(blocks, axis, 0, 0)


def swap(x, axis, flip=1):
    return lax.ppermute(x, axis, [(i, i ^ flip) for i in range(lax.axis_size(axis))])


def moved(x, axis, by):
    n = lax.axis_size(axis)
    return lax.ppermute(x, axis, [(i, (i + by) % n) for i in range(n)])


def both_ways(x):
    return moved(x, "y", 1), moved(x, "y", -1)


def after(x, *others):
    return lax.optimization_barrier((x, *others))[0]


def on_device(
    tokens,
    project_weight,
    output_weight,
    distance_slope,
    cache_keys,
    cache_values,
    cache_count,
    short_project_weight,
    short_output,
    short_slope,
):
    axes = ("y", "z", "xl", "tp")
    slots = cache_keys.shape[0]
    q, pack = project(
        cache_count, tokens, jnp.transpose(project_weight, (1, 0, 2)), cache_keys, cache_values
    )
    other = swap(pack, "xl")
    left, right = both_ways(pack)
    marked = mark(q, pack, other)
    pair = join(marked, swap(marked, "z"))
    left_other, right_other = both_ways(other)
    queries = [pair] + [moved(pair, "z", by) for by in (2, 4, 6)]
    far, far_other = moved(left, "y", 1), moved(right_other, "y", -1)
    crossed = swap(after(output_weight, other), "tp", 2)
    plane = plane_counts(queries)
    planes = [plane] + [moved(plane, "y", by) for by in (1, 2, 3)]
    packs = [pack, other, left, left_other, right, right_other, far, far_other]
    parts = attend(distance_slope, queries, planes, packs, slots)

    att = merge(exchange(parts, "z"))
    total, term, rim = layer_product(
        tokens, (att, swap(att, "tp", 2)), (output_weight, crossed)
    )
    n, tp = lax.axis_size(axes), lax.axis_size("tp")
    ahead = [(i, i + tp) for i in range(n - tp)]
    rims = [
        lax.ppermute(rim, axes, ahead),
        lax.ppermute(rim, axes, [(i, j ^ 1) for i, j in ahead]),
    ]
    layer, sq, skv = short_project(
        total, swap(term, "tp", 1), rims, jnp.transpose(short_project_weight, (1, 0, 2))
    )
    sq, skv = join_two(sq, swap(sq, "z"), skv, swap(skv, "xl"))
    sq, skv = join_two(sq, swap(sq, "z", 2), skv, swap(skv, "y"))
    sparts = short_attend(
        short_slope, sq, swap(sq, "z", 4), skv, swap(skv, "y", 2)
    )
    terms = short_merge(exchange(sparts, "z"), short_output)
    terms = [swap(t, "tp", flip) if flip else t for flip, t in enumerate(terms)]
    return final_sum(layer, terms)


def solution(mesh):
    split = Mesh(mesh.devices.reshape(4, 8, 2, 4), ("y", "z", "xl", "tp"))
    ctx = ("y", "z", "xl")
    return jax.shard_map(
        on_device,
        mesh=split,
        in_specs=(
            P(ctx, None),
            P(None, None, "tp"),
            P("tp", None),
            P("tp"),
            P(ctx, "tp"),
            P(ctx, "tp"),
            P(ctx),
            P(None, None, "tp"),
            P("tp", None),
            P("tp"),
        ),
        out_specs=P(ctx, "tp"),
        check_vma=False,
    )
```

```python
import functools
import math

import jax
import jax.numpy as jnp
from jax import lax
from jax.experimental import pallas as pl
from jax.experimental.pallas import tpu as pltpu
from jax.sharding import Mesh, PartitionSpec as P

HS = 128
GROUP = 4
NEG = -1e30
LOG2E = math.log2(math.e)
SCALE2 = HS ** -0.5 * LOG2E

VMEM = pltpu.VMEM
SMEM = pltpu.SMEM
HBM = pltpu.HBM
F32 = jnp.float32
BF16 = jnp.bfloat16


def cost(flops, moved, trans=0):
    return pl.CostEstimate(flops=flops, bytes_accessed=moved, transcendentals=trans)


def params(mib):
    return pltpu.CompilerParams(vmem_limit_bytes=mib * 1024 * 1024)


def rms_scaled(values):
    inv = lax.rsqrt(jnp.mean(values * values, axis=-1, keepdims=True) + 1e-06)
    return (values * inv).astype(BF16)


def dot_t(a, b):
    return lax.dot_general(a, b, (((1,), (1,)), ((), ())), preferred_element_type=F32)


def three_parts(x):
    hi = x.astype(BF16).astype(F32)
    mid = (x - hi).astype(BF16).astype(F32)
    lo = (x - hi - mid).astype(BF16).astype(F32)
    return hi, mid, lo


def project_kernel(
    count_ref, tok_hbm, w_hbm, ck_hbm, cv_hbm, q_ref, pack_ref, tok, weight, sems
):
    rows = tok.shape[0]
    slots = ck_hbm.shape[0]
    width = q_ref.shape[1]
    copies = [pltpu.make_async_copy(tok_hbm, tok, sems.at[0])]
    copies += [
        pltpu.make_async_copy(w_hbm.at[i], weight.at[i], sems.at[1 + i]) for i in range(3)
    ]
    copies += [
        pltpu.make_async_copy(ck_hbm, pack_ref.at[:slots], sems.at[4]),
        pltpu.make_async_copy(cv_hbm, pack_ref.at[slots : 2 * slots], sems.at[5]),
    ]
    for copy in copies:
        copy.start()
    count = jnp.full((16, width), count_ref[0], jnp.int32)
    pack_ref[2 * (slots + rows) :] = count.astype(F32).astype(BF16)
    copies[0].wait()
    normed = rms_scaled(tok[...].astype(F32))
    for i in range(3):
        copies[1 + i].wait()
        out = jnp.dot(normed, weight[i], preferred_element_type=F32)
        if i == 0:
            q_ref[...] = (out * SCALE2).astype(BF16)
        else:
            at = 2 * slots + (i - 1) * rows
            pack_ref[at : at + rows] = out.astype(BF16)
    copies[4].wait()
    copies[5].wait()


def project(count, rows, weight3, cache_keys, cache_values):
    n, d = rows.shape
    width = weight3.shape[2]
    total = 2 * (n + cache_keys.shape[0]) + 16
    hbm = pl.BlockSpec(memory_space=HBM)
    vmem = pl.BlockSpec(memory_space=VMEM)
    return pl.pallas_call(
        project_kernel,
        in_specs=[pl.BlockSpec(memory_space=SMEM), hbm, hbm, hbm, hbm],
        out_specs=[vmem, vmem],
        out_shape=[
            jax.ShapeDtypeStruct((n, width), BF16),
            jax.ShapeDtypeStruct((total, width), BF16),
        ],
        scratch_shapes=[
            VMEM((n, d), BF16),
            VMEM(weight3.shape, BF16),
            pltpu.SemaphoreType.DMA((6,)),
        ],
        compiler_params=params(60),
        cost_estimate=cost(6 * n * d * width, 2 * (n * d + 3 * d * width)),
        name="project",
    )(count, rows, weight3, cache_keys, cache_values)


def mark_kernel(q_ref, own_ref, other_ref, out_ref):
    rows = q_ref.shape[0]
    out_ref[:rows] = q_ref[...]
    step = lax.broadcasted_iota(jnp.int32, own_ref.shape, 0)
    own, other = own_ref[...].astype(F32), other_ref[...].astype(F32)
    out_ref[rows:] = jnp.where(step < 8, own, other).astype(BF16)


def mark(q, own, other):
    n, width = q.shape
    return pl.pallas_call(
        mark_kernel,
        out_shape=jax.ShapeDtypeStruct((n + 16, width), BF16),
        compiler_params=params(8),
        cost_estimate=cost(0, 4 * n * width),
        name="mark",
    )(q, own, other)


def halves_kernel(left_ref, right_ref, own_ref, other_ref):
    half = own_ref.shape[0]
    own_ref[...] = left_ref[:half]
    other_ref[...] = right_ref[half:]


def halves(left, right):
    n, width = left.shape
    out = jax.ShapeDtypeStruct((n // 2, width), BF16)
    return pl.pallas_call(
        halves_kernel,
        out_shape=[out, out],
        compiler_params=params(8),
        cost_estimate=cost(0, 4 * n * width),
        name="halves",
    )(left, right)


def join_kernel(a_ref, b_ref, out_ref):
    rows = a_ref.shape[0]
    out_ref[:rows] = a_ref[...]
    out_ref[rows:] = b_ref[...]


def join(a, b):
    n, width = a.shape
    return pl.pallas_call(
        join_kernel,
        out_shape=jax.ShapeDtypeStruct((2 * n, width), BF16),
        compiler_params=params(8),
        cost_estimate=cost(0, 8 * n * width),
        name="join",
    )(a, b)


def plane_kernel(own, left, right, far, far_other, out_ref):
    rows = []
    half = far.shape[0]
    for ref, end in (
        (own, half),
        (own, 2 * half),
        (left, half),
        (left, 2 * half),
        (far, half),
        (far_other, half),
        (right, half),
        (right, 2 * half),
    ):
        marks = ref[end - 16 : end].astype(F32)
        rows += [marks[:1], marks[8:9]]
    out_ref[...] = jnp.concatenate(rows, axis=0).astype(BF16)


def plane_counts(queries):
    return pl.pallas_call(
        plane_kernel,
        out_shape=jax.ShapeDtypeStruct((16, queries[0].shape[1]), BF16),
        compiler_params=params(8),
        cost_estimate=cost(0, 8 * queries[0].size),
        name="plane_counts",
    )(*queries)


RING = ((0, 0), (0, 1), (1, 0), (1, 1), (3, 0), (3, 1), (2, 0), (2, 1))


def place_of_device():
    return lax.axis_index("y"), lax.axis_index("z"), lax.axis_index("xl")


def columns_of(pieces):
    return [s[:, at : at + HS] for s in pieces for at in range(0, s.shape[1], HS)]


def attend_heads(qs, pieces, score, value):
    heads = len(qs)
    pending = [score(0, qs[0], j) for j in range(pieces)]
    results = []
    for h in range(heads):
        top = jnp.max(functools.reduce(jnp.maximum, columns_of(pending)), axis=1, keepdims=True)
        following = []
        both = None
        for j in range(pieces):
            term = jnp.dot(
                jnp.exp2(pending[j] - top).astype(BF16), value(h, j), preferred_element_type=F32
            )
            both = term if both is None else both + term
            if h + 1 < heads:
                following.append(score(h + 1, qs[h + 1], j))
        pending = following
        results.append((top, both[:, HS:], both[:, :HS]))
    return results


def with_ones(v):
    return jnp.concatenate([v, jnp.ones_like(v)], axis=1)


def attend_kernel(slots, slope_ref, *refs):
    queries, planes, packs = refs[:5], refs[5:9], refs[9:17]
    out_ref, q_tile, bias = refs[17:]
    tile = pl.program_id(0)
    y, z, xl = place_of_device()
    rows = q_tile.shape[0] // 2
    width = q_tile.shape[1]
    heads = width // HS
    owners = len(RING)
    cached = owners * slots

    def side_of(other):
        return 1 - xl if other else xl

    own, left, right, far, far_other = queries
    step = rows + 16
    for t, (a, b, at) in enumerate(
        ((own, own, step), (left, left, step), (far, far_other, 0), (right, right, step))
    ):

        @pl.when(tile == t)
        def _(a=a, b=b, at=at):
            q_tile[:rows] = a[:rows]
            q_tile[rows:] = b[at : at + rows]

    @pl.when(tile == 0)
    def _():
        steps = lax.broadcasted_iota(jnp.int32, (16, width), 0)
        zs = (z + 8 - 2 * (steps // 4)) % 8
        zs = jnp.where((steps // 2) % 2 == 1, zs ^ 1, zs)
        totals, parts, owns = [], [], []
        for plane in planes:
            counts = plane[...].astype(F32)
            totals.append(jnp.sum(counts, axis=0, keepdims=True))
            parts.append(jnp.sum(jnp.where(zs < z, counts, 0.0), axis=0, keepdims=True))
            owns.append((counts[0:1], counts[1:2]))
        ys = [(y + 4 - back) % 4 for back in range(4)]
        everything = functools.reduce(jnp.add, totals)
        slot = lax.broadcasted_iota(jnp.int32, (1, slots), 1).astype(F32)
        place = lax.broadcasted_iota(jnp.int32, (1, rows), 1)
        for j, (back, other) in enumerate(RING):
            side = side_of(other)
            start = parts[back] - everything
            for i in range(4):
                start = start + jnp.where(ys[i] < ys[back], totals[i], 0.0)
            start = start + jnp.where(side == 1, owns[back][1 - other], 0.0)
            spot = (place + (ys[back] * 16 + z * 2 + side) * rows).astype(F32)
            for h in range(heads):
                slope = slope_ref[h] * LOG2E
                bias[h : h + 1, j * slots : (j + 1) * slots] = jnp.where(
                    slot < owns[back][other], slope * (slot + start), NEG
                )
                at = cached + j * rows
                bias[h : h + 1, at : at + rows] = jnp.where(ys[back] <= y, slope * spot, NEG)

    row = lax.broadcasted_iota(jnp.int32, (2 * rows, 1), 0)
    first = (z + 8 - 2 * tile) % 8
    row_ctx = y * 16 + xl + 2 * jnp.where(row < rows, first, first ^ 1)
    row_pos = row_ctx * rows + jnp.where(row < rows, row, row - rows)
    place = lax.broadcasted_iota(jnp.int32, (1, rows), 1)

    def score(h, q, j):
        cols = slice(h * HS, (h + 1) * HS)
        if j < owners:
            s = dot_t(q, packs[j][:slots, cols])
            return s + bias[h : h + 1, j * slots : (j + 1) * slots]
        back, other = RING[j - owners]
        at = cached + (j - owners) * rows
        s = dot_t(q, packs[j - owners][2 * slots : 2 * slots + rows, cols])
        s = s + bias[h : h + 1, at : at + rows]
        if back == 0:
            first_key = (y * 16 + z * 2 + side_of(other)) * rows
            s = jnp.where(place + first_key <= row_pos, s, NEG)
        return s

    def value(h, j):
        cols = slice(h * HS, (h + 1) * HS)
        if j < owners:
            return with_ones(packs[j][slots : 2 * slots, cols])
        return with_ones(packs[j - owners][2 * slots + rows : 2 * (slots + rows), cols])

    lane = lax.broadcasted_iota(jnp.int32, (2 * rows, HS), 1)
    packed = jnp.zeros((2 * rows, HS), F32)
    qs = [q_tile[:, h * HS : (h + 1) * HS] for h in range(heads)]
    done = []
    for h, (top, total, acc) in enumerate(attend_heads(qs, 2 * owners, score, value)):
        done.append((acc / total).astype(BF16))
        for k, piece in enumerate(three_parts(top + jnp.log2(total))):
            packed = jnp.where(lane == 3 * h + k, piece, packed)
    both = jnp.concatenate(done, axis=1)
    odd = z % 2 == 1
    blocks = []
    for own, level in (
        (jnp.where(odd, both[rows:], both[:rows]), jnp.where(odd, packed[rows:], packed[:rows])),
        (jnp.where(odd, both[:rows], both[rows:]), jnp.where(odd, packed[:rows], packed[rows:])),
    ):
        turned = jnp.transpose(level)[:16]
        tail = jnp.concatenate([turned, jnp.zeros_like(turned)], axis=1).astype(BF16)
        blocks.append((own, tail))
    for p in range(4):

        @pl.when((z // 2 + 4 - tile) % 4 == p)
        def _(p=p):
            for b, (own, tail) in enumerate(blocks):
                out_ref[2 * p + b, :rows] = own
                out_ref[2 * p + b, rows:] = tail


def attend(slopes, queries, planes, packs, slots):
    padded, width = queries[0].shape
    rows = padded // 2 - 16
    nk = len(RING) * (slots + rows)
    whole = lambda a: pl.BlockSpec(a.shape, lambda i: (0,) * a.ndim)
    out = jax.ShapeDtypeStruct((8, rows + 16, width), BF16)
    return pl.pallas_call(
        functools.partial(attend_kernel, slots),
        grid=(4,),
        in_specs=[pl.BlockSpec(memory_space=SMEM)]
        + [whole(a) for a in (*queries, *planes, *packs)],
        out_specs=whole(out),
        out_shape=out,
        scratch_shapes=[VMEM((2 * rows, width), BF16), VMEM((8, nk), F32)],
        compiler_params=params(40),
        cost_estimate=cost(32 * rows * nk * width, 4 * nk * width, 16 * rows * nk),
        name="attend",
    )(slopes, *queries, *planes, *packs)


def merge_kernel(heads, parts_ref, out_ref):
    sources, padded, width = parts_ref.shape
    rows = padded - 16
    levels = jnp.concatenate(
        [parts_ref[s, rows:, :HS].astype(F32) for s in range(sources)], axis=0
    )
    turned = jnp.transpose(levels)
    for h in range(heads):
        cols = slice(h * HS, (h + 1) * HS)
        level = []
        for s in range(sources):
            at = s * 16 + 3 * h
            level.append(
                (turned[:, at : at + 1] + turned[:, at + 1 : at + 2]) + turned[:, at + 2 : at + 3]
            )
        top = functools.reduce(jnp.maximum, level)
        total = jnp.zeros((rows, 1), F32)
        acc = jnp.zeros((rows, HS), F32)
        for s in range(sources):
            weight = jnp.exp2(level[s] - top)
            total = total + weight
            acc = acc + weight * parts_ref[s, :rows, cols].astype(F32)
        out_ref[:, cols] = (acc / total).astype(BF16)


def merge(parts):
    sources, padded, width = parts.shape
    rows = padded - 16
    return pl.pallas_call(
        functools.partial(merge_kernel, width // HS),
        out_shape=jax.ShapeDtypeStruct((rows, width), BF16),
        compiler_params=params(16),
        cost_estimate=cost(4 * sources * rows * width, 2 * sources * padded * width),
        name="merge",
    )(parts)


def product_kernel(
    tok_hbm, a_ref, b_ref, wa_hbm, wb_hbm, sum_ref, term_ref, rim_ref, tok, wa, wb, sems
):
    chunks = wa.shape[0]
    cols = wa.shape[2]
    copies = []
    for c in range(chunks):
        at = pl.ds(c * cols, cols)
        copies.append(
            [
                pltpu.make_async_copy(src.at[:, at], dst.at[c], sems.at[i, c])
                for i, (src, dst) in enumerate(((wa_hbm, wa), (wb_hbm, wb), (tok_hbm, tok)))
            ]
        )
    for group in copies:
        for copy in group:
            copy.start()
    for c, group in enumerate(copies):
        for copy in group:
            copy.wait()
        at = slice(c * cols, (c + 1) * cols)
        term = jnp.dot(a_ref[...], wa[c], preferred_element_type=F32) + jnp.dot(
            b_ref[...], wb[c], preferred_element_type=F32
        )
        total = tok[c].astype(F32) + term
        sum_ref[:, at] = total
        term_ref[:, at] = term.astype(BF16)
        rim_ref[:16, at] = total[-16:].astype(BF16)
        rim_ref[16:, at] = term[-16:].astype(BF16)


def layer_product(tokens, atts, weights):
    rows, d = tokens.shape
    chunks = 4
    inner = weights[0].shape[0]
    hbm = pl.BlockSpec(memory_space=HBM)
    vmem = pl.BlockSpec(memory_space=VMEM)
    return pl.pallas_call(
        product_kernel,
        in_specs=[hbm, vmem, vmem, hbm, hbm],
        out_specs=[vmem] * 3,
        out_shape=[
            jax.ShapeDtypeStruct((rows, d), F32),
            jax.ShapeDtypeStruct((rows, d), BF16),
            jax.ShapeDtypeStruct((32, d), BF16),
        ],
        scratch_shapes=[
            VMEM((chunks, rows, d // chunks), BF16),
            VMEM((chunks, inner, d // chunks), BF16),
            VMEM((chunks, inner, d // chunks), BF16),
            pltpu.SemaphoreType.DMA((3, chunks)),
        ],
        compiler_params=params(16),
        cost_estimate=cost(4 * rows * d * inner, 4 * inner * d),
        name="layer_product",
    )(tokens, *atts, *weights)


def short_project_kernel(
    sum_ref, term_ref, rim_a, rim_b, w_ref, cols_ref, qkv_ref, normed
):
    step = pl.program_id(0)
    rows, d = sum_ref.shape
    groups = rows // GROUP
    rim_rows = 16
    width = w_ref.shape[2]

    @pl.when(step == 0)
    def _():
        layer = (sum_ref[...] + term_ref[...].astype(F32)).astype(BF16)
        part = d // 4
        tp = lax.axis_index("tp")
        mine = layer[:, :part]
        for t in range(1, 4):
            mine = jnp.where(tp == t, layer[:, t * part : (t + 1) * part], mine)
        cols_ref[...] = mine
        rim = (rim_a[:rim_rows].astype(F32) + rim_b[rim_rows:].astype(F32)).astype(BF16)
        g = lax.broadcasted_iota(jnp.int32, (groups, rows), 0) * GROUP
        t = lax.broadcasted_iota(jnp.int32, (groups, rows), 1)
        own = jnp.where((t <= g) & (t > g - GROUP), 1.0 / GROUP, 0.0).astype(BF16)
        g = lax.broadcasted_iota(jnp.int32, (groups, rim_rows), 0) * GROUP
        t = lax.broadcasted_iota(jnp.int32, (groups, rim_rows), 1) - rim_rows
        before = jnp.where(t > g - GROUP, 1.0 / GROUP, 0.0).astype(BF16)
        pooled = jnp.dot(own, layer, preferred_element_type=F32) + jnp.dot(
            before, rim, preferred_element_type=F32
        )
        normed[...] = rms_scaled(pooled.astype(BF16).astype(F32))

    out = jnp.dot(normed[...], w_ref[0], preferred_element_type=F32)

    scaled = jnp.where(step == 0, out * SCALE2, out).astype(BF16)
    for i in range(3):

        @pl.when(step == i)
        def _(i=i):
            for c in range(qkv_ref.shape[0]):
                qkv_ref[c, :, i * width : (i + 1) * width] = scaled


def short_project(total, term, rims, weight3, copies):
    n, d = total.shape
    groups = n // GROUP
    width = weight3.shape[2]
    whole = lambda shape: pl.BlockSpec(shape, lambda i: (0,) * len(shape))
    shapes = [(n, d // 4), (copies, groups, 3 * width)]
    return pl.pallas_call(
        short_project_kernel,
        grid=(3,),
        in_specs=[whole((n, d)), whole((n, d)), whole((32, d)), whole((32, d))]
        + [pl.BlockSpec((1, d, width), lambda i: (i, 0, 0))],
        out_specs=[whole(s) for s in shapes],
        out_shape=[jax.ShapeDtypeStruct(s, BF16) for s in shapes],
        scratch_shapes=[VMEM((groups, d), BF16)],
        compiler_params=params(16),
        cost_estimate=cost(6 * groups * d * width, 2 * (n * d + 3 * d * width)),
        name="short_project",
    )(total, term, *rims, weight3)


def keys_kernel(qkv_ref, out_ref):
    width = out_ref.shape[2]
    out_ref[...] = qkv_ref[:, :, width // 2 :]


def keys_of(qkv):
    blocks, groups, width = qkv.shape
    return pl.pallas_call(
        keys_kernel,
        out_shape=jax.ShapeDtypeStruct((blocks, groups, width // 3 * 2), BF16),
        compiler_params=params(8),
        cost_estimate=cost(0, 4 * qkv.size),
        name="keys_of",
    )(qkv)


def short_attend_kernel(slope_ref, qkv_ref, kv_ref, out_ref):
    y, z, xl = place_of_device()
    blocks, groups, padded = out_ref.shape
    width = padded - HS
    heads = width // HS
    n = blocks * groups
    row = lax.broadcasted_iota(jnp.int32, (n, 1), 0)
    row_pos = (y * 16 + xl + 2 * (row // groups)) * groups + row % groups
    key = lax.broadcasted_iota(jnp.int32, (1, n), 1)
    key_pos = ((z // 2) * 16 + z % 2 + 2 * (key // groups)) * groups + key % groups
    usable = key_pos <= row_pos
    spot = key_pos.astype(F32)
    lane = lax.broadcasted_iota(jnp.int32, (n, HS), 1)
    packed = jnp.zeros((n, HS), F32)
    outs = []
    for h in range(heads):
        cols = slice(h * HS, (h + 1) * HS)
        q = qkv_ref[:, :, cols].reshape(n, HS)
        k = kv_ref[:, :, cols].reshape(n, HS)
        v = kv_ref[:, :, width + h * HS : width + (h + 1) * HS].reshape(n, HS)
        s = dot_t(q, k) + (slope_ref[h] * LOG2E) * spot
        s = jnp.where(usable, s, NEG)
        top = jnp.max(s, axis=1, keepdims=True)
        p = jnp.exp2(s - top).astype(BF16)
        both = jnp.dot(p, with_ones(v), preferred_element_type=F32)
        weight_total = both[:, HS:]
        outs.append((both[:, :HS] / weight_total).astype(BF16))
        level = top + jnp.log2(weight_total)
        for k, piece in enumerate(three_parts(level)):
            packed = jnp.where(lane == 3 * h + k, piece, packed)
    out = jnp.concatenate(outs + [packed.astype(BF16)], axis=1)
    out_ref[...] = out.reshape(out_ref.shape)


def short_attend(slopes, qkv, kv):
    blocks, groups, width3 = qkv.shape
    width = width3 // 3
    n = blocks * groups
    smem = pl.BlockSpec(memory_space=SMEM)
    vmem = pl.BlockSpec(memory_space=VMEM)
    return pl.pallas_call(
        short_attend_kernel,
        in_specs=[smem, vmem, vmem],
        out_specs=vmem,
        out_shape=jax.ShapeDtypeStruct((blocks, groups, width + HS), BF16),
        compiler_params=params(16),
        cost_estimate=cost(4 * n * n * width, 8 * n * width),
        name="short_attend",
    )(slopes, qkv, kv)


def short_merge_kernel(heads, parts_ref, w_ref, *outs):
    sources, rows, padded = parts_ref.shape
    width = padded - HS
    merged = []
    for h in range(heads):
        cols = slice(h * HS, (h + 1) * HS)
        level = []
        for s in range(sources):
            lev = parts_ref[s, :, width:].astype(F32)
            level.append(
                (lev[:, 3 * h : 3 * h + 1] + lev[:, 3 * h + 1 : 3 * h + 2])
                + lev[:, 3 * h + 2 : 3 * h + 3]
            )
        top = functools.reduce(jnp.maximum, level)
        total = jnp.zeros((rows, 1), F32)
        acc = jnp.zeros((rows, HS), F32)
        for s in range(sources):
            weight = jnp.exp2(level[s] - top)
            total = total + weight
            acc = acc + weight * parts_ref[s, :, cols].astype(F32)
        merged.append((acc / total).astype(BF16))
    att = jnp.concatenate(merged, axis=1)
    cols = outs[0].shape[1]
    terms = [
        jnp.dot(
            att, w_ref[:, t * cols : (t + 1) * cols], preferred_element_type=F32
        ).astype(BF16)
        for t in range(4)
    ]
    tp = lax.axis_index("tp")
    for flip, out in enumerate(outs):
        chosen = terms[flip]
        for t in range(1, 4):
            chosen = jnp.where(tp == t, terms[t ^ flip], chosen)
        out[...] = chosen


def short_merge(parts, weight):
    sources, rows, padded = parts.shape
    width = padded - HS
    cols = weight.shape[1] // 4
    out = jax.ShapeDtypeStruct((rows, cols), BF16)
    return pl.pallas_call(
        functools.partial(short_merge_kernel, width // HS),
        out_shape=[out] * 4,
        compiler_params=params(16),
        cost_estimate=cost(8 * rows * width * cols, 8 * width * cols),
        name="short_merge",
    )(parts, weight)


def final_kernel(lay_ref, *refs):
    terms, out_ref = refs[:-1], refs[-1]
    rows, groups = lay_ref.shape[0], terms[0].shape[0]
    t = lax.broadcasted_iota(jnp.int32, (rows, groups), 0) // GROUP
    g = lax.broadcasted_iota(jnp.int32, (rows, groups), 1)
    spread = jnp.where(t == g, 1.0, 0.0).astype(BF16)
    branch = jnp.zeros(lay_ref.shape, F32)
    for term in terms:
        branch = branch + jnp.dot(spread, term[...], preferred_element_type=F32)
    out_ref[...] = (lay_ref[...].astype(F32) + branch).astype(BF16)


def final_sum(layer, terms):
    rows, cols = layer.shape
    groups = terms[0].shape[0]
    return pl.pallas_call(
        final_kernel,
        out_shape=jax.ShapeDtypeStruct((rows, cols), BF16),
        compiler_params=params(16),
        cost_estimate=cost(8 * rows * cols * groups, 4 * rows * cols),
        name="final_sum",
    )(layer, *terms)


def exchange(blocks, axis):
    return lax.all_to_all(blocks, axis, 0, 0)


def swap(x, axis, flip=1):
    return lax.ppermute(x, axis, [(i, i ^ flip) for i in range(lax.axis_size(axis))])


def moved(x, axis, by):
    n = lax.axis_size(axis)
    return lax.ppermute(x, axis, [(i, (i + by) % n) for i in range(n)])


def both_ways(x, axis, by):
    return moved(x, axis, by), moved(x, axis, -by)


def across(block):
    ny, nz, nx = (lax.axis_size(a) for a in ("y", "z", "xl"))
    assert ny * nx == nz
    pairs = []
    for y in range(ny):
        for z in range(nz):
            for x in range(nx):
                line = y * nx + x
                to = ((z // nx) * nz + line) * nx + z % nx
                pairs.append(((y * nz + z) * nx + x, to))
    return lax.ppermute(block, ("y", "z", "xl"), pairs)


def after(x, *others):
    return lax.optimization_barrier((x, *others))[0]


def on_device(
    tokens,
    project_weight,
    output_weight,
    distance_slope,
    cache_keys,
    cache_values,
    cache_count,
    short_project_weight,
    short_output,
    short_slope,
):
    axes = ("y", "z", "xl", "tp")
    slots = cache_keys.shape[0]
    count = jnp.broadcast_to(cache_count.astype(BF16)[None], (16, cache_keys.shape[1]))
    other_count = swap(count, "xl")
    q, pack = project(
        cache_count, tokens, jnp.transpose(project_weight, (1, 0, 2)), cache_keys, cache_values
    )
    q, pack, other_count = lax.optimization_barrier((q, pack, other_count))
    marked = mark(q, count, other_count)
    left, right = both_ways(pack, "y", 1)
    other, left, right, mate = lax.optimization_barrier(
        (swap(pack, "xl"), left, right, swap(marked, "z"))
    )
    left_other, right_other = both_ways(other, "y", 1)
    pair = join(marked, mate)
    left_pair, right_pair = both_ways(pair, "z", 2)
    near = halves(left_pair, right_pair)
    queries = [pair, left_pair, right_pair, moved(near[0], "z", 2), moved(near[1], "z", -2)]
    far, far_other = moved(left, "y", 1), moved(right_other, "y", -1)
    crossed = swap(after(output_weight, other), "tp", 2)
    plane = plane_counts(queries)
    planes = [plane] + [moved(plane, "y", by) for by in (1, 2, 3)]
    packs = [pack, other, left, left_other, right, right_other, far, far_other]
    parts = attend(distance_slope, queries, planes, packs, slots)
    parts, crossed = lax.optimization_barrier((parts, crossed))

    att = merge(exchange(parts, "z"))
    total, term, rim = layer_product(
        tokens, (att, swap(att, "tp", 2)), (output_weight, crossed)
    )
    n, tp = lax.axis_size(axes), lax.axis_size("tp")
    ahead = [(i, i + tp) for i in range(n - tp)]
    rims = [
        lax.ppermute(rim, axes, ahead),
        lax.ppermute(rim, axes, [(i, j ^ 1) for i, j in ahead]),
    ]
    layer, qkv = short_project(
        total,
        swap(term, "tp", 1),
        rims,
        jnp.transpose(short_project_weight, (1, 0, 2)),
        lax.axis_size("z"),
    )
    qkv = exchange(qkv, "z")
    sparts = short_attend(short_slope, qkv, across(keys_of(qkv)))
    terms = short_merge(exchange(sparts, "z"), short_output)
    terms = [swap(t, "tp", flip) if flip else t for flip, t in enumerate(terms)]
    return final_sum(layer, terms)


def solution(mesh):
    split = Mesh(mesh.devices.reshape(4, 8, 2, 4), ("y", "z", "xl", "tp"))
    ctx = ("y", "z", "xl")
    return jax.shard_map(
        on_device,
        mesh=split,
        in_specs=(
            P(ctx, None),
            P(None, None, "tp"),
            P("tp", None),
            P("tp"),
            P(ctx, "tp"),
            P(ctx, "tp"),
            P(ctx),
            P(None, None, "tp"),
            P("tp", None),
            P("tp"),
        ),
        out_specs=P(ctx, "tp"),
        check_vma=False,
    )
```

```python
import functools
import math

import jax
import jax.numpy as jnp
from jax import lax
from jax.experimental import pallas as pl
from jax.experimental.pallas import tpu as pltpu
from jax.sharding import Mesh, PartitionSpec as P

HS = 128
GROUP = 4
NEG = -1e30
LOG2E = math.log2(math.e)
SCALE2 = HS ** -0.5 * LOG2E

VMEM = pltpu.VMEM
SMEM = pltpu.SMEM
HBM = pltpu.HBM
F32 = jnp.float32
BF16 = jnp.bfloat16


def cost(flops, moved, trans=0):
    return pl.CostEstimate(flops=flops, bytes_accessed=moved, transcendentals=trans)


def params(mib):
    return pltpu.CompilerParams(vmem_limit_bytes=mib * 1024 * 1024)


def rms_scaled(values):
    inv = lax.rsqrt(jnp.mean(values * values, axis=-1, keepdims=True) + 1e-06)
    return (values * inv).astype(BF16)


def dot_t(a, b):
    return lax.dot_general(a, b, (((1,), (1,)), ((), ())), preferred_element_type=F32)


def three_parts(x):
    hi = x.astype(BF16).astype(F32)
    mid = (x - hi).astype(BF16).astype(F32)
    lo = (x - hi - mid).astype(BF16).astype(F32)
    return hi, mid, lo


def project_kernel(
    tok_hbm, w_hbm, ck_hbm, cv_hbm, q_ref, pack_ref, tok, weight, sems
):
    rows = tok.shape[0]
    slots = ck_hbm.shape[0]
    copies = [pltpu.make_async_copy(tok_hbm, tok, sems.at[0])]
    copies += [
        pltpu.make_async_copy(w_hbm.at[i], weight.at[i], sems.at[1 + i]) for i in range(3)
    ]
    copies += [
        pltpu.make_async_copy(ck_hbm, pack_ref.at[:slots], sems.at[4]),
        pltpu.make_async_copy(cv_hbm, pack_ref.at[slots : 2 * slots], sems.at[5]),
    ]
    for copy in copies:
        copy.start()
    copies[0].wait()
    normed = rms_scaled(tok[...].astype(F32))
    for i in range(3):
        copies[1 + i].wait()
        out = jnp.dot(normed, weight[i], preferred_element_type=F32)
        if i == 0:
            q_ref[...] = (out * SCALE2).astype(BF16)
        else:
            at = 2 * slots + (i - 1) * rows
            pack_ref[at : at + rows] = out.astype(BF16)
    copies[4].wait()
    copies[5].wait()


def project(rows, weight3, cache_keys, cache_values):
    n, d = rows.shape
    width = weight3.shape[2]
    total = 2 * (n + cache_keys.shape[0])
    hbm = pl.BlockSpec(memory_space=HBM)
    vmem = pl.BlockSpec(memory_space=VMEM)
    return pl.pallas_call(
        project_kernel,
        in_specs=[hbm] * 4,
        out_specs=[vmem, vmem],
        out_shape=[
            jax.ShapeDtypeStruct((n, width), BF16),
            jax.ShapeDtypeStruct((total, width), BF16),
        ],
        scratch_shapes=[
            VMEM((n, d), BF16),
            VMEM(weight3.shape, BF16),
            pltpu.SemaphoreType.DMA((6,)),
        ],
        compiler_params=params(60),
        cost_estimate=cost(6 * n * d * width, 2 * (n * d + 3 * d * width)),
        name="project",
    )(rows, weight3, cache_keys, cache_values)


def table_kernel(count_ref, out_ref):
    y, z, xl = place_of_device()
    lane = lax.broadcasted_iota(jnp.int32, out_ref.shape, 1)
    out_ref[...] = jnp.where(lane == y * 16 + z * 2 + xl, count_ref[0], 0).astype(F32)


def own_count(count):
    return pl.pallas_call(
        table_kernel,
        in_specs=[pl.BlockSpec(memory_space=SMEM)],
        out_shape=jax.ShapeDtypeStruct((8, HS), F32),
        compiler_params=params(8),
        cost_estimate=cost(0, 4096),
        name="own_count",
    )(count)


def add_kernel(a_ref, b_ref, out_ref):
    out_ref[...] = a_ref[...] + b_ref[...]


def added(a, b):
    return pl.pallas_call(
        add_kernel,
        out_shape=jax.ShapeDtypeStruct(a.shape, a.dtype),
        compiler_params=params(8),
        cost_estimate=cost(a.size, 12 * a.size),
        name="added",
    )(a, b)


def join_kernel(a_ref, b_ref, out_ref):
    rows = a_ref.shape[0]
    out_ref[:rows] = a_ref[...]
    out_ref[rows:] = b_ref[...]


def join(a, b):
    n, width = a.shape
    return pl.pallas_call(
        join_kernel,
        out_shape=jax.ShapeDtypeStruct((2 * n, width), BF16),
        compiler_params=params(8),
        cost_estimate=cost(0, 8 * n * width),
        name="join",
    )(a, b)


def halves_kernel(left_ref, right_ref, own_ref, other_ref):
    half = own_ref.shape[0]
    own_ref[...] = left_ref[:half]
    other_ref[...] = right_ref[half:]


def halves(left, right):
    n, width = left.shape
    out = jax.ShapeDtypeStruct((n // 2, width), BF16)
    return pl.pallas_call(
        halves_kernel,
        out_shape=[out, out],
        compiler_params=params(8),
        cost_estimate=cost(0, 4 * n * width),
        name="halves",
    )(left, right)


def join_kernel(a_ref, b_ref, out_ref):
    rows = a_ref.shape[0]
    out_ref[:rows] = a_ref[...]
    out_ref[rows:] = b_ref[...]


def join(a, b):
    n, width = a.shape
    return pl.pallas_call(
        join_kernel,
        out_shape=jax.ShapeDtypeStruct((2 * n, width), BF16),
        compiler_params=params(8),
        cost_estimate=cost(0, 8 * n * width),
        name="join",
    )(a, b)


RING = ((0, 0), (0, 1), (1, 0), (1, 1), (3, 0), (3, 1), (2, 0), (2, 1))


def place_of_device():
    return lax.axis_index("y"), lax.axis_index("z"), lax.axis_index("xl")


def columns_of(pieces):
    return [s[:, at : at + HS] for s in pieces for at in range(0, s.shape[1], HS)]


def attend_heads(qs, pieces, score, value):
    heads = len(qs)
    pending = [score(0, qs[0], j) for j in range(pieces)]
    results = []
    for h in range(heads):
        top = jnp.max(functools.reduce(jnp.maximum, columns_of(pending)), axis=1, keepdims=True)
        following = []
        both = None
        for j in range(pieces):
            term = jnp.dot(
                jnp.exp2(pending[j] - top).astype(BF16), value(h, j), preferred_element_type=F32
            )
            both = term if both is None else both + term
            if h + 1 < heads:
                following.append(score(h + 1, qs[h + 1], j))
        pending = following
        results.append((top, both[:, HS:], both[:, :HS]))
    return results


def with_ones(v):
    return jnp.concatenate([v, jnp.ones_like(v)], axis=1)


def attend_kernel(slots, slope_ref, *refs):
    queries, tables, packs = refs[:5], refs[5:7], refs[7:15]
    out_ref, q_tile, bias = refs[15:]
    tile = pl.program_id(0)
    y, z, xl = place_of_device()
    rows = q_tile.shape[0] // 2
    width = q_tile.shape[1]
    heads = width // HS
    owners = len(RING)
    cached = owners * slots

    def side_of(other):
        return 1 - xl if other else xl

    own, left, right, far, far_other = queries
    for t, (a, b, at) in enumerate(
        ((own, own, rows), (left, left, rows), (far, far_other, 0), (right, right, rows))
    ):

        @pl.when(tile == t)
        def _(a=a, b=b, at=at):
            q_tile[:rows] = a[:rows]
            q_tile[rows:] = b[at : at + rows]

    @pl.when(tile == 0)
    def _():
        table = (tables[0][...] + tables[1][...])[:1]
        lane = lax.broadcasted_iota(jnp.int32, table.shape, 1)
        everything = jnp.sum(table, axis=1, keepdims=True)
        slot = lax.broadcasted_iota(jnp.int32, (1, slots), 1).astype(F32)
        place = lax.broadcasted_iota(jnp.int32, (1, rows), 1)
        for j, (back, other) in enumerate(RING):
            yj = (y + 4 - back) % 4
            ctx = yj * 16 + z * 2 + side_of(other)
            live = jnp.sum(jnp.where(lane == ctx, table, 0.0), axis=1, keepdims=True)
            start = jnp.sum(jnp.where(lane < ctx, table, 0.0), axis=1, keepdims=True) - everything
            spot = (place + ctx * rows).astype(F32)
            for h in range(heads):
                slope = slope_ref[h] * LOG2E
                bias[h : h + 1, j * slots : (j + 1) * slots] = jnp.where(
                    slot < live, slope * (slot + start), NEG
                )
                at = cached + j * rows
                bias[h : h + 1, at : at + rows] = jnp.where(yj <= y, slope * spot, NEG)

    row = lax.broadcasted_iota(jnp.int32, (2 * rows, 1), 0)
    first = (z + 8 - 2 * tile) % 8
    row_ctx = y * 16 + xl + 2 * jnp.where(row < rows, first, first ^ 1)
    row_pos = row_ctx * rows + jnp.where(row < rows, row, row - rows)
    place = lax.broadcasted_iota(jnp.int32, (1, rows), 1)

    def score(h, q, j):
        cols = slice(h * HS, (h + 1) * HS)
        if j < owners:
            s = dot_t(q, packs[j][:slots, cols])
            return s + bias[h : h + 1, j * slots : (j + 1) * slots]
        back, other = RING[j - owners]
        at = cached + (j - owners) * rows
        s = dot_t(q, packs[j - owners][2 * slots : 2 * slots + rows, cols])
        s = s + bias[h : h + 1, at : at + rows]
        if back == 0:
            first_key = (y * 16 + z * 2 + side_of(other)) * rows
            s = jnp.where(place + first_key <= row_pos, s, NEG)
        return s

    def value(h, j):
        cols = slice(h * HS, (h + 1) * HS)
        if j < owners:
            return with_ones(packs[j][slots : 2 * slots, cols])
        return with_ones(packs[j - owners][2 * slots + rows : 2 * (slots + rows), cols])

    lane = lax.broadcasted_iota(jnp.int32, (2 * rows, HS), 1)
    packed = jnp.zeros((2 * rows, HS), F32)
    qs = [q_tile[:, h * HS : (h + 1) * HS] for h in range(heads)]
    done = []
    for h, (top, total, acc) in enumerate(attend_heads(qs, 2 * owners, score, value)):
        done.append((acc / total).astype(BF16))
        for k, piece in enumerate(three_parts(top + jnp.log2(total))):
            packed = jnp.where(lane == 3 * h + k, piece, packed)
    both = jnp.concatenate(done, axis=1)
    odd = z % 2 == 1
    blocks = []
    for own, level in (
        (jnp.where(odd, both[rows:], both[:rows]), jnp.where(odd, packed[rows:], packed[:rows])),
        (jnp.where(odd, both[:rows], both[rows:]), jnp.where(odd, packed[:rows], packed[rows:])),
    ):
        turned = jnp.transpose(level)[:16]
        tail = jnp.concatenate([turned, jnp.zeros_like(turned)], axis=1).astype(BF16)
        blocks.append((own, tail))
    for p in range(4):

        @pl.when((z // 2 + 4 - tile) % 4 == p)
        def _(p=p):
            for b, (own, tail) in enumerate(blocks):
                out_ref[2 * p + b, :rows] = own
                out_ref[2 * p + b, rows:] = tail


def attend(slopes, queries, tables, packs, slots):
    rows, width = queries[0].shape[0] // 2, queries[0].shape[1]
    nk = len(RING) * (slots + rows)
    whole = lambda a: pl.BlockSpec(a.shape, lambda i: (0,) * a.ndim)
    out = jax.ShapeDtypeStruct((8, rows + 16, width), BF16)
    return pl.pallas_call(
        functools.partial(attend_kernel, slots),
        grid=(4,),
        in_specs=[pl.BlockSpec(memory_space=SMEM)]
        + [whole(a) for a in (*queries, *tables, *packs)],
        out_specs=whole(out),
        out_shape=out,
        scratch_shapes=[VMEM((2 * rows, width), BF16), VMEM((8, nk), F32)],
        compiler_params=params(40),
        cost_estimate=cost(32 * rows * nk * width, 4 * nk * width, 16 * rows * nk),
        name="attend",
    )(slopes, *queries, *tables, *packs)


def merge_kernel(heads, parts_ref, out_ref):
    sources, padded, width = parts_ref.shape
    rows = padded - 16
    levels = jnp.concatenate(
        [parts_ref[s, rows:, :HS].astype(F32) for s in range(sources)], axis=0
    )
    turned = jnp.transpose(levels)
    for h in range(heads):
        cols = slice(h * HS, (h + 1) * HS)
        level = []
        for s in range(sources):
            at = s * 16 + 3 * h
            level.append(
                (turned[:, at : at + 1] + turned[:, at + 1 : at + 2]) + turned[:, at + 2 : at + 3]
            )
        top = functools.reduce(jnp.maximum, level)
        total = jnp.zeros((rows, 1), F32)
        acc = jnp.zeros((rows, HS), F32)
        for s in range(sources):
            weight = jnp.exp2(level[s] - top)
            total = total + weight
            acc = acc + weight * parts_ref[s, :rows, cols].astype(F32)
        out_ref[:, cols] = (acc / total).astype(BF16)


def merge(parts):
    sources, padded, width = parts.shape
    rows = padded - 16
    return pl.pallas_call(
        functools.partial(merge_kernel, width // HS),
        out_shape=jax.ShapeDtypeStruct((rows, width), BF16),
        compiler_params=params(16),
        cost_estimate=cost(4 * sources * rows * width, 2 * sources * padded * width),
        name="merge",
    )(parts)


def product_kernel(
    tok_hbm, a_ref, b_ref, wa_hbm, wb_hbm, sum_ref, term_ref, rim_ref, tok, wa, wb, sems
):
    chunks = wa.shape[0]
    cols = wa.shape[2]
    copies = []
    for c in range(chunks):
        at = pl.ds(c * cols, cols)
        copies.append(
            [
                pltpu.make_async_copy(src.at[:, at], dst.at[c], sems.at[i, c])
                for i, (src, dst) in enumerate(((wa_hbm, wa), (wb_hbm, wb), (tok_hbm, tok)))
            ]
        )
    for group in copies:
        for copy in group:
            copy.start()
    for c, group in enumerate(copies):
        for copy in group:
            copy.wait()
        at = slice(c * cols, (c + 1) * cols)
        term = jnp.dot(a_ref[...], wa[c], preferred_element_type=F32) + jnp.dot(
            b_ref[...], wb[c], preferred_element_type=F32
        )
        total = tok[c].astype(F32) + term
        sum_ref[:, at] = total
        term_ref[:, at] = term.astype(BF16)
        rim_ref[:16, at] = total[-16:].astype(BF16)
        rim_ref[16:, at] = term[-16:].astype(BF16)


def layer_product(tokens, atts, weights):
    rows, d = tokens.shape
    chunks = 4
    inner = weights[0].shape[0]
    hbm = pl.BlockSpec(memory_space=HBM)
    vmem = pl.BlockSpec(memory_space=VMEM)
    return pl.pallas_call(
        product_kernel,
        in_specs=[hbm, vmem, vmem, hbm, hbm],
        out_specs=[vmem] * 3,
        out_shape=[
            jax.ShapeDtypeStruct((rows, d), F32),
            jax.ShapeDtypeStruct((rows, d), BF16),
            jax.ShapeDtypeStruct((32, d), BF16),
        ],
        scratch_shapes=[
            VMEM((chunks, rows, d // chunks), BF16),
            VMEM((chunks, inner, d // chunks), BF16),
            VMEM((chunks, inner, d // chunks), BF16),
            pltpu.SemaphoreType.DMA((3, chunks)),
        ],
        compiler_params=params(16),
        cost_estimate=cost(4 * rows * d * inner, 4 * inner * d),
        name="layer_product",
    )(tokens, *atts, *weights)


def short_project_kernel(
    sum_ref, term_ref, rim_a, rim_b, w_ref, cols_ref, q_ref, kv_ref, normed
):
    step = pl.program_id(0)
    rows, d = sum_ref.shape
    groups = rows // GROUP
    rim_rows = 16
    width = w_ref.shape[2]

    @pl.when(step == 0)
    def _():
        layer = (sum_ref[...] + term_ref[...].astype(F32)).astype(BF16)
        part = d // 4
        tp = lax.axis_index("tp")
        mine = layer[:, :part]
        for t in range(1, 4):
            mine = jnp.where(tp == t, layer[:, t * part : (t + 1) * part], mine)
        cols_ref[...] = mine
        rim = (rim_a[:rim_rows].astype(F32) + rim_b[rim_rows:].astype(F32)).astype(BF16)
        g = lax.broadcasted_iota(jnp.int32, (groups, rows), 0) * GROUP
        t = lax.broadcasted_iota(jnp.int32, (groups, rows), 1)
        own = jnp.where((t <= g) & (t > g - GROUP), 1.0 / GROUP, 0.0).astype(BF16)
        g = lax.broadcasted_iota(jnp.int32, (groups, rim_rows), 0) * GROUP
        t = lax.broadcasted_iota(jnp.int32, (groups, rim_rows), 1) - rim_rows
        before = jnp.where(t > g - GROUP, 1.0 / GROUP, 0.0).astype(BF16)
        pooled = jnp.dot(own, layer, preferred_element_type=F32) + jnp.dot(
            before, rim, preferred_element_type=F32
        )
        normed[...] = rms_scaled(pooled.astype(BF16).astype(F32))

    out = jnp.dot(normed[...], w_ref[0], preferred_element_type=F32)

    @pl.when(step == 0)
    def _():
        scaled = (out * SCALE2).astype(BF16)
        for c in range(q_ref.shape[0]):
            q_ref[c] = scaled

    @pl.when(step == 1)
    def _():
        kv_ref[:, :width] = out.astype(BF16)

    @pl.when(step == 2)
    def _():
        kv_ref[:, width:] = out.astype(BF16)


def short_project(total, term, rims, weight3, copies):
    n, d = total.shape
    groups = n // GROUP
    width = weight3.shape[2]
    whole = lambda shape: pl.BlockSpec(shape, lambda i: (0,) * len(shape))
    shapes = [(n, d // 4), (copies, groups, width), (groups, 2 * width)]
    return pl.pallas_call(
        short_project_kernel,
        grid=(3,),
        in_specs=[whole((n, d)), whole((n, d)), whole((32, d)), whole((32, d))]
        + [pl.BlockSpec((1, d, width), lambda i: (i, 0, 0))],
        out_specs=[whole(s) for s in shapes],
        out_shape=[jax.ShapeDtypeStruct(s, BF16) for s in shapes],
        scratch_shapes=[VMEM((groups, d), BF16)],
        compiler_params=params(16),
        cost_estimate=cost(6 * groups * d * width, 2 * (n * d + 3 * d * width)),
        name="short_project",
    )(total, term, *rims, weight3)


def short_attend_kernel(slope_ref, q_ref, *refs):
    key_refs, out_ref = refs[:4], refs[4]
    y, z, xl = place_of_device()
    blocks, groups, padded = out_ref.shape
    width = padded - HS
    heads = width // HS
    n = blocks * groups
    row = lax.broadcasted_iota(jnp.int32, (n, 1), 0)
    row_pos = (y * 16 + xl + 2 * (row // groups)) * groups + row % groups
    key = lax.broadcasted_iota(jnp.int32, (1, n), 1)
    ys = (y + 4 - key // (2 * groups)) % 4
    side = jnp.where((key // groups) % 2 == 1, 1 - xl, xl)
    key_pos = (ys * 16 + z * 2 + side) * groups + key % groups
    usable = key_pos <= row_pos
    spot = key_pos.astype(F32)
    lane = lax.broadcasted_iota(jnp.int32, (n, HS), 1)
    packed = jnp.zeros((n, HS), F32)
    outs = []
    for h in range(heads):
        cols = slice(h * HS, (h + 1) * HS)
        cols_v = slice(width + h * HS, width + (h + 1) * HS)
        q = q_ref[:, :, cols].reshape(n, HS)
        k = jnp.concatenate([r[:, cols] for r in key_refs], axis=0)
        v = jnp.concatenate([r[:, cols_v] for r in key_refs], axis=0)
        s = dot_t(q, k) + (slope_ref[h] * LOG2E) * spot
        s = jnp.where(usable, s, NEG)
        top = jnp.max(s, axis=1, keepdims=True)
        p = jnp.exp2(s - top).astype(BF16)
        both = jnp.dot(p, with_ones(v), preferred_element_type=F32)
        weight_total = both[:, HS:]
        outs.append((both[:, :HS] / weight_total).astype(BF16))
        level = top + jnp.log2(weight_total)
        for k, piece in enumerate(three_parts(level)):
            packed = jnp.where(lane == 3 * h + k, piece, packed)
    out = jnp.concatenate(outs + [packed.astype(BF16)], axis=1)
    out_ref[...] = out.reshape(out_ref.shape)


def short_attend(slopes, queries, keys):
    blocks, groups, width = queries.shape
    n = blocks * groups
    smem = pl.BlockSpec(memory_space=SMEM)
    vmem = pl.BlockSpec(memory_space=VMEM)
    return pl.pallas_call(
        short_attend_kernel,
        in_specs=[smem] + [vmem] * 5,
        out_specs=vmem,
        out_shape=jax.ShapeDtypeStruct((blocks, groups, width + HS), BF16),
        compiler_params=params(16),
        cost_estimate=cost(4 * n * n * width, 8 * n * width),
        name="short_attend",
    )(slopes, queries, *keys)


def short_merge_kernel(heads, parts_ref, w_ref, *outs):
    sources, rows, padded = parts_ref.shape
    width = padded - HS
    merged = []
    for h in range(heads):
        cols = slice(h * HS, (h + 1) * HS)
        level = []
        for s in range(sources):
            lev = parts_ref[s, :, width:].astype(F32)
            level.append(
                (lev[:, 3 * h : 3 * h + 1] + lev[:, 3 * h + 1 : 3 * h + 2])
                + lev[:, 3 * h + 2 : 3 * h + 3]
            )
        top = functools.reduce(jnp.maximum, level)
        total = jnp.zeros((rows, 1), F32)
        acc = jnp.zeros((rows, HS), F32)
        for s in range(sources):
            weight = jnp.exp2(level[s] - top)
            total = total + weight
            acc = acc + weight * parts_ref[s, :, cols].astype(F32)
        merged.append((acc / total).astype(BF16))
    att = jnp.concatenate(merged, axis=1)
    cols = outs[0].shape[1]
    terms = [
        jnp.dot(
            att, w_ref[:, t * cols : (t + 1) * cols], preferred_element_type=F32
        ).astype(BF16)
        for t in range(4)
    ]
    tp = lax.axis_index("tp")
    for flip, out in enumerate(outs):
        chosen = terms[flip]
        for t in range(1, 4):
            chosen = jnp.where(tp == t, terms[t ^ flip], chosen)
        out[...] = chosen


def short_merge(parts, weight):
    sources, rows, padded = parts.shape
    width = padded - HS
    cols = weight.shape[1] // 4
    out = jax.ShapeDtypeStruct((rows, cols), BF16)
    return pl.pallas_call(
        functools.partial(short_merge_kernel, width // HS),
        out_shape=[out] * 4,
        compiler_params=params(16),
        cost_estimate=cost(8 * rows * width * cols, 8 * width * cols),
        name="short_merge",
    )(parts, weight)


def final_kernel(lay_ref, *refs):
    terms, out_ref = refs[:-1], refs[-1]
    rows, groups = lay_ref.shape[0], terms[0].shape[0]
    t = lax.broadcasted_iota(jnp.int32, (rows, groups), 0) // GROUP
    g = lax.broadcasted_iota(jnp.int32, (rows, groups), 1)
    spread = jnp.where(t == g, 1.0, 0.0).astype(BF16)
    branch = jnp.zeros(lay_ref.shape, F32)
    for term in terms:
        branch = branch + jnp.dot(spread, term[...], preferred_element_type=F32)
    out_ref[...] = (lay_ref[...].astype(F32) + branch).astype(BF16)


def final_sum(layer, terms):
    rows, cols = layer.shape
    groups = terms[0].shape[0]
    return pl.pallas_call(
        final_kernel,
        out_shape=jax.ShapeDtypeStruct((rows, cols), BF16),
        compiler_params=params(16),
        cost_estimate=cost(8 * rows * cols * groups, 4 * rows * cols),
        name="final_sum",
    )(layer, *terms)


def exchange(blocks, axis):
    return lax.all_to_all(blocks, axis, 0, 0)


def swap(x, axis, flip=1):
    return lax.ppermute(x, axis, [(i, i ^ flip) for i in range(lax.axis_size(axis))])


def moved(x, axis, by):
    n = lax.axis_size(axis)
    return lax.ppermute(x, axis, [(i, (i + by) % n) for i in range(n)])


def both_ways(x, axis, by):
    return moved(x, axis, by), moved(x, axis, -by)


def counts_along(table, axis, *flips):
    for flip in flips:
        table = added(table, swap(table, axis, flip))
    return table


def after(x, *others):
    return lax.optimization_barrier((x, *others))[0]


def on_device(
    tokens,
    project_weight,
    output_weight,
    distance_slope,
    cache_keys,
    cache_values,
    cache_count,
    short_project_weight,
    short_output,
    short_slope,
):
    axes = ("y", "z", "xl", "tp")
    slots = cache_keys.shape[0]
    q, pack = project(
        tokens, jnp.transpose(project_weight, (1, 0, 2)), cache_keys, cache_values
    )
    table = counts_along(own_count(cache_count), "xl", 1)
    q, pack, table = lax.optimization_barrier((q, pack, table))
    table = counts_along(table, "z", 1)
    left, right = both_ways(pack, "y", 1)
    other, left, right, mate, table = lax.optimization_barrier(
        (swap(pack, "xl"), left, right, swap(q, "z"), table)
    )
    pair = join(q, mate)
    left_other, right_other = both_ways(other, "y", 1)
    left_pair, right_pair = both_ways(pair, "z", 2)
    table = counts_along(table, "z", 2, 4)
    left_other, right_other, left_pair, right_pair, left, table = lax.optimization_barrier(
        (left_other, right_other, left_pair, right_pair, left, table)
    )
    table = counts_along(table, "y", 1)
    tables = [table, swap(table, "y", 2)]
    far, far_other = moved(left, "y", 1), moved(right_other, "y", -1)
    near = halves(left_pair, right_pair)
    queries = [pair, left_pair, right_pair, moved(near[0], "z", 2), moved(near[1], "z", -2)]
    crossed = swap(after(output_weight, far), "tp", 2)
    packs = [pack, other, left, left_other, right, right_other, far, far_other]
    parts = attend(distance_slope, queries, tables, packs, slots)

    att = merge(exchange(parts, "z"))
    total, term, rim = layer_product(
        tokens, (att, swap(att, "tp", 2)), (output_weight, crossed)
    )
    n, tp = lax.axis_size(axes), lax.axis_size("tp")
    ahead = [(i, i + tp) for i in range(n - tp)]
    rims = [
        lax.ppermute(rim, axes, ahead),
        lax.ppermute(rim, axes, [(i, j ^ 1) for i, j in ahead]),
    ]
    layer, sq, skv = short_project(
        total,
        swap(term, "tp", 1),
        rims,
        jnp.transpose(short_project_weight, (1, 0, 2)),
        lax.axis_size("z"),
    )
    pair = join(skv, swap(skv, "xl"))
    keys = [pair] + [moved(pair, "y", by) for by in (1, 2, 3)]
    sparts = short_attend(short_slope, exchange(sq, "z"), keys)
    terms = short_merge(exchange(sparts, "z"), short_output)
    terms = [swap(t, "tp", flip) if flip else t for flip, t in enumerate(terms)]
    return final_sum(layer, terms)


def solution(mesh):
    split = Mesh(mesh.devices.reshape(4, 8, 2, 4), ("y", "z", "xl", "tp"))
    ctx = ("y", "z", "xl")
    return jax.shard_map(
        on_device,
        mesh=split,
        in_specs=(
            P(ctx, None),
            P(None, None, "tp"),
            P("tp", None),
            P("tp"),
            P(ctx, "tp"),
            P(ctx, "tp"),
            P(ctx),
            P(None, None, "tp"),
            P("tp", None),
            P("tp"),
        ),
        out_specs=P(ctx, "tp"),
        check_vma=False,
    )
```

```python
import functools
import math

import jax
import jax.numpy as jnp
from jax import lax
from jax.experimental import pallas as pl
from jax.experimental.pallas import tpu as pltpu
from jax.sharding import Mesh, PartitionSpec as P

HS = 128
GROUP = 4
NEG = -1e30
LOG2E = math.log2(math.e)
SCALE2 = HS ** -0.5 * LOG2E

VMEM = pltpu.VMEM
SMEM = pltpu.SMEM
HBM = pltpu.HBM
F32 = jnp.float32
BF16 = jnp.bfloat16


def cost(flops, moved, trans=0):
    return pl.CostEstimate(flops=flops, bytes_accessed=moved, transcendentals=trans)


def params(mib):
    return pltpu.CompilerParams(vmem_limit_bytes=mib * 1024 * 1024)


def rms_scaled(values):
    inv = lax.rsqrt(jnp.mean(values * values, axis=-1, keepdims=True) + 1e-06)
    return (values * inv).astype(BF16)


def dot_t(a, b):
    return lax.dot_general(a, b, (((1,), (1,)), ((), ())), preferred_element_type=F32)


def three_parts(x):
    hi = x.astype(BF16).astype(F32)
    mid = (x - hi).astype(BF16).astype(F32)
    lo = (x - hi - mid).astype(BF16).astype(F32)
    return hi, mid, lo


def query_kernel(tok_hbm, w_hbm, q_ref, normed_ref, tok, weight, sems):
    copies = [
        pltpu.make_async_copy(tok_hbm, tok, sems.at[0]),
        pltpu.make_async_copy(w_hbm.at[0], weight, sems.at[1]),
    ]
    for copy in copies:
        copy.start()
    copies[0].wait()
    normed = rms_scaled(tok[...].astype(F32))
    normed_ref[...] = normed
    copies[1].wait()
    out = jnp.dot(normed, weight[...], preferred_element_type=F32)
    q_ref[...] = (out * SCALE2).astype(BF16)


def project_queries(rows, weight3):
    n, d = rows.shape
    width = weight3.shape[2]
    hbm = pl.BlockSpec(memory_space=HBM)
    vmem = pl.BlockSpec(memory_space=VMEM)
    return pl.pallas_call(
        query_kernel,
        in_specs=[hbm, hbm],
        out_specs=[vmem, vmem],
        out_shape=[jax.ShapeDtypeStruct((n, w), BF16) for w in (width, d)],
        scratch_shapes=[
            VMEM((n, d), BF16),
            VMEM((d, width), BF16),
            pltpu.SemaphoreType.DMA((2,)),
        ],
        compiler_params=params(60),
        cost_estimate=cost(2 * n * d * width, 2 * (n * d + d * width)),
        name="project_queries",
    )(rows, weight3)


def pack_kernel(normed_hbm, w_hbm, ck_hbm, cv_hbm, pack_ref, normed, weight, sems):
    rows = normed.shape[0]
    slots = ck_hbm.shape[0]
    copies = [pltpu.make_async_copy(normed_hbm, normed, sems.at[0])]
    copies += [
        pltpu.make_async_copy(w_hbm.at[1 + i], weight.at[i], sems.at[1 + i]) for i in range(2)
    ]
    copies += [
        pltpu.make_async_copy(ck_hbm, pack_ref.at[:slots], sems.at[3]),
        pltpu.make_async_copy(cv_hbm, pack_ref.at[slots : 2 * slots], sems.at[4]),
    ]
    for copy in copies:
        copy.start()
    copies[0].wait()
    for i in range(2):
        copies[1 + i].wait()
        out = jnp.dot(normed[...], weight[i], preferred_element_type=F32)
        at = 2 * slots + i * rows
        pack_ref[at : at + rows] = out.astype(BF16)
    copies[3].wait()
    copies[4].wait()


def project_pack(normed, weight3, cache_keys, cache_values):
    n, d = normed.shape
    width = weight3.shape[2]
    total = 2 * (n + cache_keys.shape[0])
    hbm = pl.BlockSpec(memory_space=HBM)
    return pl.pallas_call(
        pack_kernel,
        in_specs=[hbm] * 4,
        out_specs=pl.BlockSpec(memory_space=VMEM),
        out_shape=jax.ShapeDtypeStruct((total, width), BF16),
        scratch_shapes=[
            VMEM((n, d), BF16),
            VMEM((2, d, width), BF16),
            pltpu.SemaphoreType.DMA((5,)),
        ],
        compiler_params=params(60),
        cost_estimate=cost(4 * n * d * width, 2 * (n * d + 2 * d * width)),
        name="project_pack",
    )(normed, weight3, cache_keys, cache_values)


def table_kernel(count_ref, out_ref):
    y, z, xl = place_of_device()
    lane = lax.broadcasted_iota(jnp.int32, out_ref.shape, 1)
    out_ref[...] = jnp.where(lane == y * 16 + z * 2 + xl, count_ref[0], 0).astype(F32)


def own_count(count):
    return pl.pallas_call(
        table_kernel,
        in_specs=[pl.BlockSpec(memory_space=SMEM)],
        out_shape=jax.ShapeDtypeStruct((8, HS), F32),
        compiler_params=params(8),
        cost_estimate=cost(0, 4096),
        name="own_count",
    )(count)


def add_kernel(a_ref, b_ref, out_ref):
    out_ref[...] = a_ref[...] + b_ref[...]


def added(a, b):
    return pl.pallas_call(
        add_kernel,
        out_shape=jax.ShapeDtypeStruct(a.shape, a.dtype),
        compiler_params=params(8),
        cost_estimate=cost(a.size, 12 * a.size),
        name="added",
    )(a, b)


def join_kernel(a_ref, b_ref, out_ref):
    rows = a_ref.shape[0]
    out_ref[:rows] = a_ref[...]
    out_ref[rows:] = b_ref[...]


def join(a, b):
    n, width = a.shape
    return pl.pallas_call(
        join_kernel,
        out_shape=jax.ShapeDtypeStruct((2 * n, width), BF16),
        compiler_params=params(8),
        cost_estimate=cost(0, 8 * n * width),
        name="join",
    )(a, b)


def halves_kernel(left_ref, right_ref, own_ref, other_ref):
    half = own_ref.shape[0]
    own_ref[...] = left_ref[:half]
    other_ref[...] = right_ref[half:]


def halves(left, right):
    n, width = left.shape
    out = jax.ShapeDtypeStruct((n // 2, width), BF16)
    return pl.pallas_call(
        halves_kernel,
        out_shape=[out, out],
        compiler_params=params(8),
        cost_estimate=cost(0, 4 * n * width),
        name="halves",
    )(left, right)


def join_kernel(a_ref, b_ref, out_ref):
    rows = a_ref.shape[0]
    out_ref[:rows] = a_ref[...]
    out_ref[rows:] = b_ref[...]


def join(a, b):
    n, width = a.shape
    return pl.pallas_call(
        join_kernel,
        out_shape=jax.ShapeDtypeStruct((2 * n, width), BF16),
        compiler_params=params(8),
        cost_estimate=cost(0, 8 * n * width),
        name="join",
    )(a, b)


RING = ((0, 0), (0, 1), (1, 0), (1, 1), (3, 0), (3, 1), (2, 0), (2, 1))


def place_of_device():
    return lax.axis_index("y"), lax.axis_index("z"), lax.axis_index("xl")


def columns_of(pieces):
    return [s[:, at : at + HS] for s in pieces for at in range(0, s.shape[1], HS)]


def attend_heads(qs, pieces, score, value):
    heads = len(qs)
    pending = [score(0, qs[0], j) for j in range(pieces)]
    results = []
    for h in range(heads):
        top = jnp.max(functools.reduce(jnp.maximum, columns_of(pending)), axis=1, keepdims=True)
        following = []
        both = None
        for j in range(pieces):
            term = jnp.dot(
                jnp.exp2(pending[j] - top).astype(BF16), value(h, j), preferred_element_type=F32
            )
            both = term if both is None else both + term
            if h + 1 < heads:
                following.append(score(h + 1, qs[h + 1], j))
        pending = following
        results.append((top, both[:, HS:], both[:, :HS]))
    return results


def with_ones(v):
    return jnp.concatenate([v, jnp.ones_like(v)], axis=1)


def attend_kernel(slots, slope_ref, *refs):
    queries, tables, packs = refs[:5], refs[5:7], refs[7:15]
    out_ref, q_tile, bias = refs[15:]
    tile = pl.program_id(0)
    y, z, xl = place_of_device()
    rows = q_tile.shape[0] // 2
    width = q_tile.shape[1]
    heads = width // HS
    owners = len(RING)
    cached = owners * slots

    def side_of(other):
        return 1 - xl if other else xl

    own, left, right, far, far_other = queries
    for t, (a, b, at) in enumerate(
        ((own, own, rows), (left, left, rows), (far, far_other, 0), (right, right, rows))
    ):

        @pl.when(tile == t)
        def _(a=a, b=b, at=at):
            q_tile[:rows] = a[:rows]
            q_tile[rows:] = b[at : at + rows]

    @pl.when(tile == 0)
    def _():
        table = (tables[0][...] + tables[1][...])[:1]
        lane = lax.broadcasted_iota(jnp.int32, table.shape, 1)
        everything = jnp.sum(table, axis=1, keepdims=True)
        slot = lax.broadcasted_iota(jnp.int32, (1, slots), 1).astype(F32)
        place = lax.broadcasted_iota(jnp.int32, (1, rows), 1)
        for j, (back, other) in enumerate(RING):
            yj = (y + 4 - back) % 4
            ctx = yj * 16 + z * 2 + side_of(other)
            live = jnp.sum(jnp.where(lane == ctx, table, 0.0), axis=1, keepdims=True)
            start = jnp.sum(jnp.where(lane < ctx, table, 0.0), axis=1, keepdims=True) - everything
            spot = (place + ctx * rows).astype(F32)
            for h in range(heads):
                slope = slope_ref[h] * LOG2E
                bias[h : h + 1, j * slots : (j + 1) * slots] = jnp.where(
                    slot < live, slope * (slot + start), NEG
                )
                at = cached + j * rows
                bias[h : h + 1, at : at + rows] = jnp.where(yj <= y, slope * spot, NEG)

    row = lax.broadcasted_iota(jnp.int32, (2 * rows, 1), 0)
    first = (z + 8 - 2 * tile) % 8
    row_ctx = y * 16 + xl + 2 * jnp.where(row < rows, first, first ^ 1)
    row_pos = row_ctx * rows + jnp.where(row < rows, row, row - rows)
    place = lax.broadcasted_iota(jnp.int32, (1, rows), 1)

    def score(h, q, j):
        cols = slice(h * HS, (h + 1) * HS)
        if j < owners:
            s = dot_t(q, packs[j][:slots, cols])
            return s + bias[h : h + 1, j * slots : (j + 1) * slots]
        back, other = RING[j - owners]
        at = cached + (j - owners) * rows
        s = dot_t(q, packs[j - owners][2 * slots : 2 * slots + rows, cols])
        s = s + bias[h : h + 1, at : at + rows]
        if back == 0:
            first_key = (y * 16 + z * 2 + side_of(other)) * rows
            s = jnp.where(place + first_key <= row_pos, s, NEG)
        return s

    def value(h, j):
        cols = slice(h * HS, (h + 1) * HS)
        if j < owners:
            return with_ones(packs[j][slots : 2 * slots, cols])
        return with_ones(packs[j - owners][2 * slots + rows : 2 * (slots + rows), cols])

    lane = lax.broadcasted_iota(jnp.int32, (2 * rows, HS), 1)
    packed = jnp.zeros((2 * rows, HS), F32)
    qs = [q_tile[:, h * HS : (h + 1) * HS] for h in range(heads)]
    done = []
    for h, (top, total, acc) in enumerate(attend_heads(qs, 2 * owners, score, value)):
        done.append((acc / total).astype(BF16))
        for k, piece in enumerate(three_parts(top + jnp.log2(total))):
            packed = jnp.where(lane == 3 * h + k, piece, packed)
    both = jnp.concatenate(done, axis=1)
    odd = z % 2 == 1
    blocks = []
    for own, level in (
        (jnp.where(odd, both[rows:], both[:rows]), jnp.where(odd, packed[rows:], packed[:rows])),
        (jnp.where(odd, both[:rows], both[rows:]), jnp.where(odd, packed[:rows], packed[rows:])),
    ):
        turned = jnp.transpose(level)[:16]
        tail = jnp.concatenate([turned, jnp.zeros_like(turned)], axis=1).astype(BF16)
        blocks.append((own, tail))
    for p in range(4):

        @pl.when((z // 2 + 4 - tile) % 4 == p)
        def _(p=p):
            for b, (own, tail) in enumerate(blocks):
                out_ref[2 * p + b, :rows] = own
                out_ref[2 * p + b, rows:] = tail


def attend(slopes, queries, tables, packs, slots):
    rows, width = queries[0].shape[0] // 2, queries[0].shape[1]
    nk = len(RING) * (slots + rows)
    whole = lambda a: pl.BlockSpec(a.shape, lambda i: (0,) * a.ndim)
    out = jax.ShapeDtypeStruct((8, rows + 16, width), BF16)
    return pl.pallas_call(
        functools.partial(attend_kernel, slots),
        grid=(4,),
        in_specs=[pl.BlockSpec(memory_space=SMEM)]
        + [whole(a) for a in (*queries, *tables, *packs)],
        out_specs=whole(out),
        out_shape=out,
        scratch_shapes=[VMEM((2 * rows, width), BF16), VMEM((8, nk), F32)],
        compiler_params=params(40),
        cost_estimate=cost(32 * rows * nk * width, 4 * nk * width, 16 * rows * nk),
        name="attend",
    )(slopes, *queries, *tables, *packs)


def merge_kernel(heads, parts_ref, out_ref):
    sources, padded, width = parts_ref.shape
    rows = padded - 16
    levels = jnp.concatenate(
        [parts_ref[s, rows:, :HS].astype(F32) for s in range(sources)], axis=0
    )
    turned = jnp.transpose(levels)
    for h in range(heads):
        cols = slice(h * HS, (h + 1) * HS)
        level = []
        for s in range(sources):
            at = s * 16 + 3 * h
            level.append(
                (turned[:, at : at + 1] + turned[:, at + 1 : at + 2]) + turned[:, at + 2 : at + 3]
            )
        top = functools.reduce(jnp.maximum, level)
        total = jnp.zeros((rows, 1), F32)
        acc = jnp.zeros((rows, HS), F32)
        for s in range(sources):
            weight = jnp.exp2(level[s] - top)
            total = total + weight
            acc = acc + weight * parts_ref[s, :rows, cols].astype(F32)
        out_ref[:, cols] = (acc / total).astype(BF16)


def merge(parts):
    sources, padded, width = parts.shape
    rows = padded - 16
    return pl.pallas_call(
        functools.partial(merge_kernel, width // HS),
        out_shape=jax.ShapeDtypeStruct((rows, width), BF16),
        compiler_params=params(16),
        cost_estimate=cost(4 * sources * rows * width, 2 * sources * padded * width),
        name="merge",
    )(parts)


def product_kernel(
    tok_hbm, a_ref, b_ref, wa_hbm, wb_hbm, sum_ref, term_ref, rim_ref, tok, wa, wb, sems
):
    chunks = wa.shape[0]
    cols = wa.shape[2]
    copies = []
    for c in range(chunks):
        at = pl.ds(c * cols, cols)
        copies.append(
            [
                pltpu.make_async_copy(src.at[:, at], dst.at[c], sems.at[i, c])
                for i, (src, dst) in enumerate(((wa_hbm, wa), (wb_hbm, wb), (tok_hbm, tok)))
            ]
        )
    for group in copies:
        for copy in group:
            copy.start()
    for c, group in enumerate(copies):
        for copy in group:
            copy.wait()
        at = slice(c * cols, (c + 1) * cols)
        term = jnp.dot(a_ref[...], wa[c], preferred_element_type=F32) + jnp.dot(
            b_ref[...], wb[c], preferred_element_type=F32
        )
        total = tok[c].astype(F32) + term
        sum_ref[:, at] = total
        term_ref[:, at] = term.astype(BF16)
        rim_ref[:16, at] = total[-16:].astype(BF16)
        rim_ref[16:, at] = term[-16:].astype(BF16)


def layer_product(tokens, atts, weights):
    rows, d = tokens.shape
    chunks = 4
    inner = weights[0].shape[0]
    hbm = pl.BlockSpec(memory_space=HBM)
    vmem = pl.BlockSpec(memory_space=VMEM)
    return pl.pallas_call(
        product_kernel,
        in_specs=[hbm, vmem, vmem, hbm, hbm],
        out_specs=[vmem] * 3,
        out_shape=[
            jax.ShapeDtypeStruct((rows, d), F32),
            jax.ShapeDtypeStruct((rows, d), BF16),
            jax.ShapeDtypeStruct((32, d), BF16),
        ],
        scratch_shapes=[
            VMEM((chunks, rows, d // chunks), BF16),
            VMEM((chunks, inner, d // chunks), BF16),
            VMEM((chunks, inner, d // chunks), BF16),
            pltpu.SemaphoreType.DMA((3, chunks)),
        ],
        compiler_params=params(16),
        cost_estimate=cost(4 * rows * d * inner, 4 * inner * d),
        name="layer_product",
    )(tokens, *atts, *weights)


def short_project_kernel(
    sum_ref, term_ref, rim_a, rim_b, w_ref, cols_ref, q_ref, kv_ref, normed
):
    step = pl.program_id(0)
    rows, d = sum_ref.shape
    groups = rows // GROUP
    rim_rows = 16
    width = w_ref.shape[2]

    @pl.when(step == 0)
    def _():
        layer = (sum_ref[...] + term_ref[...].astype(F32)).astype(BF16)
        part = d // 4
        tp = lax.axis_index("tp")
        mine = layer[:, :part]
        for t in range(1, 4):
            mine = jnp.where(tp == t, layer[:, t * part : (t + 1) * part], mine)
        cols_ref[...] = mine
        rim = (rim_a[:rim_rows].astype(F32) + rim_b[rim_rows:].astype(F32)).astype(BF16)
        g = lax.broadcasted_iota(jnp.int32, (groups, rows), 0) * GROUP
        t = lax.broadcasted_iota(jnp.int32, (groups, rows), 1)
        own = jnp.where((t <= g) & (t > g - GROUP), 1.0 / GROUP, 0.0).astype(BF16)
        g = lax.broadcasted_iota(jnp.int32, (groups, rim_rows), 0) * GROUP
        t = lax.broadcasted_iota(jnp.int32, (groups, rim_rows), 1) - rim_rows
        before = jnp.where(t > g - GROUP, 1.0 / GROUP, 0.0).astype(BF16)
        pooled = jnp.dot(own, layer, preferred_element_type=F32) + jnp.dot(
            before, rim, preferred_element_type=F32
        )
        normed[...] = rms_scaled(pooled.astype(BF16).astype(F32))

    out = jnp.dot(normed[...], w_ref[0], preferred_element_type=F32)

    @pl.when(step == 0)
    def _():
        scaled = (out * SCALE2).astype(BF16)
        for c in range(q_ref.shape[0]):
            q_ref[c] = scaled

    @pl.when(step == 1)
    def _():
        kv_ref[:, :width] = out.astype(BF16)

    @pl.when(step == 2)
    def _():
        kv_ref[:, width:] = out.astype(BF16)


def short_project(total, term, rims, weight3, copies):
    n, d = total.shape
    groups = n // GROUP
    width = weight3.shape[2]
    whole = lambda shape: pl.BlockSpec(shape, lambda i: (0,) * len(shape))
    shapes = [(n, d // 4), (copies, groups, width), (groups, 2 * width)]
    return pl.pallas_call(
        short_project_kernel,
        grid=(3,),
        in_specs=[whole((n, d)), whole((n, d)), whole((32, d)), whole((32, d))]
        + [pl.BlockSpec((1, d, width), lambda i: (i, 0, 0))],
        out_specs=[whole(s) for s in shapes],
        out_shape=[jax.ShapeDtypeStruct(s, BF16) for s in shapes],
        scratch_shapes=[VMEM((groups, d), BF16)],
        compiler_params=params(16),
        cost_estimate=cost(6 * groups * d * width, 2 * (n * d + 3 * d * width)),
        name="short_project",
    )(total, term, *rims, weight3)


def short_attend_kernel(slope_ref, q_ref, *refs):
    key_refs, out_ref = refs[:4], refs[4]
    y, z, xl = place_of_device()
    blocks, groups, padded = out_ref.shape
    width = padded - HS
    heads = width // HS
    n = blocks * groups
    row = lax.broadcasted_iota(jnp.int32, (n, 1), 0)
    row_pos = (y * 16 + xl + 2 * (row // groups)) * groups + row % groups
    key = lax.broadcasted_iota(jnp.int32, (1, n), 1)
    ys = (y + 4 - key // (2 * groups)) % 4
    side = jnp.where((key // groups) % 2 == 1, 1 - xl, xl)
    key_pos = (ys * 16 + z * 2 + side) * groups + key % groups
    usable = key_pos <= row_pos
    spot = key_pos.astype(F32)
    lane = lax.broadcasted_iota(jnp.int32, (n, HS), 1)
    packed = jnp.zeros((n, HS), F32)
    outs = []
    for h in range(heads):
        cols = slice(h * HS, (h + 1) * HS)
        cols_v = slice(width + h * HS, width + (h + 1) * HS)
        q = q_ref[:, :, cols].reshape(n, HS)
        k = jnp.concatenate([r[:, cols] for r in key_refs], axis=0)
        v = jnp.concatenate([r[:, cols_v] for r in key_refs], axis=0)
        s = dot_t(q, k) + (slope_ref[h] * LOG2E) * spot
        s = jnp.where(usable, s, NEG)
        top = jnp.max(s, axis=1, keepdims=True)
        p = jnp.exp2(s - top).astype(BF16)
        both = jnp.dot(p, with_ones(v), preferred_element_type=F32)
        weight_total = both[:, HS:]
        outs.append((both[:, :HS] / weight_total).astype(BF16))
        level = top + jnp.log2(weight_total)
        for k, piece in enumerate(three_parts(level)):
            packed = jnp.where(lane == 3 * h + k, piece, packed)
    out = jnp.concatenate(outs + [packed.astype(BF16)], axis=1)
    out_ref[...] = out.reshape(out_ref.shape)


def short_attend(slopes, queries, keys):
    blocks, groups, width = queries.shape
    n = blocks * groups
    smem = pl.BlockSpec(memory_space=SMEM)
    vmem = pl.BlockSpec(memory_space=VMEM)
    return pl.pallas_call(
        short_attend_kernel,
        in_specs=[smem] + [vmem] * 5,
        out_specs=vmem,
        out_shape=jax.ShapeDtypeStruct((blocks, groups, width + HS), BF16),
        compiler_params=params(16),
        cost_estimate=cost(4 * n * n * width, 8 * n * width),
        name="short_attend",
    )(slopes, queries, *keys)


def short_merge_kernel(heads, parts_ref, w_hbm, *refs):
    outs, (w_ref, sem) = refs[:4], refs[4:]
    load = pltpu.make_async_copy(w_hbm, w_ref, sem)
    load.start()
    sources, rows, padded = parts_ref.shape
    width = padded - HS
    merged = []
    for h in range(heads):
        cols = slice(h * HS, (h + 1) * HS)
        level = []
        for s in range(sources):
            lev = parts_ref[s, :, width:].astype(F32)
            level.append(
                (lev[:, 3 * h : 3 * h + 1] + lev[:, 3 * h + 1 : 3 * h + 2])
                + lev[:, 3 * h + 2 : 3 * h + 3]
            )
        top = functools.reduce(jnp.maximum, level)
        total = jnp.zeros((rows, 1), F32)
        acc = jnp.zeros((rows, HS), F32)
        for s in range(sources):
            weight = jnp.exp2(level[s] - top)
            total = total + weight
            acc = acc + weight * parts_ref[s, :, cols].astype(F32)
        merged.append((acc / total).astype(BF16))
    att = jnp.concatenate(merged, axis=1)
    cols = outs[0].shape[1]
    load.wait()
    terms = [
        jnp.dot(
            att, w_ref[:, t * cols : (t + 1) * cols], preferred_element_type=F32
        ).astype(BF16)
        for t in range(4)
    ]
    tp = lax.axis_index("tp")
    for flip, out in enumerate(outs):
        chosen = terms[flip]
        for t in range(1, 4):
            chosen = jnp.where(tp == t, terms[t ^ flip], chosen)
        out[...] = chosen


def short_merge(parts, weight):
    sources, rows, padded = parts.shape
    width = padded - HS
    cols = weight.shape[1] // 4
    out = jax.ShapeDtypeStruct((rows, cols), BF16)
    return pl.pallas_call(
        functools.partial(short_merge_kernel, width // HS),
        in_specs=[pl.BlockSpec(memory_space=VMEM), pl.BlockSpec(memory_space=HBM)],
        out_shape=[out] * 4,
        scratch_shapes=[VMEM(weight.shape, BF16), pltpu.SemaphoreType.DMA],
        compiler_params=params(60),
        cost_estimate=cost(8 * rows * width * cols, 8 * width * cols),
        name="short_merge",
    )(parts, weight)


def final_kernel(lay_ref, *refs):
    terms, out_ref = refs[:-1], refs[-1]
    rows, groups = lay_ref.shape[0], terms[0].shape[0]
    t = lax.broadcasted_iota(jnp.int32, (rows, groups), 0) // GROUP
    g = lax.broadcasted_iota(jnp.int32, (rows, groups), 1)
    spread = jnp.where(t == g, 1.0, 0.0).astype(BF16)
    branch = jnp.zeros(lay_ref.shape, F32)
    for term in terms:
        branch = branch + jnp.dot(spread, term[...], preferred_element_type=F32)
    out_ref[...] = (lay_ref[...].astype(F32) + branch).astype(BF16)


def final_sum(layer, terms):
    rows, cols = layer.shape
    groups = terms[0].shape[0]
    return pl.pallas_call(
        final_kernel,
        out_shape=jax.ShapeDtypeStruct((rows, cols), BF16),
        compiler_params=params(16),
        cost_estimate=cost(8 * rows * cols * groups, 4 * rows * cols),
        name="final_sum",
    )(layer, *terms)


def exchange(blocks, axis):
    return lax.all_to_all(blocks, axis, 0, 0)


def swap(x, axis, flip=1):
    return lax.ppermute(x, axis, [(i, i ^ flip) for i in range(lax.axis_size(axis))])


def moved(x, axis, by):
    n = lax.axis_size(axis)
    return lax.ppermute(x, axis, [(i, (i + by) % n) for i in range(n)])


def both_ways(x, axis, by):
    return moved(x, axis, by), moved(x, axis, -by)


def counts_along(table, axis, *flips):
    for flip in flips:
        table = added(table, swap(table, axis, flip))
    return table


def after(x, *others):
    return lax.optimization_barrier((x, *others))[0]


def on_device(
    tokens,
    project_weight,
    output_weight,
    distance_slope,
    cache_keys,
    cache_values,
    cache_count,
    short_project_weight,
    short_output,
    short_slope,
):
    axes = ("y", "z", "xl", "tp")
    slots = cache_keys.shape[0]
    weight3 = jnp.transpose(project_weight, (1, 0, 2))
    table = counts_along(own_count(cache_count), "xl", 1)
    q, normed = project_queries(tokens, weight3)
    normed, table = lax.optimization_barrier((normed, table))
    table = counts_along(table, "z", 1)
    pack = project_pack(normed, weight3, cache_keys, cache_values)
    pack, table = lax.optimization_barrier((pack, table))
    table = counts_along(table, "z", 2, 4)
    left, right = both_ways(pack, "y", 1)
    other, left, right, mate, table = lax.optimization_barrier(
        (swap(pack, "xl"), left, right, swap(q, "z"), table)
    )
    pair = join(q, mate)
    left_other, right_other = both_ways(other, "y", 1)
    left_pair, right_pair = both_ways(pair, "z", 2)
    table = counts_along(table, "y", 1)
    left_other, right_other, left_pair, right_pair, left, table = lax.optimization_barrier(
        (left_other, right_other, left_pair, right_pair, left, table)
    )
    tables = [table, swap(table, "y", 2)]
    far, far_other = moved(left, "y", 1), moved(right_other, "y", -1)
    near = halves(left_pair, right_pair)
    queries = [pair, left_pair, right_pair, moved(near[0], "z", 2), moved(near[1], "z", -2)]
    crossed = swap(after(output_weight, other), "tp", 2)
    packs = [pack, other, left, left_other, right, right_other, far, far_other]
    parts = attend(distance_slope, queries, tables, packs, slots)
    parts, crossed = lax.optimization_barrier((parts, crossed))

    att = merge(exchange(parts, "z"))
    total, term, rim = layer_product(
        tokens, (att, swap(att, "tp", 2)), (output_weight, crossed)
    )
    n, tp = lax.axis_size(axes), lax.axis_size("tp")
    ahead = [(i, i + tp) for i in range(n - tp)]
    rims = [
        lax.ppermute(rim, axes, ahead),
        lax.ppermute(rim, axes, [(i, j ^ 1) for i, j in ahead]),
    ]
    layer, sq, skv = short_project(
        total,
        swap(term, "tp", 1),
        rims,
        jnp.transpose(short_project_weight, (1, 0, 2)),
        lax.axis_size("z"),
    )
    pair = join(skv, swap(skv, "xl"))
    keys = [pair] + [moved(pair, "y", by) for by in (1, 2, 3)]
    sparts = short_attend(short_slope, exchange(sq, "z"), keys)
    terms = short_merge(exchange(sparts, "z"), short_output)
    terms = [swap(t, "tp", flip) if flip else t for flip, t in enumerate(terms)]
    return final_sum(layer, terms)


def solution(mesh):
    split = Mesh(mesh.devices.reshape(4, 8, 2, 4), ("y", "z", "xl", "tp"))
    ctx = ("y", "z", "xl")
    return jax.shard_map(
        on_device,
        mesh=split,
        in_specs=(
            P(ctx, None),
            P(None, None, "tp"),
            P("tp", None),
            P("tp"),
            P(ctx, "tp"),
            P(ctx, "tp"),
            P(ctx),
            P(None, None, "tp"),
            P("tp", None),
            P("tp"),
        ),
        out_specs=P(ctx, "tp"),
        check_vma=False,
    )
```

```python
import functools
import math

import jax
import jax.numpy as jnp
from jax import lax
from jax.experimental import pallas as pl
from jax.experimental.pallas import tpu as pltpu
from jax.sharding import Mesh, PartitionSpec as P

HS = 128
GROUP = 4
NEG = -1e30
LOG2E = math.log2(math.e)
SCALE2 = HS ** -0.5 * LOG2E

VMEM = pltpu.VMEM
SMEM = pltpu.SMEM
HBM = pltpu.HBM
F32 = jnp.float32
BF16 = jnp.bfloat16


def cost(flops, moved, trans=0):
    return pl.CostEstimate(flops=flops, bytes_accessed=moved, transcendentals=trans)


def params(mib):
    return pltpu.CompilerParams(vmem_limit_bytes=mib * 1024 * 1024)


def rms_scaled(values):
    inv = lax.rsqrt(jnp.mean(values * values, axis=-1, keepdims=True) + 1e-06)
    return (values * inv).astype(BF16)


def dot_t(a, b):
    return lax.dot_general(a, b, (((1,), (1,)), ((), ())), preferred_element_type=F32)


def three_parts(x):
    hi = x.astype(BF16).astype(F32)
    mid = (x - hi).astype(BF16).astype(F32)
    lo = (x - hi - mid).astype(BF16).astype(F32)
    return hi, mid, lo


def query_kernel(tok_hbm, w_hbm, q_ref, normed_ref, tok, weight, sems):
    copies = [
        pltpu.make_async_copy(tok_hbm, tok, sems.at[0]),
        pltpu.make_async_copy(w_hbm.at[0], weight, sems.at[1]),
    ]
    for copy in copies:
        copy.start()
    copies[0].wait()
    normed = rms_scaled(tok[...].astype(F32))
    normed_ref[...] = normed
    copies[1].wait()
    out = jnp.dot(normed, weight[...], preferred_element_type=F32)
    q_ref[...] = (out * SCALE2).astype(BF16)


def project_queries(rows, weight3):
    n, d = rows.shape
    width = weight3.shape[2]
    hbm = pl.BlockSpec(memory_space=HBM)
    vmem = pl.BlockSpec(memory_space=VMEM)
    return pl.pallas_call(
        query_kernel,
        in_specs=[hbm, hbm],
        out_specs=[vmem, vmem],
        out_shape=[jax.ShapeDtypeStruct((n, w), BF16) for w in (width, d)],
        scratch_shapes=[
            VMEM((n, d), BF16),
            VMEM((d, width), BF16),
            pltpu.SemaphoreType.DMA((2,)),
        ],
        compiler_params=params(60),
        cost_estimate=cost(2 * n * d * width, 2 * (n * d + d * width)),
        name="project_queries",
    )(rows, weight3)


def pack_kernel(
    normed_hbm, w_hbm, ck_hbm, cv_hbm, table_ref, pack_ref, normed, weight, sems
):
    rows = normed.shape[0]
    slots = ck_hbm.shape[0]
    copies = [pltpu.make_async_copy(normed_hbm, normed, sems.at[0])]
    copies += [
        pltpu.make_async_copy(w_hbm.at[1 + i], weight.at[i], sems.at[1 + i]) for i in range(2)
    ]
    copies += [
        pltpu.make_async_copy(ck_hbm, pack_ref.at[:slots], sems.at[3]),
        pltpu.make_async_copy(cv_hbm, pack_ref.at[slots : 2 * slots], sems.at[4]),
    ]
    for copy in copies:
        copy.start()
    table = jnp.sum(table_ref[...].astype(F32), axis=0)
    pack_ref[2 * (slots + rows) :] = table.astype(BF16)
    copies[0].wait()
    for i in range(2):
        copies[1 + i].wait()
        out = jnp.dot(normed[...], weight[i], preferred_element_type=F32)
        at = 2 * slots + i * rows
        pack_ref[at : at + rows] = out.astype(BF16)
    copies[3].wait()
    copies[4].wait()


def project_pack(normed, weight3, cache_keys, cache_values, table):
    n, d = normed.shape
    width = weight3.shape[2]
    total = 2 * (n + cache_keys.shape[0]) + table.shape[1]
    hbm = pl.BlockSpec(memory_space=HBM)
    return pl.pallas_call(
        pack_kernel,
        in_specs=[hbm] * 4 + [pl.BlockSpec(memory_space=VMEM)],
        out_specs=pl.BlockSpec(memory_space=VMEM),
        out_shape=jax.ShapeDtypeStruct((total, width), BF16),
        scratch_shapes=[
            VMEM((n, d), BF16),
            VMEM((2, d, width), BF16),
            pltpu.SemaphoreType.DMA((5,)),
        ],
        compiler_params=params(60),
        cost_estimate=cost(4 * n * d * width, 2 * (n * d + 2 * d * width)),
        name="project_pack",
    )(normed, weight3, cache_keys, cache_values, table)


def table_kernel(count_ref, out_ref):
    y, z, xl = place_of_device()
    lane = lax.broadcasted_iota(jnp.int32, out_ref.shape, 2)
    out_ref[...] = jnp.where(lane == y * 16 + z * 2 + xl, count_ref[0], 0).astype(F32).astype(BF16)


def own_count(count, copies, width):
    return pl.pallas_call(
        table_kernel,
        in_specs=[pl.BlockSpec(memory_space=SMEM)],
        out_shape=jax.ShapeDtypeStruct((copies, 16, width), BF16),
        compiler_params=params(8),
        cost_estimate=cost(0, 32 * copies * width),
        name="own_count",
    )(count)


def join_kernel(a_ref, b_ref, out_ref):
    rows = a_ref.shape[0]
    out_ref[:rows] = a_ref[...]
    out_ref[rows:] = b_ref[...]


def join(a, b):
    n, width = a.shape
    return pl.pallas_call(
        join_kernel,
        out_shape=jax.ShapeDtypeStruct((2 * n, width), BF16),
        compiler_params=params(8),
        cost_estimate=cost(0, 8 * n * width),
        name="join",
    )(a, b)


def halves_kernel(left_ref, right_ref, own_ref, other_ref):
    half = own_ref.shape[0]
    own_ref[...] = left_ref[:half]
    other_ref[...] = right_ref[half:]


def halves(left, right):
    n, width = left.shape
    out = jax.ShapeDtypeStruct((n // 2, width), BF16)
    return pl.pallas_call(
        halves_kernel,
        out_shape=[out, out],
        compiler_params=params(8),
        cost_estimate=cost(0, 4 * n * width),
        name="halves",
    )(left, right)


def join_kernel(a_ref, b_ref, out_ref):
    rows = a_ref.shape[0]
    out_ref[:rows] = a_ref[...]
    out_ref[rows:] = b_ref[...]


def join(a, b):
    n, width = a.shape
    return pl.pallas_call(
        join_kernel,
        out_shape=jax.ShapeDtypeStruct((2 * n, width), BF16),
        compiler_params=params(8),
        cost_estimate=cost(0, 8 * n * width),
        name="join",
    )(a, b)


RING = ((0, 0), (0, 1), (1, 0), (1, 1), (3, 0), (3, 1), (2, 0), (2, 1))


def place_of_device():
    return lax.axis_index("y"), lax.axis_index("z"), lax.axis_index("xl")


def columns_of(pieces):
    return [s[:, at : at + HS] for s in pieces for at in range(0, s.shape[1], HS)]


def attend_heads(qs, pieces, score, value):
    heads = len(qs)
    pending = [score(0, qs[0], j) for j in range(pieces)]
    results = []
    for h in range(heads):
        top = jnp.max(functools.reduce(jnp.maximum, columns_of(pending)), axis=1, keepdims=True)
        following = []
        both = None
        for j in range(pieces):
            term = jnp.dot(
                jnp.exp2((pending[j] - top).astype(BF16)),
                value(h, j),
                preferred_element_type=F32,
            )
            both = term if both is None else both + term
            if h + 1 < heads:
                following.append(score(h + 1, qs[h + 1], j))
        pending = following
        results.append((top, both[:, HS:], both[:, :HS]))
    return results


def with_ones(v):
    return jnp.concatenate([v, jnp.ones_like(v)], axis=1)


def attend_kernel(slots, slope_ref, *refs):
    queries, packs = refs[:5], refs[5:13]
    out_ref, q_tile, bias = refs[13:]
    tile = pl.program_id(0)
    y, z, xl = place_of_device()
    rows = q_tile.shape[0] // 2
    width = q_tile.shape[1]
    heads = width // HS
    owners = len(RING)
    cached = owners * slots

    def side_of(other):
        return 1 - xl if other else xl

    own, left, right, far, far_other = queries
    for t, (a, b, at) in enumerate(
        ((own, own, rows), (left, left, rows), (far, far_other, 0), (right, right, rows))
    ):

        @pl.when(tile == t)
        def _(a=a, b=b, at=at):
            q_tile[:rows] = a[:rows]
            q_tile[rows:] = b[at : at + rows]

    @pl.when(tile == 0)
    def _():
        table = functools.reduce(
            jnp.add, [pack[2 * (slots + rows) :].astype(F32) for pack in packs]
        )[:1]
        lane = lax.broadcasted_iota(jnp.int32, table.shape, 1)
        everything = jnp.sum(table, axis=1, keepdims=True)
        slot = lax.broadcasted_iota(jnp.int32, (1, slots), 1).astype(F32)
        place = lax.broadcasted_iota(jnp.int32, (1, rows), 1)
        for j, (back, other) in enumerate(RING):
            yj = (y + 4 - back) % 4
            ctx = yj * 16 + z * 2 + side_of(other)
            live = jnp.sum(jnp.where(lane == ctx, table, 0.0), axis=1, keepdims=True)
            start = jnp.sum(jnp.where(lane < ctx, table, 0.0), axis=1, keepdims=True) - everything
            spot = (place + ctx * rows).astype(F32)
            for h in range(heads):
                slope = slope_ref[h] * LOG2E
                bias[h : h + 1, j * slots : (j + 1) * slots] = jnp.where(
                    slot < live, slope * (slot + start), NEG
                )
                at = cached + j * rows
                bias[h : h + 1, at : at + rows] = jnp.where(yj <= y, slope * spot, NEG)

    row = lax.broadcasted_iota(jnp.int32, (2 * rows, 1), 0)
    first = (z + 8 - 2 * tile) % 8
    row_ctx = y * 16 + xl + 2 * jnp.where(row < rows, first, first ^ 1)
    row_pos = row_ctx * rows + jnp.where(row < rows, row, row - rows)
    place = lax.broadcasted_iota(jnp.int32, (1, rows), 1)

    def score(h, q, j):
        cols = slice(h * HS, (h + 1) * HS)
        if j < owners:
            s = dot_t(q, packs[j][:slots, cols])
            return s + bias[h : h + 1, j * slots : (j + 1) * slots]
        back, other = RING[j - owners]
        at = cached + (j - owners) * rows
        s = dot_t(q, packs[j - owners][2 * slots : 2 * slots + rows, cols])
        s = s + bias[h : h + 1, at : at + rows]
        if back == 0:
            first_key = (y * 16 + z * 2 + side_of(other)) * rows
            s = jnp.where(place + first_key <= row_pos, s, NEG)
        return s

    def value(h, j):
        cols = slice(h * HS, (h + 1) * HS)
        if j < owners:
            return with_ones(packs[j][slots : 2 * slots, cols])
        return with_ones(packs[j - owners][2 * slots + rows : 2 * (slots + rows), cols])

    lane = lax.broadcasted_iota(jnp.int32, (2 * rows, HS), 1)
    packed = jnp.zeros((2 * rows, HS), F32)
    qs = [q_tile[:, h * HS : (h + 1) * HS] for h in range(heads)]
    done = []
    for h, (top, total, acc) in enumerate(attend_heads(qs, 2 * owners, score, value)):
        done.append((acc / total).astype(BF16))
        for k, piece in enumerate(three_parts(top + jnp.log2(total))):
            packed = jnp.where(lane == 3 * h + k, piece, packed)
    both = jnp.concatenate(done, axis=1)
    odd = z % 2 == 1
    blocks = []
    for own, level in (
        (jnp.where(odd, both[rows:], both[:rows]), jnp.where(odd, packed[rows:], packed[:rows])),
        (jnp.where(odd, both[:rows], both[rows:]), jnp.where(odd, packed[:rows], packed[rows:])),
    ):
        turned = jnp.transpose(level)[:16]
        tail = jnp.concatenate([turned, jnp.zeros_like(turned)], axis=1).astype(BF16)
        blocks.append((own, tail))
    for p in range(4):

        @pl.when((z // 2 + 4 - tile) % 4 == p)
        def _(p=p):
            for b, (own, tail) in enumerate(blocks):
                out_ref[2 * p + b, :rows] = own
                out_ref[2 * p + b, rows:] = tail


def attend(slopes, queries, packs, slots):
    rows, width = queries[0].shape[0] // 2, queries[0].shape[1]
    nk = len(RING) * (slots + rows)
    whole = lambda a: pl.BlockSpec(a.shape, lambda i: (0,) * a.ndim)
    out = jax.ShapeDtypeStruct((8, rows + 16, width), BF16)
    return pl.pallas_call(
        functools.partial(attend_kernel, slots),
        grid=(4,),
        in_specs=[pl.BlockSpec(memory_space=SMEM)]
        + [whole(a) for a in (*queries, *packs)],
        out_specs=whole(out),
        out_shape=out,
        scratch_shapes=[VMEM((2 * rows, width), BF16), VMEM((8, nk), F32)],
        compiler_params=params(40),
        cost_estimate=cost(32 * rows * nk * width, 4 * nk * width, 16 * rows * nk),
        name="attend",
    )(slopes, *queries, *packs)


def merge_kernel(heads, parts_ref, out_ref):
    sources, padded, width = parts_ref.shape
    rows = padded - 16
    levels = jnp.concatenate(
        [parts_ref[s, rows:, :HS].astype(F32) for s in range(sources)], axis=0
    )
    turned = jnp.transpose(levels)
    for h in range(heads):
        cols = slice(h * HS, (h + 1) * HS)
        level = []
        for s in range(sources):
            at = s * 16 + 3 * h
            level.append(
                (turned[:, at : at + 1] + turned[:, at + 1 : at + 2]) + turned[:, at + 2 : at + 3]
            )
        top = functools.reduce(jnp.maximum, level)
        total = jnp.zeros((rows, 1), F32)
        acc = jnp.zeros((rows, HS), F32)
        for s in range(sources):
            weight = jnp.exp2(level[s] - top)
            total = total + weight
            acc = acc + weight * parts_ref[s, :rows, cols].astype(F32)
        out_ref[:, cols] = (acc / total).astype(BF16)


def merge(parts):
    sources, padded, width = parts.shape
    rows = padded - 16
    return pl.pallas_call(
        functools.partial(merge_kernel, width // HS),
        out_shape=jax.ShapeDtypeStruct((rows, width), BF16),
        compiler_params=params(16),
        cost_estimate=cost(4 * sources * rows * width, 2 * sources * padded * width),
        name="merge",
    )(parts)


def product_kernel(
    tok_hbm, a_ref, b_ref, wa_hbm, wb_hbm, sum_ref, term_ref, rim_ref, tok, wa, wb, sems
):
    chunks = wa.shape[0]
    cols = wa.shape[2]
    copies = []
    for c in range(chunks):
        at = pl.ds(c * cols, cols)
        copies.append(
            [
                pltpu.make_async_copy(src.at[:, at], dst.at[c], sems.at[i, c])
                for i, (src, dst) in enumerate(((wa_hbm, wa), (wb_hbm, wb), (tok_hbm, tok)))
            ]
        )
    for group in copies:
        for copy in group:
            copy.start()
    for c, group in enumerate(copies):
        for copy in group:
            copy.wait()
        at = slice(c * cols, (c + 1) * cols)
        term = jnp.dot(a_ref[...], wa[c], preferred_element_type=F32) + jnp.dot(
            b_ref[...], wb[c], preferred_element_type=F32
        )
        total = tok[c].astype(F32) + term
        sum_ref[:, at] = total
        term_ref[:, at] = term.astype(BF16)
        rim_ref[:16, at] = total[-16:].astype(BF16)
        rim_ref[16:, at] = term[-16:].astype(BF16)


def layer_product(tokens, atts, weights):
    rows, d = tokens.shape
    chunks = 4
    inner = weights[0].shape[0]
    hbm = pl.BlockSpec(memory_space=HBM)
    vmem = pl.BlockSpec(memory_space=VMEM)
    return pl.pallas_call(
        product_kernel,
        in_specs=[hbm, vmem, vmem, hbm, hbm],
        out_specs=[vmem] * 3,
        out_shape=[
            jax.ShapeDtypeStruct((rows, d), F32),
            jax.ShapeDtypeStruct((rows, d), BF16),
            jax.ShapeDtypeStruct((32, d), BF16),
        ],
        scratch_shapes=[
            VMEM((chunks, rows, d // chunks), BF16),
            VMEM((chunks, inner, d // chunks), BF16),
            VMEM((chunks, inner, d // chunks), BF16),
            pltpu.SemaphoreType.DMA((3, chunks)),
        ],
        compiler_params=params(16),
        cost_estimate=cost(4 * rows * d * inner, 4 * inner * d),
        name="layer_product",
    )(tokens, *atts, *weights)


def short_project_kernel(
    sum_ref, term_ref, rim_a, rim_b, w_ref, cols_ref, q_ref, kv_ref, normed
):
    step = pl.program_id(0)
    rows, d = sum_ref.shape
    groups = rows // GROUP
    rim_rows = 16
    width = w_ref.shape[2]

    @pl.when(step == 0)
    def _():
        layer = (sum_ref[...] + term_ref[...].astype(F32)).astype(BF16)
        part = d // 4
        tp = lax.axis_index("tp")
        mine = layer[:, :part]
        for t in range(1, 4):
            mine = jnp.where(tp == t, layer[:, t * part : (t + 1) * part], mine)
        cols_ref[...] = mine
        rim = (rim_a[:rim_rows].astype(F32) + rim_b[rim_rows:].astype(F32)).astype(BF16)
        g = lax.broadcasted_iota(jnp.int32, (groups, rows), 0) * GROUP
        t = lax.broadcasted_iota(jnp.int32, (groups, rows), 1)
        own = jnp.where((t <= g) & (t > g - GROUP), 1.0 / GROUP, 0.0).astype(BF16)
        g = lax.broadcasted_iota(jnp.int32, (groups, rim_rows), 0) * GROUP
        t = lax.broadcasted_iota(jnp.int32, (groups, rim_rows), 1) - rim_rows
        before = jnp.where(t > g - GROUP, 1.0 / GROUP, 0.0).astype(BF16)
        pooled = jnp.dot(own, layer, preferred_element_type=F32) + jnp.dot(
            before, rim, preferred_element_type=F32
        )
        normed[...] = rms_scaled(pooled.astype(BF16).astype(F32))

    out = jnp.dot(normed[...], w_ref[0], preferred_element_type=F32)

    @pl.when(step == 0)
    def _():
        scaled = (out * SCALE2).astype(BF16)
        for c in range(q_ref.shape[0]):
            q_ref[c] = scaled

    @pl.when(step == 1)
    def _():
        kv_ref[:, :width] = out.astype(BF16)

    @pl.when(step == 2)
    def _():
        kv_ref[:, width:] = out.astype(BF16)


def short_project(total, term, rims, weight3, copies):
    n, d = total.shape
    groups = n // GROUP
    width = weight3.shape[2]
    whole = lambda shape: pl.BlockSpec(shape, lambda i: (0,) * len(shape))
    shapes = [(n, d // 4), (copies, groups, width), (groups, 2 * width)]
    return pl.pallas_call(
        short_project_kernel,
        grid=(3,),
        in_specs=[whole((n, d)), whole((n, d)), whole((32, d)), whole((32, d))]
        + [pl.BlockSpec((1, d, width), lambda i: (i, 0, 0))],
        out_specs=[whole(s) for s in shapes],
        out_shape=[jax.ShapeDtypeStruct(s, BF16) for s in shapes],
        scratch_shapes=[VMEM((groups, d), BF16)],
        compiler_params=params(16),
        cost_estimate=cost(6 * groups * d * width, 2 * (n * d + 3 * d * width)),
        name="short_project",
    )(total, term, *rims, weight3)


def short_attend_kernel(slope_ref, q_ref, *refs):
    key_refs, out_ref = refs[:4], refs[4]
    y, z, xl = place_of_device()
    blocks, groups, padded = out_ref.shape
    width = padded - HS
    heads = width // HS
    n = blocks * groups
    row = lax.broadcasted_iota(jnp.int32, (n, 1), 0)
    row_pos = (y * 16 + xl + 2 * (row // groups)) * groups + row % groups
    key = lax.broadcasted_iota(jnp.int32, (1, n), 1)
    ys = (y + 4 - key // (2 * groups)) % 4
    side = jnp.where((key // groups) % 2 == 1, 1 - xl, xl)
    key_pos = (ys * 16 + z * 2 + side) * groups + key % groups
    usable = key_pos <= row_pos
    spot = key_pos.astype(F32)
    lane = lax.broadcasted_iota(jnp.int32, (n, HS), 1)
    packed = jnp.zeros((n, HS), F32)
    outs = []
    for h in range(heads):
        cols = slice(h * HS, (h + 1) * HS)
        cols_v = slice(width + h * HS, width + (h + 1) * HS)
        q = q_ref[:, :, cols].reshape(n, HS)
        k = jnp.concatenate([r[:, cols] for r in key_refs], axis=0)
        v = jnp.concatenate([r[:, cols_v] for r in key_refs], axis=0)
        s = dot_t(q, k) + (slope_ref[h] * LOG2E) * spot
        s = jnp.where(usable, s, NEG)
        top = jnp.max(s, axis=1, keepdims=True)
        p = jnp.exp2(s - top).astype(BF16)
        both = jnp.dot(p, with_ones(v), preferred_element_type=F32)
        weight_total = both[:, HS:]
        outs.append((both[:, :HS] / weight_total).astype(BF16))
        level = top + jnp.log2(weight_total)
        for k, piece in enumerate(three_parts(level)):
            packed = jnp.where(lane == 3 * h + k, piece, packed)
    out = jnp.concatenate(outs + [packed.astype(BF16)], axis=1)
    out_ref[...] = out.reshape(out_ref.shape)


def short_attend(slopes, queries, keys):
    blocks, groups, width = queries.shape
    n = blocks * groups
    smem = pl.BlockSpec(memory_space=SMEM)
    vmem = pl.BlockSpec(memory_space=VMEM)
    return pl.pallas_call(
        short_attend_kernel,
        in_specs=[smem] + [vmem] * 5,
        out_specs=vmem,
        out_shape=jax.ShapeDtypeStruct((blocks, groups, width + HS), BF16),
        compiler_params=params(16),
        cost_estimate=cost(4 * n * n * width, 8 * n * width),
        name="short_attend",
    )(slopes, queries, *keys)


def short_merge_kernel(heads, parts_ref, w_ref, *outs):
    sources, rows, padded = parts_ref.shape
    width = padded - HS
    merged = []
    for h in range(heads):
        cols = slice(h * HS, (h + 1) * HS)
        level = []
        for s in range(sources):
            lev = parts_ref[s, :, width:].astype(F32)
            level.append(
                (lev[:, 3 * h : 3 * h + 1] + lev[:, 3 * h + 1 : 3 * h + 2])
                + lev[:, 3 * h + 2 : 3 * h + 3]
            )
        top = functools.reduce(jnp.maximum, level)
        total = jnp.zeros((rows, 1), F32)
        acc = jnp.zeros((rows, HS), F32)
        for s in range(sources):
            weight = jnp.exp2(level[s] - top)
            total = total + weight
            acc = acc + weight * parts_ref[s, :, cols].astype(F32)
        merged.append((acc / total).astype(BF16))
    att = jnp.concatenate(merged, axis=1)
    cols = outs[0].shape[1]
    terms = [
        jnp.dot(
            att, w_ref[:, t * cols : (t + 1) * cols], preferred_element_type=F32
        ).astype(BF16)
        for t in range(4)
    ]
    tp = lax.axis_index("tp")
    for flip, out in enumerate(outs):
        chosen = terms[flip]
        for t in range(1, 4):
            chosen = jnp.where(tp == t, terms[t ^ flip], chosen)
        out[...] = chosen


def short_merge(parts, weight):
    sources, rows, padded = parts.shape
    width = padded - HS
    cols = weight.shape[1] // 4
    out = jax.ShapeDtypeStruct((rows, cols), BF16)
    return pl.pallas_call(
        functools.partial(short_merge_kernel, width // HS),
        out_shape=[out] * 4,
        compiler_params=params(16),
        cost_estimate=cost(8 * rows * width * cols, 8 * width * cols),
        name="short_merge",
    )(parts, weight)


def final_kernel(lay_ref, *refs):
    terms, out_ref = refs[:-1], refs[-1]
    rows, groups = lay_ref.shape[0], terms[0].shape[0]
    t = lax.broadcasted_iota(jnp.int32, (rows, groups), 0) // GROUP
    g = lax.broadcasted_iota(jnp.int32, (rows, groups), 1)
    spread = jnp.where(t == g, 1.0, 0.0).astype(BF16)
    branch = jnp.zeros(lay_ref.shape, F32)
    for term in terms:
        branch = branch + jnp.dot(spread, term[...], preferred_element_type=F32)
    out_ref[...] = (lay_ref[...].astype(F32) + branch).astype(BF16)


def final_sum(layer, terms):
    rows, cols = layer.shape
    groups = terms[0].shape[0]
    return pl.pallas_call(
        final_kernel,
        out_shape=jax.ShapeDtypeStruct((rows, cols), BF16),
        compiler_params=params(16),
        cost_estimate=cost(8 * rows * cols * groups, 4 * rows * cols),
        name="final_sum",
    )(layer, *terms)


def exchange(blocks, axis):
    return lax.all_to_all(blocks, axis, 0, 0)


def swap(x, axis, flip=1):
    return lax.ppermute(x, axis, [(i, i ^ flip) for i in range(lax.axis_size(axis))])


def moved(x, axis, by):
    n = lax.axis_size(axis)
    return lax.ppermute(x, axis, [(i, (i + by) % n) for i in range(n)])


def both_ways(x, axis, by):
    return moved(x, axis, by), moved(x, axis, -by)


def after(x, *others):
    return lax.optimization_barrier((x, *others))[0]


def on_device(
    tokens,
    project_weight,
    output_weight,
    distance_slope,
    cache_keys,
    cache_values,
    cache_count,
    short_project_weight,
    short_output,
    short_slope,
):
    axes = ("y", "z", "xl", "tp")
    slots = cache_keys.shape[0]
    weight3 = jnp.transpose(project_weight, (1, 0, 2))
    nz = lax.axis_size("z")
    table = exchange(own_count(cache_count, nz, cache_keys.shape[1]), "z")
    q, normed = project_queries(tokens, weight3)
    pack = project_pack(normed, weight3, cache_keys, cache_values, table)
    left, right = both_ways(pack, "y", 1)
    other, left, right, mate = lax.optimization_barrier(
        (swap(pack, "xl"), left, right, swap(q, "z"))
    )
    pair = join(q, mate)
    left_other, right_other = both_ways(other, "y", 1)
    left_pair, right_pair = both_ways(pair, "z", 2)
    left_other, right_other, left_pair, right_pair, left = lax.optimization_barrier(
        (left_other, right_other, left_pair, right_pair, left)
    )
    far, far_other = moved(left, "y", 1), moved(right_other, "y", -1)
    near = halves(left_pair, right_pair)
    queries = [pair, left_pair, right_pair, moved(near[0], "z", 2), moved(near[1], "z", -2)]
    crossed = swap(after(output_weight, other), "tp", 2)
    packs = [pack, other, left, left_other, right, right_other, far, far_other]
    parts = attend(distance_slope, queries, packs, slots)
    parts, crossed = lax.optimization_barrier((parts, crossed))

    att = merge(exchange(parts, "z"))
    total, term, rim = layer_product(
        tokens, (att, swap(att, "tp", 2)), (output_weight, crossed)
    )
    n, tp = lax.axis_size(axes), lax.axis_size("tp")
    ahead = [(i, i + tp) for i in range(n - tp)]
    rims = [
        lax.ppermute(rim, axes, ahead),
        lax.ppermute(rim, axes, [(i, j ^ 1) for i, j in ahead]),
    ]
    layer, sq, skv = short_project(
        total,
        swap(term, "tp", 1),
        rims,
        jnp.transpose(short_project_weight, (1, 0, 2)),
        nz,
    )
    mate = swap(skv, "xl")
    sq, mate = lax.optimization_barrier((sq, mate))
    pair = join(skv, mate)
    keys = [pair] + [moved(pair, "y", by) for by in (1, 2, 3)]
    sparts = short_attend(short_slope, exchange(sq, "z"), keys)
    terms = short_merge(exchange(sparts, "z"), short_output)
    terms = [swap(t, "tp", flip) if flip else t for flip, t in enumerate(terms)]
    return final_sum(layer, terms)


def solution(mesh):
    split = Mesh(mesh.devices.reshape(4, 8, 2, 4), ("y", "z", "xl", "tp"))
    ctx = ("y", "z", "xl")
    return jax.shard_map(
        on_device,
        mesh=split,
        in_specs=(
            P(ctx, None),
            P(None, None, "tp"),
            P("tp", None),
            P("tp"),
            P(ctx, "tp"),
            P(ctx, "tp"),
            P(ctx),
            P(None, None, "tp"),
            P("tp", None),
            P("tp"),
        ),
        out_specs=P(ctx, "tp"),
        check_vma=False,
    )
```

```python
import functools
import math

import jax
import jax.numpy as jnp
from jax import lax
from jax.experimental import pallas as pl
from jax.experimental.pallas import tpu as pltpu
from jax.sharding import Mesh, PartitionSpec as P

HS = 128
GROUP = 4
NEG = -1e30
LOG2E = math.log2(math.e)
SCALE2 = HS ** -0.5 * LOG2E

VMEM = pltpu.VMEM
SMEM = pltpu.SMEM
HBM = pltpu.HBM
F32 = jnp.float32
BF16 = jnp.bfloat16


def cost(flops, moved, trans=0):
    return pl.CostEstimate(flops=flops, bytes_accessed=moved, transcendentals=trans)


def params(mib):
    return pltpu.CompilerParams(vmem_limit_bytes=mib * 1024 * 1024)


def rms_scaled(values):
    inv = lax.rsqrt(jnp.mean(values * values, axis=-1, keepdims=True) + 1e-06)
    return (values * inv).astype(BF16)


def dot_t(a, b):
    return lax.dot_general(a, b, (((1,), (1,)), ((), ())), preferred_element_type=F32)


def three_parts(x):
    hi = x.astype(BF16).astype(F32)
    mid = (x - hi).astype(BF16).astype(F32)
    lo = (x - hi - mid).astype(BF16).astype(F32)
    return hi, mid, lo


def query_kernel(tok_hbm, w_hbm, q_ref, normed_ref, tok, weight, sems):
    copies = [
        pltpu.make_async_copy(tok_hbm, tok, sems.at[0]),
        pltpu.make_async_copy(w_hbm.at[0], weight, sems.at[1]),
    ]
    for copy in copies:
        copy.start()
    copies[0].wait()
    normed = rms_scaled(tok[...].astype(F32))
    normed_ref[...] = normed
    copies[1].wait()
    out = jnp.dot(normed, weight[...], preferred_element_type=F32)
    q_ref[...] = (out * SCALE2).astype(BF16)


def project_queries(rows, weight3):
    n, d = rows.shape
    width = weight3.shape[2]
    hbm = pl.BlockSpec(memory_space=HBM)
    vmem = pl.BlockSpec(memory_space=VMEM)
    return pl.pallas_call(
        query_kernel,
        in_specs=[hbm, hbm],
        out_specs=[vmem, vmem],
        out_shape=[jax.ShapeDtypeStruct((n, w), BF16) for w in (width, d)],
        scratch_shapes=[
            VMEM((n, d), BF16),
            VMEM((d, width), BF16),
            pltpu.SemaphoreType.DMA((2,)),
        ],
        compiler_params=params(60),
        cost_estimate=cost(2 * n * d * width, 2 * (n * d + d * width)),
        name="project_queries",
    )(rows, weight3)


def key_kernel(normed_hbm, w_hbm, kv_ref, normed, weight, sems):
    rows = normed.shape[0]
    copies = [pltpu.make_async_copy(normed_hbm, normed, sems.at[0])]
    copies += [
        pltpu.make_async_copy(w_hbm.at[1 + i], weight.at[i], sems.at[1 + i]) for i in range(2)
    ]
    for copy in copies:
        copy.start()
    copies[0].wait()
    for i in range(2):
        copies[1 + i].wait()
        out = jnp.dot(normed[...], weight[i], preferred_element_type=F32)
        kv_ref[i * rows : (i + 1) * rows] = out.astype(BF16)


def project_keys(normed, weight3):
    n, d = normed.shape
    width = weight3.shape[2]
    hbm = pl.BlockSpec(memory_space=HBM)
    return pl.pallas_call(
        key_kernel,
        in_specs=[hbm, hbm],
        out_specs=pl.BlockSpec(memory_space=VMEM),
        out_shape=jax.ShapeDtypeStruct((2 * n, width), BF16),
        scratch_shapes=[
            VMEM((n, d), BF16),
            VMEM((2, d, width), BF16),
            pltpu.SemaphoreType.DMA((3,)),
        ],
        compiler_params=params(60),
        cost_estimate=cost(4 * n * d * width, 2 * (n * d + 2 * d * width)),
        name="project_keys",
    )(normed, weight3)


def pack_kernel(ck_hbm, cv_hbm, kv_hbm, near_ref, far_ref, pack_ref, sems):
    slots, both = ck_hbm.shape[0], kv_hbm.shape[0]
    copies = [
        pltpu.make_async_copy(ck_hbm, pack_ref.at[:slots], sems.at[0]),
        pltpu.make_async_copy(cv_hbm, pack_ref.at[slots : 2 * slots], sems.at[1]),
        pltpu.make_async_copy(kv_hbm, pack_ref.at[2 * slots : 2 * slots + both], sems.at[2]),
    ]
    for copy in copies:
        copy.start()
    table = near_ref[...].astype(F32) + far_ref[...].astype(F32)
    pack_ref[2 * slots + both :] = table.astype(BF16)
    for copy in copies:
        copy.wait()


def make_pack(cache_keys, cache_values, kv, near, far):
    total = 2 * cache_keys.shape[0] + kv.shape[0] + near.shape[0]
    width = kv.shape[1]
    hbm = pl.BlockSpec(memory_space=HBM)
    vmem = pl.BlockSpec(memory_space=VMEM)
    return pl.pallas_call(
        pack_kernel,
        in_specs=[hbm] * 3 + [vmem] * 2,
        out_specs=vmem,
        out_shape=jax.ShapeDtypeStruct((total, width), BF16),
        scratch_shapes=[pltpu.SemaphoreType.DMA((3,))],
        compiler_params=params(60),
        cost_estimate=cost(0, 4 * total * width),
        name="make_pack",
    )(cache_keys, cache_values, kv, near, far)


def table_kernel(count_ref, out_ref):
    y, z, xl = place_of_device()
    lane = lax.broadcasted_iota(jnp.int32, out_ref.shape, 1)
    out_ref[...] = jnp.where(lane == y * 16 + z * 2 + xl, count_ref[0], 0).astype(F32).astype(BF16)


def own_count(count, width):
    return pl.pallas_call(
        table_kernel,
        in_specs=[pl.BlockSpec(memory_space=SMEM)],
        out_shape=jax.ShapeDtypeStruct((16, width), BF16),
        compiler_params=params(8),
        cost_estimate=cost(0, 32 * width),
        name="own_count",
    )(count)


def add_kernel(a_ref, b_ref, out_ref):
    out_ref[...] = (a_ref[...].astype(F32) + b_ref[...].astype(F32)).astype(BF16)


def added(a, b):
    return pl.pallas_call(
        add_kernel,
        out_shape=jax.ShapeDtypeStruct(a.shape, a.dtype),
        compiler_params=params(8),
        cost_estimate=cost(a.size, 6 * a.size),
        name="added",
    )(a, b)


def join_kernel(a_ref, b_ref, out_ref):
    rows = a_ref.shape[0]
    out_ref[:rows] = a_ref[...]
    out_ref[rows:] = b_ref[...]


def join(a, b):
    n, width = a.shape
    return pl.pallas_call(
        join_kernel,
        out_shape=jax.ShapeDtypeStruct((2 * n, width), BF16),
        compiler_params=params(8),
        cost_estimate=cost(0, 8 * n * width),
        name="join",
    )(a, b)


def halves_kernel(left_ref, right_ref, own_ref, other_ref):
    half = own_ref.shape[0]
    own_ref[...] = left_ref[:half]
    other_ref[...] = right_ref[half:]


def halves(left, right):
    n, width = left.shape
    out = jax.ShapeDtypeStruct((n // 2, width), BF16)
    return pl.pallas_call(
        halves_kernel,
        out_shape=[out, out],
        compiler_params=params(8),
        cost_estimate=cost(0, 4 * n * width),
        name="halves",
    )(left, right)


def join_kernel(a_ref, b_ref, out_ref):
    rows = a_ref.shape[0]
    out_ref[:rows] = a_ref[...]
    out_ref[rows:] = b_ref[...]


def join(a, b):
    n, width = a.shape
    return pl.pallas_call(
        join_kernel,
        out_shape=jax.ShapeDtypeStruct((2 * n, width), BF16),
        compiler_params=params(8),
        cost_estimate=cost(0, 8 * n * width),
        name="join",
    )(a, b)


RING = ((0, 0), (0, 1), (1, 0), (1, 1), (3, 0), (3, 1), (2, 0), (2, 1))


def place_of_device():
    return lax.axis_index("y"), lax.axis_index("z"), lax.axis_index("xl")


def columns_of(pieces):
    return [s[:, at : at + HS] for s in pieces for at in range(0, s.shape[1], HS)]


def attend_heads(qs, pieces, score, value):
    heads = len(qs)
    pending = [score(0, qs[0], j) for j in range(pieces)]
    results = []
    for h in range(heads):
        top = jnp.max(functools.reduce(jnp.maximum, columns_of(pending)), axis=1, keepdims=True)
        following = []
        both = None
        for j in range(pieces):
            term = jnp.dot(
                jnp.exp2((pending[j] - top).astype(BF16)),
                value(h, j),
                preferred_element_type=F32,
            )
            both = term if both is None else both + term
            if h + 1 < heads:
                following.append(score(h + 1, qs[h + 1], j))
        pending = following
        results.append((top, both[:, HS:], both[:, :HS]))
    return results


def with_ones(v):
    return jnp.concatenate([v, jnp.ones_like(v)], axis=1)


def attend_kernel(slots, slope_ref, *refs):
    queries, packs = refs[:5], refs[5:13]
    out_ref, q_tile, bias = refs[13:]
    tile = pl.program_id(0)
    y, z, xl = place_of_device()
    count = q_tile.shape[0]
    rows = count // 4
    width = q_tile.shape[1]
    heads = width // HS
    owners = len(RING)
    cached = owners * slots

    def side_of(other):
        return 1 - xl if other else xl

    own, left, right, far, far_other = queries
    for t, pieces in enumerate(
        (
            ((own, 0), (own, rows), (left, 0), (left, rows)),
            ((far, 0), (far_other, 0), (right, 0), (right, rows)),
        )
    ):

        @pl.when(tile == t)
        def _(pieces=pieces):
            for b, (ref, at) in enumerate(pieces):
                q_tile[b * rows : (b + 1) * rows] = ref[at : at + rows]

    @pl.when(tile == 0)
    def _():
        table = functools.reduce(
            jnp.add, [pack[2 * (slots + rows) :].astype(F32) for pack in packs]
        )[:1]
        lane = lax.broadcasted_iota(jnp.int32, table.shape, 1)
        everything = jnp.sum(table, axis=1, keepdims=True)
        slot = lax.broadcasted_iota(jnp.int32, (1, slots), 1).astype(F32)
        place = lax.broadcasted_iota(jnp.int32, (1, rows), 1)
        for j, (back, other) in enumerate(RING):
            yj = (y + 4 - back) % 4
            ctx = yj * 16 + z * 2 + side_of(other)
            live = jnp.sum(jnp.where(lane == ctx, table, 0.0), axis=1, keepdims=True)
            start = jnp.sum(jnp.where(lane < ctx, table, 0.0), axis=1, keepdims=True) - everything
            spot = (place + ctx * rows).astype(F32)
            for h in range(heads):
                slope = slope_ref[h] * LOG2E
                bias[h : h + 1, j * slots : (j + 1) * slots] = jnp.where(
                    slot < live, slope * (slot + start), NEG
                )
                at = cached + j * rows
                bias[h : h + 1, at : at + rows] = jnp.where(yj <= y, slope * spot, NEG)

    row = lax.broadcasted_iota(jnp.int32, (count, 1), 0)
    part = row // rows
    row_z = ((z + 8 - 4 * tile - 2 * (part // 2)) % 8) ^ (part % 2)
    row_pos = (y * 16 + xl + 2 * row_z) * rows + row % rows
    place = lax.broadcasted_iota(jnp.int32, (1, rows), 1)

    def score(h, q, j):
        cols = slice(h * HS, (h + 1) * HS)
        if j < owners:
            s = dot_t(q, packs[j][:slots, cols])
            return s + bias[h : h + 1, j * slots : (j + 1) * slots]
        back, other = RING[j - owners]
        at = cached + (j - owners) * rows
        s = dot_t(q, packs[j - owners][2 * slots : 2 * slots + rows, cols])
        s = s + bias[h : h + 1, at : at + rows]
        if back == 0:
            first_key = (y * 16 + z * 2 + side_of(other)) * rows
            s = jnp.where(place + first_key <= row_pos, s, NEG)
        return s

    def value(h, j):
        cols = slice(h * HS, (h + 1) * HS)
        if j < owners:
            return with_ones(packs[j][slots : 2 * slots, cols])
        return with_ones(packs[j - owners][2 * slots + rows : 2 * (slots + rows), cols])

    lane = lax.broadcasted_iota(jnp.int32, (count, HS), 1)
    packed = jnp.zeros((count, HS), F32)
    qs = [q_tile[:, h * HS : (h + 1) * HS] for h in range(heads)]
    done = []
    for h, (top, total, acc) in enumerate(attend_heads(qs, 2 * owners, score, value)):
        done.append((acc / total).astype(BF16))
        for k, piece in enumerate(three_parts(top + jnp.log2(total))):
            packed = jnp.where(lane == 3 * h + k, piece, packed)
    both = jnp.concatenate(done, axis=1)
    odd = z % 2 == 1
    for pair in range(2):
        a, b = 2 * pair * rows, (2 * pair + 1) * rows
        end = b + rows
        blocks = []
        for own, level in (
            (jnp.where(odd, both[b:end], both[a:b]), jnp.where(odd, packed[b:end], packed[a:b])),
            (jnp.where(odd, both[a:b], both[b:end]), jnp.where(odd, packed[a:b], packed[b:end])),
        ):
            turned = jnp.transpose(level)[:16]
            tail = jnp.concatenate([turned, jnp.zeros_like(turned)], axis=1).astype(BF16)
            blocks.append((own, tail))
        for p in range(4):

            @pl.when((z // 2 + 4 - 2 * tile - pair) % 4 == p)
            def _(p=p, blocks=blocks):
                for i, (own, tail) in enumerate(blocks):
                    out_ref[2 * p + i, :rows] = own
                    out_ref[2 * p + i, rows:] = tail


def attend(slopes, queries, packs, slots):
    rows, width = queries[0].shape[0] // 2, queries[0].shape[1]
    nk = len(RING) * (slots + rows)
    whole = lambda a: pl.BlockSpec(a.shape, lambda i: (0,) * a.ndim)
    out = jax.ShapeDtypeStruct((8, rows + 16, width), BF16)
    return pl.pallas_call(
        functools.partial(attend_kernel, slots),
        grid=(2,),
        in_specs=[pl.BlockSpec(memory_space=SMEM)]
        + [whole(a) for a in (*queries, *packs)],
        out_specs=whole(out),
        out_shape=out,
        scratch_shapes=[VMEM((4 * rows, width), BF16), VMEM((8, nk), F32)],
        compiler_params=params(44),
        cost_estimate=cost(32 * rows * nk * width, 4 * nk * width, 16 * rows * nk),
        name="attend",
    )(slopes, *queries, *packs)


def merge_kernel(heads, parts_ref, out_ref):
    sources, padded, width = parts_ref.shape
    rows = padded - 16
    levels = jnp.concatenate(
        [parts_ref[s, rows:, :HS].astype(F32) for s in range(sources)], axis=0
    )
    turned = jnp.transpose(levels)
    for h in range(heads):
        cols = slice(h * HS, (h + 1) * HS)
        level = []
        for s in range(sources):
            at = s * 16 + 3 * h
            level.append(
                (turned[:, at : at + 1] + turned[:, at + 1 : at + 2]) + turned[:, at + 2 : at + 3]
            )
        top = functools.reduce(jnp.maximum, level)
        total = jnp.zeros((rows, 1), F32)
        acc = jnp.zeros((rows, HS), F32)
        for s in range(sources):
            weight = jnp.exp2(level[s] - top)
            total = total + weight
            acc = acc + weight * parts_ref[s, :rows, cols].astype(F32)
        out_ref[:, cols] = (acc / total).astype(BF16)


def merge(parts):
    sources, padded, width = parts.shape
    rows = padded - 16
    return pl.pallas_call(
        functools.partial(merge_kernel, width // HS),
        out_shape=jax.ShapeDtypeStruct((rows, width), BF16),
        compiler_params=params(16),
        cost_estimate=cost(4 * sources * rows * width, 2 * sources * padded * width),
        name="merge",
    )(parts)


def product_kernel(
    tok_hbm, a_ref, b_ref, wa_hbm, wb_hbm, sum_ref, term_ref, rim_ref, tok, wa, wb, sems
):
    chunks = wa.shape[0]
    cols = wa.shape[2]
    copies = []
    for c in range(chunks):
        at = pl.ds(c * cols, cols)
        copies.append(
            [
                pltpu.make_async_copy(src.at[:, at], dst.at[c], sems.at[i, c])
                for i, (src, dst) in enumerate(((wa_hbm, wa), (wb_hbm, wb), (tok_hbm, tok)))
            ]
        )
    for group in copies:
        for copy in group:
            copy.start()
    for c, group in enumerate(copies):
        for copy in group:
            copy.wait()
        at = slice(c * cols, (c + 1) * cols)
        term = jnp.dot(a_ref[...], wa[c], preferred_element_type=F32) + jnp.dot(
            b_ref[...], wb[c], preferred_element_type=F32
        )
        total = tok[c].astype(F32) + term
        sum_ref[:, at] = total
        term_ref[:, at] = term.astype(BF16)
        rim_ref[:16, at] = total[-16:].astype(BF16)
        rim_ref[16:, at] = term[-16:].astype(BF16)


def layer_product(tokens, atts, weights):
    rows, d = tokens.shape
    chunks = 4
    inner = weights[0].shape[0]
    hbm = pl.BlockSpec(memory_space=HBM)
    vmem = pl.BlockSpec(memory_space=VMEM)
    return pl.pallas_call(
        product_kernel,
        in_specs=[hbm, vmem, vmem, hbm, hbm],
        out_specs=[vmem] * 3,
        out_shape=[
            jax.ShapeDtypeStruct((rows, d), F32),
            jax.ShapeDtypeStruct((rows, d), BF16),
            jax.ShapeDtypeStruct((32, d), BF16),
        ],
        scratch_shapes=[
            VMEM((chunks, rows, d // chunks), BF16),
            VMEM((chunks, inner, d // chunks), BF16),
            VMEM((chunks, inner, d // chunks), BF16),
            pltpu.SemaphoreType.DMA((3, chunks)),
        ],
        compiler_params=params(16),
        cost_estimate=cost(4 * rows * d * inner, 4 * inner * d),
        name="layer_product",
    )(tokens, *atts, *weights)


def short_project_kernel(
    sum_ref, term_ref, rim_a, rim_b, w_ref, cols_ref, q_ref, kv_ref, normed
):
    step = pl.program_id(0)
    rows, d = sum_ref.shape
    groups = rows // GROUP
    rim_rows = 16
    width = w_ref.shape[2]

    @pl.when(step == 0)
    def _():
        layer = (sum_ref[...] + term_ref[...].astype(F32)).astype(BF16)
        part = d // 4
        tp = lax.axis_index("tp")
        mine = layer[:, :part]
        for t in range(1, 4):
            mine = jnp.where(tp == t, layer[:, t * part : (t + 1) * part], mine)
        cols_ref[...] = mine
        rim = (rim_a[:rim_rows].astype(F32) + rim_b[rim_rows:].astype(F32)).astype(BF16)
        g = lax.broadcasted_iota(jnp.int32, (groups, rows), 0) * GROUP
        t = lax.broadcasted_iota(jnp.int32, (groups, rows), 1)
        own = jnp.where((t <= g) & (t > g - GROUP), 1.0 / GROUP, 0.0).astype(BF16)
        g = lax.broadcasted_iota(jnp.int32, (groups, rim_rows), 0) * GROUP
        t = lax.broadcasted_iota(jnp.int32, (groups, rim_rows), 1) - rim_rows
        before = jnp.where(t > g - GROUP, 1.0 / GROUP, 0.0).astype(BF16)
        pooled = jnp.dot(own, layer, preferred_element_type=F32) + jnp.dot(
            before, rim, preferred_element_type=F32
        )
        normed[...] = rms_scaled(pooled.astype(BF16).astype(F32))

    out = jnp.dot(normed[...], w_ref[0], preferred_element_type=F32)

    @pl.when(step == 0)
    def _():
        scaled = (out * SCALE2).astype(BF16)
        for c in range(q_ref.shape[0]):
            q_ref[c] = scaled

    @pl.when(step == 1)
    def _():
        kv_ref[:, :width] = out.astype(BF16)

    @pl.when(step == 2)
    def _():
        kv_ref[:, width:] = out.astype(BF16)


def short_project(total, term, rims, weight3, copies):
    n, d = total.shape
    groups = n // GROUP
    width = weight3.shape[2]
    whole = lambda shape: pl.BlockSpec(shape, lambda i: (0,) * len(shape))
    shapes = [(n, d // 4), (copies, groups, width), (groups, 2 * width)]
    return pl.pallas_call(
        short_project_kernel,
        grid=(3,),
        in_specs=[whole((n, d)), whole((n, d)), whole((32, d)), whole((32, d))]
        + [pl.BlockSpec((1, d, width), lambda i: (i, 0, 0))],
        out_specs=[whole(s) for s in shapes],
        out_shape=[jax.ShapeDtypeStruct(s, BF16) for s in shapes],
        scratch_shapes=[VMEM((groups, d), BF16)],
        compiler_params=params(16),
        cost_estimate=cost(6 * groups * d * width, 2 * (n * d + 3 * d * width)),
        name="short_project",
    )(total, term, *rims, weight3)


def short_attend_kernel(slope_ref, q_ref, *refs):
    key_refs, out_ref = refs[:4], refs[4]
    y, z, xl = place_of_device()
    blocks, groups, padded = out_ref.shape
    width = padded - HS
    heads = width // HS
    n = blocks * groups
    row = lax.broadcasted_iota(jnp.int32, (n, 1), 0)
    row_pos = (y * 16 + xl + 2 * (row // groups)) * groups + row % groups
    key = lax.broadcasted_iota(jnp.int32, (1, n), 1)
    ys = (y + 4 - key // (2 * groups)) % 4
    side = jnp.where((key // groups) % 2 == 1, 1 - xl, xl)
    key_pos = (ys * 16 + z * 2 + side) * groups + key % groups
    usable = key_pos <= row_pos
    spot = key_pos.astype(F32)
    lane = lax.broadcasted_iota(jnp.int32, (n, HS), 1)
    packed = jnp.zeros((n, HS), F32)
    outs = []
    for h in range(heads):
        cols = slice(h * HS, (h + 1) * HS)
        cols_v = slice(width + h * HS, width + (h + 1) * HS)
        q = q_ref[:, :, cols].reshape(n, HS)
        k = jnp.concatenate([r[:, cols] for r in key_refs], axis=0)
        v = jnp.concatenate([r[:, cols_v] for r in key_refs], axis=0)
        s = dot_t(q, k) + (slope_ref[h] * LOG2E) * spot
        s = jnp.where(usable, s, NEG)
        top = jnp.max(s, axis=1, keepdims=True)
        p = jnp.exp2(s - top).astype(BF16)
        both = jnp.dot(p, with_ones(v), preferred_element_type=F32)
        weight_total = both[:, HS:]
        outs.append((both[:, :HS] / weight_total).astype(BF16))
        level = top + jnp.log2(weight_total)
        for k, piece in enumerate(three_parts(level)):
            packed = jnp.where(lane == 3 * h + k, piece, packed)
    out = jnp.concatenate(outs + [packed.astype(BF16)], axis=1)
    out_ref[...] = out.reshape(out_ref.shape)


def short_attend(slopes, queries, keys):
    blocks, groups, width = queries.shape
    n = blocks * groups
    smem = pl.BlockSpec(memory_space=SMEM)
    vmem = pl.BlockSpec(memory_space=VMEM)
    return pl.pallas_call(
        short_attend_kernel,
        in_specs=[smem] + [vmem] * 5,
        out_specs=vmem,
        out_shape=jax.ShapeDtypeStruct((blocks, groups, width + HS), BF16),
        compiler_params=params(16),
        cost_estimate=cost(4 * n * n * width, 8 * n * width),
        name="short_attend",
    )(slopes, queries, *keys)


def short_merge_kernel(heads, parts_ref, w_ref, *outs):
    sources, rows, padded = parts_ref.shape
    width = padded - HS
    merged = []
    for h in range(heads):
        cols = slice(h * HS, (h + 1) * HS)
        level = []
        for s in range(sources):
            lev = parts_ref[s, :, width:].astype(F32)
            level.append(
                (lev[:, 3 * h : 3 * h + 1] + lev[:, 3 * h + 1 : 3 * h + 2])
                + lev[:, 3 * h + 2 : 3 * h + 3]
            )
        top = functools.reduce(jnp.maximum, level)
        total = jnp.zeros((rows, 1), F32)
        acc = jnp.zeros((rows, HS), F32)
        for s in range(sources):
            weight = jnp.exp2(level[s] - top)
            total = total + weight
            acc = acc + weight * parts_ref[s, :, cols].astype(F32)
        merged.append((acc / total).astype(BF16))
    att = jnp.concatenate(merged, axis=1)
    cols = outs[0].shape[1]
    terms = [
        jnp.dot(
            att, w_ref[:, t * cols : (t + 1) * cols], preferred_element_type=F32
        ).astype(BF16)
        for t in range(4)
    ]
    tp = lax.axis_index("tp")
    for flip, out in enumerate(outs):
        chosen = terms[flip]
        for t in range(1, 4):
            chosen = jnp.where(tp == t, terms[t ^ flip], chosen)
        out[...] = chosen


def short_merge(parts, weight):
    sources, rows, padded = parts.shape
    width = padded - HS
    cols = weight.shape[1] // 4
    out = jax.ShapeDtypeStruct((rows, cols), BF16)
    return pl.pallas_call(
        functools.partial(short_merge_kernel, width // HS),
        out_shape=[out] * 4,
        compiler_params=params(16),
        cost_estimate=cost(8 * rows * width * cols, 8 * width * cols),
        name="short_merge",
    )(parts, weight)


def final_kernel(lay_ref, *refs):
    terms, out_ref = refs[:-1], refs[-1]
    rows, groups = lay_ref.shape[0], terms[0].shape[0]
    t = lax.broadcasted_iota(jnp.int32, (rows, groups), 0) // GROUP
    g = lax.broadcasted_iota(jnp.int32, (rows, groups), 1)
    spread = jnp.where(t == g, 1.0, 0.0).astype(BF16)
    branch = jnp.zeros(lay_ref.shape, F32)
    for term in terms:
        branch = branch + jnp.dot(spread, term[...], preferred_element_type=F32)
    out_ref[...] = (lay_ref[...].astype(F32) + branch).astype(BF16)


def final_sum(layer, terms):
    rows, cols = layer.shape
    groups = terms[0].shape[0]
    return pl.pallas_call(
        final_kernel,
        out_shape=jax.ShapeDtypeStruct((rows, cols), BF16),
        compiler_params=params(16),
        cost_estimate=cost(8 * rows * cols * groups, 4 * rows * cols),
        name="final_sum",
    )(layer, *terms)


def exchange(blocks, axis):
    return lax.all_to_all(blocks, axis, 0, 0)


def swap(x, axis, flip=1):
    return lax.ppermute(x, axis, [(i, i ^ flip) for i in range(lax.axis_size(axis))])


def moved(x, axis, by):
    n = lax.axis_size(axis)
    return lax.ppermute(x, axis, [(i, (i + by) % n) for i in range(n)])


def both_ways(x, axis, by):
    return moved(x, axis, by), moved(x, axis, -by)


def counts_along(table, flip):
    return added(table, swap(table, "z", flip))


def after(x, *others):
    return lax.optimization_barrier((x, *others))[0]


def on_device(
    tokens,
    project_weight,
    output_weight,
    distance_slope,
    cache_keys,
    cache_values,
    cache_count,
    short_project_weight,
    short_output,
    short_slope,
):
    axes = ("y", "z", "xl", "tp")
    slots = cache_keys.shape[0]
    weight3 = jnp.transpose(project_weight, (1, 0, 2))
    nz = lax.axis_size("z")
    near = counts_along(own_count(cache_count, cache_keys.shape[1]), 1)
    q, normed = project_queries(tokens, weight3)
    normed, near = lax.optimization_barrier((normed, near))
    near = counts_along(near, 2)
    kv = project_keys(normed, weight3)
    kv, near = lax.optimization_barrier((kv, near))
    pack = make_pack(cache_keys, cache_values, kv, near, swap(near, "z", 4))
    left, right = both_ways(pack, "y", 1)
    other, left, right, mate = lax.optimization_barrier(
        (swap(pack, "xl"), left, right, swap(q, "z"))
    )
    pair = join(q, mate)
    left_other, right_other = both_ways(other, "y", 1)
    left_pair, right_pair = both_ways(pair, "z", 2)
    left_other, right_other, left_pair, right_pair, left = lax.optimization_barrier(
        (left_other, right_other, left_pair, right_pair, left)
    )
    far, far_other = moved(left, "y", 1), moved(right_other, "y", -1)
    near = halves(left_pair, right_pair)
    queries = [pair, left_pair, right_pair, moved(near[0], "z", 2), moved(near[1], "z", -2)]
    crossed = swap(after(output_weight, other), "tp", 2)
    packs = [pack, other, left, left_other, right, right_other, far, far_other]
    parts = attend(distance_slope, queries, packs, slots)
    parts, crossed = lax.optimization_barrier((parts, crossed))

    att = merge(exchange(parts, "z"))
    total, term, rim = layer_product(
        tokens, (att, swap(att, "tp", 2)), (output_weight, crossed)
    )
    n, tp = lax.axis_size(axes), lax.axis_size("tp")
    ahead = [(i, i + tp) for i in range(n - tp)]
    rims = [
        lax.ppermute(rim, axes, ahead),
        lax.ppermute(rim, axes, [(i, j ^ 1) for i, j in ahead]),
    ]
    layer, sq, skv = short_project(
        total,
        swap(term, "tp", 1),
        rims,
        jnp.transpose(short_project_weight, (1, 0, 2)),
        nz,
    )
    mate = swap(skv, "xl")
    sq, mate = lax.optimization_barrier((sq, mate))
    pair = join(skv, mate)
    keys = [pair] + [moved(pair, "y", by) for by in (1, 2, 3)]
    sparts = short_attend(short_slope, exchange(sq, "z"), keys)
    terms = short_merge(exchange(sparts, "z"), short_output)
    terms = [swap(t, "tp", flip) if flip else t for flip, t in enumerate(terms)]
    return final_sum(layer, terms)


def solution(mesh):
    split = Mesh(mesh.devices.reshape(4, 8, 2, 4), ("y", "z", "xl", "tp"))
    ctx = ("y", "z", "xl")
    return jax.shard_map(
        on_device,
        mesh=split,
        in_specs=(
            P(ctx, None),
            P(None, None, "tp"),
            P("tp", None),
            P("tp"),
            P(ctx, "tp"),
            P(ctx, "tp"),
            P(ctx),
            P(None, None, "tp"),
            P("tp", None),
            P("tp"),
        ),
        out_specs=P(ctx, "tp"),
        check_vma=False,
    )
```

```python
import functools
import math

import jax
import jax.numpy as jnp
from jax import lax
from jax.experimental import pallas as pl
from jax.experimental.pallas import tpu as pltpu
from jax.sharding import Mesh, PartitionSpec as P

HS = 128
GROUP = 4
NEG = -1e30
LOG2E = math.log2(math.e)
SCALE2 = HS ** -0.5 * LOG2E

VMEM = pltpu.VMEM
SMEM = pltpu.SMEM
HBM = pltpu.HBM
F32 = jnp.float32
BF16 = jnp.bfloat16


def cost(flops, moved, trans=0):
    return pl.CostEstimate(flops=flops, bytes_accessed=moved, transcendentals=trans)


def params(mib):
    return pltpu.CompilerParams(vmem_limit_bytes=mib * 1024 * 1024)


def rms_scaled(values):
    inv = lax.rsqrt(jnp.mean(values * values, axis=-1, keepdims=True) + 1e-06)
    return (values * inv).astype(BF16)


def dot_t(a, b):
    return lax.dot_general(a, b, (((1,), (1,)), ((), ())), preferred_element_type=F32)


def three_parts(x):
    hi = x.astype(BF16).astype(F32)
    mid = (x - hi).astype(BF16).astype(F32)
    lo = (x - hi - mid).astype(BF16).astype(F32)
    return hi, mid, lo


def project_kernel(
    tok_hbm, w_hbm, ck_hbm, cv_hbm, q_ref, pack_ref, tok, weight, sems
):
    rows = tok.shape[0]
    slots = ck_hbm.shape[0]
    copies = [pltpu.make_async_copy(tok_hbm, tok, sems.at[0])]
    copies += [
        pltpu.make_async_copy(w_hbm.at[i], weight.at[i], sems.at[1 + i]) for i in range(3)
    ]
    copies += [
        pltpu.make_async_copy(ck_hbm, pack_ref.at[:slots], sems.at[4]),
        pltpu.make_async_copy(cv_hbm, pack_ref.at[slots : 2 * slots], sems.at[5]),
    ]
    for copy in copies:
        copy.start()
    copies[0].wait()
    normed = rms_scaled(tok[...].astype(F32))
    for i in range(3):
        copies[1 + i].wait()
        out = jnp.dot(normed, weight[i], preferred_element_type=F32)
        if i == 0:
            q_ref[...] = (out * SCALE2).astype(BF16)
        else:
            at = 2 * slots + (i - 1) * rows
            pack_ref[at : at + rows] = out.astype(BF16)
    copies[4].wait()
    copies[5].wait()


def project(rows, weight3, cache_keys, cache_values):
    n, d = rows.shape
    width = weight3.shape[2]
    total = 2 * (n + cache_keys.shape[0])
    hbm = pl.BlockSpec(memory_space=HBM)
    vmem = pl.BlockSpec(memory_space=VMEM)
    return pl.pallas_call(
        project_kernel,
        in_specs=[hbm] * 4,
        out_specs=[vmem, vmem],
        out_shape=[
            jax.ShapeDtypeStruct((n, width), BF16),
            jax.ShapeDtypeStruct((total, width), BF16),
        ],
        scratch_shapes=[
            VMEM((n, d), BF16),
            VMEM(weight3.shape, BF16),
            pltpu.SemaphoreType.DMA((6,)),
        ],
        compiler_params=params(60),
        cost_estimate=cost(6 * n * d * width, 2 * (n * d + 3 * d * width)),
        name="project",
    )(rows, weight3, cache_keys, cache_values)


def table_kernel(count_ref, out_ref):
    y, z, xl = place_of_device()
    lane = lax.broadcasted_iota(jnp.int32, out_ref.shape, 1)
    out_ref[...] = jnp.where(lane == y * 16 + z * 2 + xl, count_ref[0], 0).astype(F32).astype(BF16)


def own_count(count, width):
    return pl.pallas_call(
        table_kernel,
        in_specs=[pl.BlockSpec(memory_space=SMEM)],
        out_shape=jax.ShapeDtypeStruct((16, width), BF16),
        compiler_params=params(8),
        cost_estimate=cost(0, 32 * width),
        name="own_count",
    )(count)


def add_kernel(a_ref, b_ref, out_ref):
    out_ref[...] = (a_ref[...].astype(F32) + b_ref[...].astype(F32)).astype(BF16)


def added(a, b):
    return pl.pallas_call(
        add_kernel,
        out_shape=jax.ShapeDtypeStruct(a.shape, a.dtype),
        compiler_params=params(8),
        cost_estimate=cost(a.size, 6 * a.size),
        name="added",
    )(a, b)


def mark_kernel(q_ref, a_ref, b_ref, out_ref):
    rows = q_ref.shape[0]
    out_ref[:rows] = q_ref[...]
    out_ref[rows:] = (a_ref[...].astype(F32) + b_ref[...].astype(F32)).astype(BF16)


def mark(q, a, b):
    n, width = q.shape
    return pl.pallas_call(
        mark_kernel,
        out_shape=jax.ShapeDtypeStruct((n + a.shape[0], width), BF16),
        compiler_params=params(8),
        cost_estimate=cost(0, 4 * n * width),
        name="mark",
    )(q, a, b)


def plane_kernel(own, left, right, far, far_other, out_ref):
    half, rows = far.shape[0], out_ref.shape[0]
    total = far[half - rows :].astype(F32) + far_other[half - rows :].astype(F32)
    for ref in (own, left, right):
        for end in (half, 2 * half):
            total = total + ref[end - rows : end].astype(F32)
    out_ref[...] = total.astype(BF16)


def plane_counts(queries):
    return pl.pallas_call(
        plane_kernel,
        out_shape=jax.ShapeDtypeStruct((16, queries[0].shape[1]), BF16),
        compiler_params=params(8),
        cost_estimate=cost(0, 4096),
        name="plane_counts",
    )(*queries)


def join_kernel(a_ref, b_ref, out_ref):
    rows = a_ref.shape[0]
    out_ref[:rows] = a_ref[...]
    out_ref[rows:] = b_ref[...]


def join(a, b):
    n, width = a.shape
    return pl.pallas_call(
        join_kernel,
        out_shape=jax.ShapeDtypeStruct((2 * n, width), BF16),
        compiler_params=params(8),
        cost_estimate=cost(0, 8 * n * width),
        name="join",
    )(a, b)


def halves_kernel(left_ref, right_ref, own_ref, other_ref):
    half = own_ref.shape[0]
    own_ref[...] = left_ref[:half]
    other_ref[...] = right_ref[half:]


def halves(left, right):
    n, width = left.shape
    out = jax.ShapeDtypeStruct((n // 2, width), BF16)
    return pl.pallas_call(
        halves_kernel,
        out_shape=[out, out],
        compiler_params=params(8),
        cost_estimate=cost(0, 4 * n * width),
        name="halves",
    )(left, right)


def join_kernel(a_ref, b_ref, out_ref):
    rows = a_ref.shape[0]
    out_ref[:rows] = a_ref[...]
    out_ref[rows:] = b_ref[...]


def join(a, b):
    n, width = a.shape
    return pl.pallas_call(
        join_kernel,
        out_shape=jax.ShapeDtypeStruct((2 * n, width), BF16),
        compiler_params=params(8),
        cost_estimate=cost(0, 8 * n * width),
        name="join",
    )(a, b)


RING = ((0, 0), (0, 1), (1, 0), (1, 1), (3, 0), (3, 1), (2, 0), (2, 1))


def place_of_device():
    return lax.axis_index("y"), lax.axis_index("z"), lax.axis_index("xl")


def columns_of(pieces):
    return [s[:, at : at + HS] for s in pieces for at in range(0, s.shape[1], HS)]


def attend_heads(qs, pieces, prior, score, value):
    heads = len(qs)
    pending = [score(0, qs[0], j) for j in range(pieces)]
    results = []
    for h in range(heads):
        top = jnp.max(functools.reduce(jnp.maximum, columns_of(pending)), axis=1, keepdims=True)
        if prior is not None:
            top = jnp.maximum(top, prior[h])
        following = []
        both = None
        for j in range(pieces):
            term = jnp.dot(
                jnp.exp2((pending[j] - top).astype(BF16)),
                value(h, j),
                preferred_element_type=F32,
            )
            both = term if both is None else both + term
            if h + 1 < heads:
                following.append(score(h + 1, qs[h + 1], j))
        pending = following
        results.append((top, both[:, HS:], both[:, :HS]))
    return results


def with_ones(v):
    return jnp.concatenate([v, jnp.ones_like(v)], axis=1)


def owner_of(back, other):
    y, z, xl = place_of_device()
    return (y + 4 - back) % 4, z, (1 - xl if other else xl)


TILES = (((0, 0), (0, 1), (1, 0), (1, 1)), ((3, 0), (4, 0), (2, 0), (2, 1)))


def fill_tile(q_tile, queries, tile):
    rows = q_tile.shape[0] // 4
    for b, (ref, half) in enumerate(TILES[tile]):
        at = half * (queries[ref].shape[0] // 2)
        q_tile[b * rows : (b + 1) * rows] = queries[ref][at : at + rows]


def span_kernel(tile, slots, slope_ref, *refs):
    queries, packs = refs[:5], refs[5:13]
    acc_ref, stat_ref, q_tile, bias = refs[13:]
    y, z, xl = place_of_device()
    count, width = q_tile.shape
    rows, heads = count // 4, width // HS
    fill_tile(q_tile, queries, tile)
    place = lax.broadcasted_iota(jnp.int32, (1, rows), 1)
    for j, (back, other) in enumerate(RING):
        yj, zj, side = owner_of(back, other)
        spot = (place + (yj * 16 + zj * 2 + side) * rows).astype(F32)
        for h in range(heads):
            bias[h : h + 1, j * rows : (j + 1) * rows] = jnp.where(
                yj <= y, slope_ref[h] * LOG2E * spot, NEG
            )
    row = lax.broadcasted_iota(jnp.int32, (count, 1), 0)
    part = row // rows
    row_z = ((z + 8 - 4 * tile - 2 * (part // 2)) % 8) ^ (part % 2)
    row_pos = (y * 16 + xl + 2 * row_z) * rows + row % rows

    def score(h, q, j):
        cols = slice(h * HS, (h + 1) * HS)
        s = dot_t(q, packs[j][2 * slots : 2 * slots + rows, cols])
        s = s + bias[h : h + 1, j * rows : (j + 1) * rows]
        back, other = RING[j]
        if back == 0:
            yj, zj, side = owner_of(back, other)
            s = jnp.where(place + (yj * 16 + zj * 2 + side) * rows <= row_pos, s, NEG)
        return s

    def value(h, j):
        return with_ones(packs[j][2 * slots + rows :, h * HS : (h + 1) * HS])

    lane = lax.broadcasted_iota(jnp.int32, (count, HS), 1)
    packed = jnp.zeros((count, HS), F32)
    qs = [q_tile[:, h * HS : (h + 1) * HS] for h in range(heads)]
    for h, (top, total, acc) in enumerate(attend_heads(qs, len(RING), None, score, value)):
        acc_ref[:, h * HS : (h + 1) * HS] = acc
        packed = jnp.where(lane == h, top, packed)
        packed = jnp.where(lane == heads + h, total, packed)
    stat_ref[...] = packed


def span_attend(tile, slopes, queries, packs, slots):
    width = queries[0].shape[1]
    rows = packs[0].shape[0] // 2 - slots
    count, nk = 4 * rows, len(RING) * rows
    vmem = pl.BlockSpec(memory_space=VMEM)
    return pl.pallas_call(
        functools.partial(span_kernel, tile, slots),
        in_specs=[pl.BlockSpec(memory_space=SMEM)] + [vmem] * 13,
        out_specs=[vmem, vmem],
        out_shape=[
            jax.ShapeDtypeStruct((count, width), F32),
            jax.ShapeDtypeStruct((count, HS), F32),
        ],
        scratch_shapes=[VMEM((count, width), BF16), VMEM((8, nk), F32)],
        compiler_params=params(32),
        cost_estimate=cost(4 * count * nk * width, 4 * nk * width, 2 * count * nk),
        name="span_attend",
    )(slopes, *queries, *packs)


def cache_kernel(slots, slope_ref, *refs):
    queries, packs, tables, states = refs[:5], refs[5:13], refs[13:15], refs[15:19]
    out_ref, q_tile, acc_tile, stat_tile, bias = refs[19:]
    tile = pl.program_id(0)
    y, z, xl = place_of_device()
    count, width = q_tile.shape
    rows, heads = count // 4, width // HS
    for t in range(2):

        @pl.when(tile == t)
        def _(t=t):
            fill_tile(q_tile, queries, t)
            acc_tile[...] = states[2 * t][...]
            stat_tile[...] = states[2 * t + 1][...]

    @pl.when(tile == 0)
    def _():
        table = (tables[0][...].astype(F32) + tables[1][...].astype(F32))[:1]
        lane = lax.broadcasted_iota(jnp.int32, table.shape, 1)
        everything = jnp.sum(table, axis=1, keepdims=True)
        slot = lax.broadcasted_iota(jnp.int32, (1, slots), 1).astype(F32)
        for j, (back, other) in enumerate(RING):
            yj, zj, side = owner_of(back, other)
            ctx = yj * 16 + zj * 2 + side
            live = jnp.sum(jnp.where(lane == ctx, table, 0.0), axis=1, keepdims=True)
            start = jnp.sum(jnp.where(lane < ctx, table, 0.0), axis=1, keepdims=True) - everything
            for h in range(heads):
                bias[h : h + 1, j * slots : (j + 1) * slots] = jnp.where(
                    slot < live, slope_ref[h] * LOG2E * (slot + start), NEG
                )

    def score(h, q, j):
        s = dot_t(q, packs[j][:slots, h * HS : (h + 1) * HS])
        return s + bias[h : h + 1, j * slots : (j + 1) * slots]

    def value(h, j):
        return with_ones(packs[j][slots : 2 * slots, h * HS : (h + 1) * HS])

    lane = lax.broadcasted_iota(jnp.int32, (count, HS), 1)
    packed = jnp.zeros((count, HS), F32)
    qs = [q_tile[:, h * HS : (h + 1) * HS] for h in range(heads)]
    prior = [stat_tile[:, h : h + 1] for h in range(heads)]
    done = []
    for h, (top, total, acc) in enumerate(attend_heads(qs, len(RING), prior, score, value)):
        fade = jnp.exp2(prior[h] - top)
        total = total + fade * stat_tile[:, heads + h : heads + h + 1]
        acc = acc + fade * acc_tile[:, h * HS : (h + 1) * HS]
        done.append((acc / total).astype(BF16))
        for k, piece in enumerate(three_parts(top + jnp.log2(total))):
            packed = jnp.where(lane == 3 * h + k, piece, packed)
    both = jnp.concatenate(done, axis=1)
    odd = z % 2 == 1
    for pair in range(2):
        a, b = 2 * pair * rows, (2 * pair + 1) * rows
        end = b + rows
        blocks = []
        for own, level in (
            (jnp.where(odd, both[b:end], both[a:b]), jnp.where(odd, packed[b:end], packed[a:b])),
            (jnp.where(odd, both[a:b], both[b:end]), jnp.where(odd, packed[a:b], packed[b:end])),
        ):
            turned = jnp.transpose(level)[:16]
            tail = jnp.concatenate([turned, jnp.zeros_like(turned)], axis=1).astype(BF16)
            blocks.append((own, tail))
        for p in range(4):

            @pl.when((z // 2 + 4 - 2 * tile - pair) % 4 == p)
            def _(p=p, blocks=blocks):
                for i, (own, tail) in enumerate(blocks):
                    out_ref[2 * p + i, :rows] = own
                    out_ref[2 * p + i, rows:] = tail


def cache_attend(slopes, queries, packs, tables, states, slots):
    width = queries[0].shape[1]
    rows = packs[0].shape[0] // 2 - slots
    count, nk = 4 * rows, len(RING) * slots
    whole = lambda a: pl.BlockSpec(a.shape, lambda i: (0,) * a.ndim)
    operands = (*queries, *packs, *tables, *states)
    out = jax.ShapeDtypeStruct((8, rows + 16, width), BF16)
    return pl.pallas_call(
        functools.partial(cache_kernel, slots),
        grid=(2,),
        in_specs=[pl.BlockSpec(memory_space=SMEM)] + [whole(a) for a in operands],
        out_specs=whole(out),
        out_shape=out,
        scratch_shapes=[
            VMEM((count, width), BF16),
            VMEM((count, width), F32),
            VMEM((count, HS), F32),
            VMEM((8, nk), F32),
        ],
        compiler_params=params(44),
        cost_estimate=cost(8 * count * nk * width, 4 * nk * width, 4 * count * nk),
        name="cache_attend",
    )(slopes, *operands)


def merge_kernel(heads, parts_ref, out_ref):
    sources, padded, width = parts_ref.shape
    rows = padded - 16
    levels = jnp.concatenate(
        [parts_ref[s, rows:, :HS].astype(F32) for s in range(sources)], axis=0
    )
    turned = jnp.transpose(levels)
    for h in range(heads):
        cols = slice(h * HS, (h + 1) * HS)
        level = []
        for s in range(sources):
            at = s * 16 + 3 * h
            level.append(
                (turned[:, at : at + 1] + turned[:, at + 1 : at + 2]) + turned[:, at + 2 : at + 3]
            )
        top = functools.reduce(jnp.maximum, level)
        total = jnp.zeros((rows, 1), F32)
        acc = jnp.zeros((rows, HS), F32)
        for s in range(sources):
            weight = jnp.exp2(level[s] - top)
            total = total + weight
            acc = acc + weight * parts_ref[s, :rows, cols].astype(F32)
        out_ref[:, cols] = (acc / total).astype(BF16)


def merge(parts):
    sources, padded, width = parts.shape
    rows = padded - 16
    return pl.pallas_call(
        functools.partial(merge_kernel, width // HS),
        out_shape=jax.ShapeDtypeStruct((rows, width), BF16),
        compiler_params=params(16),
        cost_estimate=cost(4 * sources * rows * width, 2 * sources * padded * width),
        name="merge",
    )(parts)


def product_kernel(
    tok_hbm, a_ref, b_ref, wa_hbm, wb_hbm, sum_ref, term_ref, rim_ref, tok, wa, wb, sems
):
    chunks = wa.shape[0]
    cols = wa.shape[2]
    copies = []
    for c in range(chunks):
        at = pl.ds(c * cols, cols)
        copies.append(
            [
                pltpu.make_async_copy(src.at[:, at], dst.at[c], sems.at[i, c])
                for i, (src, dst) in enumerate(((wa_hbm, wa), (wb_hbm, wb), (tok_hbm, tok)))
            ]
        )
    for group in copies:
        for copy in group:
            copy.start()
    for c, group in enumerate(copies):
        for copy in group:
            copy.wait()
        at = slice(c * cols, (c + 1) * cols)
        term = jnp.dot(a_ref[...], wa[c], preferred_element_type=F32) + jnp.dot(
            b_ref[...], wb[c], preferred_element_type=F32
        )
        total = tok[c].astype(F32) + term
        sum_ref[:, at] = total
        term_ref[:, at] = term.astype(BF16)
        rim_ref[:16, at] = total[-16:].astype(BF16)
        rim_ref[16:, at] = term[-16:].astype(BF16)


def layer_product(tokens, atts, weights):
    rows, d = tokens.shape
    chunks = 4
    inner = weights[0].shape[0]
    hbm = pl.BlockSpec(memory_space=HBM)
    vmem = pl.BlockSpec(memory_space=VMEM)
    return pl.pallas_call(
        product_kernel,
        in_specs=[hbm, vmem, vmem, hbm, hbm],
        out_specs=[vmem] * 3,
        out_shape=[
            jax.ShapeDtypeStruct((rows, d), F32),
            jax.ShapeDtypeStruct((rows, d), BF16),
            jax.ShapeDtypeStruct((32, d), BF16),
        ],
        scratch_shapes=[
            VMEM((chunks, rows, d // chunks), BF16),
            VMEM((chunks, inner, d // chunks), BF16),
            VMEM((chunks, inner, d // chunks), BF16),
            pltpu.SemaphoreType.DMA((3, chunks)),
        ],
        compiler_params=params(16),
        cost_estimate=cost(4 * rows * d * inner, 4 * inner * d),
        name="layer_product",
    )(tokens, *atts, *weights)


def short_project_kernel(
    sum_ref, term_ref, rim_a, rim_b, w_ref, cols_ref, q_ref, kv_ref, normed
):
    step = pl.program_id(0)
    rows, d = sum_ref.shape
    groups = rows // GROUP
    rim_rows = 16
    width = w_ref.shape[2]

    @pl.when(step == 0)
    def _():
        layer = (sum_ref[...] + term_ref[...].astype(F32)).astype(BF16)
        part = d // 4
        tp = lax.axis_index("tp")
        mine = layer[:, :part]
        for t in range(1, 4):
            mine = jnp.where(tp == t, layer[:, t * part : (t + 1) * part], mine)
        cols_ref[...] = mine
        rim = (rim_a[:rim_rows].astype(F32) + rim_b[rim_rows:].astype(F32)).astype(BF16)
        g = lax.broadcasted_iota(jnp.int32, (groups, rows), 0) * GROUP
        t = lax.broadcasted_iota(jnp.int32, (groups, rows), 1)
        own = jnp.where((t <= g) & (t > g - GROUP), 1.0 / GROUP, 0.0).astype(BF16)
        g = lax.broadcasted_iota(jnp.int32, (groups, rim_rows), 0) * GROUP
        t = lax.broadcasted_iota(jnp.int32, (groups, rim_rows), 1) - rim_rows
        before = jnp.where(t > g - GROUP, 1.0 / GROUP, 0.0).astype(BF16)
        pooled = jnp.dot(own, layer, preferred_element_type=F32) + jnp.dot(
            before, rim, preferred_element_type=F32
        )
        normed[...] = rms_scaled(pooled.astype(BF16).astype(F32))

    out = jnp.dot(normed[...], w_ref[0], preferred_element_type=F32)

    @pl.when(step == 0)
    def _():
        scaled = (out * SCALE2).astype(BF16)
        for c in range(q_ref.shape[0]):
            q_ref[c] = scaled

    @pl.when(step == 1)
    def _():
        kv_ref[:, :width] = out.astype(BF16)

    @pl.when(step == 2)
    def _():
        kv_ref[:, width:] = out.astype(BF16)


def short_project(total, term, rims, weight3, copies):
    n, d = total.shape
    groups = n // GROUP
    width = weight3.shape[2]
    whole = lambda shape: pl.BlockSpec(shape, lambda i: (0,) * len(shape))
    shapes = [(n, d // 4), (copies, groups, width), (groups, 2 * width)]
    return pl.pallas_call(
        short_project_kernel,
        grid=(3,),
        in_specs=[whole((n, d)), whole((n, d)), whole((32, d)), whole((32, d))]
        + [pl.BlockSpec((1, d, width), lambda i: (i, 0, 0))],
        out_specs=[whole(s) for s in shapes],
        out_shape=[jax.ShapeDtypeStruct(s, BF16) for s in shapes],
        scratch_shapes=[VMEM((groups, d), BF16)],
        compiler_params=params(16),
        cost_estimate=cost(6 * groups * d * width, 2 * (n * d + 3 * d * width)),
        name="short_project",
    )(total, term, *rims, weight3)


def short_attend_kernel(slope_ref, q_ref, *refs):
    key_refs, out_ref = refs[:4], refs[4]
    y, z, xl = place_of_device()
    blocks, groups, padded = out_ref.shape
    width = padded - HS
    heads = width // HS
    n = blocks * groups
    row = lax.broadcasted_iota(jnp.int32, (n, 1), 0)
    row_pos = (y * 16 + xl + 2 * (row // groups)) * groups + row % groups
    key = lax.broadcasted_iota(jnp.int32, (1, n), 1)
    ys = (y + 4 - key // (2 * groups)) % 4
    side = jnp.where((key // groups) % 2 == 1, 1 - xl, xl)
    key_pos = (ys * 16 + z * 2 + side) * groups + key % groups
    usable = key_pos <= row_pos
    spot = key_pos.astype(F32)
    lane = lax.broadcasted_iota(jnp.int32, (n, HS), 1)
    packed = jnp.zeros((n, HS), F32)
    outs = []
    for h in range(heads):
        cols = slice(h * HS, (h + 1) * HS)
        cols_v = slice(width + h * HS, width + (h + 1) * HS)
        q = q_ref[:, :, cols].reshape(n, HS)
        k = jnp.concatenate([r[:, cols] for r in key_refs], axis=0)
        v = jnp.concatenate([r[:, cols_v] for r in key_refs], axis=0)
        s = dot_t(q, k) + (slope_ref[h] * LOG2E) * spot
        s = jnp.where(usable, s, NEG)
        top = jnp.max(s, axis=1, keepdims=True)
        p = jnp.exp2(s - top).astype(BF16)
        both = jnp.dot(p, with_ones(v), preferred_element_type=F32)
        weight_total = both[:, HS:]
        outs.append((both[:, :HS] / weight_total).astype(BF16))
        level = top + jnp.log2(weight_total)
        for k, piece in enumerate(three_parts(level)):
            packed = jnp.where(lane == 3 * h + k, piece, packed)
    out = jnp.concatenate(outs + [packed.astype(BF16)], axis=1)
    out_ref[...] = out.reshape(out_ref.shape)


def short_attend(slopes, queries, keys):
    blocks, groups, width = queries.shape
    n = blocks * groups
    smem = pl.BlockSpec(memory_space=SMEM)
    vmem = pl.BlockSpec(memory_space=VMEM)
    return pl.pallas_call(
        short_attend_kernel,
        in_specs=[smem] + [vmem] * 5,
        out_specs=vmem,
        out_shape=jax.ShapeDtypeStruct((blocks, groups, width + HS), BF16),
        compiler_params=params(16),
        cost_estimate=cost(4 * n * n * width, 8 * n * width),
        name="short_attend",
    )(slopes, queries, *keys)


def short_merge_kernel(heads, parts_ref, w_ref, *outs):
    sources, rows, padded = parts_ref.shape
    width = padded - HS
    merged = []
    for h in range(heads):
        cols = slice(h * HS, (h + 1) * HS)
        level = []
        for s in range(sources):
            lev = parts_ref[s, :, width:].astype(F32)
            level.append(
                (lev[:, 3 * h : 3 * h + 1] + lev[:, 3 * h + 1 : 3 * h + 2])
                + lev[:, 3 * h + 2 : 3 * h + 3]
            )
        top = functools.reduce(jnp.maximum, level)
        total = jnp.zeros((rows, 1), F32)
        acc = jnp.zeros((rows, HS), F32)
        for s in range(sources):
            weight = jnp.exp2(level[s] - top)
            total = total + weight
            acc = acc + weight * parts_ref[s, :, cols].astype(F32)
        merged.append((acc / total).astype(BF16))
    att = jnp.concatenate(merged, axis=1)
    cols = outs[0].shape[1]
    terms = [
        jnp.dot(
            att, w_ref[:, t * cols : (t + 1) * cols], preferred_element_type=F32
        ).astype(BF16)
        for t in range(4)
    ]
    tp = lax.axis_index("tp")
    for flip, out in enumerate(outs):
        chosen = terms[flip]
        for t in range(1, 4):
            chosen = jnp.where(tp == t, terms[t ^ flip], chosen)
        out[...] = chosen


def short_merge(parts, weight):
    sources, rows, padded = parts.shape
    width = padded - HS
    cols = weight.shape[1] // 4
    out = jax.ShapeDtypeStruct((rows, cols), BF16)
    return pl.pallas_call(
        functools.partial(short_merge_kernel, width // HS),
        out_shape=[out] * 4,
        compiler_params=params(16),
        cost_estimate=cost(8 * rows * width * cols, 8 * width * cols),
        name="short_merge",
    )(parts, weight)


def final_kernel(lay_ref, *refs):
    terms, out_ref = refs[:-1], refs[-1]
    rows, groups = lay_ref.shape[0], terms[0].shape[0]
    t = lax.broadcasted_iota(jnp.int32, (rows, groups), 0) // GROUP
    g = lax.broadcasted_iota(jnp.int32, (rows, groups), 1)
    spread = jnp.where(t == g, 1.0, 0.0).astype(BF16)
    branch = jnp.zeros(lay_ref.shape, F32)
    for term in terms:
        branch = branch + jnp.dot(spread, term[...], preferred_element_type=F32)
    out_ref[...] = (lay_ref[...].astype(F32) + branch).astype(BF16)


def final_sum(layer, terms):
    rows, cols = layer.shape
    groups = terms[0].shape[0]
    return pl.pallas_call(
        final_kernel,
        out_shape=jax.ShapeDtypeStruct((rows, cols), BF16),
        compiler_params=params(16),
        cost_estimate=cost(8 * rows * cols * groups, 4 * rows * cols),
        name="final_sum",
    )(layer, *terms)


def exchange(blocks, axis):
    return lax.all_to_all(blocks, axis, 0, 0)


def swap(x, axis, flip=1):
    return lax.ppermute(x, axis, [(i, i ^ flip) for i in range(lax.axis_size(axis))])


def moved(x, axis, by):
    n = lax.axis_size(axis)
    return lax.ppermute(x, axis, [(i, (i + by) % n) for i in range(n)])


def both_ways(x, axis, by):
    return moved(x, axis, by), moved(x, axis, -by)


def after(x, *others):
    return lax.optimization_barrier((x, *others))[0]


def on_device(
    tokens,
    project_weight,
    output_weight,
    distance_slope,
    cache_keys,
    cache_values,
    cache_count,
    short_project_weight,
    short_output,
    short_slope,
):
    axes = ("y", "z", "xl", "tp")
    slots = cache_keys.shape[0]
    nz = lax.axis_size("z")
    count = own_count(cache_count, cache_keys.shape[1])
    other_count = swap(count, "xl")
    q, pack = project(
        tokens, jnp.transpose(project_weight, (1, 0, 2)), cache_keys, cache_values
    )
    q, pack, other_count = lax.optimization_barrier((q, pack, other_count))
    marked = mark(q, count, other_count)
    left, right = both_ways(pack, "y", 1)
    other, left, right, mate = lax.optimization_barrier(
        (swap(pack, "xl"), left, right, swap(marked, "z"))
    )
    pair = join(marked, mate)
    left_other, right_other = both_ways(other, "y", 1)
    left_pair, right_pair = both_ways(pair, "z", 2)
    left_other, right_other, left_pair, right_pair, left = lax.optimization_barrier(
        (left_other, right_other, left_pair, right_pair, left)
    )
    far, far_other = moved(left, "y", 1), moved(right_other, "y", -1)
    near = halves(left_pair, right_pair)
    queries = [pair, left_pair, right_pair, moved(near[0], "z", 2), moved(near[1], "z", -2)]
    crossed = swap(after(output_weight, other), "tp", 2)
    packs = [pack, other, left, left_other, right, right_other, far, far_other]
    plane = plane_counts(queries)
    beside = swap(plane, "y")
    first = span_attend(0, distance_slope, queries, packs, slots)
    plane, beside, first = lax.optimization_barrier((plane, beside, first))
    line = added(plane, beside)
    beyond = swap(line, "y", 2)
    second = span_attend(1, distance_slope, queries, packs, slots)
    second, beyond = lax.optimization_barrier((second, beyond))
    parts = cache_attend(
        distance_slope, queries, packs, (line, beyond), (*first, *second), slots
    )
    parts, crossed = lax.optimization_barrier((parts, crossed))

    att = merge(exchange(parts, "z"))
    total, term, rim = layer_product(
        tokens, (att, swap(att, "tp", 2)), (output_weight, crossed)
    )
    n, tp = lax.axis_size(axes), lax.axis_size("tp")
    ahead = [(i, i + tp) for i in range(n - tp)]
    rims = [
        lax.ppermute(rim, axes, ahead),
        lax.ppermute(rim, axes, [(i, j ^ 1) for i, j in ahead]),
    ]
    layer, sq, skv = short_project(
        total,
        swap(term, "tp", 1),
        rims,
        jnp.transpose(short_project_weight, (1, 0, 2)),
        nz,
    )
    mate = swap(skv, "xl")
    sq, mate = lax.optimization_barrier((sq, mate))
    pair = join(skv, mate)
    keys = [pair] + [moved(pair, "y", by) for by in (1, 2, 3)]
    sparts = short_attend(short_slope, exchange(sq, "z"), keys)
    terms = short_merge(exchange(sparts, "z"), short_output)
    terms = [swap(t, "tp", flip) if flip else t for flip, t in enumerate(terms)]
    return final_sum(layer, terms)


def solution(mesh):
    split = Mesh(mesh.devices.reshape(4, 8, 2, 4), ("y", "z", "xl", "tp"))
    ctx = ("y", "z", "xl")
    return jax.shard_map(
        on_device,
        mesh=split,
        in_specs=(
            P(ctx, None),
            P(None, None, "tp"),
            P("tp", None),
            P("tp"),
            P(ctx, "tp"),
            P(ctx, "tp"),
            P(ctx),
            P(None, None, "tp"),
            P("tp", None),
            P("tp"),
        ),
        out_specs=P(ctx, "tp"),
        check_vma=False,
    )
```

```python
import functools
import math

import jax
import jax.numpy as jnp
from jax import lax
from jax.experimental import pallas as pl
from jax.experimental.pallas import tpu as pltpu
from jax.sharding import Mesh, PartitionSpec as P

HS = 128
GROUP = 4
HALO = 16
NEG = -1e30
LOG2E = math.log2(math.e)
SCALE2 = HS ** -0.5 * LOG2E

VMEM = pltpu.VMEM
SMEM = pltpu.SMEM
HBM = pltpu.HBM
F32 = jnp.float32
BF16 = jnp.bfloat16


def cost(flops, moved, trans=0):
    return pl.CostEstimate(flops=flops, bytes_accessed=moved, transcendentals=trans)


def params(mib):
    return pltpu.CompilerParams(vmem_limit_bytes=mib * 1024 * 1024)


def rms_scaled(values):
    inv = lax.rsqrt(jnp.mean(values * values, axis=-1, keepdims=True) + 1e-06)
    return (values * inv).astype(BF16)


def dot_t(a, b):
    return lax.dot_general(a, b, (((1,), (1,)), ((), ())), preferred_element_type=F32)


def three_parts(x):
    hi = x.astype(BF16).astype(F32)
    mid = (x - hi).astype(BF16).astype(F32)
    lo = (x - hi - mid).astype(BF16).astype(F32)
    return hi, mid, lo


def project_kernel(
    tok_hbm, w_hbm, ck_hbm, cv_hbm, q_ref, pack_ref, tok, weight, sems
):
    rows = tok.shape[0]
    slots = ck_hbm.shape[0]
    copies = [pltpu.make_async_copy(tok_hbm, tok, sems.at[0])]
    copies += [
        pltpu.make_async_copy(w_hbm.at[i], weight.at[i], sems.at[1 + i]) for i in range(3)
    ]
    copies += [
        pltpu.make_async_copy(ck_hbm, pack_ref.at[:slots], sems.at[4]),
        pltpu.make_async_copy(cv_hbm, pack_ref.at[slots : 2 * slots], sems.at[5]),
    ]
    for copy in copies:
        copy.start()
    copies[0].wait()
    normed = rms_scaled(tok[...].astype(F32))
    for i in range(3):
        copies[1 + i].wait()
        out = jnp.dot(normed, weight[i], preferred_element_type=F32)
        if i == 0:
            q_ref[...] = (out * SCALE2).astype(BF16)
        else:
            at = 2 * slots + (i - 1) * rows
            pack_ref[at : at + rows] = out.astype(BF16)
    copies[4].wait()
    copies[5].wait()


def project(rows, weight3, cache_keys, cache_values):
    n, d = rows.shape
    width = weight3.shape[2]
    total = 2 * (n + cache_keys.shape[0])
    hbm = pl.BlockSpec(memory_space=HBM)
    vmem = pl.BlockSpec(memory_space=VMEM)
    return pl.pallas_call(
        project_kernel,
        in_specs=[hbm] * 4,
        out_specs=[vmem, vmem],
        out_shape=[
            jax.ShapeDtypeStruct((n, width), BF16),
            jax.ShapeDtypeStruct((total, width), BF16),
        ],
        scratch_shapes=[
            VMEM((n, d), BF16),
            VMEM(weight3.shape, BF16),
            pltpu.SemaphoreType.DMA((6,)),
        ],
        compiler_params=params(60),
        cost_estimate=cost(6 * n * d * width, 2 * (n * d + 3 * d * width)),
        name="project",
    )(rows, weight3, cache_keys, cache_values)


def table_kernel(count_ref, out_ref):
    y, z, xl = place_of_device()
    lane = lax.broadcasted_iota(jnp.int32, out_ref.shape, 1)
    out_ref[...] = jnp.where(lane == y * 16 + z * 2 + xl, count_ref[0], 0).astype(F32).astype(BF16)


def own_count(count, width):
    return pl.pallas_call(
        table_kernel,
        in_specs=[pl.BlockSpec(memory_space=SMEM)],
        out_shape=jax.ShapeDtypeStruct((16, width), BF16),
        compiler_params=params(8),
        cost_estimate=cost(0, 32 * width),
        name="own_count",
    )(count)


def add_kernel(a_ref, b_ref, out_ref):
    out_ref[...] = (a_ref[...].astype(F32) + b_ref[...].astype(F32)).astype(BF16)


def added(a, b):
    return pl.pallas_call(
        add_kernel,
        out_shape=jax.ShapeDtypeStruct(a.shape, a.dtype),
        compiler_params=params(8),
        cost_estimate=cost(a.size, 6 * a.size),
        name="added",
    )(a, b)


def mark_kernel(halo_hbm, w_hbm, q_hbm, a_hbm, b_hbm, out_ref, halo, weight, a, b, sems):
    rows = q_hbm.shape[0]
    copies = [
        pltpu.make_async_copy(src, dst, sems.at[i])
        for i, (src, dst) in enumerate(
            (
                (halo_hbm, halo),
                (w_hbm.at[0], weight),
                (q_hbm, out_ref.at[:rows]),
                (a_hbm, a),
                (b_hbm, b),
            )
        )
    ]
    for copy in copies:
        copy.start()
    for copy in copies:
        copy.wait()
    normed = rms_scaled(halo[...].astype(F32))
    out = jnp.dot(normed, weight[...], preferred_element_type=F32)
    out_ref[rows : rows + HALO] = (out * SCALE2).astype(BF16)
    out_ref[rows + HALO :] = (a[...].astype(F32) + b[...].astype(F32)).astype(BF16)


def mark(halo, weight3, q, a, b):
    n, width = q.shape
    d = halo.shape[1]
    hbm = pl.BlockSpec(memory_space=HBM)
    return pl.pallas_call(
        mark_kernel,
        in_specs=[hbm] * 5,
        out_specs=pl.BlockSpec(memory_space=VMEM),
        out_shape=jax.ShapeDtypeStruct((n + HALO + a.shape[0], width), BF16),
        scratch_shapes=[
            VMEM(halo.shape, BF16),
            VMEM((d, width), BF16),
            VMEM(a.shape, BF16),
            VMEM(b.shape, BF16),
            pltpu.SemaphoreType.DMA((5,)),
        ],
        compiler_params=params(60),
        cost_estimate=cost(2 * HALO * d * width, 2 * d * width),
        name="mark",
    )(halo, weight3, q, a, b)


def plane_kernel(own, left, right, far, far_other, out_ref):
    half, rows = far.shape[0], out_ref.shape[0]
    total = far[half - rows :].astype(F32) + far_other[half - rows :].astype(F32)
    for ref in (own, left, right):
        for end in (half, 2 * half):
            total = total + ref[end - rows : end].astype(F32)
    out_ref[...] = total.astype(BF16)


def plane_counts(queries):
    return pl.pallas_call(
        plane_kernel,
        out_shape=jax.ShapeDtypeStruct((16, queries[0].shape[1]), BF16),
        compiler_params=params(8),
        cost_estimate=cost(0, 4096),
        name="plane_counts",
    )(*queries)


def join_kernel(a_ref, b_ref, out_ref):
    rows = a_ref.shape[0]
    out_ref[:rows] = a_ref[...]
    out_ref[rows:] = b_ref[...]


def join(a, b):
    n, width = a.shape
    return pl.pallas_call(
        join_kernel,
        out_shape=jax.ShapeDtypeStruct((2 * n, width), BF16),
        compiler_params=params(8),
        cost_estimate=cost(0, 8 * n * width),
        name="join",
    )(a, b)


def halves_kernel(left_ref, right_ref, own_ref, other_ref):
    half = own_ref.shape[0]
    own_ref[...] = left_ref[:half]
    other_ref[...] = right_ref[half:]


def halves(left, right):
    n, width = left.shape
    out = jax.ShapeDtypeStruct((n // 2, width), BF16)
    return pl.pallas_call(
        halves_kernel,
        out_shape=[out, out],
        compiler_params=params(8),
        cost_estimate=cost(0, 4 * n * width),
        name="halves",
    )(left, right)


def join_kernel(a_ref, b_ref, out_ref):
    rows = a_ref.shape[0]
    out_ref[:rows] = a_ref[...]
    out_ref[rows:] = b_ref[...]


def join(a, b):
    n, width = a.shape
    return pl.pallas_call(
        join_kernel,
        out_shape=jax.ShapeDtypeStruct((2 * n, width), BF16),
        compiler_params=params(8),
        cost_estimate=cost(0, 8 * n * width),
        name="join",
    )(a, b)


RING = ((0, 0), (0, 1), (1, 0), (1, 1), (3, 0), (3, 1), (2, 0), (2, 1))


def place_of_device():
    return lax.axis_index("y"), lax.axis_index("z"), lax.axis_index("xl")


def columns_of(pieces):
    return [s[:, at : at + HS] for s in pieces for at in range(0, s.shape[1], HS)]


def attend_heads(qs, pieces, prior, score, value):
    heads = len(qs)
    pending = [score(0, qs[0], j) for j in range(pieces)]
    results = []
    for h in range(heads):
        top = jnp.max(functools.reduce(jnp.maximum, columns_of(pending)), axis=1, keepdims=True)
        if prior is not None:
            top = jnp.maximum(top, prior[h])
        following = []
        both = None
        for j in range(pieces):
            term = jnp.dot(
                jnp.exp2(pending[j] - top).astype(BF16), value(h, j), preferred_element_type=F32
            )
            both = term if both is None else both + term
            if h + 1 < heads:
                following.append(score(h + 1, qs[h + 1], j))
        pending = following
        results.append((top, both[:, HS:], both[:, :HS]))
    return results


def with_ones(v):
    return jnp.concatenate([v, jnp.ones_like(v)], axis=1)


def owner_of(back, other):
    y, z, xl = place_of_device()
    return (y + 4 - back) % 4, z, (1 - xl if other else xl)


TILES = (((0, 0), (0, 1), (1, 0), (1, 1)), ((3, 0), (4, 0), (2, 0), (2, 1)))


def fill_tile(q_tile, queries, tile):
    rows = q_tile.shape[0] // 4
    for b, (ref, half) in enumerate(TILES[tile]):
        at = half * (rows + 16)
        q_tile[b * rows : (b + 1) * rows] = queries[ref][at : at + rows]


def span_kernel(tile, slots, slope_ref, *refs):
    queries, packs = refs[:5], refs[5:13]
    acc_ref, stat_ref, q_tile, bias = refs[13:]
    y, z, xl = place_of_device()
    count, width = q_tile.shape
    block, heads = count // 4, width // HS
    rows = block - HALO
    fill_tile(q_tile, queries, tile)
    place = lax.broadcasted_iota(jnp.int32, (1, rows), 1)
    for j, (back, other) in enumerate(RING):
        yj, zj, side = owner_of(back, other)
        spot = (place + (yj * 16 + zj * 2 + side) * rows).astype(F32)
        for h in range(heads):
            bias[h : h + 1, j * rows : (j + 1) * rows] = jnp.where(
                yj <= y, slope_ref[h] * LOG2E * spot, NEG
            )
    row = lax.broadcasted_iota(jnp.int32, (count, 1), 0)
    row_pos = jnp.zeros((count, 1), jnp.int32)
    for part in range(4):
        row_z = ((z + 8 - 4 * tile - 2 * (part // 2)) % 8) ^ (part % 2)
        first = (y * 16 + xl + 2 * row_z) * rows
        at = row - part * block
        at = jnp.where(at < rows, at, at - block)
        row_pos = jnp.where(row >= part * block, first + at, row_pos)

    def score(h, q, j):
        cols = slice(h * HS, (h + 1) * HS)
        s = dot_t(q, packs[j][2 * slots : 2 * slots + rows, cols])
        s = s + bias[h : h + 1, j * rows : (j + 1) * rows]
        back, other = RING[j]
        if back <= 1:
            yj, zj, side = owner_of(back, other)
            s = jnp.where(place + (yj * 16 + zj * 2 + side) * rows <= row_pos, s, NEG)
        return s

    def value(h, j):
        return with_ones(packs[j][2 * slots + rows :, h * HS : (h + 1) * HS])

    lane = lax.broadcasted_iota(jnp.int32, (count, HS), 1)
    packed = jnp.zeros((count, HS), F32)
    qs = [q_tile[:, h * HS : (h + 1) * HS] for h in range(heads)]
    for h, (top, total, acc) in enumerate(attend_heads(qs, len(RING), None, score, value)):
        acc_ref[:, h * HS : (h + 1) * HS] = acc
        packed = jnp.where(lane == h, top, packed)
        packed = jnp.where(lane == heads + h, total, packed)
    stat_ref[...] = packed


def span_attend(tile, slopes, queries, packs, slots):
    width = queries[0].shape[1]
    rows = packs[0].shape[0] // 2 - slots
    count, nk = 4 * (rows + HALO), len(RING) * rows
    vmem = pl.BlockSpec(memory_space=VMEM)
    return pl.pallas_call(
        functools.partial(span_kernel, tile, slots),
        in_specs=[pl.BlockSpec(memory_space=SMEM)] + [vmem] * 13,
        out_specs=[vmem, vmem],
        out_shape=[
            jax.ShapeDtypeStruct((count, width), F32),
            jax.ShapeDtypeStruct((count, HS), F32),
        ],
        scratch_shapes=[VMEM((count, width), BF16), VMEM((8, nk), F32)],
        compiler_params=params(32),
        cost_estimate=cost(4 * count * nk * width, 4 * nk * width, 2 * count * nk),
        name="span_attend",
    )(slopes, *queries, *packs)


def cache_kernel(slots, slope_ref, *refs):
    queries, packs, tables, states = refs[:5], refs[5:13], refs[13:15], refs[15:19]
    out_ref, q_tile, acc_tile, stat_tile, bias = refs[19:]
    tile = pl.program_id(0)
    y, z, xl = place_of_device()
    count, width = q_tile.shape
    block, heads = count // 4, width // HS
    rows = block - HALO
    for t in range(2):

        @pl.when(tile == t)
        def _(t=t):
            fill_tile(q_tile, queries, t)
            acc_tile[...] = states[2 * t][...]
            stat_tile[...] = states[2 * t + 1][...]

    @pl.when(tile == 0)
    def _():
        table = (tables[0][...].astype(F32) + tables[1][...].astype(F32))[:1]
        lane = lax.broadcasted_iota(jnp.int32, table.shape, 1)
        everything = jnp.sum(table, axis=1, keepdims=True)
        slot = lax.broadcasted_iota(jnp.int32, (1, slots), 1).astype(F32)
        for j, (back, other) in enumerate(RING):
            yj, zj, side = owner_of(back, other)
            ctx = yj * 16 + zj * 2 + side
            live = jnp.sum(jnp.where(lane == ctx, table, 0.0), axis=1, keepdims=True)
            start = jnp.sum(jnp.where(lane < ctx, table, 0.0), axis=1, keepdims=True) - everything
            for h in range(heads):
                bias[h : h + 1, j * slots : (j + 1) * slots] = jnp.where(
                    slot < live, slope_ref[h] * LOG2E * (slot + start), NEG
                )

    def score(h, q, j):
        s = dot_t(q, packs[j][:slots, h * HS : (h + 1) * HS])
        return s + bias[h : h + 1, j * slots : (j + 1) * slots]

    def value(h, j):
        return with_ones(packs[j][slots : 2 * slots, h * HS : (h + 1) * HS])

    lane = lax.broadcasted_iota(jnp.int32, (count, HS), 1)
    packed = jnp.zeros((count, HS), F32)
    qs = [q_tile[:, h * HS : (h + 1) * HS] for h in range(heads)]
    prior = [stat_tile[:, h : h + 1] for h in range(heads)]
    done = []
    for h, (top, total, acc) in enumerate(attend_heads(qs, len(RING), prior, score, value)):
        fade = jnp.exp2(prior[h] - top)
        total = total + fade * stat_tile[:, heads + h : heads + h + 1]
        acc = acc + fade * acc_tile[:, h * HS : (h + 1) * HS]
        done.append((acc / total).astype(BF16))
        for k, piece in enumerate(three_parts(top + jnp.log2(total))):
            packed = jnp.where(lane == 3 * h + k, piece, packed)
    both = jnp.concatenate(done, axis=1)
    odd = z % 2 == 1
    for pair in range(2):
        a, b = 2 * pair * block, (2 * pair + 1) * block
        end = b + block
        blocks = []
        for own, level in (
            (jnp.where(odd, both[b:end], both[a:b]), jnp.where(odd, packed[b:end], packed[a:b])),
            (jnp.where(odd, both[a:b], both[b:end]), jnp.where(odd, packed[a:b], packed[b:end])),
        ):
            ahead = jnp.concatenate(
                [level[rows:], jnp.zeros((HS - HALO, HS), F32)], axis=0
            )
            tail = [jnp.transpose(level[:rows])[:16], jnp.transpose(ahead)[:16]]
            blocks.append((own, jnp.concatenate(tail, axis=1).astype(BF16)))
        for p in range(4):

            @pl.when((z // 2 + 4 - 2 * tile - pair) % 4 == p)
            def _(p=p, blocks=blocks):
                for i, (own, tail) in enumerate(blocks):
                    out_ref[2 * p + i, :block] = own
                    out_ref[2 * p + i, block:] = tail


def cache_attend(slopes, queries, packs, tables, states, slots):
    width = queries[0].shape[1]
    rows = packs[0].shape[0] // 2 - slots + HALO
    count, nk = 4 * rows, len(RING) * slots
    whole = lambda a: pl.BlockSpec(a.shape, lambda i: (0,) * a.ndim)
    operands = (*queries, *packs, *tables, *states)
    out = jax.ShapeDtypeStruct((8, rows + 16, width), BF16)
    return pl.pallas_call(
        functools.partial(cache_kernel, slots),
        grid=(2,),
        in_specs=[pl.BlockSpec(memory_space=SMEM)] + [whole(a) for a in operands],
        out_specs=whole(out),
        out_shape=out,
        scratch_shapes=[
            VMEM((count, width), BF16),
            VMEM((count, width), F32),
            VMEM((count, HS), F32),
            VMEM((8, nk), F32),
        ],
        compiler_params=params(44),
        cost_estimate=cost(8 * count * nk * width, 4 * nk * width, 4 * count * nk),
        name="cache_attend",
    )(slopes, *operands)


def merge_kernel(heads, parts_ref, out_ref):
    sources, padded, width = parts_ref.shape
    rows = padded - 16
    levels = [
        jnp.concatenate(
            [parts_ref[s, rows:, cols].astype(F32) for s in range(sources)], axis=0
        )
        for cols in (slice(0, HS), slice(HS, 2 * HS))
    ]
    turned = jnp.concatenate(
        [jnp.transpose(levels[0]), jnp.transpose(levels[1])[: rows - HS]], axis=0
    )
    for h in range(heads):
        cols = slice(h * HS, (h + 1) * HS)
        level = []
        for s in range(sources):
            at = s * 16 + 3 * h
            level.append(
                (turned[:, at : at + 1] + turned[:, at + 1 : at + 2]) + turned[:, at + 2 : at + 3]
            )
        top = functools.reduce(jnp.maximum, level)
        total = jnp.zeros((rows, 1), F32)
        acc = jnp.zeros((rows, HS), F32)
        for s in range(sources):
            weight = jnp.exp2(level[s] - top)
            total = total + weight
            acc = acc + weight * parts_ref[s, :rows, cols].astype(F32)
        out_ref[:, cols] = (acc / total).astype(BF16)


def merge(parts):
    sources, padded, width = parts.shape
    rows = padded - 16
    return pl.pallas_call(
        functools.partial(merge_kernel, width // HS),
        out_shape=jax.ShapeDtypeStruct((rows, width), BF16),
        compiler_params=params(16),
        cost_estimate=cost(4 * sources * rows * width, 2 * sources * padded * width),
        name="merge",
    )(parts)


def product_kernel(
    tok_hbm, halo_hbm, a_ref, b_ref, wa_hbm, wb_hbm, sum_ref, term_ref, tok, wa, wb, sems
):
    chunks = wa.shape[0]
    cols = wa.shape[2]
    copies = []
    for c in range(chunks):
        at = pl.ds(c * cols, cols)
        copies.append(
            [
                pltpu.make_async_copy(src.at[:, at], dst.at[c], sems.at[i, c])
                for i, (src, dst) in enumerate(((wa_hbm, wa), (wb_hbm, wb)))
            ]
        )
        rows = tok_hbm.shape[0]
        for i, (src, to) in enumerate(
            ((tok_hbm, pl.ds(0, rows)), (halo_hbm, pl.ds(rows, HALO)))
        ):
            copies[-1].append(
                pltpu.make_async_copy(src.at[:, at], tok.at[c, to], sems.at[2 + i, c])
            )
    for group in copies:
        for copy in group:
            copy.start()
    for c, group in enumerate(copies):
        for copy in group:
            copy.wait()
        at = slice(c * cols, (c + 1) * cols)
        term = jnp.dot(a_ref[...], wa[c], preferred_element_type=F32) + jnp.dot(
            b_ref[...], wb[c], preferred_element_type=F32
        )
        total = tok[c].astype(F32) + term
        sum_ref[:, at] = total
        term_ref[:, at] = term.astype(BF16)


def layer_product(tokens, halo, atts, weights):
    rows, d = tokens.shape[0] + HALO, tokens.shape[1]
    chunks = 4
    inner = weights[0].shape[0]
    hbm = pl.BlockSpec(memory_space=HBM)
    vmem = pl.BlockSpec(memory_space=VMEM)
    return pl.pallas_call(
        product_kernel,
        in_specs=[hbm, hbm, vmem, vmem, hbm, hbm],
        out_specs=[vmem] * 2,
        out_shape=[
            jax.ShapeDtypeStruct((rows, d), F32),
            jax.ShapeDtypeStruct((rows, d), BF16),
        ],
        scratch_shapes=[
            VMEM((chunks, rows, d // chunks), BF16),
            VMEM((chunks, inner, d // chunks), BF16),
            VMEM((chunks, inner, d // chunks), BF16),
            pltpu.SemaphoreType.DMA((4, chunks)),
        ],
        compiler_params=params(16),
        cost_estimate=cost(4 * rows * d * inner, 4 * inner * d),
        name="layer_product",
    )(tokens, halo, *atts, *weights)


def short_project_kernel(
    sum_ref, term_ref, w_ref, cols_ref, q_ref, kv_ref, normed
):
    step = pl.program_id(0)
    rows, d = sum_ref.shape[0] - HALO, sum_ref.shape[1]
    groups = rows // GROUP
    width = w_ref.shape[2]

    @pl.when(step == 0)
    def _():
        layer = (sum_ref[...] + term_ref[...].astype(F32)).astype(BF16)
        y, z, xl = place_of_device()
        rim = jnp.where(y * 16 + z * 2 + xl > 0, layer[rows:], jnp.zeros((HALO, d), BF16))
        layer = layer[:rows]
        part = d // 4
        tp = lax.axis_index("tp")
        mine = layer[:, :part]
        for t in range(1, 4):
            mine = jnp.where(tp == t, layer[:, t * part : (t + 1) * part], mine)
        cols_ref[...] = mine
        g = lax.broadcasted_iota(jnp.int32, (groups, rows), 0) * GROUP
        t = lax.broadcasted_iota(jnp.int32, (groups, rows), 1)
        own = jnp.where((t <= g) & (t > g - GROUP), 1.0 / GROUP, 0.0).astype(BF16)
        g = lax.broadcasted_iota(jnp.int32, (groups, HALO), 0) * GROUP
        t = lax.broadcasted_iota(jnp.int32, (groups, HALO), 1) - HALO
        before = jnp.where(t > g - GROUP, 1.0 / GROUP, 0.0).astype(BF16)
        pooled = jnp.dot(own, layer, preferred_element_type=F32) + jnp.dot(
            before, rim, preferred_element_type=F32
        )
        normed[...] = rms_scaled(pooled.astype(BF16).astype(F32))

    out = jnp.dot(normed[...], w_ref[0], preferred_element_type=F32)

    @pl.when(step == 0)
    def _():
        scaled = (out * SCALE2).astype(BF16)
        for c in range(q_ref.shape[0]):
            q_ref[c] = scaled

    @pl.when(step == 1)
    def _():
        kv_ref[:, :width] = out.astype(BF16)

    @pl.when(step == 2)
    def _():
        kv_ref[:, width:] = out.astype(BF16)


def short_project(total, term, weight3, copies):
    n, d = total.shape[0] - HALO, total.shape[1]
    groups = n // GROUP
    width = weight3.shape[2]
    whole = lambda shape: pl.BlockSpec(shape, lambda i: (0,) * len(shape))
    shapes = [(n, d // 4), (copies, groups, width), (groups, 2 * width)]
    return pl.pallas_call(
        short_project_kernel,
        grid=(3,),
        in_specs=[whole(total.shape), whole(term.shape)]
        + [pl.BlockSpec((1, d, width), lambda i: (i, 0, 0))],
        out_specs=[whole(s) for s in shapes],
        out_shape=[jax.ShapeDtypeStruct(s, BF16) for s in shapes],
        scratch_shapes=[VMEM((groups, d), BF16)],
        compiler_params=params(16),
        cost_estimate=cost(6 * groups * d * width, 2 * (n * d + 3 * d * width)),
        name="short_project",
    )(total, term, weight3)


def short_attend_kernel(slope_ref, q_ref, *refs):
    key_refs, out_ref = refs[:4], refs[4]
    y, z, xl = place_of_device()
    blocks, groups, padded = out_ref.shape
    width = padded - HS
    heads = width // HS
    n = blocks * groups
    row = lax.broadcasted_iota(jnp.int32, (n, 1), 0)
    row_pos = (y * 16 + xl + 2 * (row // groups)) * groups + row % groups
    key = lax.broadcasted_iota(jnp.int32, (1, n), 1)
    ys = (y + 4 - key // (2 * groups)) % 4
    side = jnp.where((key // groups) % 2 == 1, 1 - xl, xl)
    key_pos = (ys * 16 + z * 2 + side) * groups + key % groups
    usable = key_pos <= row_pos
    spot = key_pos.astype(F32)
    lane = lax.broadcasted_iota(jnp.int32, (n, HS), 1)
    packed = jnp.zeros((n, HS), F32)
    outs = []
    for h in range(heads):
        cols = slice(h * HS, (h + 1) * HS)
        cols_v = slice(width + h * HS, width + (h + 1) * HS)
        q = q_ref[:, :, cols].reshape(n, HS)
        k = jnp.concatenate([r[:, cols] for r in key_refs], axis=0)
        v = jnp.concatenate([r[:, cols_v] for r in key_refs], axis=0)
        s = dot_t(q, k) + (slope_ref[h] * LOG2E) * spot
        s = jnp.where(usable, s, NEG)
        top = jnp.max(s, axis=1, keepdims=True)
        p = jnp.exp2(s - top).astype(BF16)
        both = jnp.dot(p, with_ones(v), preferred_element_type=F32)
        weight_total = both[:, HS:]
        outs.append((both[:, :HS] / weight_total).astype(BF16))
        level = top + jnp.log2(weight_total)
        for k, piece in enumerate(three_parts(level)):
            packed = jnp.where(lane == 3 * h + k, piece, packed)
    out = jnp.concatenate(outs + [packed.astype(BF16)], axis=1)
    out_ref[...] = out.reshape(out_ref.shape)


def short_attend(slopes, queries, keys):
    blocks, groups, width = queries.shape
    n = blocks * groups
    smem = pl.BlockSpec(memory_space=SMEM)
    vmem = pl.BlockSpec(memory_space=VMEM)
    return pl.pallas_call(
        short_attend_kernel,
        in_specs=[smem] + [vmem] * 5,
        out_specs=vmem,
        out_shape=jax.ShapeDtypeStruct((blocks, groups, width + HS), BF16),
        compiler_params=params(16),
        cost_estimate=cost(4 * n * n * width, 8 * n * width),
        name="short_attend",
    )(slopes, queries, *keys)


def short_merge_kernel(heads, parts_ref, w_ref, *outs):
    sources, rows, padded = parts_ref.shape
    width = padded - HS
    merged = []
    for h in range(heads):
        cols = slice(h * HS, (h + 1) * HS)
        level = []
        for s in range(sources):
            lev = parts_ref[s, :, width:].astype(F32)
            level.append(
                (lev[:, 3 * h : 3 * h + 1] + lev[:, 3 * h + 1 : 3 * h + 2])
                + lev[:, 3 * h + 2 : 3 * h + 3]
            )
        top = functools.reduce(jnp.maximum, level)
        total = jnp.zeros((rows, 1), F32)
        acc = jnp.zeros((rows, HS), F32)
        for s in range(sources):
            weight = jnp.exp2(level[s] - top)
            total = total + weight
            acc = acc + weight * parts_ref[s, :, cols].astype(F32)
        merged.append((acc / total).astype(BF16))
    att = jnp.concatenate(merged, axis=1)
    cols = outs[0].shape[1]
    terms = [
        jnp.dot(
            att, w_ref[:, t * cols : (t + 1) * cols], preferred_element_type=F32
        ).astype(BF16)
        for t in range(4)
    ]
    tp = lax.axis_index("tp")
    for flip, out in enumerate(outs):
        chosen = terms[flip]
        for t in range(1, 4):
            chosen = jnp.where(tp == t, terms[t ^ flip], chosen)
        out[...] = chosen


def short_merge(parts, weight):
    sources, rows, padded = parts.shape
    width = padded - HS
    cols = weight.shape[1] // 4
    out = jax.ShapeDtypeStruct((rows, cols), BF16)
    return pl.pallas_call(
        functools.partial(short_merge_kernel, width // HS),
        out_shape=[out] * 4,
        compiler_params=params(16),
        cost_estimate=cost(8 * rows * width * cols, 8 * width * cols),
        name="short_merge",
    )(parts, weight)


def final_kernel(lay_ref, *refs):
    terms, out_ref = refs[:-1], refs[-1]
    rows, groups = lay_ref.shape[0], terms[0].shape[0]
    t = lax.broadcasted_iota(jnp.int32, (rows, groups), 0) // GROUP
    g = lax.broadcasted_iota(jnp.int32, (rows, groups), 1)
    spread = jnp.where(t == g, 1.0, 0.0).astype(BF16)
    branch = jnp.zeros(lay_ref.shape, F32)
    for term in terms:
        branch = branch + jnp.dot(spread, term[...], preferred_element_type=F32)
    out_ref[...] = (lay_ref[...].astype(F32) + branch).astype(BF16)


def final_sum(layer, terms):
    rows, cols = layer.shape
    groups = terms[0].shape[0]
    return pl.pallas_call(
        final_kernel,
        out_shape=jax.ShapeDtypeStruct((rows, cols), BF16),
        compiler_params=params(16),
        cost_estimate=cost(8 * rows * cols * groups, 4 * rows * cols),
        name="final_sum",
    )(layer, *terms)


def exchange(blocks, axis):
    return lax.all_to_all(blocks, axis, 0, 0)


def swap(x, axis, flip=1):
    return lax.ppermute(x, axis, [(i, i ^ flip) for i in range(lax.axis_size(axis))])


def moved(x, axis, by):
    n = lax.axis_size(axis)
    return lax.ppermute(x, axis, [(i, (i + by) % n) for i in range(n)])


def both_ways(x, axis, by):
    return moved(x, axis, by), moved(x, axis, -by)


def after(x, *others):
    return lax.optimization_barrier((x, *others))[0]


def on_device(
    tokens,
    project_weight,
    output_weight,
    distance_slope,
    cache_keys,
    cache_values,
    cache_count,
    short_project_weight,
    short_output,
    short_slope,
):
    axes = ("y", "z", "xl", "tp")
    slots = cache_keys.shape[0]
    nz = lax.axis_size("z")
    count = own_count(cache_count, cache_keys.shape[1])
    other_count = swap(count, "xl")
    n, tp = lax.axis_size(axes), lax.axis_size("tp")
    halo = lax.ppermute(tokens[-HALO:], axes, [(i, i + tp) for i in range(n - tp)])
    weight3 = jnp.transpose(project_weight, (1, 0, 2))
    q, pack = project(tokens, weight3, cache_keys, cache_values)
    q, pack, other_count, halo = lax.optimization_barrier((q, pack, other_count, halo))
    marked = mark(halo, weight3, q, count, other_count)
    marked, pack = lax.optimization_barrier((marked, pack))
    left, right = both_ways(pack, "y", 1)
    other, left, right, mate = lax.optimization_barrier(
        (swap(pack, "xl"), left, right, swap(marked, "z"))
    )
    pair = join(marked, mate)
    left_other, right_other = both_ways(other, "y", 1)
    left_pair, right_pair = both_ways(pair, "z", 2)
    left_other, right_other, left_pair, right_pair, left = lax.optimization_barrier(
        (left_other, right_other, left_pair, right_pair, left)
    )
    far, far_other = moved(left, "y", 1), moved(right_other, "y", -1)
    near = halves(left_pair, right_pair)
    queries = [pair, left_pair, right_pair, moved(near[0], "z", 2), moved(near[1], "z", -2)]
    crossed = swap(after(output_weight, other), "tp", 2)
    packs = [pack, other, left, left_other, right, right_other, far, far_other]
    plane = plane_counts(queries)
    beside = swap(plane, "y")
    first = span_attend(0, distance_slope, queries, packs, slots)
    plane, beside, first = lax.optimization_barrier((plane, beside, first))
    line = added(plane, beside)
    beyond = swap(line, "y", 2)
    second = span_attend(1, distance_slope, queries, packs, slots)
    second, beyond = lax.optimization_barrier((second, beyond))
    parts = cache_attend(
        distance_slope, queries, packs, (line, beyond), (*first, *second), slots
    )
    parts, crossed = lax.optimization_barrier((parts, crossed))

    att = merge(exchange(parts, "z"))
    total, term = layer_product(
        tokens, halo, (att, swap(att, "tp", 2)), (output_weight, crossed)
    )
    layer, sq, skv = short_project(
        total,
        swap(term, "tp", 1),
        jnp.transpose(short_project_weight, (1, 0, 2)),
        nz,
    )
    mate = swap(skv, "xl")
    sq, mate = lax.optimization_barrier((sq, mate))
    pair = join(skv, mate)
    keys = [pair] + [moved(pair, "y", by) for by in (1, 2, 3)]
    sparts = short_attend(short_slope, exchange(sq, "z"), keys)
    terms = short_merge(exchange(sparts, "z"), short_output)
    terms = [swap(t, "tp", flip) if flip else t for flip, t in enumerate(terms)]
    return final_sum(layer, terms)


def solution(mesh):
    split = Mesh(mesh.devices.reshape(4, 8, 2, 4), ("y", "z", "xl", "tp"))
    ctx = ("y", "z", "xl")
    return jax.shard_map(
        on_device,
        mesh=split,
        in_specs=(
            P(ctx, None),
            P(None, None, "tp"),
            P("tp", None),
            P("tp"),
            P(ctx, "tp"),
            P(ctx, "tp"),
            P(ctx),
            P(None, None, "tp"),
            P("tp", None),
            P("tp"),
        ),
        out_specs=P(ctx, "tp"),
        check_vma=False,
    )
```

```python
import functools
import math

import jax
import jax.numpy as jnp
from jax import lax
from jax.experimental import pallas as pl
from jax.experimental.pallas import tpu as pltpu
from jax.sharding import Mesh, PartitionSpec as P

HS = 128
GROUP = 4
HALO = 16
NEG = -1e30
LOG2E = math.log2(math.e)
SCALE2 = HS ** -0.5 * LOG2E

VMEM = pltpu.VMEM
SMEM = pltpu.SMEM
HBM = pltpu.HBM
F32 = jnp.float32
BF16 = jnp.bfloat16


def cost(flops, moved, trans=0):
    return pl.CostEstimate(flops=flops, bytes_accessed=moved, transcendentals=trans)


def params(mib):
    return pltpu.CompilerParams(vmem_limit_bytes=mib * 1024 * 1024)


def rms_scaled(values):
    inv = lax.rsqrt(jnp.mean(values * values, axis=-1, keepdims=True) + 1e-06)
    return (values * inv).astype(BF16)


def dot_t(a, b):
    return lax.dot_general(a, b, (((1,), (1,)), ((), ())), preferred_element_type=F32)


def three_parts(x):
    hi = x.astype(BF16).astype(F32)
    mid = (x - hi).astype(BF16).astype(F32)
    lo = (x - hi - mid).astype(BF16).astype(F32)
    return hi, mid, lo


def project_kernel(
    tok_hbm, w_hbm, ck_hbm, cv_hbm, q_ref, pack_ref, tok, weight, sems
):
    rows = tok.shape[0]
    slots = ck_hbm.shape[0]
    copies = [pltpu.make_async_copy(tok_hbm, tok, sems.at[0])]
    copies += [
        pltpu.make_async_copy(w_hbm.at[i], weight.at[i], sems.at[1 + i]) for i in range(3)
    ]
    copies += [
        pltpu.make_async_copy(ck_hbm, pack_ref.at[:slots], sems.at[4]),
        pltpu.make_async_copy(cv_hbm, pack_ref.at[slots : 2 * slots], sems.at[5]),
    ]
    for copy in copies:
        copy.start()
    copies[0].wait()
    normed = rms_scaled(tok[...].astype(F32))
    for i in range(3):
        copies[1 + i].wait()
        out = jnp.dot(normed, weight[i], preferred_element_type=F32)
        if i == 0:
            q_ref[...] = (out * SCALE2).astype(BF16)
        else:
            at = 2 * slots + (i - 1) * rows
            pack_ref[at : at + rows] = out.astype(BF16)
    copies[4].wait()
    copies[5].wait()


def project(rows, weight3, cache_keys, cache_values):
    n, d = rows.shape
    width = weight3.shape[2]
    total = 2 * (n + cache_keys.shape[0])
    hbm = pl.BlockSpec(memory_space=HBM)
    vmem = pl.BlockSpec(memory_space=VMEM)
    return pl.pallas_call(
        project_kernel,
        in_specs=[hbm] * 4,
        out_specs=[vmem, vmem],
        out_shape=[
            jax.ShapeDtypeStruct((n, width), BF16),
            jax.ShapeDtypeStruct((total, width), BF16),
        ],
        scratch_shapes=[
            VMEM((n, d), BF16),
            VMEM(weight3.shape, BF16),
            pltpu.SemaphoreType.DMA((6,)),
        ],
        compiler_params=params(60),
        cost_estimate=cost(6 * n * d * width, 2 * (n * d + 3 * d * width)),
        name="project",
    )(rows, weight3, cache_keys, cache_values)


def table_kernel(count_ref, out_ref):
    y, z, xl = place_of_device()
    lane = lax.broadcasted_iota(jnp.int32, out_ref.shape, 1)
    out_ref[...] = jnp.where(lane == y * 16 + z * 2 + xl, count_ref[0], 0).astype(F32).astype(BF16)


def own_count(count, width):
    return pl.pallas_call(
        table_kernel,
        in_specs=[pl.BlockSpec(memory_space=SMEM)],
        out_shape=jax.ShapeDtypeStruct((16, width), BF16),
        compiler_params=params(8),
        cost_estimate=cost(0, 32 * width),
        name="own_count",
    )(count)


def add_kernel(a_ref, b_ref, out_ref):
    out_ref[...] = (a_ref[...].astype(F32) + b_ref[...].astype(F32)).astype(BF16)


def added(a, b):
    return pl.pallas_call(
        add_kernel,
        out_shape=jax.ShapeDtypeStruct(a.shape, a.dtype),
        compiler_params=params(8),
        cost_estimate=cost(a.size, 6 * a.size),
        name="added",
    )(a, b)


def mark_kernel(halo_hbm, w_hbm, q_hbm, a_hbm, b_hbm, out_ref, halo, weight, a, b, sems):
    rows = q_hbm.shape[0]
    copies = [
        pltpu.make_async_copy(src, dst, sems.at[i])
        for i, (src, dst) in enumerate(
            (
                (halo_hbm, halo),
                (w_hbm.at[0], weight),
                (q_hbm, out_ref.at[:rows]),
                (a_hbm, a),
                (b_hbm, b),
            )
        )
    ]
    for copy in copies:
        copy.start()
    for copy in copies:
        copy.wait()
    normed = rms_scaled(halo[...].astype(F32))
    out = jnp.dot(normed, weight[...], preferred_element_type=F32)
    out_ref[rows : rows + HALO] = (out * SCALE2).astype(BF16)
    out_ref[rows + HALO :] = (a[...].astype(F32) + b[...].astype(F32)).astype(BF16)


def mark(halo, weight3, q, a, b):
    n, width = q.shape
    d = halo.shape[1]
    hbm = pl.BlockSpec(memory_space=HBM)
    return pl.pallas_call(
        mark_kernel,
        in_specs=[hbm] * 5,
        out_specs=pl.BlockSpec(memory_space=VMEM),
        out_shape=jax.ShapeDtypeStruct((n + HALO + a.shape[0], width), BF16),
        scratch_shapes=[
            VMEM(halo.shape, BF16),
            VMEM((d, width), BF16),
            VMEM(a.shape, BF16),
            VMEM(b.shape, BF16),
            pltpu.SemaphoreType.DMA((5,)),
        ],
        compiler_params=params(60),
        cost_estimate=cost(2 * HALO * d * width, 2 * d * width),
        name="mark",
    )(halo, weight3, q, a, b)


def plane_kernel(own, left, right, far, far_other, out_ref):
    half, rows = far.shape[0], out_ref.shape[0]
    total = far[half - rows :].astype(F32) + far_other[half - rows :].astype(F32)
    for ref in (own, left, right):
        for end in (half, 2 * half):
            total = total + ref[end - rows : end].astype(F32)
    out_ref[...] = total.astype(BF16)


def plane_counts(queries):
    return pl.pallas_call(
        plane_kernel,
        out_shape=jax.ShapeDtypeStruct((16, queries[0].shape[1]), BF16),
        compiler_params=params(8),
        cost_estimate=cost(0, 4096),
        name="plane_counts",
    )(*queries)


def join_kernel(a_ref, b_ref, out_ref):
    rows = a_ref.shape[0]
    out_ref[:rows] = a_ref[...]
    out_ref[rows:] = b_ref[...]


def join(a, b):
    n, width = a.shape
    return pl.pallas_call(
        join_kernel,
        out_shape=jax.ShapeDtypeStruct((2 * n, width), BF16),
        compiler_params=params(8),
        cost_estimate=cost(0, 8 * n * width),
        name="join",
    )(a, b)


def halves_kernel(left_ref, right_ref, own_ref, other_ref):
    half = own_ref.shape[0]
    own_ref[...] = left_ref[:half]
    other_ref[...] = right_ref[half:]


def halves(left, right):
    n, width = left.shape
    out = jax.ShapeDtypeStruct((n // 2, width), BF16)
    return pl.pallas_call(
        halves_kernel,
        out_shape=[out, out],
        compiler_params=params(8),
        cost_estimate=cost(0, 4 * n * width),
        name="halves",
    )(left, right)


def join_kernel(a_ref, b_ref, out_ref):
    rows = a_ref.shape[0]
    out_ref[:rows] = a_ref[...]
    out_ref[rows:] = b_ref[...]


def join(a, b):
    n, width = a.shape
    return pl.pallas_call(
        join_kernel,
        out_shape=jax.ShapeDtypeStruct((2 * n, width), BF16),
        compiler_params=params(8),
        cost_estimate=cost(0, 8 * n * width),
        name="join",
    )(a, b)


RING = ((0, 0), (0, 1), (1, 0), (1, 1), (3, 0), (3, 1), (2, 0), (2, 1))


def place_of_device():
    return lax.axis_index("y"), lax.axis_index("z"), lax.axis_index("xl")


def columns_of(pieces):
    return [s[:, at : at + HS] for s in pieces for at in range(0, s.shape[1], HS)]


def attend_heads(qs, pieces, prior, score, value):
    heads = len(qs)
    pending = [score(0, qs[0], j) for j in range(pieces)]
    results = []
    for h in range(heads):
        top = jnp.max(functools.reduce(jnp.maximum, columns_of(pending)), axis=1, keepdims=True)
        if prior is not None:
            top = jnp.maximum(top, prior[h])
        following = []
        both = None
        for j in range(pieces):
            term = jnp.dot(
                jnp.exp2(pending[j] - top).astype(BF16), value(h, j), preferred_element_type=F32
            )
            both = term if both is None else both + term
            if h + 1 < heads:
                following.append(score(h + 1, qs[h + 1], j))
        pending = following
        results.append((top, both[:, HS:], both[:, :HS]))
    return results


def with_ones(v):
    return jnp.concatenate([v, jnp.ones_like(v)], axis=1)


def owner_of(back, other):
    y, z, xl = place_of_device()
    return (y + 4 - back) % 4, z, (1 - xl if other else xl)


TILES = (((0, 0), (0, 1), (1, 0), (1, 1)), ((3, 0), (4, 0), (2, 0), (2, 1)))


def fill_tile(q_tile, queries, tile):
    rows = q_tile.shape[0] // 4
    for b, (ref, half) in enumerate(TILES[tile]):
        at = half * (rows + 16)
        q_tile[b * rows : (b + 1) * rows] = queries[ref][at : at + rows]


def span_kernel(tile, slots, slope_ref, *refs):
    queries, packs = refs[:5], refs[5:13]
    acc_ref, stat_ref, q_tile, bias = refs[13:]
    y, z, xl = place_of_device()
    count, width = q_tile.shape
    block, heads = count // 4, width // HS
    rows = block - HALO
    fill_tile(q_tile, queries, tile)
    place = lax.broadcasted_iota(jnp.int32, (1, rows), 1)
    for j, (back, other) in enumerate(RING):
        yj, zj, side = owner_of(back, other)
        spot = (place + (yj * 16 + zj * 2 + side) * rows).astype(F32)
        for h in range(heads):
            bias[h : h + 1, j * rows : (j + 1) * rows] = jnp.where(
                yj <= y, slope_ref[h] * LOG2E * spot, NEG
            )
    row = lax.broadcasted_iota(jnp.int32, (count, 1), 0)
    row_pos = jnp.zeros((count, 1), jnp.int32)
    for part in range(4):
        row_z = ((z + 8 - 4 * tile - 2 * (part // 2)) % 8) ^ (part % 2)
        first = (y * 16 + xl + 2 * row_z) * rows
        at = row - part * block
        at = jnp.where(at < rows, at, at - block)
        row_pos = jnp.where(row >= part * block, first + at, row_pos)

    def score(h, q, j):
        cols = slice(h * HS, (h + 1) * HS)
        s = dot_t(q, packs[j][2 * slots : 2 * slots + rows, cols])
        s = s + bias[h : h + 1, j * rows : (j + 1) * rows]
        back, other = RING[j]
        if back <= 1:
            yj, zj, side = owner_of(back, other)
            s = jnp.where(place + (yj * 16 + zj * 2 + side) * rows <= row_pos, s, NEG)
        return s

    def value(h, j):
        return with_ones(packs[j][2 * slots + rows :, h * HS : (h + 1) * HS])

    lane = lax.broadcasted_iota(jnp.int32, (count, HS), 1)
    packed = jnp.zeros((count, HS), F32)
    qs = [q_tile[:, h * HS : (h + 1) * HS] for h in range(heads)]
    for h, (top, total, acc) in enumerate(attend_heads(qs, len(RING), None, score, value)):
        acc_ref[:, h * HS : (h + 1) * HS] = acc
        packed = jnp.where(lane == h, top, packed)
        packed = jnp.where(lane == heads + h, total, packed)
    stat_ref[...] = packed


def span_attend(tile, slopes, queries, packs, slots):
    width = queries[0].shape[1]
    rows = packs[0].shape[0] // 2 - slots
    count, nk = 4 * (rows + HALO), len(RING) * rows
    vmem = pl.BlockSpec(memory_space=VMEM)
    return pl.pallas_call(
        functools.partial(span_kernel, tile, slots),
        in_specs=[pl.BlockSpec(memory_space=SMEM)] + [vmem] * 13,
        out_specs=[vmem, vmem],
        out_shape=[
            jax.ShapeDtypeStruct((count, width), F32),
            jax.ShapeDtypeStruct((count, HS), F32),
        ],
        scratch_shapes=[VMEM((count, width), BF16), VMEM((8, nk), F32)],
        compiler_params=params(32),
        cost_estimate=cost(4 * count * nk * width, 4 * nk * width, 2 * count * nk),
        name="span_attend",
    )(slopes, *queries, *packs)


def cache_kernel(slots, slope_ref, *refs):
    queries, packs, tables, states = refs[:5], refs[5:13], refs[13:15], refs[15:19]
    out_ref, q_tile, acc_tile, stat_tile, bias = refs[19:]
    tile = pl.program_id(0)
    y, z, xl = place_of_device()
    count, width = q_tile.shape
    block, heads = count // 4, width // HS
    rows = block - HALO
    for t in range(2):

        @pl.when(tile == t)
        def _(t=t):
            fill_tile(q_tile, queries, t)
            acc_tile[...] = states[2 * t][...]
            stat_tile[...] = states[2 * t + 1][...]

    @pl.when(tile == 0)
    def _():
        table = (tables[0][...].astype(F32) + tables[1][...].astype(F32))[:1]
        lane = lax.broadcasted_iota(jnp.int32, table.shape, 1)
        everything = jnp.sum(table, axis=1, keepdims=True)
        slot = lax.broadcasted_iota(jnp.int32, (1, slots), 1).astype(F32)
        for j, (back, other) in enumerate(RING):
            yj, zj, side = owner_of(back, other)
            ctx = yj * 16 + zj * 2 + side
            live = jnp.sum(jnp.where(lane == ctx, table, 0.0), axis=1, keepdims=True)
            start = jnp.sum(jnp.where(lane < ctx, table, 0.0), axis=1, keepdims=True) - everything
            for h in range(heads):
                bias[h : h + 1, j * slots : (j + 1) * slots] = jnp.where(
                    slot < live, slope_ref[h] * LOG2E * (slot + start), NEG
                )

    def score(h, q, j):
        s = dot_t(q, packs[j][:slots, h * HS : (h + 1) * HS])
        return s + bias[h : h + 1, j * slots : (j + 1) * slots]

    def value(h, j):
        return with_ones(packs[j][slots : 2 * slots, h * HS : (h + 1) * HS])

    lane = lax.broadcasted_iota(jnp.int32, (count, HS), 1)
    packed = jnp.zeros((count, HS), F32)
    qs = [q_tile[:, h * HS : (h + 1) * HS] for h in range(heads)]
    prior = [stat_tile[:, h : h + 1] for h in range(heads)]
    done = []
    for h, (top, total, acc) in enumerate(attend_heads(qs, len(RING), prior, score, value)):
        fade = jnp.exp2(prior[h] - top)
        total = total + fade * stat_tile[:, heads + h : heads + h + 1]
        acc = acc + fade * acc_tile[:, h * HS : (h + 1) * HS]
        done.append((acc / total).astype(BF16))
        for k, piece in enumerate(three_parts(top + jnp.log2(total))):
            packed = jnp.where(lane == 3 * h + k, piece, packed)
    both = jnp.concatenate(done, axis=1)
    odd = z % 2 == 1
    for pair in range(2):
        a, b = 2 * pair * block, (2 * pair + 1) * block
        end = b + block
        blocks = []
        for own, level in (
            (jnp.where(odd, both[b:end], both[a:b]), jnp.where(odd, packed[b:end], packed[a:b])),
            (jnp.where(odd, both[a:b], both[b:end]), jnp.where(odd, packed[a:b], packed[b:end])),
        ):
            ahead = jnp.concatenate(
                [level[rows:], jnp.zeros((HS - HALO, HS), F32)], axis=0
            )
            tail = [jnp.transpose(level[:rows])[:16], jnp.transpose(ahead)[:16]]
            blocks.append((own, jnp.concatenate(tail, axis=1).astype(BF16)))
        for p in range(4):

            @pl.when((z // 2 + 4 - 2 * tile - pair) % 4 == p)
            def _(p=p, blocks=blocks):
                for i, (own, tail) in enumerate(blocks):
                    out_ref[2 * p + i, :block] = own
                    out_ref[2 * p + i, block:] = tail


def cache_attend(slopes, queries, packs, tables, states, slots):
    width = queries[0].shape[1]
    rows = packs[0].shape[0] // 2 - slots + HALO
    count, nk = 4 * rows, len(RING) * slots
    whole = lambda a: pl.BlockSpec(a.shape, lambda i: (0,) * a.ndim)
    operands = (*queries, *packs, *tables, *states)
    out = jax.ShapeDtypeStruct((8, rows + 16, width), BF16)
    return pl.pallas_call(
        functools.partial(cache_kernel, slots),
        grid=(2,),
        in_specs=[pl.BlockSpec(memory_space=SMEM)] + [whole(a) for a in operands],
        out_specs=whole(out),
        out_shape=out,
        scratch_shapes=[
            VMEM((count, width), BF16),
            VMEM((count, width), F32),
            VMEM((count, HS), F32),
            VMEM((8, nk), F32),
        ],
        compiler_params=params(44),
        cost_estimate=cost(8 * count * nk * width, 4 * nk * width, 4 * count * nk),
        name="cache_attend",
    )(slopes, *operands)


def merge_kernel(heads, parts_ref, out_ref):
    sources, padded, width = parts_ref.shape
    rows = padded - 16
    levels = [
        jnp.concatenate(
            [parts_ref[s, rows:, cols].astype(F32) for s in range(sources)], axis=0
        )
        for cols in (slice(0, HS), slice(HS, 2 * HS))
    ]
    turned = jnp.concatenate(
        [jnp.transpose(levels[0]), jnp.transpose(levels[1])[: rows - HS]], axis=0
    )
    for h in range(heads):
        cols = slice(h * HS, (h + 1) * HS)
        level = []
        for s in range(sources):
            at = s * 16 + 3 * h
            level.append(
                (turned[:, at : at + 1] + turned[:, at + 1 : at + 2]) + turned[:, at + 2 : at + 3]
            )
        top = functools.reduce(jnp.maximum, level)
        total = jnp.zeros((rows, 1), F32)
        acc = jnp.zeros((rows, HS), F32)
        for s in range(sources):
            weight = jnp.exp2(level[s] - top)
            total = total + weight
            acc = acc + weight * parts_ref[s, :rows, cols].astype(F32)
        out_ref[:, cols] = (acc / total).astype(BF16)


def merge(parts):
    sources, padded, width = parts.shape
    rows = padded - 16
    return pl.pallas_call(
        functools.partial(merge_kernel, width // HS),
        out_shape=jax.ShapeDtypeStruct((rows, width), BF16),
        compiler_params=params(16),
        cost_estimate=cost(4 * sources * rows * width, 2 * sources * padded * width),
        name="merge",
    )(parts)


def product_kernel(
    tok_hbm, halo_hbm, a_ref, b_ref, wa_hbm, wb_hbm, sum_ref, term_ref, tok, wa, wb, sems
):
    chunks = wa.shape[0]
    cols = wa.shape[2]
    copies = []
    for c in range(chunks):
        at = pl.ds(c * cols, cols)
        copies.append(
            [
                pltpu.make_async_copy(src.at[:, at], dst.at[c], sems.at[i, c])
                for i, (src, dst) in enumerate(((wa_hbm, wa), (wb_hbm, wb)))
            ]
        )
        rows = tok_hbm.shape[0]
        for i, (src, to) in enumerate(
            ((tok_hbm, pl.ds(0, rows)), (halo_hbm, pl.ds(rows, HALO)))
        ):
            copies[-1].append(
                pltpu.make_async_copy(src.at[:, at], tok.at[c, to], sems.at[2 + i, c])
            )
    for group in copies:
        for copy in group:
            copy.start()
    for c, group in enumerate(copies):
        for copy in group:
            copy.wait()
        at = slice(c * cols, (c + 1) * cols)
        term = jnp.dot(a_ref[...], wa[c], preferred_element_type=F32) + jnp.dot(
            b_ref[...], wb[c], preferred_element_type=F32
        )
        total = tok[c].astype(F32) + term
        sum_ref[:, at] = total
        term_ref[:, at] = term.astype(BF16)


def layer_product(tokens, halo, atts, weights):
    rows, d = tokens.shape[0] + HALO, tokens.shape[1]
    chunks = 4
    inner = weights[0].shape[0]
    hbm = pl.BlockSpec(memory_space=HBM)
    vmem = pl.BlockSpec(memory_space=VMEM)
    return pl.pallas_call(
        product_kernel,
        in_specs=[hbm, hbm, vmem, vmem, hbm, hbm],
        out_specs=[vmem] * 2,
        out_shape=[
            jax.ShapeDtypeStruct((rows, d), F32),
            jax.ShapeDtypeStruct((rows, d), BF16),
        ],
        scratch_shapes=[
            VMEM((chunks, rows, d // chunks), BF16),
            VMEM((chunks, inner, d // chunks), BF16),
            VMEM((chunks, inner, d // chunks), BF16),
            pltpu.SemaphoreType.DMA((4, chunks)),
        ],
        compiler_params=params(16),
        cost_estimate=cost(4 * rows * d * inner, 4 * inner * d),
        name="layer_product",
    )(tokens, halo, *atts, *weights)


def short_project_kernel(
    sum_ref, term_ref, w_ref, cols_ref, q_ref, kv_ref, normed
):
    step = pl.program_id(0)
    rows, d = sum_ref.shape[0] - HALO, sum_ref.shape[1]
    groups = rows // GROUP
    width = w_ref.shape[2]

    @pl.when(step == 0)
    def _():
        layer = (sum_ref[...] + term_ref[...].astype(F32)).astype(BF16)
        y, z, xl = place_of_device()
        rim = jnp.where(y * 16 + z * 2 + xl > 0, layer[rows:], jnp.zeros((HALO, d), BF16))
        layer = layer[:rows]
        part = d // 4
        tp = lax.axis_index("tp")
        mine = layer[:, :part]
        for t in range(1, 4):
            mine = jnp.where(tp == t, layer[:, t * part : (t + 1) * part], mine)
        cols_ref[...] = mine
        g = lax.broadcasted_iota(jnp.int32, (groups, rows), 0) * GROUP
        t = lax.broadcasted_iota(jnp.int32, (groups, rows), 1)
        own = jnp.where((t <= g) & (t > g - GROUP), 1.0 / GROUP, 0.0).astype(BF16)
        g = lax.broadcasted_iota(jnp.int32, (groups, HALO), 0) * GROUP
        t = lax.broadcasted_iota(jnp.int32, (groups, HALO), 1) - HALO
        before = jnp.where(t > g - GROUP, 1.0 / GROUP, 0.0).astype(BF16)
        pooled = jnp.dot(own, layer, preferred_element_type=F32) + jnp.dot(
            before, rim, preferred_element_type=F32
        )
        normed[...] = rms_scaled(pooled.astype(BF16).astype(F32))

    out = jnp.dot(normed[...], w_ref[0], preferred_element_type=F32)

    @pl.when(step == 0)
    def _():
        q_ref[...] = (out * SCALE2).astype(BF16)

    @pl.when(step == 1)
    def _():
        kv_ref[:, :width] = out.astype(BF16)

    @pl.when(step == 2)
    def _():
        kv_ref[:, width:] = out.astype(BF16)


def short_project(total, term, weight3):
    n, d = total.shape[0] - HALO, total.shape[1]
    groups = n // GROUP
    width = weight3.shape[2]
    whole = lambda shape: pl.BlockSpec(shape, lambda i: (0,) * len(shape))
    shapes = [(n, d // 4), (groups, width), (groups, 2 * width)]
    return pl.pallas_call(
        short_project_kernel,
        grid=(3,),
        in_specs=[whole(total.shape), whole(term.shape)]
        + [pl.BlockSpec((1, d, width), lambda i: (i, 0, 0))],
        out_specs=[whole(s) for s in shapes],
        out_shape=[jax.ShapeDtypeStruct(s, BF16) for s in shapes],
        scratch_shapes=[VMEM((groups, d), BF16)],
        compiler_params=params(16),
        cost_estimate=cost(6 * groups * d * width, 2 * (n * d + 3 * d * width)),
        name="short_project",
    )(total, term, weight3)


def short_attend_kernel(slope_ref, *refs):
    queries, key_refs, out_ref = refs[:4], refs[4:8], refs[8]
    y, z, xl = place_of_device()
    blocks, groups, padded = out_ref.shape
    width = padded - HS
    heads = width // HS
    n = blocks * groups
    row = lax.broadcasted_iota(jnp.int32, (n, 1), 0)
    zs = row // groups
    row_pos = (y * 16 + xl + 2 * zs) * groups + row % groups
    back = (z // 2 + 4 - zs // 2) % 4
    came = (2 * back + (zs ^ z) % 2) * groups + row % groups
    order = jnp.where(lax.broadcasted_iota(jnp.int32, (n, n), 1) == came, 1.0, 0.0).astype(BF16)
    lined = jnp.concatenate([r[...] for r in queries], axis=0)
    lined = jnp.dot(order, lined, preferred_element_type=F32).astype(BF16)
    key = lax.broadcasted_iota(jnp.int32, (1, n), 1)
    ys = (y + 4 - key // (2 * groups)) % 4
    side = jnp.where((key // groups) % 2 == 1, 1 - xl, xl)
    key_pos = (ys * 16 + z * 2 + side) * groups + key % groups
    usable = key_pos <= row_pos
    spot = key_pos.astype(F32)
    lane = lax.broadcasted_iota(jnp.int32, (n, HS), 1)
    packed = jnp.zeros((n, HS), F32)
    outs = []
    for h in range(heads):
        cols = slice(h * HS, (h + 1) * HS)
        cols_v = slice(width + h * HS, width + (h + 1) * HS)
        q = lined[:, cols]
        k = jnp.concatenate([r[:, cols] for r in key_refs], axis=0)
        v = jnp.concatenate([r[:, cols_v] for r in key_refs], axis=0)
        s = dot_t(q, k) + (slope_ref[h] * LOG2E) * spot
        s = jnp.where(usable, s, NEG)
        top = jnp.max(s, axis=1, keepdims=True)
        p = jnp.exp2(s - top).astype(BF16)
        both = jnp.dot(p, with_ones(v), preferred_element_type=F32)
        weight_total = both[:, HS:]
        outs.append((both[:, :HS] / weight_total).astype(BF16))
        level = top + jnp.log2(weight_total)
        for k, piece in enumerate(three_parts(level)):
            packed = jnp.where(lane == 3 * h + k, piece, packed)
    out = jnp.concatenate(outs + [packed.astype(BF16)], axis=1)
    out_ref[...] = out.reshape(out_ref.shape)


def short_attend(slopes, queries, keys):
    blocks, groups, width = 8, queries[0].shape[0] // 2, queries[0].shape[1]
    n = blocks * groups
    smem = pl.BlockSpec(memory_space=SMEM)
    vmem = pl.BlockSpec(memory_space=VMEM)
    return pl.pallas_call(
        short_attend_kernel,
        in_specs=[smem] + [vmem] * 8,
        out_specs=vmem,
        out_shape=jax.ShapeDtypeStruct((blocks, groups, width + HS), BF16),
        compiler_params=params(16),
        cost_estimate=cost(4 * n * n * width, 8 * n * width),
        name="short_attend",
    )(slopes, *queries, *keys)


def short_merge_kernel(heads, parts_ref, w_ref, *outs):
    sources, rows, padded = parts_ref.shape
    width = padded - HS
    merged = []
    for h in range(heads):
        cols = slice(h * HS, (h + 1) * HS)
        level = []
        for s in range(sources):
            lev = parts_ref[s, :, width:].astype(F32)
            level.append(
                (lev[:, 3 * h : 3 * h + 1] + lev[:, 3 * h + 1 : 3 * h + 2])
                + lev[:, 3 * h + 2 : 3 * h + 3]
            )
        top = functools.reduce(jnp.maximum, level)
        total = jnp.zeros((rows, 1), F32)
        acc = jnp.zeros((rows, HS), F32)
        for s in range(sources):
            weight = jnp.exp2(level[s] - top)
            total = total + weight
            acc = acc + weight * parts_ref[s, :, cols].astype(F32)
        merged.append((acc / total).astype(BF16))
    att = jnp.concatenate(merged, axis=1)
    cols = outs[0].shape[1]
    terms = [
        jnp.dot(
            att, w_ref[:, t * cols : (t + 1) * cols], preferred_element_type=F32
        ).astype(BF16)
        for t in range(4)
    ]
    tp = lax.axis_index("tp")
    for flip, out in enumerate(outs):
        chosen = terms[flip]
        for t in range(1, 4):
            chosen = jnp.where(tp == t, terms[t ^ flip], chosen)
        out[...] = chosen


def short_merge(parts, weight):
    sources, rows, padded = parts.shape
    width = padded - HS
    cols = weight.shape[1] // 4
    out = jax.ShapeDtypeStruct((rows, cols), BF16)
    return pl.pallas_call(
        functools.partial(short_merge_kernel, width // HS),
        out_shape=[out] * 4,
        compiler_params=params(16),
        cost_estimate=cost(8 * rows * width * cols, 8 * width * cols),
        name="short_merge",
    )(parts, weight)


def final_kernel(lay_ref, *refs):
    terms, out_ref = refs[:-1], refs[-1]
    rows, groups = lay_ref.shape[0], terms[0].shape[0]
    t = lax.broadcasted_iota(jnp.int32, (rows, groups), 0) // GROUP
    g = lax.broadcasted_iota(jnp.int32, (rows, groups), 1)
    spread = jnp.where(t == g, 1.0, 0.0).astype(BF16)
    branch = jnp.zeros(lay_ref.shape, F32)
    for term in terms:
        branch = branch + jnp.dot(spread, term[...], preferred_element_type=F32)
    out_ref[...] = (lay_ref[...].astype(F32) + branch).astype(BF16)


def final_sum(layer, terms):
    rows, cols = layer.shape
    groups = terms[0].shape[0]
    return pl.pallas_call(
        final_kernel,
        out_shape=jax.ShapeDtypeStruct((rows, cols), BF16),
        compiler_params=params(16),
        cost_estimate=cost(8 * rows * cols * groups, 4 * rows * cols),
        name="final_sum",
    )(layer, *terms)


def exchange(blocks, axis):
    return lax.all_to_all(blocks, axis, 0, 0)


def swap(x, axis, flip=1):
    return lax.ppermute(x, axis, [(i, i ^ flip) for i in range(lax.axis_size(axis))])


def moved(x, axis, by):
    n = lax.axis_size(axis)
    return lax.ppermute(x, axis, [(i, (i + by) % n) for i in range(n)])


def both_ways(x, axis, by):
    return moved(x, axis, by), moved(x, axis, -by)


def after(x, *others):
    return lax.optimization_barrier((x, *others))[0]


def on_device(
    tokens,
    project_weight,
    output_weight,
    distance_slope,
    cache_keys,
    cache_values,
    cache_count,
    short_project_weight,
    short_output,
    short_slope,
):
    axes = ("y", "z", "xl", "tp")
    slots = cache_keys.shape[0]
    count = own_count(cache_count, cache_keys.shape[1])
    other_count = swap(count, "xl")
    n, tp = lax.axis_size(axes), lax.axis_size("tp")
    halo = lax.ppermute(tokens[-HALO:], axes, [(i, i + tp) for i in range(n - tp)])
    weight3 = jnp.transpose(project_weight, (1, 0, 2))
    q, pack = project(tokens, weight3, cache_keys, cache_values)
    q, pack, other_count, halo = lax.optimization_barrier((q, pack, other_count, halo))
    marked = mark(halo, weight3, q, count, other_count)
    marked, pack = lax.optimization_barrier((marked, pack))
    left, right = both_ways(pack, "y", 1)
    other, left, right, mate = lax.optimization_barrier(
        (swap(pack, "xl"), left, right, swap(marked, "z"))
    )
    pair = join(marked, mate)
    left_other, right_other = both_ways(other, "y", 1)
    left_pair, right_pair = both_ways(pair, "z", 2)
    left_other, right_other, left_pair, right_pair, left = lax.optimization_barrier(
        (left_other, right_other, left_pair, right_pair, left)
    )
    far, far_other = moved(left, "y", 1), moved(right_other, "y", -1)
    near = halves(left_pair, right_pair)
    queries = [pair, left_pair, right_pair, moved(near[0], "z", 2), moved(near[1], "z", -2)]
    crossed = swap(after(output_weight, left), "tp", 2)
    packs = [pack, other, left, left_other, right, right_other, far, far_other]
    plane = plane_counts(queries)
    beside = swap(plane, "y")
    first = span_attend(0, distance_slope, queries, packs, slots)
    plane, beside, first = lax.optimization_barrier((plane, beside, first))
    line = added(plane, beside)
    beyond = swap(line, "y", 2)
    second = span_attend(1, distance_slope, queries, packs, slots)
    second, beyond = lax.optimization_barrier((second, beyond))
    parts = cache_attend(
        distance_slope, queries, packs, (line, beyond), (*first, *second), slots
    )
    parts, crossed = lax.optimization_barrier((parts, crossed))

    att = merge(exchange(parts, "z"))
    total, term = layer_product(
        tokens, halo, (att, swap(att, "tp", 2)), (output_weight, crossed)
    )
    layer, sq, skv = short_project(
        total,
        swap(term, "tp", 1),
        jnp.transpose(short_project_weight, (1, 0, 2)),
    )
    pair = join(sq, swap(sq, "z"))
    queries = [pair] + [moved(pair, "z", by) for by in (2, 4, 6)]
    pair = join(skv, swap(skv, "xl"))
    keys = [pair] + [moved(pair, "y", by) for by in (1, 2, 3)]
    sparts = short_attend(short_slope, queries, keys)
    terms = short_merge(exchange(sparts, "z"), short_output)
    terms = [swap(t, "tp", flip) if flip else t for flip, t in enumerate(terms)]
    return final_sum(layer, terms)


def solution(mesh):
    split = Mesh(mesh.devices.reshape(4, 8, 2, 4), ("y", "z", "xl", "tp"))
    ctx = ("y", "z", "xl")
    return jax.shard_map(
        on_device,
        mesh=split,
        in_specs=(
            P(ctx, None),
            P(None, None, "tp"),
            P("tp", None),
            P("tp"),
            P(ctx, "tp"),
            P(ctx, "tp"),
            P(ctx),
            P(None, None, "tp"),
            P("tp", None),
            P("tp"),
        ),
        out_specs=P(ctx, "tp"),
        check_vma=False,
    )
```

```python
import functools
import math

import jax
import jax.numpy as jnp
from jax import lax
from jax.experimental import pallas as pl
from jax.experimental.pallas import tpu as pltpu
from jax.sharding import Mesh, PartitionSpec as P

HS = 128
GROUP = 4
HALO = 16
NEG = -1e30
LOG2E = math.log2(math.e)
SCALE2 = HS ** -0.5 * LOG2E

VMEM = pltpu.VMEM
SMEM = pltpu.SMEM
HBM = pltpu.HBM
F32 = jnp.float32
BF16 = jnp.bfloat16


def cost(flops, moved, trans=0):
    return pl.CostEstimate(flops=flops, bytes_accessed=moved, transcendentals=trans)


def params(mib):
    return pltpu.CompilerParams(vmem_limit_bytes=mib * 1024 * 1024)


def rms_scaled(values):
    inv = lax.rsqrt(jnp.mean(values * values, axis=-1, keepdims=True) + 1e-06)
    return (values * inv).astype(BF16)


def dot_t(a, b):
    return lax.dot_general(a, b, (((1,), (1,)), ((), ())), preferred_element_type=F32)


def three_parts(x):
    hi = x.astype(BF16).astype(F32)
    mid = (x - hi).astype(BF16).astype(F32)
    lo = (x - hi - mid).astype(BF16).astype(F32)
    return hi, mid, lo


def project_kernel(
    tok_hbm, w_hbm, ck_hbm, cv_hbm, q_ref, pack_ref, tok, weight, sems
):
    rows = tok.shape[0]
    slots = ck_hbm.shape[0]
    copies = [pltpu.make_async_copy(tok_hbm, tok, sems.at[0])]
    copies += [
        pltpu.make_async_copy(w_hbm.at[i], weight.at[i], sems.at[1 + i]) for i in range(3)
    ]
    copies += [
        pltpu.make_async_copy(ck_hbm, pack_ref.at[:slots], sems.at[4]),
        pltpu.make_async_copy(cv_hbm, pack_ref.at[slots : 2 * slots], sems.at[5]),
    ]
    for copy in copies:
        copy.start()
    copies[0].wait()
    normed = rms_scaled(tok[...].astype(F32))
    for i in range(3):
        copies[1 + i].wait()
        out = jnp.dot(normed, weight[i], preferred_element_type=F32)
        if i == 0:
            q_ref[...] = (out * SCALE2).astype(BF16)
        else:
            at = 2 * slots + (i - 1) * rows
            pack_ref[at : at + rows] = out.astype(BF16)
    copies[4].wait()
    copies[5].wait()


def project(rows, weight3, cache_keys, cache_values):
    n, d = rows.shape
    width = weight3.shape[2]
    total = 2 * (n + cache_keys.shape[0])
    hbm = pl.BlockSpec(memory_space=HBM)
    vmem = pl.BlockSpec(memory_space=VMEM)
    return pl.pallas_call(
        project_kernel,
        in_specs=[hbm] * 4,
        out_specs=[vmem, vmem],
        out_shape=[
            jax.ShapeDtypeStruct((n, width), BF16),
            jax.ShapeDtypeStruct((total, width), BF16),
        ],
        scratch_shapes=[
            VMEM((n, d), BF16),
            VMEM(weight3.shape, BF16),
            pltpu.SemaphoreType.DMA((6,)),
        ],
        compiler_params=params(60),
        cost_estimate=cost(6 * n * d * width, 2 * (n * d + 3 * d * width)),
        name="project",
    )(rows, weight3, cache_keys, cache_values)


def table_kernel(count_ref, out_ref):
    y, z, xl = place_of_device()
    lane = lax.broadcasted_iota(jnp.int32, out_ref.shape, 1)
    out_ref[...] = jnp.where(lane == y * 16 + z * 2 + xl, count_ref[0], 0).astype(F32).astype(BF16)


def own_count(count, width):
    return pl.pallas_call(
        table_kernel,
        in_specs=[pl.BlockSpec(memory_space=SMEM)],
        out_shape=jax.ShapeDtypeStruct((16, width), BF16),
        compiler_params=params(8),
        cost_estimate=cost(0, 32 * width),
        name="own_count",
    )(count)


def add_kernel(a_ref, b_ref, out_ref):
    out_ref[...] = (a_ref[...].astype(F32) + b_ref[...].astype(F32)).astype(BF16)


def added(a, b):
    return pl.pallas_call(
        add_kernel,
        out_shape=jax.ShapeDtypeStruct(a.shape, a.dtype),
        compiler_params=params(8),
        cost_estimate=cost(a.size, 6 * a.size),
        name="added",
    )(a, b)


def mark_kernel(halo_hbm, w_hbm, q_hbm, a_hbm, b_hbm, out_ref, halo, weight, a, b, sems):
    rows = q_hbm.shape[0]
    copies = [
        pltpu.make_async_copy(src, dst, sems.at[i])
        for i, (src, dst) in enumerate(
            (
                (halo_hbm, halo),
                (w_hbm.at[0], weight),
                (q_hbm, out_ref.at[:rows]),
                (a_hbm, a),
                (b_hbm, b),
            )
        )
    ]
    for copy in copies:
        copy.start()
    for copy in copies:
        copy.wait()
    normed = rms_scaled(halo[...].astype(F32))
    out = jnp.dot(normed, weight[...], preferred_element_type=F32)
    out_ref[rows : rows + HALO] = (out * SCALE2).astype(BF16)
    out_ref[rows + HALO :] = (a[...].astype(F32) + b[...].astype(F32)).astype(BF16)


def mark(halo, weight3, q, a, b):
    n, width = q.shape
    d = halo.shape[1]
    hbm = pl.BlockSpec(memory_space=HBM)
    return pl.pallas_call(
        mark_kernel,
        in_specs=[hbm] * 5,
        out_specs=pl.BlockSpec(memory_space=VMEM),
        out_shape=jax.ShapeDtypeStruct((n + HALO + a.shape[0], width), BF16),
        scratch_shapes=[
            VMEM(halo.shape, BF16),
            VMEM((d, width), BF16),
            VMEM(a.shape, BF16),
            VMEM(b.shape, BF16),
            pltpu.SemaphoreType.DMA((5,)),
        ],
        compiler_params=params(16),
        cost_estimate=cost(2 * HALO * d * width, 2 * d * width),
        name="mark",
    )(halo, weight3, q, a, b)


def plane_kernel(own, left, right, far, far_other, out_ref):
    half, rows = far.shape[0], out_ref.shape[0]
    total = far[half - rows :].astype(F32) + far_other[half - rows :].astype(F32)
    for ref in (own, left, right):
        for end in (half, 2 * half):
            total = total + ref[end - rows : end].astype(F32)
    out_ref[...] = total.astype(BF16)


def plane_counts(queries):
    return pl.pallas_call(
        plane_kernel,
        out_shape=jax.ShapeDtypeStruct((16, queries[0].shape[1]), BF16),
        compiler_params=params(8),
        cost_estimate=cost(0, 4096),
        name="plane_counts",
    )(*queries)


def join_kernel(a_ref, b_ref, out_ref):
    rows = a_ref.shape[0]
    out_ref[:rows] = a_ref[...]
    out_ref[rows:] = b_ref[...]


def join(a, b):
    n, width = a.shape
    return pl.pallas_call(
        join_kernel,
        out_shape=jax.ShapeDtypeStruct((2 * n, width), BF16),
        compiler_params=params(8),
        cost_estimate=cost(0, 8 * n * width),
        name="join",
    )(a, b)


def halves_kernel(left_ref, right_ref, own_ref, other_ref):
    half = own_ref.shape[0]
    own_ref[...] = left_ref[:half]
    other_ref[...] = right_ref[half:]


def halves(left, right):
    n, width = left.shape
    out = jax.ShapeDtypeStruct((n // 2, width), BF16)
    return pl.pallas_call(
        halves_kernel,
        out_shape=[out, out],
        compiler_params=params(8),
        cost_estimate=cost(0, 4 * n * width),
        name="halves",
    )(left, right)


def join_kernel(a_ref, b_ref, out_ref):
    rows = a_ref.shape[0]
    out_ref[:rows] = a_ref[...]
    out_ref[rows:] = b_ref[...]


def join(a, b):
    n, width = a.shape
    return pl.pallas_call(
        join_kernel,
        out_shape=jax.ShapeDtypeStruct((2 * n, width), BF16),
        compiler_params=params(8),
        cost_estimate=cost(0, 8 * n * width),
        name="join",
    )(a, b)


RING = ((0, 0), (0, 1), (1, 0), (1, 1), (3, 0), (3, 1), (2, 0), (2, 1))


def place_of_device():
    return lax.axis_index("y"), lax.axis_index("z"), lax.axis_index("xl")


def columns_of(pieces):
    return [s[:, at : at + HS] for s in pieces for at in range(0, s.shape[1], HS)]


def attend_heads(qs, pieces, prior, score, value):
    heads = len(qs)
    pending = [score(0, qs[0], j) for j in range(pieces)]
    results = []
    for h in range(heads):
        top = jnp.max(functools.reduce(jnp.maximum, columns_of(pending)), axis=1, keepdims=True)
        if prior is not None:
            top = jnp.maximum(top, prior[h])
        following = []
        both = None
        for j in range(pieces):
            term = jnp.dot(
                jnp.exp2(pending[j] - top).astype(BF16), value(h, j), preferred_element_type=F32
            )
            both = term if both is None else both + term
            if h + 1 < heads:
                following.append(score(h + 1, qs[h + 1], j))
        pending = following
        results.append((top, both[:, HS:], both[:, :HS]))
    return results


def with_ones(v):
    return jnp.concatenate([v, jnp.ones_like(v)], axis=1)


def owner_of(back, other):
    y, z, xl = place_of_device()
    return (y + 4 - back) % 4, z, (1 - xl if other else xl)


TILES = (((0, 0), (0, 1), (1, 0), (1, 1)), ((3, 0), (4, 0), (2, 0), (2, 1)))


def fill_tile(q_tile, queries, tile):
    rows = q_tile.shape[0] // 4
    for b, (ref, half) in enumerate(TILES[tile]):
        at = half * (rows + 16)
        q_tile[b * rows : (b + 1) * rows] = queries[ref][at : at + rows]


def span_kernel(tile, slots, slope_ref, *refs):
    queries, packs = refs[:5], refs[5:13]
    acc_ref, stat_ref, q_tile, bias = refs[13:]
    y, z, xl = place_of_device()
    count, width = q_tile.shape
    block, heads = count // 4, width // HS
    rows = block - HALO
    fill_tile(q_tile, queries, tile)
    place = lax.broadcasted_iota(jnp.int32, (1, rows), 1)
    for j, (back, other) in enumerate(RING):
        yj, zj, side = owner_of(back, other)
        spot = (place + (yj * 16 + zj * 2 + side) * rows).astype(F32)
        for h in range(heads):
            bias[h : h + 1, j * rows : (j + 1) * rows] = jnp.where(
                yj <= y, slope_ref[h] * LOG2E * spot, NEG
            )
    row = lax.broadcasted_iota(jnp.int32, (count, 1), 0)
    row_pos = jnp.zeros((count, 1), jnp.int32)
    for part in range(4):
        row_z = ((z + 8 - 4 * tile - 2 * (part // 2)) % 8) ^ (part % 2)
        first = (y * 16 + xl + 2 * row_z) * rows
        at = row - part * block
        at = jnp.where(at < rows, at, at - block)
        row_pos = jnp.where(row >= part * block, first + at, row_pos)

    def score(h, q, j):
        cols = slice(h * HS, (h + 1) * HS)
        s = dot_t(q, packs[j][2 * slots : 2 * slots + rows, cols])
        s = s + bias[h : h + 1, j * rows : (j + 1) * rows]
        back, other = RING[j]
        if back <= 1:
            yj, zj, side = owner_of(back, other)
            s = jnp.where(place + (yj * 16 + zj * 2 + side) * rows <= row_pos, s, NEG)
        return s

    def value(h, j):
        return with_ones(packs[j][2 * slots + rows :, h * HS : (h + 1) * HS])

    lane = lax.broadcasted_iota(jnp.int32, (count, HS), 1)
    packed = jnp.zeros((count, HS), F32)
    qs = [q_tile[:, h * HS : (h + 1) * HS] for h in range(heads)]
    for h, (top, total, acc) in enumerate(attend_heads(qs, len(RING), None, score, value)):
        acc_ref[:, h * HS : (h + 1) * HS] = acc
        packed = jnp.where(lane == h, top, packed)
        packed = jnp.where(lane == heads + h, total, packed)
    stat_ref[...] = packed


def span_attend(tile, slopes, queries, packs, slots):
    width = queries[0].shape[1]
    rows = packs[0].shape[0] // 2 - slots
    count, nk = 4 * (rows + HALO), len(RING) * rows
    vmem = pl.BlockSpec(memory_space=VMEM)
    return pl.pallas_call(
        functools.partial(span_kernel, tile, slots),
        in_specs=[pl.BlockSpec(memory_space=SMEM)] + [vmem] * 13,
        out_specs=[vmem, vmem],
        out_shape=[
            jax.ShapeDtypeStruct((count, width), F32),
            jax.ShapeDtypeStruct((count, HS), F32),
        ],
        scratch_shapes=[VMEM((count, width), BF16), VMEM((8, nk), F32)],
        compiler_params=params(32),
        cost_estimate=cost(4 * count * nk * width, 4 * nk * width, 2 * count * nk),
        name="span_attend",
    )(slopes, *queries, *packs)


def cache_kernel(slots, slope_ref, *refs):
    queries, packs, tables, states = refs[:5], refs[5:13], refs[13:15], refs[15:19]
    out_ref, q_tile, acc_tile, stat_tile, bias = refs[19:]
    tile = pl.program_id(0)
    y, z, xl = place_of_device()
    count, width = q_tile.shape
    block, heads = count // 4, width // HS
    rows = block - HALO
    for t in range(2):

        @pl.when(tile == t)
        def _(t=t):
            fill_tile(q_tile, queries, t)
            acc_tile[...] = states[2 * t][...]
            stat_tile[...] = states[2 * t + 1][...]

    @pl.when(tile == 0)
    def _():
        table = (tables[0][...].astype(F32) + tables[1][...].astype(F32))[:1]
        lane = lax.broadcasted_iota(jnp.int32, table.shape, 1)
        everything = jnp.sum(table, axis=1, keepdims=True)
        slot = lax.broadcasted_iota(jnp.int32, (1, slots), 1).astype(F32)
        for j, (back, other) in enumerate(RING):
            yj, zj, side = owner_of(back, other)
            ctx = yj * 16 + zj * 2 + side
            live = jnp.sum(jnp.where(lane == ctx, table, 0.0), axis=1, keepdims=True)
            start = jnp.sum(jnp.where(lane < ctx, table, 0.0), axis=1, keepdims=True) - everything
            for h in range(heads):
                bias[h : h + 1, j * slots : (j + 1) * slots] = jnp.where(
                    slot < live, slope_ref[h] * LOG2E * (slot + start), NEG
                )

    def score(h, q, j):
        s = dot_t(q, packs[j][:slots, h * HS : (h + 1) * HS])
        return s + bias[h : h + 1, j * slots : (j + 1) * slots]

    def value(h, j):
        return with_ones(packs[j][slots : 2 * slots, h * HS : (h + 1) * HS])

    lane = lax.broadcasted_iota(jnp.int32, (count, HS), 1)
    packed = jnp.zeros((count, HS), F32)
    qs = [q_tile[:, h * HS : (h + 1) * HS] for h in range(heads)]
    prior = [stat_tile[:, h : h + 1] for h in range(heads)]
    done = []
    for h, (top, total, acc) in enumerate(attend_heads(qs, len(RING), prior, score, value)):
        fade = jnp.exp2(prior[h] - top)
        total = total + fade * stat_tile[:, heads + h : heads + h + 1]
        acc = acc + fade * acc_tile[:, h * HS : (h + 1) * HS]
        done.append((acc / total).astype(BF16))
        for k, piece in enumerate(three_parts(top + jnp.log2(total))):
            packed = jnp.where(lane == 3 * h + k, piece, packed)
    both = jnp.concatenate(done, axis=1)
    odd = z % 2 == 1
    for pair in range(2):
        a, b = 2 * pair * block, (2 * pair + 1) * block
        end = b + block
        blocks = []
        for own, level in (
            (jnp.where(odd, both[b:end], both[a:b]), jnp.where(odd, packed[b:end], packed[a:b])),
            (jnp.where(odd, both[a:b], both[b:end]), jnp.where(odd, packed[a:b], packed[b:end])),
        ):
            ahead = jnp.concatenate(
                [level[rows:], jnp.zeros((HS - HALO, HS), F32)], axis=0
            )
            tail = [jnp.transpose(level[:rows])[:16], jnp.transpose(ahead)[:16]]
            blocks.append((own, jnp.concatenate(tail, axis=1).astype(BF16)))
        for p in range(4):

            @pl.when((z // 2 + 4 - 2 * tile - pair) % 4 == p)
            def _(p=p, blocks=blocks):
                for i, (own, tail) in enumerate(blocks):
                    out_ref[2 * p + i, :block] = own
                    out_ref[2 * p + i, block:] = tail


def cache_attend(slopes, queries, packs, tables, states, slots):
    width = queries[0].shape[1]
    rows = packs[0].shape[0] // 2 - slots + HALO
    count, nk = 4 * rows, len(RING) * slots
    whole = lambda a: pl.BlockSpec(a.shape, lambda i: (0,) * a.ndim)
    operands = (*queries, *packs, *tables, *states)
    out = jax.ShapeDtypeStruct((8, rows + 16, width), BF16)
    return pl.pallas_call(
        functools.partial(cache_kernel, slots),
        grid=(2,),
        in_specs=[pl.BlockSpec(memory_space=SMEM)] + [whole(a) for a in operands],
        out_specs=whole(out),
        out_shape=out,
        scratch_shapes=[
            VMEM((count, width), BF16),
            VMEM((count, width), F32),
            VMEM((count, HS), F32),
            VMEM((8, nk), F32),
        ],
        compiler_params=params(44),
        cost_estimate=cost(8 * count * nk * width, 4 * nk * width, 4 * count * nk),
        name="cache_attend",
    )(slopes, *operands)


def merge_kernel(heads, parts_ref, out_ref):
    sources, padded, width = parts_ref.shape
    rows = padded - 16
    levels = [
        jnp.concatenate(
            [parts_ref[s, rows:, cols].astype(F32) for s in range(sources)], axis=0
        )
        for cols in (slice(0, HS), slice(HS, 2 * HS))
    ]
    turned = jnp.concatenate(
        [jnp.transpose(levels[0]), jnp.transpose(levels[1])[: rows - HS]], axis=0
    )
    for h in range(heads):
        cols = slice(h * HS, (h + 1) * HS)
        level = []
        for s in range(sources):
            at = s * 16 + 3 * h
            level.append(
                (turned[:, at : at + 1] + turned[:, at + 1 : at + 2]) + turned[:, at + 2 : at + 3]
            )
        top = functools.reduce(jnp.maximum, level)
        total = jnp.zeros((rows, 1), F32)
        acc = jnp.zeros((rows, HS), F32)
        for s in range(sources):
            weight = jnp.exp2(level[s] - top)
            total = total + weight
            acc = acc + weight * parts_ref[s, :rows, cols].astype(F32)
        out_ref[:, cols] = (acc / total).astype(BF16)


def merge(parts):
    sources, padded, width = parts.shape
    rows = padded - 16
    return pl.pallas_call(
        functools.partial(merge_kernel, width // HS),
        out_shape=jax.ShapeDtypeStruct((rows, width), BF16),
        compiler_params=params(16),
        cost_estimate=cost(4 * sources * rows * width, 2 * sources * padded * width),
        name="merge",
    )(parts)


def product_kernel(
    tok_hbm, halo_hbm, a_ref, b_ref, wa_hbm, wb_hbm, sum_ref, term_ref, tok, wa, wb, sems
):
    chunks = wa.shape[0]
    cols = wa.shape[2]
    copies = []
    for c in range(chunks):
        at = pl.ds(c * cols, cols)
        copies.append(
            [
                pltpu.make_async_copy(src.at[:, at], dst.at[c], sems.at[i, c])
                for i, (src, dst) in enumerate(((wa_hbm, wa), (wb_hbm, wb)))
            ]
        )
        rows = tok_hbm.shape[0]
        for i, (src, to) in enumerate(
            ((tok_hbm, pl.ds(0, rows)), (halo_hbm, pl.ds(rows, HALO)))
        ):
            copies[-1].append(
                pltpu.make_async_copy(src.at[:, at], tok.at[c, to], sems.at[2 + i, c])
            )
    for group in copies:
        for copy in group:
            copy.start()
    for c, group in enumerate(copies):
        for copy in group:
            copy.wait()
        at = slice(c * cols, (c + 1) * cols)
        term = jnp.dot(a_ref[...], wa[c], preferred_element_type=F32) + jnp.dot(
            b_ref[...], wb[c], preferred_element_type=F32
        )
        total = tok[c].astype(F32) + term
        sum_ref[:, at] = total
        term_ref[:, at] = term.astype(BF16)


def layer_product(tokens, halo, atts, weights):
    rows, d = tokens.shape[0] + HALO, tokens.shape[1]
    chunks = 4
    inner = weights[0].shape[0]
    hbm = pl.BlockSpec(memory_space=HBM)
    vmem = pl.BlockSpec(memory_space=VMEM)
    return pl.pallas_call(
        product_kernel,
        in_specs=[hbm, hbm, vmem, vmem, hbm, hbm],
        out_specs=[vmem] * 2,
        out_shape=[
            jax.ShapeDtypeStruct((rows, d), F32),
            jax.ShapeDtypeStruct((rows, d), BF16),
        ],
        scratch_shapes=[
            VMEM((chunks, rows, d // chunks), BF16),
            VMEM((chunks, inner, d // chunks), BF16),
            VMEM((chunks, inner, d // chunks), BF16),
            pltpu.SemaphoreType.DMA((4, chunks)),
        ],
        compiler_params=params(16),
        cost_estimate=cost(4 * rows * d * inner, 4 * inner * d),
        name="layer_product",
    )(tokens, halo, *atts, *weights)


def short_project_kernel(
    sum_ref, term_ref, w_ref, cols_ref, q_ref, kv_ref, normed
):
    step = pl.program_id(0)
    rows, d = sum_ref.shape[0] - HALO, sum_ref.shape[1]
    groups = rows // GROUP
    width = w_ref.shape[2]

    @pl.when(step == 0)
    def _():
        layer = (sum_ref[...] + term_ref[...].astype(F32)).astype(BF16)
        y, z, xl = place_of_device()
        rim = jnp.where(y * 16 + z * 2 + xl > 0, layer[rows:], jnp.zeros((HALO, d), BF16))
        layer = layer[:rows]
        part = d // 4
        tp = lax.axis_index("tp")
        mine = layer[:, :part]
        for t in range(1, 4):
            mine = jnp.where(tp == t, layer[:, t * part : (t + 1) * part], mine)
        cols_ref[...] = mine
        g = lax.broadcasted_iota(jnp.int32, (groups, rows), 0) * GROUP
        t = lax.broadcasted_iota(jnp.int32, (groups, rows), 1)
        own = jnp.where((t <= g) & (t > g - GROUP), 1.0 / GROUP, 0.0).astype(BF16)
        g = lax.broadcasted_iota(jnp.int32, (groups, HALO), 0) * GROUP
        t = lax.broadcasted_iota(jnp.int32, (groups, HALO), 1) - HALO
        before = jnp.where(t > g - GROUP, 1.0 / GROUP, 0.0).astype(BF16)
        pooled = jnp.dot(own, layer, preferred_element_type=F32) + jnp.dot(
            before, rim, preferred_element_type=F32
        )
        normed[...] = rms_scaled(pooled.astype(BF16).astype(F32))

    out = jnp.dot(normed[...], w_ref[0], preferred_element_type=F32)

    @pl.when(step == 0)
    def _():
        q_ref[...] = (out * SCALE2).astype(BF16)

    @pl.when(step == 1)
    def _():
        kv_ref[:, :width] = out.astype(BF16)

    @pl.when(step == 2)
    def _():
        kv_ref[:, width:] = out.astype(BF16)


def short_project(total, term, weight3):
    n, d = total.shape[0] - HALO, total.shape[1]
    groups = n // GROUP
    width = weight3.shape[2]
    whole = lambda shape: pl.BlockSpec(shape, lambda i: (0,) * len(shape))
    shapes = [(n, d // 4), (groups, width), (groups, 2 * width)]
    return pl.pallas_call(
        short_project_kernel,
        grid=(3,),
        in_specs=[whole(total.shape), whole(term.shape)]
        + [pl.BlockSpec((1, d, width), lambda i: (i, 0, 0))],
        out_specs=[whole(s) for s in shapes],
        out_shape=[jax.ShapeDtypeStruct(s, BF16) for s in shapes],
        scratch_shapes=[VMEM((groups, d), BF16)],
        compiler_params=params(16),
        cost_estimate=cost(6 * groups * d * width, 2 * (n * d + 3 * d * width)),
        name="short_project",
    )(total, term, weight3)


def short_attend_kernel(slope_ref, *refs):
    queries, key_refs, out_ref = refs[:4], refs[4:8], refs[8]
    y, z, xl = place_of_device()
    blocks, groups, padded = out_ref.shape
    width = padded - HS
    heads = width // HS
    n = blocks * groups
    row = lax.broadcasted_iota(jnp.int32, (n, 1), 0)
    zs = row // groups
    row_pos = (y * 16 + xl + 2 * zs) * groups + row % groups
    back = (z // 2 + 4 - zs // 2) % 4
    came = (2 * back + (zs ^ z) % 2) * groups + row % groups
    order = jnp.where(lax.broadcasted_iota(jnp.int32, (n, n), 1) == came, 1.0, 0.0).astype(BF16)
    lined = jnp.concatenate([r[...] for r in queries], axis=0)
    lined = jnp.dot(order, lined, preferred_element_type=F32).astype(BF16)
    key = lax.broadcasted_iota(jnp.int32, (1, n), 1)
    ys = (y + 4 - key // (2 * groups)) % 4
    side = jnp.where((key // groups) % 2 == 1, 1 - xl, xl)
    key_pos = (ys * 16 + z * 2 + side) * groups + key % groups
    usable = key_pos <= row_pos
    spot = key_pos.astype(F32)
    lane = lax.broadcasted_iota(jnp.int32, (n, HS), 1)
    packed = jnp.zeros((n, HS), F32)
    outs = []
    for h in range(heads):
        cols = slice(h * HS, (h + 1) * HS)
        cols_v = slice(width + h * HS, width + (h + 1) * HS)
        q = lined[:, cols]
        k = jnp.concatenate([r[:, cols] for r in key_refs], axis=0)
        v = jnp.concatenate([r[:, cols_v] for r in key_refs], axis=0)
        s = dot_t(q, k) + (slope_ref[h] * LOG2E) * spot
        s = jnp.where(usable, s, NEG)
        top = jnp.max(s, axis=1, keepdims=True)
        p = jnp.exp2(s - top).astype(BF16)
        both = jnp.dot(p, with_ones(v), preferred_element_type=F32)
        weight_total = both[:, HS:]
        outs.append((both[:, :HS] / weight_total).astype(BF16))
        level = top + jnp.log2(weight_total)
        for k, piece in enumerate(three_parts(level)):
            packed = jnp.where(lane == 3 * h + k, piece, packed)
    out = jnp.concatenate(outs + [packed.astype(BF16)], axis=1)
    out_ref[...] = out.reshape(out_ref.shape)


def short_attend(slopes, queries, keys):
    blocks, groups, width = 8, queries[0].shape[0] // 2, queries[0].shape[1]
    n = blocks * groups
    smem = pl.BlockSpec(memory_space=SMEM)
    vmem = pl.BlockSpec(memory_space=VMEM)
    return pl.pallas_call(
        short_attend_kernel,
        in_specs=[smem] + [vmem] * 8,
        out_specs=vmem,
        out_shape=jax.ShapeDtypeStruct((blocks, groups, width + HS), BF16),
        compiler_params=params(16),
        cost_estimate=cost(4 * n * n * width, 8 * n * width),
        name="short_attend",
    )(slopes, *queries, *keys)


def short_merge_kernel(heads, parts_ref, w_ref, *outs):
    sources, rows, padded = parts_ref.shape
    width = padded - HS
    merged = []
    for h in range(heads):
        cols = slice(h * HS, (h + 1) * HS)
        level = []
        for s in range(sources):
            lev = parts_ref[s, :, width:].astype(F32)
            level.append(
                (lev[:, 3 * h : 3 * h + 1] + lev[:, 3 * h + 1 : 3 * h + 2])
                + lev[:, 3 * h + 2 : 3 * h + 3]
            )
        top = functools.reduce(jnp.maximum, level)
        total = jnp.zeros((rows, 1), F32)
        acc = jnp.zeros((rows, HS), F32)
        for s in range(sources):
            weight = jnp.exp2(level[s] - top)
            total = total + weight
            acc = acc + weight * parts_ref[s, :, cols].astype(F32)
        merged.append((acc / total).astype(BF16))
    att = jnp.concatenate(merged, axis=1)
    cols = outs[0].shape[1]
    terms = [
        jnp.dot(
            att, w_ref[:, t * cols : (t + 1) * cols], preferred_element_type=F32
        ).astype(BF16)
        for t in range(4)
    ]
    tp = lax.axis_index("tp")
    for flip, out in enumerate(outs):
        chosen = terms[flip]
        for t in range(1, 4):
            chosen = jnp.where(tp == t, terms[t ^ flip], chosen)
        out[...] = chosen


def short_merge(parts, weight):
    sources, rows, padded = parts.shape
    width = padded - HS
    cols = weight.shape[1] // 4
    out = jax.ShapeDtypeStruct((rows, cols), BF16)
    return pl.pallas_call(
        functools.partial(short_merge_kernel, width // HS),
        out_shape=[out] * 4,
        compiler_params=params(16),
        cost_estimate=cost(8 * rows * width * cols, 8 * width * cols),
        name="short_merge",
    )(parts, weight)


def final_kernel(lay_ref, *refs):
    terms, out_ref = refs[:-1], refs[-1]
    rows, groups = lay_ref.shape[0], terms[0].shape[0]
    t = lax.broadcasted_iota(jnp.int32, (rows, groups), 0) // GROUP
    g = lax.broadcasted_iota(jnp.int32, (rows, groups), 1)
    spread = jnp.where(t == g, 1.0, 0.0).astype(BF16)
    branch = jnp.zeros(lay_ref.shape, F32)
    for term in terms:
        branch = branch + jnp.dot(spread, term[...], preferred_element_type=F32)
    out_ref[...] = (lay_ref[...].astype(F32) + branch).astype(BF16)


def final_sum(layer, terms):
    rows, cols = layer.shape
    groups = terms[0].shape[0]
    return pl.pallas_call(
        final_kernel,
        out_shape=jax.ShapeDtypeStruct((rows, cols), BF16),
        compiler_params=params(16),
        cost_estimate=cost(8 * rows * cols * groups, 4 * rows * cols),
        name="final_sum",
    )(layer, *terms)


def exchange(blocks, axis):
    return lax.all_to_all(blocks, axis, 0, 0)


def swap(x, axis, flip=1):
    return lax.ppermute(x, axis, [(i, i ^ flip) for i in range(lax.axis_size(axis))])


def moved(x, axis, by):
    n = lax.axis_size(axis)
    return lax.ppermute(x, axis, [(i, (i + by) % n) for i in range(n)])


def both_ways(x, axis, by):
    return moved(x, axis, by), moved(x, axis, -by)


def after(x, *others):
    return lax.optimization_barrier((x, *others))[0]


def on_device(
    tokens,
    project_weight,
    output_weight,
    distance_slope,
    cache_keys,
    cache_values,
    cache_count,
    short_project_weight,
    short_output,
    short_slope,
):
    axes = ("y", "z", "xl", "tp")
    slots = cache_keys.shape[0]
    count = own_count(cache_count, cache_keys.shape[1])
    other_count = swap(count, "xl")
    n, tp = lax.axis_size(axes), lax.axis_size("tp")
    halo = lax.ppermute(tokens[-HALO:], axes, [(i, i + tp) for i in range(n - tp)])
    weight3 = jnp.transpose(project_weight, (1, 0, 2))
    q, pack = project(tokens, weight3, cache_keys, cache_values)
    q, pack, other_count, halo = lax.optimization_barrier((q, pack, other_count, halo))
    marked = mark(halo, weight3, q, count, other_count)
    left, right = both_ways(pack, "y", 1)
    other, left, right, mate = lax.optimization_barrier(
        (swap(pack, "xl"), left, right, swap(marked, "z"))
    )
    pair = join(marked, mate)
    left_other, right_other = both_ways(other, "y", 1)
    left_pair, right_pair = both_ways(pair, "z", 2)
    left_other, right_other, left_pair, right_pair, left = lax.optimization_barrier(
        (left_other, right_other, left_pair, right_pair, left)
    )
    far, far_other = moved(left, "y", 1), moved(right_other, "y", -1)
    near = halves(left_pair, right_pair)
    queries = [pair, left_pair, right_pair, moved(near[0], "z", 2), moved(near[1], "z", -2)]
    crossed = swap(after(output_weight, left), "tp", 2)
    packs = [pack, other, left, left_other, right, right_other, far, far_other]
    plane = plane_counts(queries)
    beside = swap(plane, "y")
    first = span_attend(0, distance_slope, queries, packs, slots)
    plane, beside, first = lax.optimization_barrier((plane, beside, first))
    line = added(plane, beside)
    beyond = swap(line, "y", 2)
    second = span_attend(1, distance_slope, queries, packs, slots)
    second, beyond = lax.optimization_barrier((second, beyond))
    parts = cache_attend(
        distance_slope, queries, packs, (line, beyond), (*first, *second), slots
    )
    parts, crossed = lax.optimization_barrier((parts, crossed))

    att = merge(exchange(parts, "z"))
    total, term = layer_product(
        tokens, halo, (att, swap(att, "tp", 2)), (output_weight, crossed)
    )
    layer, sq, skv = short_project(
        total,
        swap(term, "tp", 1),
        jnp.transpose(short_project_weight, (1, 0, 2)),
    )
    pair = join(sq, swap(sq, "z"))
    queries = [pair] + [moved(pair, "z", by) for by in (2, 4, 6)]
    pair = join(skv, swap(skv, "xl"))
    keys = [pair] + [moved(pair, "y", by) for by in (1, 2, 3)]
    sparts = short_attend(short_slope, queries, keys)
    terms = short_merge(exchange(sparts, "z"), short_output)
    terms = [swap(t, "tp", flip) if flip else t for flip, t in enumerate(terms)]
    return final_sum(layer, terms)


def solution(mesh):
    split = Mesh(mesh.devices.reshape(4, 8, 2, 4), ("y", "z", "xl", "tp"))
    ctx = ("y", "z", "xl")
    return jax.shard_map(
        on_device,
        mesh=split,
        in_specs=(
            P(ctx, None),
            P(None, None, "tp"),
            P("tp", None),
            P("tp"),
            P(ctx, "tp"),
            P(ctx, "tp"),
            P(ctx),
            P(None, None, "tp"),
            P("tp", None),
            P("tp"),
        ),
        out_specs=P(ctx, "tp"),
        check_vma=False,
    )
```

```python
import functools
import math

import jax
import jax.numpy as jnp
from jax import lax
from jax.experimental import pallas as pl
from jax.experimental.pallas import tpu as pltpu
from jax.sharding import Mesh, PartitionSpec as P

HS = 128
GROUP = 4
HALO = 16
NEG = -1e30
LOG2E = math.log2(math.e)
SCALE2 = HS ** -0.5 * LOG2E

VMEM = pltpu.VMEM
SMEM = pltpu.SMEM
HBM = pltpu.HBM
F32 = jnp.float32
BF16 = jnp.bfloat16


def cost(flops, moved, trans=0):
    return pl.CostEstimate(flops=flops, bytes_accessed=moved, transcendentals=trans)


def params(mib):
    return pltpu.CompilerParams(vmem_limit_bytes=mib * 1024 * 1024)


def rms_scaled(values):
    inv = lax.rsqrt(jnp.mean(values * values, axis=-1, keepdims=True) + 1e-06)
    return (values * inv).astype(BF16)


def dot_t(a, b):
    return lax.dot_general(a, b, (((1,), (1,)), ((), ())), preferred_element_type=F32)


def three_parts(x):
    hi = x.astype(BF16).astype(F32)
    mid = (x - hi).astype(BF16).astype(F32)
    lo = (x - hi - mid).astype(BF16).astype(F32)
    return hi, mid, lo


def project_kernel(
    tok_hbm, w_hbm, ck_hbm, cv_hbm, q_ref, pack_ref, tok, weight, sems
):
    rows = tok.shape[0]
    slots = ck_hbm.shape[0]
    copies = [pltpu.make_async_copy(tok_hbm, tok, sems.at[0])]
    copies += [
        pltpu.make_async_copy(w_hbm.at[i], weight.at[i], sems.at[1 + i]) for i in range(3)
    ]
    copies += [
        pltpu.make_async_copy(ck_hbm, pack_ref.at[:slots], sems.at[4]),
        pltpu.make_async_copy(cv_hbm, pack_ref.at[slots : 2 * slots], sems.at[5]),
    ]
    for copy in copies:
        copy.start()
    copies[0].wait()
    normed = rms_scaled(tok[...].astype(F32))
    for i in range(3):
        copies[1 + i].wait()
        out = jnp.dot(normed, weight[i], preferred_element_type=F32)
        if i == 0:
            q_ref[...] = (out * SCALE2).astype(BF16)
        else:
            at = 2 * slots + (i - 1) * rows
            pack_ref[at : at + rows] = out.astype(BF16)
    copies[4].wait()
    copies[5].wait()


def project(rows, weight3, cache_keys, cache_values):
    n, d = rows.shape
    width = weight3.shape[2]
    total = 2 * (n + cache_keys.shape[0])
    hbm = pl.BlockSpec(memory_space=HBM)
    vmem = pl.BlockSpec(memory_space=VMEM)
    return pl.pallas_call(
        project_kernel,
        in_specs=[hbm] * 4,
        out_specs=[vmem, vmem],
        out_shape=[
            jax.ShapeDtypeStruct((n, width), BF16),
            jax.ShapeDtypeStruct((total, width), BF16),
        ],
        scratch_shapes=[
            VMEM((n, d), BF16),
            VMEM(weight3.shape, BF16),
            pltpu.SemaphoreType.DMA((6,)),
        ],
        compiler_params=params(60),
        cost_estimate=cost(6 * n * d * width, 2 * (n * d + 3 * d * width)),
        name="project",
    )(rows, weight3, cache_keys, cache_values)


def table_kernel(count_ref, out_ref):
    y, z, xl = place_of_device()
    lane = lax.broadcasted_iota(jnp.int32, out_ref.shape, 1)
    out_ref[...] = jnp.where(lane == y * 16 + z * 2 + xl, count_ref[0], 0).astype(F32).astype(BF16)


def own_count(count, width):
    return pl.pallas_call(
        table_kernel,
        in_specs=[pl.BlockSpec(memory_space=SMEM)],
        out_shape=jax.ShapeDtypeStruct((16, width), BF16),
        compiler_params=params(8),
        cost_estimate=cost(0, 32 * width),
        name="own_count",
    )(count)


def add_kernel(a_ref, b_ref, out_ref):
    out_ref[...] = (a_ref[...].astype(F32) + b_ref[...].astype(F32)).astype(BF16)


def added(a, b):
    return pl.pallas_call(
        add_kernel,
        out_shape=jax.ShapeDtypeStruct(a.shape, a.dtype),
        compiler_params=params(8),
        cost_estimate=cost(a.size, 6 * a.size),
        name="added",
    )(a, b)


def mark_kernel(halo_hbm, w_hbm, q_hbm, a_hbm, b_hbm, out_ref, halo, weight, a, b, sems):
    rows = q_hbm.shape[0]
    copies = [
        pltpu.make_async_copy(src, dst, sems.at[i])
        for i, (src, dst) in enumerate(
            (
                (halo_hbm, halo),
                (w_hbm.at[0], weight),
                (q_hbm, out_ref.at[:rows]),
                (a_hbm, a),
                (b_hbm, b),
            )
        )
    ]
    for copy in copies:
        copy.start()
    for copy in copies:
        copy.wait()
    normed = rms_scaled(halo[...].astype(F32))
    out = jnp.dot(normed, weight[...], preferred_element_type=F32)
    out_ref[rows : rows + HALO] = (out * SCALE2).astype(BF16)
    out_ref[rows + HALO :] = (a[...].astype(F32) + b[...].astype(F32)).astype(BF16)


def mark(halo, weight3, q, a, b):
    n, width = q.shape
    d = halo.shape[1]
    hbm = pl.BlockSpec(memory_space=HBM)
    return pl.pallas_call(
        mark_kernel,
        in_specs=[hbm] * 5,
        out_specs=pl.BlockSpec(memory_space=VMEM),
        out_shape=jax.ShapeDtypeStruct((n + HALO + a.shape[0], width), BF16),
        scratch_shapes=[
            VMEM(halo.shape, BF16),
            VMEM((d, width), BF16),
            VMEM(a.shape, BF16),
            VMEM(b.shape, BF16),
            pltpu.SemaphoreType.DMA((5,)),
        ],
        compiler_params=params(16),
        cost_estimate=cost(2 * HALO * d * width, 2 * d * width),
        name="mark",
    )(halo, weight3, q, a, b)


def plane_kernel(own, left, right, far, far_other, out_ref):
    half, rows = far.shape[0], out_ref.shape[0]
    total = far[half - rows :].astype(F32) + far_other[half - rows :].astype(F32)
    for ref in (own, left, right):
        for end in (half, 2 * half):
            total = total + ref[end - rows : end].astype(F32)
    out_ref[...] = total.astype(BF16)


def plane_counts(queries):
    return pl.pallas_call(
        plane_kernel,
        out_shape=jax.ShapeDtypeStruct((16, queries[0].shape[1]), BF16),
        compiler_params=params(8),
        cost_estimate=cost(0, 4096),
        name="plane_counts",
    )(*queries)


def join_kernel(a_ref, b_ref, out_ref):
    rows = a_ref.shape[0]
    out_ref[:rows] = a_ref[...]
    out_ref[rows:] = b_ref[...]


def join(a, b):
    n, width = a.shape
    return pl.pallas_call(
        join_kernel,
        out_shape=jax.ShapeDtypeStruct((2 * n, width), BF16),
        compiler_params=params(8),
        cost_estimate=cost(0, 8 * n * width),
        name="join",
    )(a, b)


def halves_kernel(left_ref, right_ref, own_ref, other_ref):
    half = own_ref.shape[0]
    own_ref[...] = left_ref[:half]
    other_ref[...] = right_ref[half:]


def halves(left, right):
    n, width = left.shape
    out = jax.ShapeDtypeStruct((n // 2, width), BF16)
    return pl.pallas_call(
        halves_kernel,
        out_shape=[out, out],
        compiler_params=params(8),
        cost_estimate=cost(0, 4 * n * width),
        name="halves",
    )(left, right)


def join_kernel(a_ref, b_ref, out_ref):
    rows = a_ref.shape[0]
    out_ref[:rows] = a_ref[...]
    out_ref[rows:] = b_ref[...]


def join(a, b):
    n, width = a.shape
    return pl.pallas_call(
        join_kernel,
        out_shape=jax.ShapeDtypeStruct((2 * n, width), BF16),
        compiler_params=params(8),
        cost_estimate=cost(0, 8 * n * width),
        name="join",
    )(a, b)


RING = ((0, 0), (0, 1), (1, 0), (1, 1), (3, 0), (3, 1), (2, 0), (2, 1))


def place_of_device():
    return lax.axis_index("y"), lax.axis_index("z"), lax.axis_index("xl")


def columns_of(pieces):
    return [s[:, at : at + HS] for s in pieces for at in range(0, s.shape[1], HS)]


def attend_heads(qs, pieces, prior, score, value):
    heads = len(qs)
    pending = [score(0, qs[0], j) for j in range(pieces)]
    results = []
    for h in range(heads):
        top = jnp.max(functools.reduce(jnp.maximum, columns_of(pending)), axis=1, keepdims=True)
        if prior is not None:
            top = jnp.maximum(top, prior[h])
        following = []
        both = None
        for j in range(pieces):
            term = jnp.dot(
                jnp.exp2(pending[j] - top).astype(BF16), value(h, j), preferred_element_type=F32
            )
            both = term if both is None else both + term
            if h + 1 < heads:
                following.append(score(h + 1, qs[h + 1], j))
        pending = following
        results.append((top, both[:, HS:], both[:, :HS]))
    return results


def with_ones(v):
    return jnp.concatenate([v, jnp.ones_like(v)], axis=1)


def owner_of(back, other):
    y, z, xl = place_of_device()
    return (y + 4 - back) % 4, z, (1 - xl if other else xl)


TILES = (((0, 0), (0, 1), (1, 0), (1, 1)), ((3, 0), (4, 0), (2, 0), (2, 1)))


def fill_tile(q_tile, queries, tile):
    rows = q_tile.shape[0] // 4
    for b, (ref, half) in enumerate(TILES[tile]):
        at = half * (rows + 16)
        q_tile[b * rows : (b + 1) * rows] = queries[ref][at : at + rows]


def span_kernel(tile, slots, slope_ref, *refs):
    queries, packs = refs[:5], refs[5:13]
    acc_ref, stat_ref, q_tile, bias = refs[13:]
    y, z, xl = place_of_device()
    count, width = q_tile.shape
    block, heads = count // 4, width // HS
    rows = block - HALO
    fill_tile(q_tile, queries, tile)
    place = lax.broadcasted_iota(jnp.int32, (1, rows), 1)
    for j, (back, other) in enumerate(RING):
        yj, zj, side = owner_of(back, other)
        spot = (place + (yj * 16 + zj * 2 + side) * rows).astype(F32)
        for h in range(heads):
            bias[h : h + 1, j * rows : (j + 1) * rows] = jnp.where(
                yj <= y, slope_ref[h] * LOG2E * spot, NEG
            )
    row = lax.broadcasted_iota(jnp.int32, (count, 1), 0)
    row_pos = jnp.zeros((count, 1), jnp.int32)
    for part in range(4):
        row_z = ((z + 8 - 4 * tile - 2 * (part // 2)) % 8) ^ (part % 2)
        first = (y * 16 + xl + 2 * row_z) * rows
        at = row - part * block
        at = jnp.where(at < rows, at, at - block)
        row_pos = jnp.where(row >= part * block, first + at, row_pos)

    def score(h, q, j):
        cols = slice(h * HS, (h + 1) * HS)
        s = dot_t(q, packs[j][2 * slots : 2 * slots + rows, cols])
        s = s + bias[h : h + 1, j * rows : (j + 1) * rows]
        back, other = RING[j]
        if back <= 1:
            yj, zj, side = owner_of(back, other)
            s = jnp.where(place + (yj * 16 + zj * 2 + side) * rows <= row_pos, s, NEG)
        return s

    def value(h, j):
        return with_ones(packs[j][2 * slots + rows :, h * HS : (h + 1) * HS])

    lane = lax.broadcasted_iota(jnp.int32, (count, HS), 1)
    packed = jnp.zeros((count, HS), F32)
    qs = [q_tile[:, h * HS : (h + 1) * HS] for h in range(heads)]
    for h, (top, total, acc) in enumerate(attend_heads(qs, len(RING), None, score, value)):
        acc_ref[:, h * HS : (h + 1) * HS] = acc
        packed = jnp.where(lane == h, top, packed)
        packed = jnp.where(lane == heads + h, total, packed)
    stat_ref[...] = packed


def span_attend(tile, slopes, queries, packs, slots):
    width = queries[0].shape[1]
    rows = packs[0].shape[0] // 2 - slots
    count, nk = 4 * (rows + HALO), len(RING) * rows
    vmem = pl.BlockSpec(memory_space=VMEM)
    return pl.pallas_call(
        functools.partial(span_kernel, tile, slots),
        in_specs=[pl.BlockSpec(memory_space=SMEM)] + [vmem] * 13,
        out_specs=[vmem, vmem],
        out_shape=[
            jax.ShapeDtypeStruct((count, width), F32),
            jax.ShapeDtypeStruct((count, HS), F32),
        ],
        scratch_shapes=[VMEM((count, width), BF16), VMEM((8, nk), F32)],
        compiler_params=params(32),
        cost_estimate=cost(4 * count * nk * width, 4 * nk * width, 2 * count * nk),
        name="span_attend",
    )(slopes, *queries, *packs)


def cache_kernel(slots, slope_ref, *refs):
    queries, packs, tables, states = refs[:5], refs[5:13], refs[13:15], refs[15:19]
    out_ref, q_tile, acc_tile, stat_tile, bias = refs[19:]
    tile = pl.program_id(0)
    y, z, xl = place_of_device()
    count, width = q_tile.shape
    block, heads = count // 4, width // HS
    rows = block - HALO
    for t in range(2):

        @pl.when(tile == t)
        def _(t=t):
            fill_tile(q_tile, queries, t)
            acc_tile[...] = states[2 * t][...]
            stat_tile[...] = states[2 * t + 1][...]

    @pl.when(tile == 0)
    def _():
        table = (tables[0][...].astype(F32) + tables[1][...].astype(F32))[:1]
        lane = lax.broadcasted_iota(jnp.int32, table.shape, 1)
        everything = jnp.sum(table, axis=1, keepdims=True)
        slot = lax.broadcasted_iota(jnp.int32, (1, slots), 1).astype(F32)
        for j, (back, other) in enumerate(RING):
            yj, zj, side = owner_of(back, other)
            ctx = yj * 16 + zj * 2 + side
            live = jnp.sum(jnp.where(lane == ctx, table, 0.0), axis=1, keepdims=True)
            start = jnp.sum(jnp.where(lane < ctx, table, 0.0), axis=1, keepdims=True) - everything
            for h in range(heads):
                bias[h : h + 1, j * slots : (j + 1) * slots] = jnp.where(
                    slot < live, slope_ref[h] * LOG2E * (slot + start), NEG
                )

    def score(h, q, j):
        s = dot_t(q, packs[j][:slots, h * HS : (h + 1) * HS])
        return s + bias[h : h + 1, j * slots : (j + 1) * slots]

    def value(h, j):
        return with_ones(packs[j][slots : 2 * slots, h * HS : (h + 1) * HS])

    lane = lax.broadcasted_iota(jnp.int32, (count, HS), 1)
    packed = jnp.zeros((count, HS), F32)
    qs = [q_tile[:, h * HS : (h + 1) * HS] for h in range(heads)]
    prior = [stat_tile[:, h : h + 1] for h in range(heads)]
    done = []
    for h, (top, total, acc) in enumerate(attend_heads(qs, len(RING), prior, score, value)):
        fade = jnp.exp2(prior[h] - top)
        total = total + fade * stat_tile[:, heads + h : heads + h + 1]
        acc = acc + fade * acc_tile[:, h * HS : (h + 1) * HS]
        done.append((acc / total).astype(BF16))
        for k, piece in enumerate(three_parts(top + jnp.log2(total))):
            packed = jnp.where(lane == 3 * h + k, piece, packed)
    both = jnp.concatenate(done, axis=1)
    odd = z % 2 == 1
    for pair in range(2):
        a, b = 2 * pair * block, (2 * pair + 1) * block
        end = b + block
        blocks = []
        for own, level in (
            (jnp.where(odd, both[b:end], both[a:b]), jnp.where(odd, packed[b:end], packed[a:b])),
            (jnp.where(odd, both[a:b], both[b:end]), jnp.where(odd, packed[a:b], packed[b:end])),
        ):
            ahead = jnp.concatenate(
                [level[rows:], jnp.zeros((HS - HALO, HS), F32)], axis=0
            )
            tail = [jnp.transpose(level[:rows])[:16], jnp.transpose(ahead)[:16]]
            blocks.append((own, jnp.concatenate(tail, axis=1).astype(BF16)))
        for p in range(4):

            @pl.when((z // 2 + 4 - 2 * tile - pair) % 4 == p)
            def _(p=p, blocks=blocks):
                for i, (own, tail) in enumerate(blocks):
                    out_ref[2 * p + i, :block] = own
                    out_ref[2 * p + i, block:] = tail


def cache_attend(slopes, queries, packs, tables, states, slots):
    width = queries[0].shape[1]
    rows = packs[0].shape[0] // 2 - slots + HALO
    count, nk = 4 * rows, len(RING) * slots
    whole = lambda a: pl.BlockSpec(a.shape, lambda i: (0,) * a.ndim)
    operands = (*queries, *packs, *tables, *states)
    out = jax.ShapeDtypeStruct((8, rows + 16, width), BF16)
    return pl.pallas_call(
        functools.partial(cache_kernel, slots),
        grid=(2,),
        in_specs=[pl.BlockSpec(memory_space=SMEM)] + [whole(a) for a in operands],
        out_specs=whole(out),
        out_shape=out,
        scratch_shapes=[
            VMEM((count, width), BF16),
            VMEM((count, width), F32),
            VMEM((count, HS), F32),
            VMEM((8, nk), F32),
        ],
        compiler_params=params(44),
        cost_estimate=cost(8 * count * nk * width, 4 * nk * width, 4 * count * nk),
        name="cache_attend",
    )(slopes, *operands)


def merge_kernel(heads, parts_ref, out_ref):
    sources, padded, width = parts_ref.shape
    rows = padded - 16
    levels = [
        jnp.concatenate(
            [parts_ref[s, rows:, cols].astype(F32) for s in range(sources)], axis=0
        )
        for cols in (slice(0, HS), slice(HS, 2 * HS))
    ]
    turned = jnp.concatenate(
        [jnp.transpose(levels[0]), jnp.transpose(levels[1])[: rows - HS]], axis=0
    )
    for h in range(heads):
        cols = slice(h * HS, (h + 1) * HS)
        level = []
        for s in range(sources):
            at = s * 16 + 3 * h
            level.append(
                (turned[:, at : at + 1] + turned[:, at + 1 : at + 2]) + turned[:, at + 2 : at + 3]
            )
        top = functools.reduce(jnp.maximum, level)
        total = jnp.zeros((rows, 1), F32)
        acc = jnp.zeros((rows, HS), F32)
        for s in range(sources):
            weight = jnp.exp2(level[s] - top)
            total = total + weight
            acc = acc + weight * parts_ref[s, :rows, cols].astype(F32)
        out_ref[:, cols] = (acc / total).astype(BF16)


def merge(parts):
    sources, padded, width = parts.shape
    rows = padded - 16
    return pl.pallas_call(
        functools.partial(merge_kernel, width // HS),
        out_shape=jax.ShapeDtypeStruct((rows, width), BF16),
        compiler_params=params(16),
        cost_estimate=cost(4 * sources * rows * width, 2 * sources * padded * width),
        name="merge",
    )(parts)


def product_kernel(
    tok_hbm, halo_hbm, a_ref, b_ref, wa_hbm, wb_hbm, sum_ref, term_ref, tok, wa, wb, sems
):
    chunks = wa.shape[0]
    cols = wa.shape[2]
    copies = []
    for c in range(chunks):
        at = pl.ds(c * cols, cols)
        copies.append(
            [
                pltpu.make_async_copy(src.at[:, at], dst.at[c], sems.at[i, c])
                for i, (src, dst) in enumerate(((wa_hbm, wa), (wb_hbm, wb)))
            ]
        )
        rows = tok_hbm.shape[0]
        for i, (src, to) in enumerate(
            ((tok_hbm, pl.ds(0, rows)), (halo_hbm, pl.ds(rows, HALO)))
        ):
            copies[-1].append(
                pltpu.make_async_copy(src.at[:, at], tok.at[c, to], sems.at[2 + i, c])
            )
    for group in copies:
        for copy in group:
            copy.start()
    for c, group in enumerate(copies):
        for copy in group:
            copy.wait()
        at = slice(c * cols, (c + 1) * cols)
        term = jnp.dot(a_ref[...], wa[c], preferred_element_type=F32) + jnp.dot(
            b_ref[...], wb[c], preferred_element_type=F32
        )
        total = tok[c].astype(F32) + term
        sum_ref[:, at] = total
        term_ref[:, at] = term.astype(BF16)


def layer_product(tokens, halo, atts, weights):
    rows, d = tokens.shape[0] + HALO, tokens.shape[1]
    chunks = 4
    inner = weights[0].shape[0]
    hbm = pl.BlockSpec(memory_space=HBM)
    vmem = pl.BlockSpec(memory_space=VMEM)
    return pl.pallas_call(
        product_kernel,
        in_specs=[hbm, hbm, vmem, vmem, hbm, hbm],
        out_specs=[vmem] * 2,
        out_shape=[
            jax.ShapeDtypeStruct((rows, d), F32),
            jax.ShapeDtypeStruct((rows, d), BF16),
        ],
        scratch_shapes=[
            VMEM((chunks, rows, d // chunks), BF16),
            VMEM((chunks, inner, d // chunks), BF16),
            VMEM((chunks, inner, d // chunks), BF16),
            pltpu.SemaphoreType.DMA((4, chunks)),
        ],
        compiler_params=params(16),
        cost_estimate=cost(4 * rows * d * inner, 4 * inner * d),
        name="layer_product",
    )(tokens, halo, *atts, *weights)


def short_project_kernel(
    sum_ref, term_ref, w_ref, cols_ref, q_ref, kv_ref, normed
):
    step = pl.program_id(0)
    rows, d = sum_ref.shape[0] - HALO, sum_ref.shape[1]
    groups = rows // GROUP
    width = w_ref.shape[2]

    @pl.when(step == 0)
    def _():
        layer = (sum_ref[...] + term_ref[...].astype(F32)).astype(BF16)
        y, z, xl = place_of_device()
        rim = jnp.where(y * 16 + z * 2 + xl > 0, layer[rows:], jnp.zeros((HALO, d), BF16))
        layer = layer[:rows]
        part = d // 4
        tp = lax.axis_index("tp")
        mine = layer[:, :part]
        for t in range(1, 4):
            mine = jnp.where(tp == t, layer[:, t * part : (t + 1) * part], mine)
        cols_ref[...] = mine
        g = lax.broadcasted_iota(jnp.int32, (groups, rows), 0) * GROUP
        t = lax.broadcasted_iota(jnp.int32, (groups, rows), 1)
        own = jnp.where((t <= g) & (t > g - GROUP), 1.0 / GROUP, 0.0).astype(BF16)
        g = lax.broadcasted_iota(jnp.int32, (groups, HALO), 0) * GROUP
        t = lax.broadcasted_iota(jnp.int32, (groups, HALO), 1) - HALO
        before = jnp.where(t > g - GROUP, 1.0 / GROUP, 0.0).astype(BF16)
        pooled = jnp.dot(own, layer, preferred_element_type=F32) + jnp.dot(
            before, rim, preferred_element_type=F32
        )
        normed[...] = rms_scaled(pooled.astype(BF16).astype(F32))

    out = jnp.dot(normed[...], w_ref[0], preferred_element_type=F32)

    @pl.when(step == 0)
    def _():
        q_ref[...] = (out * SCALE2).astype(BF16)

    @pl.when(step == 1)
    def _():
        kv_ref[:, :width] = out.astype(BF16)

    @pl.when(step == 2)
    def _():
        kv_ref[:, width:] = out.astype(BF16)


def short_project(total, term, weight3):
    n, d = total.shape[0] - HALO, total.shape[1]
    groups = n // GROUP
    width = weight3.shape[2]
    whole = lambda shape: pl.BlockSpec(shape, lambda i: (0,) * len(shape))
    shapes = [(n, d // 4), (groups, width), (groups, 2 * width)]
    return pl.pallas_call(
        short_project_kernel,
        grid=(3,),
        in_specs=[whole(total.shape), whole(term.shape)]
        + [pl.BlockSpec((1, d, width), lambda i: (i, 0, 0))],
        out_specs=[whole(s) for s in shapes],
        out_shape=[jax.ShapeDtypeStruct(s, BF16) for s in shapes],
        scratch_shapes=[VMEM((groups, d), BF16)],
        compiler_params=params(16),
        cost_estimate=cost(6 * groups * d * width, 2 * (n * d + 3 * d * width)),
        name="short_project",
    )(total, term, weight3)


def short_attend_kernel(slope_ref, *refs):
    queries, key_refs, out_ref = refs[:4], refs[4:8], refs[8]
    y, z, xl = place_of_device()
    blocks, groups, padded = out_ref.shape
    width = padded - HS
    heads = width // HS
    n = blocks * groups
    row = lax.broadcasted_iota(jnp.int32, (n, 1), 0)
    zs = row // groups
    row_pos = (y * 16 + xl + 2 * zs) * groups + row % groups
    back = (z // 2 + 4 - zs // 2) % 4
    came = (2 * back + (zs ^ z) % 2) * groups + row % groups
    order = jnp.where(lax.broadcasted_iota(jnp.int32, (n, n), 1) == came, 1.0, 0.0).astype(BF16)
    lined = jnp.concatenate([r[...] for r in queries], axis=0)
    lined = jnp.dot(order, lined, preferred_element_type=F32).astype(BF16)
    key = lax.broadcasted_iota(jnp.int32, (1, n), 1)
    ys = (y + 4 - key // (2 * groups)) % 4
    side = jnp.where((key // groups) % 2 == 1, 1 - xl, xl)
    key_pos = (ys * 16 + z * 2 + side) * groups + key % groups
    usable = key_pos <= row_pos
    spot = key_pos.astype(F32)
    lane = lax.broadcasted_iota(jnp.int32, (n, HS), 1)
    packed = jnp.zeros((n, HS), F32)
    outs = []
    for h in range(heads):
        cols = slice(h * HS, (h + 1) * HS)
        cols_v = slice(width + h * HS, width + (h + 1) * HS)
        q = lined[:, cols]
        k = jnp.concatenate([r[:, cols] for r in key_refs], axis=0)
        v = jnp.concatenate([r[:, cols_v] for r in key_refs], axis=0)
        s = dot_t(q, k) + (slope_ref[h] * LOG2E) * spot
        s = jnp.where(usable, s, NEG)
        top = jnp.max(s, axis=1, keepdims=True)
        p = jnp.exp2(s - top).astype(BF16)
        both = jnp.dot(p, with_ones(v), preferred_element_type=F32)
        weight_total = both[:, HS:]
        outs.append((both[:, :HS] / weight_total).astype(BF16))
        level = top + jnp.log2(weight_total)
        for k, piece in enumerate(three_parts(level)):
            packed = jnp.where(lane == 3 * h + k, piece, packed)
    out = jnp.concatenate(outs + [packed.astype(BF16)], axis=1)
    out_ref[...] = out.reshape(out_ref.shape)


def short_attend(slopes, queries, keys):
    blocks, groups, width = 8, queries[0].shape[0] // 2, queries[0].shape[1]
    n = blocks * groups
    smem = pl.BlockSpec(memory_space=SMEM)
    vmem = pl.BlockSpec(memory_space=VMEM)
    return pl.pallas_call(
        short_attend_kernel,
        in_specs=[smem] + [vmem] * 8,
        out_specs=vmem,
        out_shape=jax.ShapeDtypeStruct((blocks, groups, width + HS), BF16),
        compiler_params=params(16),
        cost_estimate=cost(4 * n * n * width, 8 * n * width),
        name="short_attend",
    )(slopes, *queries, *keys)


def short_merge_kernel(heads, parts_ref, w_ref, *outs):
    sources, rows, padded = parts_ref.shape
    width = padded - HS
    merged = []
    for h in range(heads):
        cols = slice(h * HS, (h + 1) * HS)
        level = []
        for s in range(sources):
            lev = parts_ref[s, :, width:].astype(F32)
            level.append(
                (lev[:, 3 * h : 3 * h + 1] + lev[:, 3 * h + 1 : 3 * h + 2])
                + lev[:, 3 * h + 2 : 3 * h + 3]
            )
        top = functools.reduce(jnp.maximum, level)
        total = jnp.zeros((rows, 1), F32)
        acc = jnp.zeros((rows, HS), F32)
        for s in range(sources):
            weight = jnp.exp2(level[s] - top)
            total = total + weight
            acc = acc + weight * parts_ref[s, :, cols].astype(F32)
        merged.append((acc / total).astype(BF16))
    att = jnp.concatenate(merged, axis=1)
    cols = outs[0].shape[1]
    terms = [
        jnp.dot(
            att, w_ref[:, t * cols : (t + 1) * cols], preferred_element_type=F32
        ).astype(BF16)
        for t in range(4)
    ]
    tp = lax.axis_index("tp")
    for flip, out in enumerate(outs):
        chosen = terms[flip]
        for t in range(1, 4):
            chosen = jnp.where(tp == t, terms[t ^ flip], chosen)
        out[...] = chosen


def short_merge(parts, weight):
    sources, rows, padded = parts.shape
    width = padded - HS
    cols = weight.shape[1] // 4
    out = jax.ShapeDtypeStruct((rows, cols), BF16)
    return pl.pallas_call(
        functools.partial(short_merge_kernel, width // HS),
        out_shape=[out] * 4,
        compiler_params=params(16),
        cost_estimate=cost(8 * rows * width * cols, 8 * width * cols),
        name="short_merge",
    )(parts, weight)


def final_kernel(lay_ref, *refs):
    terms, out_ref = refs[:-1], refs[-1]
    rows, groups = lay_ref.shape[0], terms[0].shape[0]
    t = lax.broadcasted_iota(jnp.int32, (rows, groups), 0) // GROUP
    g = lax.broadcasted_iota(jnp.int32, (rows, groups), 1)
    spread = jnp.where(t == g, 1.0, 0.0).astype(BF16)
    branch = jnp.zeros(lay_ref.shape, F32)
    for term in terms:
        branch = branch + jnp.dot(spread, term[...], preferred_element_type=F32)
    out_ref[...] = (lay_ref[...].astype(F32) + branch).astype(BF16)


def final_sum(layer, terms):
    rows, cols = layer.shape
    groups = terms[0].shape[0]
    return pl.pallas_call(
        final_kernel,
        out_shape=jax.ShapeDtypeStruct((rows, cols), BF16),
        compiler_params=params(16),
        cost_estimate=cost(8 * rows * cols * groups, 4 * rows * cols),
        name="final_sum",
    )(layer, *terms)


def exchange(blocks, axis):
    return lax.all_to_all(blocks, axis, 0, 0)


def swap(x, axis, flip=1):
    return lax.ppermute(x, axis, [(i, i ^ flip) for i in range(lax.axis_size(axis))])


def moved(x, axis, by):
    n = lax.axis_size(axis)
    return lax.ppermute(x, axis, [(i, (i + by) % n) for i in range(n)])


def both_ways(x, axis, by):
    return moved(x, axis, by), moved(x, axis, -by)


def after(x, *others):
    return lax.optimization_barrier((x, *others))[0]


def on_device(
    tokens,
    project_weight,
    output_weight,
    distance_slope,
    cache_keys,
    cache_values,
    cache_count,
    short_project_weight,
    short_output,
    short_slope,
):
    axes = ("y", "z", "xl", "tp")
    slots = cache_keys.shape[0]
    n, tp = lax.axis_size(axes), lax.axis_size("tp")
    weight3 = jnp.transpose(project_weight, (1, 0, 2))
    q, pack = project(tokens, weight3, cache_keys, cache_values)
    last, live, q, pack = lax.optimization_barrier((tokens, cache_count, q, pack))
    halo = lax.ppermute(last[-HALO:], axes, [(i, i + tp) for i in range(n - tp)])
    count = own_count(live, cache_keys.shape[1])
    other_count = swap(count, "xl")
    marked = mark(halo, weight3, q, count, other_count)
    left, right = both_ways(pack, "y", 1)
    other, left, right, mate = lax.optimization_barrier(
        (swap(pack, "xl"), left, right, swap(marked, "z"))
    )
    pair = join(marked, mate)
    left_other, right_other = both_ways(other, "y", 1)
    left_pair, right_pair = both_ways(pair, "z", 2)
    left_other, right_other, left_pair, right_pair, left = lax.optimization_barrier(
        (left_other, right_other, left_pair, right_pair, left)
    )
    far, far_other = moved(left, "y", 1), moved(right_other, "y", -1)
    near = halves(left_pair, right_pair)
    queries = [pair, left_pair, right_pair, moved(near[0], "z", 2), moved(near[1], "z", -2)]
    crossed = swap(after(output_weight, left), "tp", 2)
    packs = [pack, other, left, left_other, right, right_other, far, far_other]
    plane = plane_counts(queries)
    beside = swap(plane, "y")
    first = span_attend(0, distance_slope, queries, packs, slots)
    plane, beside, first = lax.optimization_barrier((plane, beside, first))
    line = added(plane, beside)
    beyond = swap(line, "y", 2)
    second = span_attend(1, distance_slope, queries, packs, slots)
    second, beyond = lax.optimization_barrier((second, beyond))
    parts = cache_attend(
        distance_slope, queries, packs, (line, beyond), (*first, *second), slots
    )
    parts, crossed = lax.optimization_barrier((parts, crossed))

    att = merge(exchange(parts, "z"))
    total, term = layer_product(
        tokens, halo, (att, swap(att, "tp", 2)), (output_weight, crossed)
    )
    layer, sq, skv = short_project(
        total,
        swap(term, "tp", 1),
        jnp.transpose(short_project_weight, (1, 0, 2)),
    )
    pair = join(sq, swap(sq, "z"))
    queries = [pair] + [moved(pair, "z", by) for by in (2, 4, 6)]
    pair = join(skv, swap(skv, "xl"))
    keys = [pair] + [moved(pair, "y", by) for by in (1, 2, 3)]
    sparts = short_attend(short_slope, queries, keys)
    terms = short_merge(exchange(sparts, "z"), short_output)
    terms = [swap(t, "tp", flip) if flip else t for flip, t in enumerate(terms)]
    return final_sum(layer, terms)


def solution(mesh):
    split = Mesh(mesh.devices.reshape(4, 8, 2, 4), ("y", "z", "xl", "tp"))
    ctx = ("y", "z", "xl")
    return jax.shard_map(
        on_device,
        mesh=split,
        in_specs=(
            P(ctx, None),
            P(None, None, "tp"),
            P("tp", None),
            P("tp"),
            P(ctx, "tp"),
            P(ctx, "tp"),
            P(ctx),
            P(None, None, "tp"),
            P("tp", None),
            P("tp"),
        ),
        out_specs=P(ctx, "tp"),
        check_vma=False,
    )
```
